32 devices in a mesh: parts: 2 (over y), lon: 4 (over z), ch: 2 (over x), sub: 2 (over core).
Axes of the slice: x: 2, y: 2, z: 4, core: 2. Of those that a mesh axis runs over, the one named last changes fastest.
Arguments:
- features: bfloat16 [512, 8192], P('ch', ('parts', 'lon', 'sub')), parts along dimension 1, may hold values from -6 to 6
- cotangent: bfloat16 [512, 8192], P('ch', ('parts', 'lon', 'sub')), parts along dimension 1, may hold values from -6 to 6
- senders: int32 [12, 8192], P(None, ('parts', 'lon', 'sub')), parts along dimension 1, may hold values from 0 to 2047, as said below
- in_degree: int32 [8192], P(('parts', 'lon', 'sub')), parts along dimension 0, may hold values from 1 to 12
- tile_count: int32 [16], P(('parts', 'lon', 'sub')), parts along dimension 0, may hold values from 2 to 4, as said below
- send_tiles: int32 [16, 6, 2], P(('parts', 'lon', 'sub')), parts along dimension 0, may hold values from 0 to 3, as said below
- w_send: bfloat16 [512, 512], replicated, may hold values from -0.25 to 0.25
- w_recv: bfloat16 [512, 512], replicated, may hold values from -0.25 to 0.25
- bias_edge: float32 [512], replicated, may hold values from -4 to 4
- w_msg: bfloat16 [512, 512], replicated, may hold values from -0.25 to 0.25
- w_node_v: bfloat16 [512, 512], replicated, may hold values from -0.1875 to 0.1875
- w_node_a: bfloat16 [512, 512], replicated, may hold values from -0.1875 to 0.1875
- bias_node: float32 [512], replicated, may hold values from -4 to 4
- w_out: bfloat16 [512, 512], replicated, may hold values from -0.25 to 0.25
Outputs:
- updated: bfloat16 [512, 8192], P('ch', ('parts', 'lon', 'sub')), parts along dimension 1
- grad_features: bfloat16 [512, 8192], P('ch', ('parts', 'lon', 'sub')), parts along dimension 1
- grad_w_send: float32 [1024, 512], P(('parts', 'ch'), ('lon', 'sub')), parts along dimension 0
The draws below stay inside these ranges and needn't reach their ends.
There are 2 independent parts, one for each index of `parts`. The reference program is written for one: setup_inputs(seed, part) draws one part's arguments, and reference() takes and returns one part's arrays. A program takes and returns all parts, laid end to end along the dimension named above; an argument that names none is the same for every part. Nothing has to cross between parts.
Inputs may be any that keep to these rules, and one draw needn't show every extreme that they name: `tile_count`: some shard has all 4 tiles active. send_tiles[s, j, :] are active tiles of shard s; for j < 3 they lie in the upper half of its active tiles, else in the lower half; repeats may occur. `senders`: positions below 512 name active nodes of the receiver's own shard.
All inputs are finite; a program needn't handle non-finite values.
Results may differ from the reference program's by a relative error of at most 0.015.
Values may be sent and summed in bfloat16 or wider, within the bound.
No kernel may reach another device: no remote copies, remote signals or barrier semaphores. Data moves between devices by JAX's collectives and lax.ppermute only.
A program may use at most 64 MiB of HBM per device.

```python
import math
import jax
import jax.numpy as jnp
from jax import lax

D = 512
HID = 512
TILE = 128
TILES_DEV = 4
SEND_T = 2
HOPS = 3
DEG = 12
SHARDS = 8
NODES_DEV = 512
NODES = 4096


def band_counts(key):
    lower_bound = TILES_DEV // 2
    counts = jax.random.randint(jax.random.fold_in(key, 101), (SHARDS,), lower_bound, TILES_DEV + 1)
    full_place = jax.random.randint(jax.random.fold_in(key, 102), (), 0, SHARDS)
    return counts.at[full_place].set(TILES_DEV).astype(jnp.int32)


def draw_tile_count(key, part):
    return band_counts(key)


def draw_send_tiles(key, part):
    counts = band_counts(key)
    key = jax.random.fold_in(key, 3)
    raw_bits = jax.random.randint(key, (SHARDS, 2 * HOPS, SEND_T), 0, 1 << 20)
    edge_reach = ((counts + 1) // 2)[:, None, None]
    edge_depth = raw_bits % edge_reach
    eastward = (jnp.arange(2 * HOPS) < HOPS)[None, :, None]
    tile_ids = jnp.where(eastward, counts[:, None, None] - 1 - edge_depth, edge_depth)
    return tile_ids.astype(jnp.int32)


def draw_senders(key, part):
    counts = band_counts(key)
    key = jax.random.fold_in(key, 5)
    key_pick, key_own, key_far = jax.random.split(key, 3)
    shard_of = jnp.arange(NODES) // NODES_DEV
    own_span = counts[shard_of] * TILE
    import_slots = 2 * HOPS * SEND_T * TILE
    choose_kind = jax.random.randint(key_pick, (DEG, NODES), 0, 5)
    own_ids = jax.random.randint(key_own, (DEG, NODES), 0, 1 << 24) % own_span[None, :]
    far_ids = NODES_DEV + jax.random.randint(key_far, (DEG, NODES), 0, import_slots)
    return jnp.where(choose_kind < 3, own_ids, far_ids).astype(jnp.int32)


def with_ends(result, own_key, smallest, top_value):
    longest = result.shape.index(max(result.shape))
    spots = []
    for shift in (0, 1):
        where = [jax.random.randint(jax.random.fold_in(own_key, axis), (), 0, length) for axis, length in enumerate(result.shape)]
        where[longest] = (where[longest] + shift) % result.shape[longest]
        spots.append(tuple(where))
    return result.at[spots[0]].set(smallest).at[spots[1]].set(top_value)


def steps_of(stream_key, shape, cuts, least, high):
    def one(position, parts):
        draws = jax.random.uniform(jax.random.fold_in(jax.random.fold_in(stream_key, 6), position), (parts,), jnp.float32, least / len(cuts), high / len(cuts))
        return jnp.repeat(jnp.exp(draws), shape[position] // parts).reshape((-1,) + (1,) * (len(shape) - position - 1))

    factor_of = one(*cuts[0])
    for cut in cuts[1:]:
        factor_of = factor_of * one(*cut)
    return factor_of


def centred(stream_key, dims, width, reach, cuts=(), kind=jnp.bfloat16):
    gain = steps_of(stream_key, dims, cuts, -0.22, 0.18) if cuts else 1.0
    entries = jax.random.normal(stream_key, dims, jnp.float32) * width * gain
    return jnp.minimum(jnp.maximum(entries, -reach), reach).astype(kind)


def setup_inputs(seed: int = 0, part: int = 0) -> dict:
    keys = jax.random.split(jax.random.key(seed), 15)
    part_splits = jax.random.split(jax.random.fold_in(keys[14], part), 15)
    features = centred(part_splits[0], (D, NODES), 1.0, 6.0, ((0, 2), (1, 8)))
    cotangent = centred(part_splits[1], (D, NODES), 1.0, 6.0, ((0, 2), (1, 8)))
    senders = draw_senders(jax.random.fold_in(jax.random.fold_in(keys[14], part), 71), part)
    in_degree = with_ends(jax.random.randint(part_splits[3], (NODES,), 1, DEG + 1), jax.random.fold_in(part_splits[3], 1), 1, DEG).astype(jnp.int32)
    tile_count = draw_tile_count(jax.random.fold_in(jax.random.fold_in(keys[14], part), 71), part)
    send_tiles = draw_send_tiles(jax.random.fold_in(jax.random.fold_in(keys[14], part), 71), part)
    w_send = centred(keys[6], (HID, D), D ** -0.5, 0.25)
    w_recv = centred(keys[7], (HID, D), D ** -0.5, 0.25)
    bias_edge = centred(keys[8], (HID,), 1.0, 4.0, (), jnp.float32)
    w_msg = centred(keys[9], (D, HID), HID ** -0.5, 0.25)
    w_node_v = centred(keys[10], (HID, D), (2 * D) ** -0.5, 0.1875)
    w_node_a = centred(keys[11], (HID, D), (2 * D) ** -0.5, 0.1875)
    bias_node = centred(keys[12], (HID,), 1.0, 4.0, (), jnp.float32)
    w_out = centred(keys[13], (D, HID), HID ** -0.5, 0.25)
    return dict(features=features, cotangent=cotangent, senders=senders, in_degree=in_degree, tile_count=tile_count, send_tiles=send_tiles, w_send=w_send, w_recv=w_recv, bias_edge=bias_edge, w_msg=w_msg, w_node_v=w_node_v, w_node_a=w_node_a, bias_node=bias_node, w_out=w_out)


def swish_grad(pre_value):
    sigmoid_v = jax.nn.sigmoid(pre_value)
    return sigmoid_v * (1.0 + pre_value * (1.0 - sigmoid_v))

def reference(features, cotangent, senders, in_degree, tile_count, send_tiles, w_send, w_recv, bias_edge, w_msg, w_node_v, w_node_a, bias_node, w_out):
    total_nodes = NODES_DEV * SHARDS
    offsets = [number + 1 for number in range(HOPS)] + [-(number + 1) for number in range(HOPS)]
    local_ids = jnp.arange(NODES_DEV, dtype=jnp.int32)
    tile_span = jnp.arange(TILE, dtype=jnp.int32)
    active = ((local_ids // TILE)[None, :] < tile_count[:, None]).reshape(-1)
    active_f = active.astype(jnp.float32)
    proj_send = jnp.dot(w_send, features, preferred_element_type=jnp.float32).astype(jnp.bfloat16)
    proj_recv = jnp.dot(w_recv, features, preferred_element_type=jnp.float32).astype(jnp.bfloat16)

    def edge_terms(shard_idx):
        pieces = [shard_idx * NODES_DEV + local_ids]
        for slot_idx, offset in enumerate(offsets):
            source = (shard_idx - offset) % SHARDS
            chosen = send_tiles[source, slot_idx]
            pieces.append((source * NODES_DEV + chosen[:, None] * TILE + tile_span[None, :]).reshape(-1).astype(jnp.int32))
        ext_ids = jnp.concatenate(pieces).astype(jnp.int32)
        local_send = lax.dynamic_slice_in_dim(senders, shard_idx * NODES_DEV, NODES_DEV, 1)
        global_ids = ext_ids[local_send]
        recv_rows = lax.dynamic_slice_in_dim(proj_recv, shard_idx * NODES_DEV, NODES_DEV, 1)
        edge_pre = proj_send[:, global_ids].astype(jnp.float32) + recv_rows.astype(jnp.float32)[:, None, :] + bias_edge[:, None, None]
        degree_rows = lax.dynamic_slice_in_dim(in_degree, shard_idx * NODES_DEV, NODES_DEV, 0)
        active_rows = lax.dynamic_slice_in_dim(active, shard_idx * NODES_DEV, NODES_DEV, 0)
        edge_valid = (jnp.arange(DEG, dtype=jnp.int32)[:, None] < degree_rows[None, :]) & active_rows[None, :]
        return (global_ids, edge_pre, edge_valid, degree_rows.astype(jnp.float32))

    def shard_message(shard_idx):
        global_ids, edge_pre, edge_valid, degree_rows = edge_terms(shard_idx)
        summed = lax.optimization_barrier(jnp.sum(jnp.where(edge_valid[None], jax.nn.silu(edge_pre), 0.0), axis=1))
        return (summed / degree_rows[None, :]).astype(jnp.bfloat16)
    shard_ids = jnp.arange(SHARDS, dtype=jnp.int32)
    message = jnp.transpose(lax.map(shard_message, shard_ids), (1, 0, 2)).reshape(HID, total_nodes)
    aggregate = jnp.dot(w_msg, message, preferred_element_type=jnp.float32).astype(jnp.bfloat16)
    node_pre = jnp.dot(w_node_v, features, preferred_element_type=jnp.float32) + jnp.dot(w_node_a, aggregate, preferred_element_type=jnp.float32) + bias_node[:, None]
    node_hidden = jax.nn.silu(node_pre).astype(jnp.bfloat16)
    node_out = jnp.dot(w_out, node_hidden, preferred_element_type=jnp.float32)
    updated = (features.astype(jnp.float32) + active_f[None, :] * node_out).astype(jnp.bfloat16)
    masked_cot = cotangent * active.astype(jnp.bfloat16)[None, :]
    grad_hidden = jnp.dot(w_out.T, masked_cot, preferred_element_type=jnp.float32)
    grad_pre = (grad_hidden * swish_grad(node_pre)).astype(jnp.bfloat16)
    grad_agg = jnp.dot(w_node_a.T, grad_pre, preferred_element_type=jnp.float32).astype(jnp.bfloat16)
    grad_msg = jnp.dot(w_msg.T, grad_agg, preferred_element_type=jnp.float32).astype(jnp.bfloat16)

    def shard_grads(grad_acc, shard_idx):
        global_ids, edge_pre, edge_valid, degree_rows = edge_terms(shard_idx)
        grad_rows = lax.dynamic_slice_in_dim(grad_msg, shard_idx * NODES_DEV, NODES_DEV, 1).astype(jnp.float32) / degree_rows[None, :]
        grad_edge = jnp.where(edge_valid[None], grad_rows[:, None, :] * swish_grad(edge_pre), 0.0)
        grad_acc = grad_acc.at[:, global_ids.reshape(-1)].add(grad_edge.reshape(HID, -1))
        return (grad_acc, lax.optimization_barrier(jnp.sum(grad_edge, axis=1)))
    grad_send_acc, grad_recv_parts = lax.scan(shard_grads, jnp.zeros((HID, total_nodes), jnp.float32), shard_ids)
    grad_send = grad_send_acc.astype(jnp.bfloat16)
    grad_recv = jnp.transpose(grad_recv_parts, (1, 0, 2)).reshape(HID, total_nodes).astype(jnp.bfloat16)
    grad_features = (cotangent.astype(jnp.float32) + jnp.dot(w_node_v.T, grad_pre, preferred_element_type=jnp.float32) + jnp.dot(w_send.T, grad_send, preferred_element_type=jnp.float32) + jnp.dot(w_recv.T, grad_recv, preferred_element_type=jnp.float32)).astype(jnp.bfloat16)
    grad_w_send = jnp.dot(grad_send, features.T, preferred_element_type=jnp.float32) * (1.0 / math.sqrt(total_nodes))
    return (updated, grad_features, grad_w_send)
```

```python
import functools
import math

import jax
import jax.numpy as jnp
from jax import lax
from jax.experimental import pallas as pl
from jax.experimental.pallas import tpu as pltpu
from jax.sharding import PartitionSpec as P

TILE = 128
CHUNK = 256
LANES = 128
PACK = 16
MIB = 1 << 20


def shifted(block, axis, distance):
    size = lax.axis_size(axis)
    route = [((i - distance) % size, i) for i in range(size)]
    return lax.ppermute(block, axis, route)


def gathered(block, axis):
    return [block] + [shifted(block, axis, k) for k in range(1, lax.axis_size(axis))]


def dot(left, right):
    return jnp.dot(left, right, preferred_element_type=jnp.float32)


def dot_nt(left, right):
    return lax.dot_general(
        left, right, (((1,), (1,)), ((), ())), preferred_element_type=jnp.float32
    )


def sigmoid(value):
    return 0.5 * jnp.tanh(0.5 * value) + 0.5


def call(kernel, out_shape, operands, flops, scratch=(), scalars=1, limit=32):
    vmem = pl.BlockSpec(memory_space=pltpu.VMEM)
    smem = pl.BlockSpec(memory_space=pltpu.SMEM)
    moved = sum(math.prod(x.shape) * x.dtype.itemsize for x in operands)
    return pl.pallas_call(
        kernel,
        out_shape=out_shape,
        in_specs=[smem] * scalars + [vmem] * (len(operands) - scalars),
        out_specs=jax.tree.map(lambda _: vmem, out_shape),
        scratch_shapes=scratch,
        compiler_params=pltpu.CompilerParams(vmem_limit_bytes=limit * MIB),
        cost_estimate=pl.CostEstimate(flops=flops, bytes_accessed=moved, transcendentals=0),
    )(*operands)


def assemble(whole_ref, blocks, first):
    count = len(blocks)
    rows = blocks[0].shape[0]
    for k, block in enumerate(blocks):
        place = lax.rem(first - k + count, count) * rows
        whole_ref[pl.ds(pl.multiple_of(place, rows), rows), :] = block[...]


def project_kernel(count, info, *refs):
    blocks = refs[:count]
    w_send, w_recv, bias, feats, proj, base, parcels = refs[count:]
    assemble(feats, blocks, info[0])
    whole = feats[...]
    proj[...] = dot(w_send[...], whole).T.astype(jnp.bfloat16)
    base[...] = (dot(w_recv[...], whole).astype(jnp.bfloat16).astype(jnp.float32) + bias[...]).T
    slots, rows, _ = parcels.shape
    per_slot = rows // TILE
    for slot in range(slots):
        for place in range(per_slot):
            tile = info[2 + slot * per_slot + place]
            parcels[slot, place * TILE : (place + 1) * TILE, :] = proj[
                pl.ds(pl.multiple_of(tile * TILE, TILE), TILE), :
            ]


def prepare_kernel(count, info, *refs):
    blocks = refs[:count]
    feats, w_node_v, bias, w_out_t, cots, pre, grad_hidden = refs[count:]
    assemble(cots, blocks, info[0])
    pre[...] = dot(w_node_v[...], feats[...]) + bias[...]
    lane = lax.broadcasted_iota(jnp.int32, (1, cots.shape[1]), 1)
    active = (lane < info[1] * TILE).astype(jnp.bfloat16)
    grad_hidden[...] = dot(w_out_t[...], cots[...] * active)


def forward_kernel(slots, low, high, base, inv_deg, proj, *refs):
    arrivals = refs[:slots]
    message, slope, ext, total = refs[slots:]
    own = proj.shape[0]
    rows = arrivals[0].shape[0]
    ext[:own, :] = proj[...]
    for slot in range(slots):
        ext[own + slot * rows : own + (slot + 1) * rows, :] = arrivals[slot][...]
    chunks = ext.shape[0] // CHUNK
    halves = CHUNK // LANES
    total[...] = jnp.zeros_like(total)
    lane = lax.broadcasted_iota(jnp.int32, (own, LANES), 1)

    def step(m, carry):
        low_m, high_m = low[m], high[m]
        one = jnp.bfloat16(1.0)
        zero = jnp.bfloat16(0.0)
        marks = [
            jnp.where(low_m == (lane + half * LANES).astype(jnp.bfloat16), one, zero)
            for half in range(halves)
        ]
        picker = jnp.concatenate(
            [
                jnp.where(high_m == jnp.bfloat16(chunk), mark, zero)
                for chunk in range(chunks)
                for mark in marks
            ],
            axis=1,
        )
        pre = dot(picker, ext[...]) + base[...]
        valid = high_m[:, :1].astype(jnp.float32) < chunks
        sig = sigmoid(pre)
        act = pre * sig
        total[...] += jnp.where(valid, act, 0.0)
        slope[m] = jnp.where(valid, sig + act * (1.0 - sig), 0.0).astype(jnp.bfloat16)
        return carry

    lax.fori_loop(0, low.shape[0], step, 0)
    message[...] = (total[...] * inv_deg[...]).astype(jnp.bfloat16)


def node_kernel(count, inv_deg, *refs):
    blocks = refs[:count]
    w_msg, w_node_a, w_node_a_t, w_msg_t, pre, grad_hidden, hidden, grad_pre, scale = refs[count:]
    agg = dot_nt(w_msg[0], blocks[0][...])
    for k in range(1, count):
        agg += dot_nt(w_msg[k], blocks[k][...])
    node_pre = pre[...] + dot(w_node_a[...], agg.astype(jnp.bfloat16))
    sig = sigmoid(node_pre)
    act = node_pre * sig
    hidden[...] = act.astype(jnp.bfloat16)
    low_grad = (grad_hidden[...] * (sig + act * (1.0 - sig))).astype(jnp.bfloat16)
    grad_pre[...] = low_grad
    grad_agg = dot(w_node_a_t[...], low_grad).astype(jnp.bfloat16)
    grad_msg = dot(w_msg_t[...], grad_agg)
    scale[...] = (grad_msg.astype(jnp.bfloat16).astype(jnp.float32) * inv_deg[...]).T


def far_kernel(low, high, slope, scale, *refs):
    outs, (grads, recv, total, recv_total) = refs[:-4], refs[-4:]
    slots = len(outs)
    rows = outs[0].shape[0]
    nodes = scale.shape[0]
    first = nodes // CHUNK
    chunks = slots * rows // CHUNK
    total[...] = jnp.zeros_like(total)
    recv_total[...] = jnp.zeros_like(recv_total)
    groups = CHUNK // PACK
    place = lax.broadcasted_iota(jnp.int32, (groups, PACK, nodes), 0) * PACK
    place = place + lax.broadcasted_iota(jnp.int32, (groups, PACK, nodes), 1)

    def step(m, carry):
        grad = slope[m].astype(jnp.float32) * scale[...]
        recv_total[...] += grad
        grad_low = grad.astype(jnp.bfloat16)
        grads[m] = grad_low
        one = jnp.bfloat16(1.0)
        zero = jnp.bfloat16(0.0)
        mark = jnp.where(low[m][None] == place.astype(jnp.bfloat16), one, zero)
        picker = jnp.concatenate(
            [
                jnp.where(high[m][None] == jnp.bfloat16(first + chunk), mark, zero)
                for chunk in range(chunks)
            ],
            axis=0,
        ).reshape(chunks * CHUNK, nodes)
        total[...] += dot(picker, grad_low)
        return carry

    lax.fori_loop(0, slope.shape[0], step, 0)
    for slot in range(slots):
        outs[slot][...] = total[slot * rows : (slot + 1) * rows, :].astype(jnp.bfloat16)
    recv[...] = recv_total[...].astype(jnp.bfloat16)


def own_kernel(low, high, grads, total):
    nodes = total.shape[0]
    chunks = nodes // CHUNK
    groups = CHUNK // PACK
    total[...] = jnp.zeros_like(total)
    place = lax.broadcasted_iota(jnp.int32, (groups, PACK, nodes), 0) * PACK
    place = place + lax.broadcasted_iota(jnp.int32, (groups, PACK, nodes), 1)

    def step(m, carry):
        one = jnp.bfloat16(1.0)
        zero = jnp.bfloat16(0.0)
        mark = jnp.where(low[m][None] == place.astype(jnp.bfloat16), one, zero)
        picker = jnp.concatenate(
            [
                jnp.where(high[m][None] == jnp.bfloat16(chunk), mark, zero)
                for chunk in range(chunks)
            ],
            axis=0,
        ).reshape(chunks * CHUNK, nodes)
        total[...] += dot(picker, grads[m])
        return carry

    lax.fori_loop(0, grads.shape[0], step, 0)


def output_kernel(info, feats, cots, hidden, grad_pre, w_out, w_node_v_t, updated, direct):
    lane = lax.broadcasted_iota(jnp.int32, (1, feats.shape[1]), 1)
    active = (lane < info[1] * TILE).astype(jnp.float32)
    updated[...] = (
        feats[...].astype(jnp.float32) + active * dot(w_out[...], hidden[...])
    ).astype(jnp.bfloat16)
    direct[...] = cots[...].astype(jnp.float32) + dot(w_node_v_t[...], grad_pre[...])


def final_kernel(inv_root, info, own, recv, direct, feats, w_send_t, w_recv_t, *refs):
    returned, (kept, sent, weight, total) = refs[:-4], refs[-4:]
    total[...] = own[...]
    per_slot = returned[0].shape[0] // TILE
    for slot, block in enumerate(returned):
        for place in range(per_slot):
            tile = info[2 + slot * per_slot + place]
            rows = pl.ds(pl.multiple_of(tile * TILE, TILE), TILE)
            total[rows, :] += block[place * TILE : (place + 1) * TILE, :].astype(jnp.float32)
    grad_send = total[...].T.astype(jnp.bfloat16)
    grad_recv = recv[...].astype(jnp.float32).T.astype(jnp.bfloat16)
    chans = direct.shape[0]
    terms = dot(w_send_t[...], grad_send) + dot(w_recv_t[...], grad_recv)
    kept[...] = direct[...] + terms[:chans]
    for k in range(sent.shape[0]):
        sent[k] = terms[(k + 1) * chans : (k + 2) * chans].astype(jnp.bfloat16)
    weight[...] = (dot_nt(grad_send, feats[...]) * inv_root).astype(jnp.bfloat16)


def shards(
    features,
    cotangent,
    senders,
    in_degree,
    tile_count,
    send_tiles,
    w_send,
    w_recv,
    bias_edge,
    w_msg,
    w_node_v,
    w_node_a,
    bias_node,
    w_out,
):
    chans, nodes = features.shape
    count = lax.axis_size("ch")
    mine = lax.axis_index("ch")
    hidden_all, chans_all = w_send.shape
    hid = hidden_all // count
    hid_start = mine * hid
    chan_start = mine * chans
    cycle = ("lon", "sub")
    shard_count = lax.axis_size(cycle)
    total_nodes = nodes * shard_count
    degree = senders.shape[0]
    hop_count = send_tiles.shape[1] // 2
    slots = 2 * hop_count
    slot_rows = send_tiles.shape[2] * TILE
    offsets = [number + 1 for number in range(hop_count)] + [
        -(number + 1) for number in range(hop_count)
    ]
    ext_len = nodes + slots * slot_rows
    chunks = ext_len // CHUNK
    bf16, f32 = jnp.bfloat16, jnp.float32
    shape = jax.ShapeDtypeStruct

    info = jnp.concatenate(
        [mine.reshape(1).astype(jnp.int32), tile_count, send_tiles.reshape(-1)]
    )
    feat_blocks = gathered(features, "ch")
    cot_blocks = gathered(cotangent, "ch")

    rows_of = lambda w, k: lax.dynamic_slice_in_dim(w, (mine + k) % count * hid, hid, 0)
    cols_of = lambda w, k: lax.dynamic_slice_in_dim(w, (mine + k) % count * hid, hid, 1)
    w_send_my, w_recv_my = rows_of(w_send, 0), rows_of(w_recv, 0)
    bias_my = lax.dynamic_slice_in_dim(bias_edge, hid_start, hid, 0)[:, None]
    roll = lambda w: jnp.concatenate(
        [
            lax.dynamic_slice_in_dim(w, (mine + k) % count * chans, chans, 0)
            for k in range(count)
        ],
        axis=0,
    )
    w_send_t, w_recv_t = roll(w_send_my.T), roll(w_recv_my.T)
    w_msg_rolled = jnp.stack([cols_of(w_msg, (count - k) % count) for k in range(count)])
    w_msg_t = cols_of(w_msg, 0).T
    w_out_my = lax.dynamic_slice_in_dim(w_out, chan_start, chans, 0)
    w_node_v_t = lax.dynamic_slice_in_dim(w_node_v, chan_start, chans, 1).T

    active = jnp.arange(nodes) < tile_count[0] * TILE
    valid = (jnp.arange(degree)[:, None] < in_degree[None, :]) & active[None, :]
    low = (senders % CHUNK).astype(bf16)
    high = jnp.where(valid, senders // CHUNK, chunks).astype(bf16)
    low_cols = jnp.broadcast_to(low[:, :, None], (degree, nodes, LANES))
    high_cols = jnp.broadcast_to(high[:, :, None], (degree, nodes, LANES))
    low_rows = jnp.broadcast_to(low[:, None, :], (degree, PACK, nodes))
    high_rows = jnp.broadcast_to(high[:, None, :], (degree, PACK, nodes))
    inv_deg = 1.0 / in_degree.astype(f32)

    feats, proj, base, parcels = call(
        functools.partial(project_kernel, count),
        (
            shape((chans_all, nodes), bf16),
            shape((nodes, hid), bf16),
            shape((nodes, hid), f32),
            shape((slots, slot_rows, hid), bf16),
        ),
        [info] + feat_blocks + [w_send_my, w_recv_my, bias_my],
        flops=4 * hid * chans_all * nodes,
    )
    arrivals = [shifted(parcels[slot], cycle, offsets[slot]) for slot in range(slots)]

    cots, pre, grad_hidden = call(
        functools.partial(prepare_kernel, count),
        (
            shape((chans_all, nodes), bf16),
            shape((hidden_all, nodes), f32),
            shape((hidden_all, nodes), f32),
        ),
        [info] + cot_blocks + [feats, w_node_v, bias_node[:, None], w_out.T],
        flops=4 * hidden_all * chans_all * nodes,
    )

    message, slope = call(
        functools.partial(forward_kernel, slots),
        (shape((nodes, hid), bf16), shape((degree, nodes, hid), bf16)),
        [low_cols, high_cols, base, inv_deg[:, None], proj] + arrivals,
        flops=2 * degree * nodes * ext_len * hid,
        scratch=[pltpu.VMEM((ext_len, hid), bf16), pltpu.VMEM((nodes, hid), f32)],
        scalars=0,
    )
    messages = gathered(message, "ch")

    hidden, grad_pre, scale = call(
        functools.partial(node_kernel, count),
        (
            shape((hidden_all, nodes), bf16),
            shape((hidden_all, nodes), bf16),
            shape((nodes, hid), f32),
        ),
        [inv_deg[None, :]]
        + messages
        + [w_msg_rolled, w_node_a, w_node_a.T, w_msg_t, pre, grad_hidden],
        flops=6 * hidden_all * chans_all * nodes,
        scalars=0,
    )

    *far, grads, grad_recv = call(
        far_kernel,
        (
            *[shape((slot_rows, hid), bf16)] * slots,
            shape((degree, nodes, hid), bf16),
            shape((nodes, hid), bf16),
        ),
        [low_rows, high_rows, slope, scale],
        flops=2 * degree * nodes * (ext_len - nodes) * hid,
        scratch=[pltpu.VMEM((ext_len - nodes, hid), f32), pltpu.VMEM((nodes, hid), f32)],
        scalars=0,
    )
    returned = [shifted(far[slot], cycle, -offsets[slot]) for slot in range(slots)]

    own = call(
        own_kernel,
        shape((nodes, hid), f32),
        [low_rows, high_rows, grads],
        flops=2 * degree * nodes * nodes * hid,
        scalars=0,
    )
    updated, direct = call(
        output_kernel,
        (shape((chans, nodes), bf16), shape((chans, nodes), f32)),
        [info, features, cotangent, hidden, grad_pre, w_out_my, w_node_v_t],
        flops=4 * hidden_all * chans * nodes,
    )

    kept, sent, weight = call(
        functools.partial(final_kernel, 1.0 / math.sqrt(total_nodes)),
        (
            shape((chans, nodes), f32),
            shape((count - 1, chans, nodes), bf16),
            shape((hid, chans_all), bf16),
        ),
        [info, own, grad_recv, direct, feats, w_send_t, w_recv_t] + returned,
        flops=6 * hid * chans_all * nodes,
        scratch=[pltpu.VMEM((nodes, hid), f32)],
    )
    for k in range(1, count):
        kept = kept + shifted(sent[k - 1], "ch", k).astype(f32)
    grad_features = kept.astype(bf16)

    columns = chans_all // shard_count
    weight_terms = jnp.moveaxis(weight.reshape(hid, shard_count, columns), 1, 0)
    weight_terms = lax.all_to_all(weight_terms, cycle, split_axis=0, concat_axis=0)
    grad_w_send = jnp.sum(weight_terms.astype(f32), axis=0)
    return (updated, grad_features, grad_w_send)


def solution(mesh):
    nodes_last = P("ch", ("parts", "lon", "sub"))
    spread = ("parts", "lon", "sub")
    placed = (nodes_last, nodes_last, P(None, spread), P(spread), P(spread), P(spread, None, None))
    return jax.shard_map(
        shards,
        mesh=mesh,
        in_specs=placed + (P(),) * 8,
        out_specs=(nodes_last, nodes_last, P(("parts", "ch"), ("lon", "sub"))),
        check_vma=False,
    )
```

```python
import functools
import math

import jax
import jax.numpy as jnp
from jax import lax
from jax.experimental import pallas as pl
from jax.experimental.pallas import tpu as pltpu
from jax.sharding import PartitionSpec as P

TILE = 128
CHUNK = 256
LANES = 128
PACK = 16
MIB = 1 << 20
NO_CHUNK = 64
CH, TILES, SUB, FIRST, LON, PLACES, PICKS = 0, 1, 2, 3, 4, 5, 11


def shifted(block, axis, distance):
    size = lax.axis_size(axis)
    route = [((i - distance) % size, i) for i in range(size)]
    return lax.ppermute(block, axis, route)


def gathered(block, axis):
    return [block] + [shifted(block, axis, k) for k in range(1, lax.axis_size(axis))]


def dot(left, right):
    return jnp.dot(left, right, preferred_element_type=jnp.float32)


def dot_nt(left, right):
    return lax.dot_general(
        left, right, (((1,), (1,)), ((), ())), preferred_element_type=jnp.float32
    )


def sigmoid(value):
    return 0.5 * jnp.tanh(0.5 * value) + 0.5


def call(kernel, out_shape, operands, flops, scratch=(), scalars=1, limit=32):
    vmem = pl.BlockSpec(memory_space=pltpu.VMEM)
    smem = pl.BlockSpec(memory_space=pltpu.SMEM)
    moved = sum(math.prod(x.shape) * x.dtype.itemsize for x in operands)
    return pl.pallas_call(
        kernel,
        out_shape=out_shape,
        in_specs=[smem] * scalars + [vmem] * (len(operands) - scalars),
        out_specs=jax.tree.map(lambda _: vmem, out_shape),
        scratch_shapes=scratch,
        compiler_params=pltpu.CompilerParams(vmem_limit_bytes=limit * MIB),
        cost_estimate=pl.CostEstimate(flops=flops, bytes_accessed=moved, transcendentals=0),
    )(*operands)


def assemble(whole_ref, blocks, first):
    count = len(blocks)
    rows = blocks[0].shape[0]
    for k, block in enumerate(blocks):
        place = lax.rem(first - k + count, count) * rows
        whole_ref[pl.ds(pl.multiple_of(place, rows), rows), :] = block[...]


def mine_of(ref, index, rows):
    return ref[pl.ds(pl.multiple_of(index * rows, rows), rows), :]


def weights_kernel(
    info,
    senders,
    in_degree,
    w_send,
    w_recv,
    w_msg,
    w_node_v,
    w_node_a,
    w_out,
    w_send_t,
    w_recv_t,
    w_msg_t,
    w_node_v_t,
    w_node_a_t,
    w_out_t,
    low_cols,
    high_cols,
    low_rows,
    high_rows,
    turned,
):
    mine, tiles = info[CH], info[TILES]
    hid = w_send_t.shape[1]
    w_send_t[...] = mine_of(w_send, mine, hid).T
    w_recv_t[...] = mine_of(w_recv, mine, hid).T
    w_out_t[...] = w_out[...].T
    w_node_a_t[...] = w_node_a[...].T
    turned[...] = w_msg[...].T
    w_msg_t[...] = mine_of(turned, mine, hid)
    turned[...] = w_node_v[...].T
    w_node_v_t[...] = mine_of(turned, mine, w_node_v_t.shape[0])

    degree, nodes = senders.shape
    lane = lax.broadcasted_iota(jnp.int32, (degree, nodes), 1)
    row = lax.broadcasted_iota(jnp.int32, (degree, nodes), 0)
    valid = (row < in_degree[...]) & (lane < tiles * TILE)
    ids = senders[...]
    low = (ids & (CHUNK - 1)).astype(jnp.float32)
    high = jnp.where(valid, ids // CHUNK, NO_CHUNK).astype(jnp.float32)
    for m in range(degree):
        shape = (PACK, nodes)
        low_rows[m] = jnp.broadcast_to(low[m : m + 1], shape).astype(jnp.bfloat16)
        high_rows[m] = jnp.broadcast_to(high[m : m + 1], shape).astype(jnp.bfloat16)
    fill = jnp.zeros((PACK - degree, nodes), jnp.float32)
    depth = 2 * PACK
    both = jnp.concatenate([low, fill, high, fill], axis=0).T.astype(jnp.bfloat16)
    width = degree * LANES
    spot = lax.broadcasted_iota(jnp.int32, (depth, width), 0)
    group = lax.broadcasted_iota(jnp.int32, (depth, width), 1) // LANES
    for first, out in ((0, low_cols), (PACK, high_cols)):
        pick = (spot == group + first).astype(jnp.bfloat16)
        spread = dot(both, pick).astype(jnp.bfloat16)
        for m in range(degree):
            out[m] = spread[:, m * LANES : (m + 1) * LANES]


def project_kernel(count, info, bias, *refs):
    blocks = refs[:count]
    w_send, w_recv, feats, proj, base, upper, lower, cross, beside = refs[count:]
    mine, sub, first = info[CH], info[SUB], info[FIRST]
    assemble(feats, blocks, mine)
    whole = feats[...]
    hid = proj.shape[1]
    proj[...] = dot(mine_of(w_send, mine, hid), whole).T.astype(jnp.bfloat16)
    my_bias = jnp.zeros((1, hid), jnp.float32)
    for k in range(count):
        my_bias += jnp.where(mine == k, bias[:, k * hid : (k + 1) * hid], 0.0)
    recv = dot(mine_of(w_recv, mine, hid), whole).T
    base[...] = recv.astype(jnp.bfloat16).astype(jnp.float32) + my_bias
    rows = upper.shape[0] - PACK
    upper[:rows, :] = proj[pl.ds(pl.multiple_of(first * TILE, TILE), rows), :]
    lower[:rows, :] = proj[:rows, :]
    spot = lax.broadcasted_iota(jnp.int32, (PACK, hid), 0)
    half = info.shape[0] - PICKS
    half = half // 2
    for start, out in ((0, upper), (half, lower)):
        marks = jnp.zeros((PACK, hid), jnp.float32)
        for k in range(half):
            rel = info[PICKS + start + k]
            marks = jnp.where(spot == k, rel.astype(jnp.float32), marks)
        out[rows:, :] = marks.astype(jnp.bfloat16)

    @pl.when(sub == 0)
    def _():
        cross[...] = lower[...]
        beside[...] = upper[...]

    @pl.when(sub != 0)
    def _():
        cross[...] = upper[...]
        beside[...] = lower[...]


def prepare_kernel(count, info, *refs):
    blocks = refs[:count]
    feats, w_node_v, bias, w_out_t, cots, pre, grad_hidden = refs[count:]
    assemble(cots, blocks, info[CH])
    column = jnp.broadcast_to(bias[...], (8, bias.shape[1])).T[:, :1]
    pre[...] = dot(w_node_v[...], feats[...]) + column
    lane = lax.broadcasted_iota(jnp.int32, (1, cots.shape[1]), 1)
    active = (lane < info[TILES] * TILE).astype(jnp.bfloat16)
    grad_hidden[...] = dot(w_out_t[...], cots[...] * active)


def forward_kernel(info, low, high, base, in_degree, proj, *refs):
    arrivals = refs[:6]
    message, slope, rels, ext, total, held = refs[6:]
    own = proj.shape[0]
    rows = held.shape[1] - PACK
    per_slot = rows // TILE
    slots = len(arrivals)
    ext[:own, :] = proj[...]
    for place, block in enumerate(arrivals):
        held[place] = block[...]
    rels[...] = jnp.zeros_like(rels)
    for slot in range(slots):
        place = info[PLACES + slot]
        group = slot % (slots // 2)
        for t in range(per_slot):
            index = group * per_slot + t
            rel = held[place, rows : rows + PACK, :][index : index + 1, :].astype(jnp.float32)
            number = slot * per_slot + t
            rels[number : number + 1, :] = rel
            start = own + number * TILE
            ext[start : start + TILE, :] = jnp.where(
                rel > 0.5, held[place, TILE : 2 * TILE, :], held[place, :TILE, :]
            )
    chunks = ext.shape[0] // CHUNK
    halves = CHUNK // LANES
    total[...] = jnp.zeros_like(total)
    lane = lax.broadcasted_iota(jnp.int32, (own, LANES), 1)

    def step(m, carry):
        low_m, high_m = low[m], high[m]
        one = jnp.bfloat16(1.0)
        zero = jnp.bfloat16(0.0)
        marks = [
            jnp.where(low_m == (lane + half * LANES).astype(jnp.bfloat16), one, zero)
            for half in range(halves)
        ]
        picker = jnp.concatenate(
            [
                jnp.where(high_m == jnp.bfloat16(chunk), mark, zero)
                for chunk in range(chunks)
                for mark in marks
            ],
            axis=1,
        )
        pre = dot(picker, ext[...]) + base[...]
        valid = high_m[:, :1].astype(jnp.float32) < chunks
        sig = sigmoid(pre)
        act = pre * sig
        total[...] += jnp.where(valid, act, 0.0)
        slope[m] = jnp.where(valid, sig + act * (1.0 - sig), 0.0).astype(jnp.bfloat16)
        return carry

    lax.fori_loop(0, low.shape[0], step, 0)
    degree = in_degree[...].astype(jnp.float32)
    message[...] = (total[...].T / degree).astype(jnp.bfloat16)


def node_kernel(count, info, in_degree, *refs):
    blocks = refs[:count]
    w_msg, w_node_a, w_node_a_t, w_msg_t, pre, grad_hidden = refs[count : count + 6]
    hidden, grad_pre, scale, messages = refs[count + 6 :]
    assemble(messages, blocks, info[CH])
    agg = dot(w_msg[...], messages[...])
    node_pre = pre[...] + dot(w_node_a[...], agg.astype(jnp.bfloat16))
    sig = sigmoid(node_pre)
    act = node_pre * sig
    hidden[...] = act.astype(jnp.bfloat16)
    low_grad = (grad_hidden[...] * (sig + act * (1.0 - sig))).astype(jnp.bfloat16)
    grad_pre[...] = low_grad
    grad_agg = dot(w_node_a_t[...], low_grad).astype(jnp.bfloat16)
    grad_msg = dot(w_msg_t[...], grad_agg).astype(jnp.bfloat16).astype(jnp.float32)
    scale[...] = (grad_msg / in_degree[...].astype(jnp.float32)).T


def far_kernel(info, low, high, slope, scale, rels, *refs):
    to_west, to_east, to_cross, to_beside, grads, recv, total, recv_total, held = refs
    slots = held.shape[0]
    rows = held.shape[1]
    per_slot = rows // TILE
    nodes = scale.shape[0]
    first = nodes // CHUNK
    chunks = slots * rows // CHUNK
    total[...] = jnp.zeros_like(total)
    recv_total[...] = jnp.zeros_like(recv_total)
    groups = CHUNK // PACK
    place = lax.broadcasted_iota(jnp.int32, (groups, PACK, nodes), 0) * PACK
    place = place + lax.broadcasted_iota(jnp.int32, (groups, PACK, nodes), 1)

    def step(m, carry):
        grad = slope[m].astype(jnp.float32) * scale[...]
        recv_total[...] += grad
        grad_low = grad.astype(jnp.bfloat16)
        grads[m] = grad_low
        one = jnp.bfloat16(1.0)
        zero = jnp.bfloat16(0.0)
        mark = jnp.where(low[m][None] == place.astype(jnp.bfloat16), one, zero)
        picker = jnp.concatenate(
            [
                jnp.where(high[m][None] == jnp.bfloat16(first + chunk), mark, zero)
                for chunk in range(chunks)
            ],
            axis=0,
        ).reshape(chunks * CHUNK, nodes)
        total[...] += dot(picker, grad_low)
        return carry

    lax.fori_loop(0, slope.shape[0], step, 0)
    for slot in range(slots):
        spot = info[PLACES + slot]
        for half in range(per_slot):
            terms = jnp.zeros((TILE, scale.shape[1]), jnp.float32)
            for t in range(per_slot):
                number = slot * per_slot + t
                hit = jnp.abs(rels[number : number + 1, :] - half) < 0.5
                tile = total[number * TILE : (number + 1) * TILE, :]
                terms += jnp.where(hit, tile, 0.0)
            held[spot, half * TILE : (half + 1) * TILE, :] = terms.astype(jnp.bfloat16)
    to_west[...] = held[1]
    to_east[...] = held[2]
    to_cross[...] = held[3]
    to_beside[0] = held[0]
    to_beside[1] = held[4]
    to_beside[2] = held[5]
    recv[...] = recv_total[...].astype(jnp.bfloat16)


def own_kernel(low, high, grads, total):
    nodes = total.shape[0]
    chunks = nodes // CHUNK
    groups = CHUNK // PACK
    total[...] = jnp.zeros_like(total)
    place = lax.broadcasted_iota(jnp.int32, (groups, PACK, nodes), 0) * PACK
    place = place + lax.broadcasted_iota(jnp.int32, (groups, PACK, nodes), 1)

    def step(m, carry):
        one = jnp.bfloat16(1.0)
        zero = jnp.bfloat16(0.0)
        mark = jnp.where(low[m][None] == place.astype(jnp.bfloat16), one, zero)
        picker = jnp.concatenate(
            [
                jnp.where(high[m][None] == jnp.bfloat16(chunk), mark, zero)
                for chunk in range(chunks)
            ],
            axis=0,
        ).reshape(chunks * CHUNK, nodes)
        total[...] += dot(picker, grads[m])
        return carry

    lax.fori_loop(0, grads.shape[0], step, 0)


def output_kernel(info, feats, cots, hidden, grad_pre, w_out, w_node_v_t, updated, direct):
    chans = feats.shape[0]
    lane = lax.broadcasted_iota(jnp.int32, (1, feats.shape[1]), 1)
    active = (lane < info[TILES] * TILE).astype(jnp.float32)
    node_out = dot(mine_of(w_out, info[CH], chans), hidden[...])
    updated[...] = (feats[...].astype(jnp.float32) + active * node_out).astype(jnp.bfloat16)
    direct[...] = cots[...].astype(jnp.float32) + dot(w_node_v_t[...], grad_pre[...])


def add_kernel(left, more, right, west, east):
    west[...] = (left[...].astype(jnp.float32) + more[1].astype(jnp.float32)).astype(jnp.bfloat16)
    east[...] = (right[...].astype(jnp.float32) + more[2].astype(jnp.float32)).astype(jnp.bfloat16)


def final_kernel(
    inv_root,
    info,
    own,
    recv,
    direct,
    feats,
    w_send_t,
    w_recv_t,
    upper,
    lower,
    across,
    beside,
    kept,
    sent,
    w_mine,
    w_beside,
    total,
    terms,
):
    rows = upper.shape[0]
    mine, sub, lon = info[CH], info[SUB], info[LON]
    start = info[FIRST] * TILE
    total[...] = own[...]

    def put(offset, block):
        spot = pl.ds(pl.multiple_of(offset, TILE), rows)
        total[spot, :] += block.astype(jnp.float32)

    put(start, upper[...])
    put(0, lower[...])
    put(jnp.where(sub == 0, 0, start), across[...])
    put(jnp.where(sub == 0, start, 0), beside[0])
    grad_send = total[...].astype(jnp.bfloat16)
    grad_send_t = total[...].T.astype(jnp.bfloat16)
    grad_recv_t = recv[...].astype(jnp.float32).T.astype(jnp.bfloat16)
    chans = direct.shape[0]
    terms[...] = dot(w_send_t[...], grad_send_t) + dot(w_recv_t[...], grad_recv_t)
    kept[...] = direct[...] + mine_of(terms, mine, chans)
    count = sent.shape[0] + 1
    for k in range(1, count):
        sent[k - 1] = mine_of(terms, lax.rem(mine + k, count), chans).astype(jnp.bfloat16)
    weight = dot(feats[...], grad_send) * inv_root
    terms[:, : weight.shape[1]] = weight
    lons, columns, hid = w_mine.shape
    for k in range(lons):
        band = lax.rem(lon + k, lons) * 2
        for out, core in ((w_mine, sub), (w_beside, 1 - sub)):
            spot = pl.multiple_of((band + core) * columns, columns)
            out[k] = terms[pl.ds(spot, columns), :hid].astype(out.dtype)


def sum_kernel(w_mine, w_beside, near, sent):
    near[...] = w_mine[0] + w_beside[0].astype(jnp.float32)
    for k in range(sent.shape[0]):
        sent[k] = (w_mine[k + 1] + w_beside[k + 1].astype(jnp.float32)).astype(jnp.bfloat16)


def weight_kernel(near, *refs):
    out = refs[-1]
    total = near[...]
    for ref in refs[:-1]:
        total += ref[...].astype(jnp.float32)
    out[...] = total.T


def shards(
    features,
    cotangent,
    senders,
    in_degree,
    tile_count,
    send_tiles,
    w_send,
    w_recv,
    bias_edge,
    w_msg,
    w_node_v,
    w_node_a,
    bias_node,
    w_out,
):
    chans, nodes = features.shape
    count = lax.axis_size("ch")
    mine = lax.axis_index("ch")
    sub = lax.axis_index("sub")
    lons = lax.axis_size("lon")
    hidden_all, chans_all = w_send.shape
    hid = hidden_all // count
    cycle = ("lon", "sub")
    shard_count = lax.axis_size(cycle)
    total_nodes = nodes * shard_count
    degree = senders.shape[0]
    slots = send_tiles.shape[1]
    slot_rows = send_tiles.shape[2] * TILE
    ext_len = nodes + slots * slot_rows
    bf16, f32 = jnp.bfloat16, jnp.float32
    shape = jax.ShapeDtypeStruct

    first_tile = tile_count[0] // 2
    places = jnp.where(sub == 0, jnp.array([4, 1, 3, 0, 2, 5]), jnp.array([0, 1, 4, 5, 2, 3]))
    lift = jnp.where(jnp.arange(slots) < slots // 2, first_tile, 0)[:, None]
    scalars = jnp.stack([mine, tile_count[0], sub, first_tile, lax.axis_index("lon")])
    info = jnp.concatenate([scalars, places, (send_tiles[0] - lift).reshape(-1)]).astype(jnp.int32)
    across_route = [(i, (i + (3 if i % 2 else -3)) % shard_count) for i in range(shard_count)]
    across = lambda block: lax.ppermute(block, cycle, across_route)
    degrees = in_degree[None, :]

    feat_blocks = gathered(features, "ch")
    cot_blocks = gathered(cotangent, "ch")

    (
        w_send_t,
        w_recv_t,
        w_msg_t,
        w_node_v_t,
        w_node_a_t,
        w_out_t,
        low_cols,
        high_cols,
        low_rows,
        high_rows,
    ) = call(
        weights_kernel,
        (
            shape((chans_all, hid), bf16),
            shape((chans_all, hid), bf16),
            shape((hid, chans_all), bf16),
            shape((chans, hidden_all), bf16),
            shape((chans_all, hidden_all), bf16),
            shape((hidden_all, chans_all), bf16),
            shape((degree, nodes, LANES), bf16),
            shape((degree, nodes, LANES), bf16),
            shape((degree, PACK, nodes), bf16),
            shape((degree, PACK, nodes), bf16),
        ),
        [info, senders, degrees, w_send, w_recv, w_msg, w_node_v, w_node_a, w_out],
        flops=4 * hidden_all * chans_all * nodes,
        scratch=[pltpu.VMEM((chans_all, hidden_all), bf16)],
    )

    block = shape((slot_rows + PACK, hid), bf16)
    feats, proj, base, upper, lower, cross, beside = call(
        functools.partial(project_kernel, count),
        (
            shape((chans_all, nodes), bf16),
            shape((nodes, hid), bf16),
            shape((nodes, hid), f32),
            block,
            block,
            block,
            block,
        ),
        [info, bias_edge[None, :]] + feat_blocks + [w_send, w_recv],
        flops=4 * hid * chans_all * nodes,
    )
    west = shifted(upper, "lon", 1)
    east = shifted(lower, "lon", -1)
    beside = shifted(beside, "sub", 1)
    cross = across(cross)
    west_too = shifted(west, "sub", 1)
    east_too = shifted(east, "sub", 1)
    arrivals = [beside, west, east, cross, west_too, east_too]

    cots, pre, grad_hidden = call(
        functools.partial(prepare_kernel, count),
        (
            shape((chans_all, nodes), bf16),
            shape((hidden_all, nodes), f32),
            shape((hidden_all, nodes), f32),
        ),
        [info] + cot_blocks + [feats, w_node_v, bias_node[None, :], w_out_t],
        flops=4 * hidden_all * chans_all * nodes,
    )

    message, slope, rels = call(
        forward_kernel,
        (
            shape((hid, nodes), bf16),
            shape((degree, nodes, hid), bf16),
            shape((PACK, hid), f32),
        ),
        [info, low_cols, high_cols, base, degrees, proj] + arrivals,
        flops=2 * degree * nodes * ext_len * hid,
        scratch=[
            pltpu.VMEM((ext_len, hid), bf16),
            pltpu.VMEM((nodes, hid), f32),
            pltpu.VMEM((slots, slot_rows + PACK, hid), bf16),
        ],
    )
    messages = gathered(message, "ch")

    hidden, grad_pre, scale = call(
        functools.partial(node_kernel, count),
        (
            shape((hidden_all, nodes), bf16),
            shape((hidden_all, nodes), bf16),
            shape((nodes, hid), f32),
        ),
        [info, degrees] + messages + [w_msg, w_node_a, w_node_a_t, w_msg_t, pre, grad_hidden],
        flops=6 * hidden_all * chans_all * nodes,
        scratch=[pltpu.VMEM((hidden_all, nodes), bf16)],
    )

    block = shape((slot_rows, hid), bf16)
    to_west, to_east, to_cross, to_beside, grads, grad_recv = call(
        far_kernel,
        (
            block,
            block,
            block,
            shape((3, slot_rows, hid), bf16),
            shape((degree, nodes, hid), bf16),
            shape((nodes, hid), bf16),
        ),
        [info, low_rows, high_rows, slope, scale, rels],
        flops=2 * degree * nodes * (ext_len - nodes) * hid,
        scratch=[
            pltpu.VMEM((ext_len - nodes, hid), f32),
            pltpu.VMEM((nodes, hid), f32),
            pltpu.VMEM((slots, slot_rows, hid), bf16),
        ],
    )
    from_beside = shifted(to_beside, "sub", 1)
    from_cross = across(to_cross)
    to_west, to_east = call(
        add_kernel, (block, block), [to_west, from_beside, to_east], flops=0, scalars=0
    )
    from_upper = shifted(to_west, "lon", -1)
    from_lower = shifted(to_east, "lon", 1)

    own = call(
        own_kernel,
        shape((nodes, hid), f32),
        [low_rows, high_rows, grads],
        flops=2 * degree * nodes * nodes * hid,
        scalars=0,
    )
    updated, direct = call(
        output_kernel,
        (shape((chans, nodes), bf16), shape((chans, nodes), f32)),
        [info, features, cotangent, hidden, grad_pre, w_out, w_node_v_t],
        flops=4 * hidden_all * chans * nodes,
    )

    columns = chans_all // shard_count
    kept, sent, w_mine, w_beside = call(
        functools.partial(final_kernel, 1.0 / math.sqrt(total_nodes)),
        (
            shape((chans, nodes), f32),
            shape((count - 1, chans, nodes), bf16),
            shape((lons, columns, hid), f32),
            shape((lons, columns, hid), bf16),
        ),
        [info, own, grad_recv, direct, feats, w_send_t, w_recv_t]
        + [from_upper, from_lower, from_cross, from_beside],
        flops=6 * hid * chans_all * nodes,
        scratch=[pltpu.VMEM((nodes, hid), f32), pltpu.VMEM((chans_all, nodes), f32)],
    )
    w_beside = shifted(w_beside, "sub", 1)
    for k in range(1, count):
        kept = kept + shifted(sent[k - 1], "ch", k).astype(f32)
    grad_features = kept.astype(bf16)

    near, w_sent = call(
        sum_kernel,
        (shape((columns, hid), f32), shape((lons - 1, columns, hid), bf16)),
        [w_mine, w_beside],
        flops=0,
        scalars=0,
    )
    w_terms = [shifted(w_sent[k - 1], "lon", k) for k in range(1, lons)]
    grad_w_send = call(
        weight_kernel, shape((hid, columns), f32), [near] + w_terms, flops=0, scalars=0
    )
    return (updated, grad_features, grad_w_send)


def solution(mesh):
    nodes_last = P("ch", ("parts", "lon", "sub"))
    spread = ("parts", "lon", "sub")
    placed = (nodes_last, nodes_last, P(None, spread), P(spread), P(spread), P(spread, None, None))
    return jax.shard_map(
        shards,
        mesh=mesh,
        in_specs=placed + (P(),) * 8,
        out_specs=(nodes_last, nodes_last, P(("parts", "ch"), ("lon", "sub"))),
        check_vma=False,
    )
```

```python
import functools
import math

import jax
import jax.numpy as jnp
from jax import lax
from jax.experimental import pallas as pl
from jax.experimental.pallas import tpu as pltpu
from jax.sharding import PartitionSpec as P

TILE = 128
CHUNK = 256
LANES = 128
PACK = 16
MIB = 1 << 20
NO_CHUNK = 64
EARLY, LATE = (0, 2, 3, 5), (1, 4)


def shifted(block, axis, distance):
    size = lax.axis_size(axis)
    route = [((i - distance) % size, i) for i in range(size)]
    return lax.ppermute(block, axis, route)


def gathered(block, axis):
    return [block] + [shifted(block, axis, k) for k in range(1, lax.axis_size(axis))]


def dot(left, right):
    return jnp.dot(left, right, preferred_element_type=jnp.float32)


def dot_nt(left, right):
    return lax.dot_general(
        left, right, (((1,), (1,)), ((), ())), preferred_element_type=jnp.float32
    )


def sigmoid(value):
    return 0.5 * jnp.tanh(0.5 * value) + 0.5


def call(kernel, out_shape, operands, flops, scratch=(), scalars=2, away=0, limit=24):
    vmem = pl.BlockSpec(memory_space=pltpu.VMEM)
    smem = pl.BlockSpec(memory_space=pltpu.SMEM)
    anywhere = pl.BlockSpec(memory_space=pl.ANY)
    moved = sum(math.prod(x.shape) * x.dtype.itemsize for x in operands)
    return pl.pallas_call(
        kernel,
        out_shape=out_shape,
        in_specs=[smem] * scalars
        + [anywhere] * away
        + [vmem] * (len(operands) - scalars - away),
        out_specs=jax.tree.map(lambda _: vmem, out_shape),
        scratch_shapes=scratch,
        compiler_params=pltpu.CompilerParams(vmem_limit_bytes=limit * MIB),
        cost_estimate=pl.CostEstimate(flops=flops, bytes_accessed=moved, transcendentals=0),
    )(*operands)


def place_of(slot, slots):
    sub = lax.axis_index("sub")
    return jnp.where(sub == 0, (4, 1, 3, 0, 2, 5)[slot], (0, 1, 4, 5, 2, 3)[slot])


def assemble(whole_ref, blocks, first):
    count = len(blocks)
    rows = blocks[0].shape[0]
    for k, block in enumerate(blocks):
        place = lax.rem(first - k + count, count) * rows
        whole_ref[pl.ds(pl.multiple_of(place, rows), rows), :] = block[...]


def mine_of(ref, index, rows):
    return ref[pl.ds(pl.multiple_of(index * rows, rows), rows), :]


def weights_kernel(tiles, picks, *refs):
    sources, refs = refs[:12], refs[12:]
    held, refs = refs[:12], refs[12:]
    w_send_t, w_recv_t, w_msg_t, w_node_v_t, w_node_a_t, w_out_t, *refs = refs
    low_cols, high_cols, low_rows, high_rows, turned, w_out_all, sems = refs
    w_send, w_recv, w_msg, w_node_v, w_node_a, w_out, senders, in_degree = held[:8]
    mine = lax.axis_index("ch")
    hid = w_send.shape[0]
    copies = []
    for k, (source, target) in enumerate(zip(sources, held)):
        if k in (0, 1):
            source = source.at[pl.ds(pl.multiple_of(mine * hid, hid), hid), :]
        target = w_out_all if k == 5 else target
        copies.append(pltpu.make_async_copy(source, target, sems.at[k]))
    order = (6, 7, 0, 1, 2, 3, 4, 5, 8, 9, 10, 11)
    for k in order:
        copies[k].start()

    copies[6].wait()
    copies[7].wait()
    degree, nodes = senders.shape
    lane = lax.broadcasted_iota(jnp.int32, (degree, nodes), 1)
    row = lax.broadcasted_iota(jnp.int32, (degree, nodes), 0)
    valid = (row < in_degree[...]) & (lane < tiles[0] * TILE)
    ids = senders[...]
    low = (ids & (CHUNK - 1)).astype(jnp.float32)
    high = jnp.where(valid, ids // CHUNK, NO_CHUNK).astype(jnp.float32)
    for m in range(degree):
        shape = (PACK, nodes)
        low_rows[m] = jnp.broadcast_to(low[m : m + 1], shape).astype(jnp.bfloat16)
        high_rows[m] = jnp.broadcast_to(high[m : m + 1], shape).astype(jnp.bfloat16)
    fill = jnp.zeros((PACK - degree, nodes), jnp.float32)
    depth = 2 * PACK
    both = jnp.concatenate([low, fill, high, fill], axis=0).T.astype(jnp.bfloat16)
    width = degree * LANES
    spot = lax.broadcasted_iota(jnp.int32, (depth, width), 0)
    group = lax.broadcasted_iota(jnp.int32, (depth, width), 1) // LANES
    for first, out in ((0, low_cols), (PACK, high_cols)):
        pick = (spot == group + first).astype(jnp.bfloat16)
        spread = dot(both, pick).astype(jnp.bfloat16)
        for m in range(degree):
            out[m] = spread[:, m * LANES : (m + 1) * LANES]

    for k in order[2:]:
        copies[k].wait()
    w_send_t[...] = w_send[...].T
    w_recv_t[...] = w_recv[...].T
    w_node_a_t[...] = w_node_a[...].T
    w_out_t[...] = w_out_all[...].T
    w_out[...] = mine_of(w_out_all, mine, w_out.shape[0])
    turned[...] = w_msg[...].T
    w_msg_t[...] = mine_of(turned, mine, hid)
    turned[...] = w_node_v[...].T
    w_node_v_t[...] = mine_of(turned, mine, w_node_v_t.shape[0])


def project_kernel(count, tiles, picks, bias, *refs):
    blocks = refs[:count]
    w_send, w_recv, feats, proj, base, upper, lower, cross, beside = refs[count:]
    mine, sub = lax.axis_index("ch"), lax.axis_index("sub")
    first = tiles[0] // 2
    assemble(feats, blocks, mine)
    whole = feats[...]
    hid = proj.shape[1]
    proj[...] = dot(w_send[...], whole).T.astype(jnp.bfloat16)
    rows = upper.shape[0] - PACK
    upper[:rows, :] = proj[pl.ds(pl.multiple_of(first * TILE, TILE), rows), :]
    lower[:rows, :] = proj[:rows, :]
    spot = lax.broadcasted_iota(jnp.int32, (PACK, hid), 0)
    _, slots, per_slot = picks.shape
    half = slots // 2
    for start, out, lift in ((0, upper, first), (half, lower, 0)):
        marks = jnp.zeros((PACK, hid), jnp.float32)
        for k in range(half * per_slot):
            rel = picks[0, start + k // per_slot, k % per_slot] - lift
            marks = jnp.where(spot == k, rel.astype(jnp.float32), marks)
        out[rows:, :] = marks.astype(jnp.bfloat16)

    @pl.when(sub == 0)
    def _():
        cross[...] = lower[...]
        beside[...] = upper[...]

    @pl.when(sub != 0)
    def _():
        cross[...] = upper[...]
        beside[...] = lower[...]

    my_bias = jnp.zeros((1, hid), jnp.float32)
    for k in range(count):
        my_bias += jnp.where(mine == k, bias[:, k * hid : (k + 1) * hid], 0.0)
    recv = dot(w_recv[...], whole).T
    base[...] = recv.astype(jnp.bfloat16).astype(jnp.float32) + my_bias


def prepare_kernel(count, tiles, *refs):
    blocks = refs[:count]
    feats, w_node_v, bias, w_out_t, cots, pre, grad_hidden = refs[count:]
    assemble(cots, blocks, lax.axis_index("ch"))
    column = jnp.broadcast_to(bias[...], (8, bias.shape[1])).T[:, :1]
    pre[...] = dot(w_node_v[...], feats[...]) + column
    lane = lax.broadcasted_iota(jnp.int32, (1, cots.shape[1]), 1)
    active = (lane < tiles[0] * TILE).astype(jnp.bfloat16)
    grad_hidden[...] = dot(w_out_t[...], cots[...] * active)


def forward_kernel(low, high, base, in_degree, proj, *refs):
    arrivals = refs[:6]
    message, slope, rels, ext, total, held = refs[6:]
    own = proj.shape[0]
    rows = held.shape[1] - PACK
    per_slot = rows // TILE
    slots = len(arrivals)
    ext[:own, :] = proj[...]
    for place, block in enumerate(arrivals):
        held[place] = block[...]
    rels[...] = jnp.zeros_like(rels)
    for slot in range(slots):
        place = place_of(slot, slots)
        group = slot % (slots // 2)
        for t in range(per_slot):
            index = group * per_slot + t
            rel = held[place, rows : rows + PACK, :][index : index + 1, :].astype(jnp.float32)
            number = slot * per_slot + t
            rels[number : number + 1, :] = rel
            start = own + number * TILE
            ext[start : start + TILE, :] = jnp.where(
                rel > 0.5, held[place, TILE : 2 * TILE, :], held[place, :TILE, :]
            )
    chunks = ext.shape[0] // CHUNK
    halves = CHUNK // LANES
    total[...] = jnp.zeros_like(total)
    lane = lax.broadcasted_iota(jnp.int32, (own, LANES), 1)

    def step(m, carry):
        low_m, high_m = low[m], high[m]
        one = jnp.bfloat16(1.0)
        zero = jnp.bfloat16(0.0)
        marks = [
            jnp.where(low_m == (lane + half * LANES).astype(jnp.bfloat16), one, zero)
            for half in range(halves)
        ]
        picker = jnp.concatenate(
            [
                jnp.where(high_m == jnp.bfloat16(chunk), mark, zero)
                for chunk in range(chunks)
                for mark in marks
            ],
            axis=1,
        )
        pre = dot(picker, ext[...]) + base[...]
        valid = high_m[:, :1].astype(jnp.float32) < chunks
        sig = sigmoid(pre)
        act = pre * sig
        total[...] += jnp.where(valid, act, 0.0)
        slope[m] = jnp.where(valid, sig + act * (1.0 - sig), 0.0).astype(jnp.bfloat16)
        return carry

    lax.fori_loop(0, low.shape[0], step, 0, unroll=True)
    degree = in_degree[...].astype(jnp.float32)
    message[...] = (total[...].T / degree).astype(jnp.bfloat16)


def node_kernel(count, in_degree, *refs):
    blocks = refs[:count]
    w_msg, w_node_a, w_node_a_t, w_msg_t, pre, grad_hidden = refs[count : count + 6]
    hidden, grad_pre, scale, messages = refs[count + 6 :]
    assemble(messages, blocks, lax.axis_index("ch"))
    agg = dot(w_msg[...], messages[...])
    node_pre = pre[...] + dot(w_node_a[...], agg.astype(jnp.bfloat16))
    sig = sigmoid(node_pre)
    act = node_pre * sig
    hidden[...] = act.astype(jnp.bfloat16)
    low_grad = (grad_hidden[...] * (sig + act * (1.0 - sig))).astype(jnp.bfloat16)
    grad_pre[...] = low_grad
    grad_agg = dot(w_node_a_t[...], low_grad).astype(jnp.bfloat16)
    grad_msg = dot(w_msg_t[...], grad_agg).astype(jnp.bfloat16).astype(jnp.float32)
    scale[...] = (grad_msg / in_degree[...].astype(jnp.float32)).T


def scatter(low, high, grad_of, chunks, total):
    nodes = low.shape[2]
    groups = CHUNK // PACK
    place = lax.broadcasted_iota(jnp.int32, (groups, PACK, nodes), 0) * PACK
    place = place + lax.broadcasted_iota(jnp.int32, (groups, PACK, nodes), 1)
    total[...] = jnp.zeros_like(total)

    def step(m, carry):
        one = jnp.bfloat16(1.0)
        zero = jnp.bfloat16(0.0)
        mark = jnp.where(low[m][None] == place.astype(jnp.bfloat16), one, zero)
        picker = jnp.concatenate(
            [jnp.where(high[m][None] == jnp.bfloat16(chunk), mark, zero) for chunk in chunks],
            axis=0,
        ).reshape(len(chunks) * CHUNK, nodes)
        total[...] += dot(picker, grad_of(m))
        return carry

    lax.fori_loop(0, low.shape[0], step, 0, unroll=True)


def fold(slots, index, rels, total):
    rows = CHUNK // TILE
    halves = []
    for half in range(rows):
        terms = 0.0
        for t in range(rows):
            number = slots[index] * rows + t
            hit = jnp.abs(rels[number : number + 1, :] - half) < 0.5
            tile = total[(index * rows + t) * TILE : (index * rows + t + 1) * TILE, :]
            terms += jnp.where(hit, tile, 0.0)
        halves.append(terms)
    return jnp.concatenate(halves, axis=0).astype(jnp.bfloat16)


def early_kernel(low, high, slope, scale, rels, to_cross, to_beside, grads, total, held):
    first = scale.shape[0] // CHUNK

    def grad_of(m):
        grads[m] = (slope[m].astype(jnp.float32) * scale[...]).astype(jnp.bfloat16)
        return grads[m]

    scatter(low, high, grad_of, [first + slot for slot in EARLY], total)
    for index, slot in enumerate(EARLY):
        held[place_of(slot, 6)] = fold(EARLY, index, rels, total)
    to_cross[...] = held[3]
    to_beside[0] = held[0]
    to_beside[1] = held[4]
    to_beside[2] = held[5]


def late_kernel(low, high, grads, rels, to_west, to_east, total):
    first = low.shape[2] // CHUNK
    scatter(low, high, lambda m: grads[m], [first + slot for slot in LATE], total)
    to_west[...] = fold(LATE, 0, rels, total)
    to_east[...] = fold(LATE, 1, rels, total)


def own_kernel(low, high, grads, total, recv, recv_total):
    chunks = list(range(total.shape[0] // CHUNK))
    scatter(low, high, lambda m: grads[m], chunks, total)
    recv_total[...] = jnp.zeros_like(recv_total)

    def step(m, carry):
        recv_total[...] += grads[m].astype(jnp.float32)
        return carry

    lax.fori_loop(0, grads.shape[0], step, 0)
    recv[...] = recv_total[...].T.astype(jnp.bfloat16)


def output_kernel(tiles, feats, cots, hidden, grad_pre, w_out, w_node_v_t, updated, direct):
    lane = lax.broadcasted_iota(jnp.int32, (1, feats.shape[1]), 1)
    active = (lane < tiles[0] * TILE).astype(jnp.float32)
    node_out = dot(w_out[...], hidden[...])
    updated[...] = (feats[...].astype(jnp.float32) + active * node_out).astype(jnp.bfloat16)
    direct[...] = cots[...].astype(jnp.float32) + dot(w_node_v_t[...], grad_pre[...])


def add_kernel(left, more, right, west, east):
    west[...] = (left[...].astype(jnp.float32) + more[1].astype(jnp.float32)).astype(jnp.bfloat16)
    east[...] = (right[...].astype(jnp.float32) + more[2].astype(jnp.float32)).astype(jnp.bfloat16)


def final_kernel(
    inv_root,
    tiles,
    own,
    recv,
    direct,
    feats,
    w_send_t,
    w_recv_t,
    upper,
    lower,
    across,
    beside,
    kept,
    sent,
    w_mine,
    w_beside,
    total,
    terms,
):
    rows = upper.shape[0]
    mine, sub, lon = lax.axis_index("ch"), lax.axis_index("sub"), lax.axis_index("lon")
    start = tiles[0] // 2 * TILE
    total[...] = own[...]

    def put(offset, block):
        spot = pl.ds(pl.multiple_of(offset, TILE), rows)
        total[spot, :] += block.astype(jnp.float32)

    put(start, upper[...])
    put(0, lower[...])
    put(jnp.where(sub == 0, 0, start), across[...])
    put(jnp.where(sub == 0, start, 0), beside[0])
    grad_send = total[...].astype(jnp.bfloat16)
    grad_send_t = total[...].T.astype(jnp.bfloat16)
    chans = direct.shape[0]
    terms[...] = dot(w_send_t[...], grad_send_t) + dot(w_recv_t[...], recv[...])
    kept[...] = direct[...] + mine_of(terms, mine, chans)
    count = sent.shape[0] + 1
    for k in range(1, count):
        sent[k - 1] = mine_of(terms, lax.rem(mine + k, count), chans).astype(jnp.bfloat16)
    weight = dot(feats[...], grad_send) * inv_root
    terms[:, : weight.shape[1]] = weight
    lons, columns, hid = w_mine.shape
    for k in range(lons):
        band = lax.rem(lon + k, lons) * 2
        for out, core in ((w_mine, sub), (w_beside, 1 - sub)):
            spot = pl.multiple_of((band + core) * columns, columns)
            out[k] = terms[pl.ds(spot, columns), :hid].astype(out.dtype)


def sum_kernel(w_mine, w_beside, near, sent):
    near[...] = w_mine[0] + w_beside[0].astype(jnp.float32)
    for k in range(sent.shape[0]):
        sent[k] = (w_mine[k + 1] + w_beside[k + 1].astype(jnp.float32)).astype(jnp.bfloat16)


def weight_kernel(near, *refs):
    out = refs[-1]
    total = near[...]
    for ref in refs[:-1]:
        total += ref[...].astype(jnp.float32)
    out[...] = total.T


def shards(
    features,
    cotangent,
    senders,
    in_degree,
    tile_count,
    send_tiles,
    w_send,
    w_recv,
    bias_edge,
    w_msg,
    w_node_v,
    w_node_a,
    bias_node,
    w_out,
):
    chans, nodes = features.shape
    count = lax.axis_size("ch")
    lons = lax.axis_size("lon")
    hidden_all, chans_all = w_send.shape
    hid = hidden_all // count
    cycle = ("lon", "sub")
    shard_count = lax.axis_size(cycle)
    total_nodes = nodes * shard_count
    degree = senders.shape[0]
    slots = send_tiles.shape[1]
    slot_rows = send_tiles.shape[2] * TILE
    ext_len = nodes + slots * slot_rows
    bf16, f32 = jnp.bfloat16, jnp.float32
    shape = jax.ShapeDtypeStruct

    across_route = [(i, (i + (3 if i % 2 else -3)) % shard_count) for i in range(shard_count)]
    across = lambda block: lax.ppermute(block, cycle, across_route)
    degrees = in_degree[None, :]

    feat_blocks = gathered(features, "ch")
    cot_blocks = gathered(cotangent, "ch")

    fixed = (
        [shape((hid, chans_all), bf16)] * 2
        + [shape((chans_all, hidden_all), bf16), shape((hidden_all, chans_all), bf16)]
        + [shape((hidden_all, chans_all), bf16), shape((chans, hidden_all), bf16)]
    )
    inputs = [senders, degrees, features, cotangent, bias_edge[None, :], bias_node[None, :]]
    held = call(
        weights_kernel,
        (
            *fixed,
            *[shape(x.shape, x.dtype) for x in inputs],
            shape((chans_all, hid), bf16),
            shape((chans_all, hid), bf16),
            shape((hid, chans_all), bf16),
            shape((chans, hidden_all), bf16),
            shape((chans_all, hidden_all), bf16),
            shape((hidden_all, chans_all), bf16),
            shape((degree, nodes, LANES), bf16),
            shape((degree, nodes, LANES), bf16),
            shape((degree, PACK, nodes), bf16),
            shape((degree, PACK, nodes), bf16),
        ),
        [tile_count, send_tiles, w_send, w_recv, w_msg, w_node_v, w_node_a, w_out] + inputs,
        flops=4 * hidden_all * chans_all * nodes,
        away=12,
        scratch=[
            pltpu.VMEM((chans_all, hidden_all), bf16),
            pltpu.VMEM((chans_all, hidden_all), bf16),
            pltpu.SemaphoreType.DMA((12,)),
        ],
    )
    w_send_my, w_recv_my, w_msg, w_node_v, w_node_a, w_out_my, _, degrees = held[:8]
    features_held, cotangent_held, bias_edge, bias_node = held[8:12]
    w_send_t, w_recv_t, w_msg_t, w_node_v_t, w_node_a_t, w_out_t = held[12:18]
    low_cols, high_cols, low_rows, high_rows = held[18:]
    feat_blocks[0], cot_blocks[0] = features_held, cotangent_held

    block = shape((slot_rows + PACK, hid), bf16)
    feats, proj, base, upper, lower, cross, beside = call(
        functools.partial(project_kernel, count),
        (
            shape((chans_all, nodes), bf16),
            shape((nodes, hid), bf16),
            shape((nodes, hid), f32),
            block,
            block,
            block,
            block,
        ),
        [tile_count, send_tiles, bias_edge] + feat_blocks + [w_send_my, w_recv_my],
        flops=4 * hid * chans_all * nodes,
    )
    west = shifted(upper, "lon", 1)
    east = shifted(lower, "lon", -1)
    beside = shifted(beside, "sub", 1)
    cross = across(cross)
    west_too = shifted(west, "sub", 1)
    east_too = shifted(east, "sub", 1)
    arrivals = [beside, west, east, cross, west_too, east_too]

    cots, pre, grad_hidden = call(
        functools.partial(prepare_kernel, count),
        (
            shape((chans_all, nodes), bf16),
            shape((hidden_all, nodes), f32),
            shape((hidden_all, nodes), f32),
        ),
        [tile_count] + cot_blocks + [feats, w_node_v, bias_node, w_out_t],
        flops=4 * hidden_all * chans_all * nodes,
        scalars=1,
    )

    message, slope, rels = call(
        forward_kernel,
        (
            shape((hid, nodes), bf16),
            shape((degree, nodes, hid), bf16),
            shape((PACK, hid), f32),
        ),
        [low_cols, high_cols, base, degrees, proj] + arrivals,
        flops=2 * degree * nodes * ext_len * hid,
        scratch=[
            pltpu.VMEM((ext_len, hid), bf16),
            pltpu.VMEM((nodes, hid), f32),
            pltpu.VMEM((slots, slot_rows + PACK, hid), bf16),
        ],
        scalars=0,
    )
    messages = gathered(message, "ch")

    hidden, grad_pre, scale = call(
        functools.partial(node_kernel, count),
        (
            shape((hidden_all, nodes), bf16),
            shape((hidden_all, nodes), bf16),
            shape((nodes, hid), f32),
        ),
        [degrees] + messages + [w_msg, w_node_a, w_node_a_t, w_msg_t, pre, grad_hidden],
        flops=6 * hidden_all * chans_all * nodes,
        scratch=[pltpu.VMEM((hidden_all, nodes), bf16)],
        scalars=0,
    )

    block = shape((slot_rows, hid), bf16)
    to_cross, to_beside, grads = call(
        early_kernel,
        (block, shape((3, slot_rows, hid), bf16), shape((degree, nodes, hid), bf16)),
        [low_rows, high_rows, slope, scale, rels],
        flops=2 * degree * nodes * len(EARLY) * slot_rows * hid,
        scratch=[
            pltpu.VMEM((len(EARLY) * slot_rows, hid), f32),
            pltpu.VMEM((slots, slot_rows, hid), bf16),
        ],
        scalars=0,
    )
    from_beside = shifted(to_beside, "sub", 1)
    from_cross = across(to_cross)
    to_west, to_east = call(
        late_kernel,
        (block, block),
        [low_rows, high_rows, grads, rels],
        flops=2 * degree * nodes * len(LATE) * slot_rows * hid,
        scratch=[pltpu.VMEM((len(LATE) * slot_rows, hid), f32)],
        scalars=0,
    )
    to_west, to_east = call(
        add_kernel, (block, block), [to_west, from_beside, to_east], flops=0, scalars=0
    )
    from_upper = shifted(to_west, "lon", -1)
    from_lower = shifted(to_east, "lon", 1)

    own, grad_recv = call(
        own_kernel,
        (shape((nodes, hid), f32), shape((hid, nodes), bf16)),
        [low_rows, high_rows, grads],
        flops=2 * degree * nodes * nodes * hid,
        scratch=[pltpu.VMEM((nodes, hid), f32)],
        scalars=0,
    )
    updated, direct = call(
        output_kernel,
        (shape((chans, nodes), bf16), shape((chans, nodes), f32)),
        [tile_count, features_held, cotangent_held, hidden, grad_pre, w_out_my, w_node_v_t],
        flops=4 * hidden_all * chans * nodes,
        scalars=1,
    )

    columns = chans_all // shard_count
    kept, sent, w_mine, w_beside = call(
        functools.partial(final_kernel, 1.0 / math.sqrt(total_nodes)),
        (
            shape((chans, nodes), f32),
            shape((count - 1, chans, nodes), bf16),
            shape((lons, columns, hid), f32),
            shape((lons, columns, hid), bf16),
        ),
        [tile_count, own, grad_recv, direct, feats, w_send_t, w_recv_t]
        + [from_upper, from_lower, from_cross, from_beside],
        flops=6 * hid * chans_all * nodes,
        scratch=[pltpu.VMEM((nodes, hid), f32), pltpu.VMEM((chans_all, nodes), f32)],
        scalars=1,
    )
    w_beside = shifted(w_beside, "sub", 1)
    for k in range(1, count):
        kept = kept + shifted(sent[k - 1], "ch", k).astype(f32)
    grad_features = kept.astype(bf16)

    near, w_sent = call(
        sum_kernel,
        (shape((columns, hid), f32), shape((lons - 1, columns, hid), bf16)),
        [w_mine, w_beside],
        flops=0,
        scalars=0,
    )
    w_terms = [shifted(w_sent[k - 1], "lon", k) for k in range(1, lons)]
    grad_w_send = call(
        weight_kernel, shape((hid, columns), f32), [near] + w_terms, flops=0, scalars=0
    )
    return (updated, grad_features, grad_w_send)


def solution(mesh):
    nodes_last = P("ch", ("parts", "lon", "sub"))
    spread = ("parts", "lon", "sub")
    placed = (nodes_last, nodes_last, P(None, spread), P(spread), P(spread), P(spread, None, None))
    return jax.shard_map(
        shards,
        mesh=mesh,
        in_specs=placed + (P(),) * 8,
        out_specs=(nodes_last, nodes_last, P(("parts", "ch"), ("lon", "sub"))),
        check_vma=False,
    )
```

```python
import functools
import math

import jax
import jax.numpy as jnp
from jax import lax
from jax.experimental import pallas as pl
from jax.experimental.pallas import tpu as pltpu
from jax.sharding import PartitionSpec as P

TILE = 128
CHUNK = 256
LANES = 128
PACK = 16
MIB = 1 << 20
NO_CHUNK = 64
SLOT_OF = ((3, 0), (1, 1), (4, 4), (2, 5), (0, 2), (5, 3))
EARLY, LATE = (0, 3, 4, 5), (1, 2)
OFF = -1e4


def shifted(block, axis, distance):
    size = lax.axis_size(axis)
    route = [((i - distance) % size, i) for i in range(size)]
    return lax.ppermute(block, axis, route)


def gathered(block, axis):
    return [block] + [shifted(block, axis, k) for k in range(1, lax.axis_size(axis))]


def dot(left, right):
    return jnp.dot(left, right, preferred_element_type=jnp.float32)


def dot_nt(left, right):
    return lax.dot_general(
        left, right, (((1,), (1,)), ((), ())), preferred_element_type=jnp.float32
    )


def sigmoid(value):
    return 0.5 * jnp.tanh(0.5 * value) + 0.5


def call(kernel, out_shape, operands, flops, scratch=(), scalars=2, away=0, limit=24):
    vmem = pl.BlockSpec(memory_space=pltpu.VMEM)
    smem = pl.BlockSpec(memory_space=pltpu.SMEM)
    anywhere = pl.BlockSpec(memory_space=pltpu.HBM)
    moved = sum(math.prod(x.shape) * x.dtype.itemsize for x in operands)
    return pl.pallas_call(
        kernel,
        out_shape=out_shape,
        in_specs=[smem] * scalars
        + [anywhere] * away
        + [vmem] * (len(operands) - scalars - away),
        out_specs=jax.tree.map(lambda _: vmem, out_shape),
        scratch_shapes=scratch,
        compiler_params=pltpu.CompilerParams(vmem_limit_bytes=limit * MIB),
        cost_estimate=pl.CostEstimate(flops=flops, bytes_accessed=moved, transcendentals=0),
    )(*operands)


def assemble(whole_ref, blocks, first):
    count = len(blocks)
    rows = blocks[0].shape[0]
    for k, block in enumerate(blocks):
        place = lax.rem(first - k + count, count) * rows
        whole_ref[pl.ds(pl.multiple_of(place, rows), rows), :] = block[...]


def mine_of(ref, index, rows):
    return ref[pl.ds(pl.multiple_of(index * rows, rows), rows), :]


def weights_kernel(tiles, picks, *refs):
    sources, refs = refs[:12], refs[12:]
    held, refs = refs[:12], refs[12:]
    w_send_t, w_recv_t, w_msg_t, w_node_v_t, w_node_a_t, w_out_t, *refs = refs
    low_cols, high_cols, low_rows, high_rows, turned, w_out_all, sems = refs
    w_send, w_recv, w_msg, w_node_v, w_node_a, w_out, senders, in_degree = held[:8]
    mine = lax.axis_index("ch")
    hid = w_send.shape[0]
    copies = []
    for k, (source, target) in enumerate(zip(sources, held)):
        if k in (0, 1):
            source = source.at[pl.ds(pl.multiple_of(mine * hid, hid), hid), :]
        target = w_out_all if k == 5 else target
        copies.append(pltpu.make_async_copy(source, target, sems.at[k]))
    order = (6, 7, 0, 1, 2, 3, 4, 5, 8, 9, 10, 11)
    for k in order:
        copies[k].start()

    copies[6].wait()
    copies[7].wait()
    degree, nodes = senders.shape
    lane = lax.broadcasted_iota(jnp.int32, (degree, nodes), 1)
    row = lax.broadcasted_iota(jnp.int32, (degree, nodes), 0)
    valid = (row < in_degree[...]) & (lane < tiles[0] * TILE)
    ids = senders[...]
    low = (ids & (CHUNK - 1)).astype(jnp.float32)
    high = jnp.where(valid, ids // CHUNK, NO_CHUNK).astype(jnp.float32)
    for m in range(degree):
        shape = (PACK, nodes)
        low_rows[m] = jnp.broadcast_to(low[m : m + 1], shape).astype(jnp.bfloat16)
        high_rows[m] = jnp.broadcast_to(high[m : m + 1], shape).astype(jnp.bfloat16)
    fill = jnp.zeros((PACK - degree, nodes), jnp.float32)
    depth = 2 * PACK
    both = jnp.concatenate([low, fill, high, fill], axis=0).T.astype(jnp.bfloat16)
    width = degree * LANES
    spot = lax.broadcasted_iota(jnp.int32, (depth, width), 0)
    group = lax.broadcasted_iota(jnp.int32, (depth, width), 1) // LANES
    for first, out in ((0, low_cols), (PACK, high_cols)):
        pick = (spot == group + first).astype(jnp.bfloat16)
        spread = dot(both, pick).astype(jnp.bfloat16)
        for m in range(degree):
            out[m] = spread[:, m * LANES : (m + 1) * LANES]

    for k in order[2:]:
        copies[k].wait()
    w_send_t[...] = w_send[...].T
    w_recv_t[...] = w_recv[...].T
    w_node_a_t[...] = w_node_a[...].T
    w_out_t[...] = w_out_all[...].T
    w_out[...] = mine_of(w_out_all, mine, w_out.shape[0])
    turned[...] = w_msg[...].T
    w_msg_t[...] = mine_of(turned, mine, hid)
    turned[...] = w_node_v[...].T
    w_node_v_t[...] = mine_of(turned, mine, w_node_v_t.shape[0])


def project_kernel(count, tiles, picks, bias, *refs):
    blocks = refs[:count]
    w_send, w_recv, feats, proj, base, upper, lower, cross, beside = refs[count:]
    mine, sub = lax.axis_index("ch"), lax.axis_index("sub")
    first = tiles[0] // 2
    assemble(feats, blocks, mine)
    whole = feats[...]
    hid = proj.shape[1]
    proj[...] = (0.5 * dot(w_send[...], whole).T).astype(jnp.bfloat16)
    rows = upper.shape[0] - PACK
    upper[:rows, :] = proj[pl.ds(pl.multiple_of(first * TILE, TILE), rows), :]
    lower[:rows, :] = proj[:rows, :]
    spot = lax.broadcasted_iota(jnp.int32, (PACK, hid), 0)
    _, slots, per_slot = picks.shape
    half = slots // 2
    for start, out, lift in ((0, upper, first), (half, lower, 0)):
        marks = jnp.zeros((PACK, hid), jnp.float32)
        for k in range(half * per_slot):
            rel = picks[0, start + k // per_slot, k % per_slot] - lift
            marks = jnp.where(spot == k, rel.astype(jnp.float32), marks)
        out[rows:, :] = marks.astype(jnp.bfloat16)

    @pl.when(sub == 0)
    def _():
        cross[...] = lower[...]
        beside[...] = upper[...]

    @pl.when(sub != 0)
    def _():
        cross[...] = upper[...]
        beside[...] = lower[...]

    my_bias = jnp.zeros((1, hid), jnp.float32)
    for k in range(count):
        my_bias += jnp.where(mine == k, bias[:, k * hid : (k + 1) * hid], 0.0)
    recv = dot(w_recv[...], whole).T
    base[...] = 0.5 * (recv.astype(jnp.bfloat16).astype(jnp.float32) + my_bias)


def prepare_kernel(count, tiles, *refs):
    blocks = refs[:count]
    feats, w_node_v, bias, w_out_t, cots, pre, grad_hidden = refs[count:]
    assemble(cots, blocks, lax.axis_index("ch"))
    column = jnp.broadcast_to(bias[...], (8, bias.shape[1])).T[:, :1]
    pre[...] = dot(w_node_v[...], feats[...]) + column
    lane = lax.broadcasted_iota(jnp.int32, (1, cots.shape[1]), 1)
    active = (lane < tiles[0] * TILE).astype(jnp.bfloat16)
    grad_hidden[...] = dot(w_out_t[...], cots[...] * active)


def chunk_of(place, first, shape):
    on_zero, on_one = (float(first + slot) for slot in SLOT_OF[place])
    chunk = jnp.where(lax.axis_index("sub") == 0, on_zero, on_one)
    return jnp.full(shape, chunk, jnp.float32).astype(jnp.bfloat16)


def picks_of(block, place):
    marks = block[CHUNK : CHUNK + PACK, :].astype(jnp.float32)
    per_slot = CHUNK // TILE
    half = len(SLOT_OF) // 2
    starts = [slot % half * per_slot for slot in SLOT_OF[place]]
    sub = lax.axis_index("sub")
    return [
        jnp.where(
            sub == 0,
            marks[starts[0] + t : starts[0] + t + 1],
            marks[starts[1] + t : starts[1] + t + 1],
        )
        for t in range(per_slot)
    ]


def fill(ext, start, block, place):
    for t, pick in enumerate(picks_of(block, place)):
        ext[start + t * TILE : start + (t + 1) * TILE, :] = jnp.where(
            pick > 0.5, block[TILE : 2 * TILE, :], block[:TILE, :]
        )


def pick_rows(low, high, chunks, ext):
    one = jnp.bfloat16(1.0)
    zero = jnp.bfloat16(0.0)
    lane = lax.broadcasted_iota(jnp.int32, low.shape, 1)
    marks = [
        jnp.where(low == (lane + half * LANES).astype(jnp.bfloat16), one, zero)
        for half in range(CHUNK // LANES)
    ]
    picker = jnp.concatenate(
        [jnp.where(high == chunk, mark, zero) for chunk in chunks for mark in marks], axis=1
    )
    return dot(picker, ext[...])


def near_kernel(low, high, proj, beside, part, ext):
    own = proj.shape[0]
    ext[:own, :] = proj[...]
    fill(ext, own, beside, 0)
    first = own // CHUNK
    chunks = [jnp.bfloat16(chunk) for chunk in range(first)]
    chunks.append(chunk_of(0, first, low.shape[1:]))

    def step(m, carry):
        part[m] = pick_rows(low[m], high[m], chunks, ext).astype(jnp.bfloat16)
        return carry

    lax.fori_loop(0, low.shape[0], step, 0, unroll=True)


def line_kernel(low, high, before, west, east, part, ext):
    first = low.shape[1] // CHUNK
    chunks = []
    for index, (place, block) in enumerate(((1, west), (2, east))):
        fill(ext, index * CHUNK, block, place)
        chunks.append(jnp.bfloat16(first + SLOT_OF[place][0]))

    def step(m, carry):
        more = pick_rows(low[m], high[m], chunks, ext)
        part[m] = (before[m].astype(jnp.float32) + more).astype(jnp.bfloat16)
        return carry

    lax.fori_loop(0, low.shape[0], step, 0, unroll=True)


def message_kernel(
    start, low, high, base, in_degree, part, cross, west, east, message, slope, ext, total
):
    nodes = low.shape[1]
    degree, rows, hid = slope.shape
    first = nodes // CHUNK
    together = nodes // rows
    span = slice(start, start + rows)
    chunks = []
    for index, (place, block) in enumerate(((3, cross), (4, west), (5, east))):
        fill(ext, index * CHUNK, block, place)
        chunks.append(chunk_of(place, first, (nodes, LANES)))
    total[...] = jnp.zeros_like(total)

    def rows_of(ref, k):
        return jnp.concatenate([ref[k * together + i, span, :] for i in range(together)], axis=0)

    def step(k, carry):
        low_k, high_k = rows_of(low, k), rows_of(high, k)
        half = pick_rows(low_k, high_k, chunks, ext) + rows_of(part, k).astype(jnp.float32)
        half += jnp.concatenate([base[span, :]] * together, axis=0)
        wide = jnp.concatenate([high_k] * pl.cdiv(hid, LANES), axis=1)[:, :hid]
        half = jnp.where(wide.astype(jnp.float32) < NO_CHUNK, half, OFF)
        twice = jnp.tanh(half) + 1.0
        act = half * twice
        grad = (twice + act * (2.0 - twice)).astype(jnp.bfloat16)
        terms = 0.0
        for i in range(together):
            terms += act[i * rows : (i + 1) * rows]
            slope[k * together + i] = grad[i * rows : (i + 1) * rows]
        total[...] += terms
        return carry

    lax.fori_loop(0, degree // together, step, 0, unroll=True)
    count = in_degree[:, span].astype(jnp.float32)
    message[...] = (total[...].T / count).astype(jnp.bfloat16)


def node_kernel(count, start, in_degree, *refs):
    blocks = refs[:count]
    w_msg, w_node_a, w_node_a_t, w_msg_t, pre, grad_hidden = refs[count : count + 6]
    hidden, grad_pre, scale, messages = refs[count + 6 :]
    assemble(messages, blocks, lax.axis_index("ch"))
    span = slice(start, start + hidden.shape[1])
    agg = dot(w_msg[...], messages[...])
    half = 0.5 * (pre[:, span] + dot(w_node_a[...], agg.astype(jnp.bfloat16)))
    twice = jnp.tanh(half) + 1.0
    act = half * twice
    hidden[...] = act.astype(jnp.bfloat16)
    slope = 0.5 * (twice + act * (2.0 - twice))
    low_grad = (grad_hidden[:, span] * slope).astype(jnp.bfloat16)
    grad_pre[...] = low_grad
    grad_agg = dot(w_node_a_t[...], low_grad).astype(jnp.bfloat16)
    grad_msg = dot(w_msg_t[...], grad_agg).astype(jnp.bfloat16).astype(jnp.float32)
    scale[...] = (grad_msg * (0.5 / in_degree[:, span].astype(jnp.float32))).T


def scatter(low, high, edges, chunks, total):
    one = jnp.bfloat16(1.0)
    zero = jnp.bfloat16(0.0)
    groups = CHUNK // PACK
    for step in edges:
        width = sum(rows for _, _, rows, _ in step)
        place = lax.broadcasted_iota(jnp.int32, (groups, PACK, width), 0) * PACK
        place = place + lax.broadcasted_iota(jnp.int32, (groups, PACK, width), 1)
        low_k = jnp.concatenate([low[m, :, s : s + r] for m, s, r, _ in step], axis=1)
        high_k = jnp.concatenate([high[m, :, s : s + r] for m, s, r, _ in step], axis=1)
        grads = jnp.concatenate([grad() for _, _, _, grad in step], axis=0)
        mark = jnp.where(low_k[None] == place.astype(jnp.bfloat16), one, zero)
        picker = jnp.concatenate(
            [jnp.where(high_k[None] == chunk, mark, zero) for chunk in chunks], axis=0
        ).reshape(len(chunks) * CHUNK, width)
        total[...] += dot(picker, grads)


def pairs(start, ref, nodes, grad_of):
    degree, rows, _ = ref.shape
    together = nodes // rows
    return [
        [
            (m, start, rows, functools.partial(grad_of, ref, m))
            for m in range(k * together, (k + 1) * together)
        ]
        for k in range(degree // together)
    ]


def fold(block, place, index, total):
    picks = picks_of(block, place)
    halves = []
    for half in range(len(picks)):
        terms = 0.0
        for t, pick in enumerate(picks):
            start = index * CHUNK + t * TILE
            hit = jnp.abs(pick - half) < 0.5
            terms += jnp.where(hit, total[start : start + TILE, :], 0.0)
        halves.append(terms)
    return jnp.concatenate(halves, axis=0).astype(jnp.bfloat16)


def early_kernel(start, low, high, slope, scale, *refs):
    if start:
        before, beside, cross, west, east, to_cross, to_beside, grads, total = refs
        total[...] = before[...]
    else:
        grads, total = refs
        total[...] = jnp.zeros_like(total)
    nodes = low.shape[2]
    first = nodes // CHUNK

    def grad_of(ref, m):
        grads[m] = (ref[m].astype(jnp.float32) * scale[...]).astype(jnp.bfloat16)
        return grads[m]

    chunks = [chunk_of(place, first, (1, PACK, nodes)) for place in EARLY]
    scatter(low, high, pairs(start, slope, nodes, grad_of), chunks, total)
    if start:
        to_beside[0] = fold(beside, 0, 0, total)
        to_cross[...] = fold(cross, 3, 1, total)
        to_beside[1] = fold(west, 4, 2, total)
        to_beside[2] = fold(east, 5, 3, total)


def all_pairs(parts, nodes):
    start, steps = 0, []
    for part in parts:
        steps += pairs(start, part, nodes, lambda ref, m: ref[m])
        start += part.shape[1]
    return steps


def late_kernel(low, high, *refs):
    *parts, west, east, to_west, to_east, total = refs
    nodes = low.shape[2]
    first = nodes // CHUNK
    chunks = [jnp.bfloat16(first + SLOT_OF[place][0]) for place in LATE]
    total[...] = jnp.zeros_like(total)
    scatter(low, high, all_pairs(parts, nodes), chunks, total)
    to_west[...] = fold(west, 1, 0, total)
    to_east[...] = fold(east, 2, 1, total)


def own_kernel(low, high, *refs):
    *parts, total, recv = refs
    nodes = low.shape[2]
    chunks = [jnp.bfloat16(chunk) for chunk in range(nodes // CHUNK)]
    total[...] = jnp.zeros_like(total)
    scatter(low, high, all_pairs(parts, nodes), chunks, total)
    start = 0
    for part in parts:
        degree, rows, _ = part.shape
        terms = 0.0
        for m in range(degree):
            terms += part[m].astype(jnp.float32)
        recv[:, start : start + rows] = terms.T.astype(jnp.bfloat16)
        start += rows


def output_kernel(tiles, feats, cots, w_out, w_node_v_t, *refs):
    *parts, updated, direct = refs
    count = len(parts) // 2
    rows = parts[0].shape[1]
    for k in range(count):
        hidden, grad_pre = parts[k], parts[count + k]
        span = slice(k * rows, (k + 1) * rows)
        lane = lax.broadcasted_iota(jnp.int32, (1, rows), 1) + k * rows
        active = (lane < tiles[0] * TILE).astype(jnp.float32)
        node_out = dot(w_out[...], hidden[...])
        new = feats[:, span].astype(jnp.float32) + active * node_out
        updated[:, span] = new.astype(jnp.bfloat16)
        direct[:, span] = cots[:, span].astype(jnp.float32) + dot(w_node_v_t[...], grad_pre[...])


def add_kernel(left, more, right, west, east):
    west[...] = (left[...].astype(jnp.float32) + more[1].astype(jnp.float32)).astype(jnp.bfloat16)
    east[...] = (right[...].astype(jnp.float32) + more[2].astype(jnp.float32)).astype(jnp.bfloat16)


def final_kernel(
    inv_root,
    tiles,
    own,
    recv,
    direct,
    feats,
    w_send_t,
    w_recv_t,
    upper,
    lower,
    across,
    beside,
    kept,
    sent,
    w_mine,
    w_beside,
    total,
    terms,
):
    rows = upper.shape[0]
    mine, sub, lon = lax.axis_index("ch"), lax.axis_index("sub"), lax.axis_index("lon")
    start = tiles[0] // 2 * TILE
    total[...] = own[...]

    def put(offset, block):
        spot = pl.ds(pl.multiple_of(offset, TILE), rows)
        total[spot, :] += block.astype(jnp.float32)

    put(start, upper[...])
    put(0, lower[...])
    put(jnp.where(sub == 0, 0, start), across[...])
    put(jnp.where(sub == 0, start, 0), beside[0])
    grad_send = total[...].astype(jnp.bfloat16)
    grad_send_t = total[...].T.astype(jnp.bfloat16)
    chans = direct.shape[0]
    terms[...] = dot(w_send_t[...], grad_send_t) + dot(w_recv_t[...], recv[...])
    kept[...] = direct[...] + mine_of(terms, mine, chans)
    count = sent.shape[0] + 1
    for k in range(1, count):
        sent[k - 1] = mine_of(terms, lax.rem(mine + k, count), chans).astype(jnp.bfloat16)
    weight = dot(feats[...], grad_send) * inv_root
    terms[:, : weight.shape[1]] = weight
    lons, columns, hid = w_mine.shape
    for k in range(lons):
        band = lax.rem(lon + k, lons) * 2
        for out, core in ((w_mine, sub), (w_beside, 1 - sub)):
            spot = pl.multiple_of((band + core) * columns, columns)
            out[k] = terms[pl.ds(spot, columns), :hid].astype(out.dtype)


def sum_kernel(w_mine, w_beside, near, sent):
    near[...] = w_mine[0] + w_beside[0].astype(jnp.float32)
    for k in range(sent.shape[0]):
        sent[k] = (w_mine[k + 1] + w_beside[k + 1].astype(jnp.float32)).astype(jnp.bfloat16)


def weight_kernel(near, *refs):
    out = refs[-1]
    total = near[...]
    for ref in refs[:-1]:
        total += ref[...].astype(jnp.float32)
    out[...] = total.T


def shards(
    features,
    cotangent,
    senders,
    in_degree,
    tile_count,
    send_tiles,
    w_send,
    w_recv,
    bias_edge,
    w_msg,
    w_node_v,
    w_node_a,
    bias_node,
    w_out,
):
    chans, nodes = features.shape
    count = lax.axis_size("ch")
    lons = lax.axis_size("lon")
    hidden_all, chans_all = w_send.shape
    hid = hidden_all // count
    cycle = ("lon", "sub")
    shard_count = lax.axis_size(cycle)
    total_nodes = nodes * shard_count
    degree = senders.shape[0]
    slots = send_tiles.shape[1]
    slot_rows = send_tiles.shape[2] * TILE
    ext_len = nodes + slots * slot_rows
    bf16, f32 = jnp.bfloat16, jnp.float32
    shape = jax.ShapeDtypeStruct

    across_route = [(i, (i + (3 if i % 2 else -3)) % shard_count) for i in range(shard_count)]
    across = lambda block: lax.ppermute(block, cycle, across_route)
    degrees = in_degree[None, :]

    feat_blocks = gathered(features, "ch")
    cot_blocks = gathered(cotangent, "ch")

    fixed = (
        [shape((hid, chans_all), bf16)] * 2
        + [shape((chans_all, hidden_all), bf16), shape((hidden_all, chans_all), bf16)]
        + [shape((hidden_all, chans_all), bf16), shape((chans, hidden_all), bf16)]
    )
    inputs = [senders, degrees, features, cotangent, bias_edge[None, :], bias_node[None, :]]
    held = call(
        weights_kernel,
        (
            *fixed,
            *[shape(x.shape, x.dtype) for x in inputs],
            shape((chans_all, hid), bf16),
            shape((chans_all, hid), bf16),
            shape((hid, chans_all), bf16),
            shape((chans, hidden_all), bf16),
            shape((chans_all, hidden_all), bf16),
            shape((hidden_all, chans_all), bf16),
            shape((degree, nodes, LANES), bf16),
            shape((degree, nodes, LANES), bf16),
            shape((degree, PACK, nodes), bf16),
            shape((degree, PACK, nodes), bf16),
        ),
        [tile_count, send_tiles, w_send, w_recv, w_msg, w_node_v, w_node_a, w_out] + inputs,
        flops=4 * hidden_all * chans_all * nodes,
        away=12,
        scratch=[
            pltpu.VMEM((chans_all, hidden_all), bf16),
            pltpu.VMEM((chans_all, hidden_all), bf16),
            pltpu.SemaphoreType.DMA((12,)),
        ],
    )
    w_send_my, w_recv_my, w_msg, w_node_v, w_node_a, w_out_my, _, degrees = held[:8]
    features_held, cotangent_held, bias_edge, bias_node = held[8:12]
    w_send_t, w_recv_t, w_msg_t, w_node_v_t, w_node_a_t, w_out_t = held[12:18]
    low_cols, high_cols, low_rows, high_rows = held[18:]
    feat_blocks[0], cot_blocks[0] = features_held, cotangent_held

    block = shape((slot_rows + PACK, hid), bf16)
    feats, proj, base, upper, lower, cross, beside = call(
        functools.partial(project_kernel, count),
        (
            shape((chans_all, nodes), bf16),
            shape((nodes, hid), bf16),
            shape((nodes, hid), f32),
            block,
            block,
            block,
            block,
        ),
        [tile_count, send_tiles, bias_edge] + feat_blocks + [w_send_my, w_recv_my],
        flops=4 * hid * chans_all * nodes,
    )
    west = shifted(upper, "lon", 1)
    east = shifted(lower, "lon", -1)
    beside = shifted(beside, "sub", 1)
    cross = across(cross)
    west_too = shifted(west, "sub", 1)
    east_too = shifted(east, "sub", 1)
    cots, pre, grad_hidden = call(
        functools.partial(prepare_kernel, count),
        (
            shape((chans_all, nodes), bf16),
            shape((hidden_all, nodes), f32),
            shape((hidden_all, nodes), f32),
        ),
        [tile_count] + cot_blocks + [feats, w_node_v, bias_node, w_out_t],
        flops=4 * hidden_all * chans_all * nodes,
        scalars=1,
    )

    part_shape = shape((degree, nodes, hid), bf16)
    part = call(
        near_kernel,
        part_shape,
        [low_cols, high_cols, proj, beside],
        flops=2 * degree * nodes * (nodes + slot_rows) * hid,
        scratch=[pltpu.VMEM((nodes + slot_rows, hid), bf16)],
        scalars=0,
    )
    part = call(
        line_kernel,
        part_shape,
        [low_cols, high_cols, part, west, east],
        flops=2 * degree * nodes * 2 * slot_rows * hid,
        scratch=[pltpu.VMEM((2 * slot_rows, hid), bf16)],
        scalars=0,
    )
    halves = 2
    rows = nodes // halves
    slopes, messages, hiddens, grad_pres, grads = [], [], [], [], []
    for k in range(halves):
        message, slope = call(
            functools.partial(message_kernel, k * rows),
            (shape((hid, rows), bf16), shape((degree, rows, hid), bf16)),
            [low_cols, high_cols, base, degrees, part, cross, west_too, east_too],
            flops=2 * degree * rows * 3 * slot_rows * hid,
            scratch=[pltpu.VMEM((3 * slot_rows, hid), bf16), pltpu.VMEM((rows, hid), f32)],
            scalars=0,
        )
        slopes.append(slope)
        messages.append(gathered(message, "ch"))

    block = shape((slot_rows, hid), bf16)
    sums = shape((len(EARLY) * slot_rows, hid), f32)
    grad_shape = shape((degree, rows, hid), bf16)
    for k in range(halves):
        hidden, grad_pre, scale = call(
            functools.partial(node_kernel, count, k * rows),
            (
                shape((hidden_all, rows), bf16),
                shape((hidden_all, rows), bf16),
                shape((rows, hid), f32),
            ),
            [degrees] + messages[k] + [w_msg, w_node_a, w_node_a_t, w_msg_t, pre, grad_hidden],
            flops=6 * hidden_all * chans_all * rows,
            scratch=[pltpu.VMEM((hidden_all, rows), bf16)],
            scalars=0,
        )
        hiddens.append(hidden)
        grad_pres.append(grad_pre)
        operands = [low_rows, high_rows, slopes[k], scale]
        flops = 2 * degree * rows * len(EARLY) * slot_rows * hid
        kernel = functools.partial(early_kernel, k * rows)
        if k == 0:
            grad, before = call(kernel, (grad_shape, sums), operands, flops=flops, scalars=0)
        else:
            to_cross, to_beside, grad = call(
                kernel,
                (block, shape((3, slot_rows, hid), bf16), grad_shape),
                operands + [before, beside, cross, west_too, east_too],
                flops=flops,
                scratch=[pltpu.VMEM(sums.shape, f32)],
                scalars=0,
            )
        grads.append(grad)

    from_beside = shifted(to_beside, "sub", 1)
    from_cross = across(to_cross)
    to_west, to_east = call(
        late_kernel,
        (block, block),
        [low_rows, high_rows] + grads + [west, east],
        flops=2 * degree * nodes * len(LATE) * slot_rows * hid,
        scratch=[pltpu.VMEM((len(LATE) * slot_rows, hid), f32)],
        scalars=0,
    )
    to_west, to_east = call(
        add_kernel, (block, block), [to_west, from_beside, to_east], flops=0, scalars=0
    )
    from_upper = shifted(to_west, "lon", -1)
    from_lower = shifted(to_east, "lon", 1)

    own, grad_recv = call(
        own_kernel,
        (shape((nodes, hid), f32), shape((hid, nodes), bf16)),
        [low_rows, high_rows] + grads,
        flops=2 * degree * nodes * nodes * hid,
        scalars=0,
    )
    updated, direct = call(
        output_kernel,
        (shape((chans, nodes), bf16), shape((chans, nodes), f32)),
        [tile_count, features_held, cotangent_held, w_out_my, w_node_v_t] + hiddens + grad_pres,
        flops=4 * hidden_all * chans * nodes,
        scalars=1,
    )

    columns = chans_all // shard_count
    kept, sent, w_mine, w_beside = call(
        functools.partial(final_kernel, 1.0 / math.sqrt(total_nodes)),
        (
            shape((chans, nodes), f32),
            shape((count - 1, chans, nodes), bf16),
            shape((lons, columns, hid), f32),
            shape((lons, columns, hid), bf16),
        ),
        [tile_count, own, grad_recv, direct, feats, w_send_t, w_recv_t]
        + [from_upper, from_lower, from_cross, from_beside],
        flops=6 * hid * chans_all * nodes,
        scratch=[pltpu.VMEM((nodes, hid), f32), pltpu.VMEM((chans_all, nodes), f32)],
        scalars=1,
    )
    w_beside = shifted(w_beside, "sub", 1)
    for k in range(1, count):
        kept = kept + shifted(sent[k - 1], "ch", k).astype(f32)
    grad_features = kept.astype(bf16)

    near, w_sent = call(
        sum_kernel,
        (shape((columns, hid), f32), shape((lons - 1, columns, hid), bf16)),
        [w_mine, w_beside],
        flops=0,
        scalars=0,
    )
    w_terms = [shifted(w_sent[k - 1], "lon", k) for k in range(1, lons)]
    grad_w_send = call(
        weight_kernel, shape((hid, columns), f32), [near] + w_terms, flops=0, scalars=0
    )
    return (updated, grad_features, grad_w_send)


def solution(mesh):
    nodes_last = P("ch", ("parts", "lon", "sub"))
    spread = ("parts", "lon", "sub")
    placed = (nodes_last, nodes_last, P(None, spread), P(spread), P(spread), P(spread, None, None))
    return jax.shard_map(
        shards,
        mesh=mesh,
        in_specs=placed + (P(),) * 8,
        out_specs=(nodes_last, nodes_last, P(("parts", "ch"), ("lon", "sub"))),
        check_vma=False,
    )
```

```python
import functools
import math

import jax
import jax.numpy as jnp
from jax import lax
from jax.experimental import pallas as pl
from jax.experimental.pallas import tpu as pltpu
from jax.sharding import PartitionSpec as P

TILE = 128
CHUNK = 256
LANES = 128
PACK = 16
MIB = 1 << 20
WEIGHTS_LIMIT = 52
NO_CHUNK = 64
SLOT_OF = ((3, 0), (1, 1), (4, 4), (2, 5), (0, 2), (5, 3))
EARLY, LATE = (0, 3, 4, 5), (1, 2)
OFF = -1e4


def shifted(block, axis, distance):
    size = lax.axis_size(axis)
    route = [((i - distance) % size, i) for i in range(size)]
    return lax.ppermute(block, axis, route)


def gathered(block, axis):
    return [block] + [shifted(block, axis, k) for k in range(1, lax.axis_size(axis))]


def dot(left, right):
    return jnp.dot(left, right, preferred_element_type=jnp.float32)


def dot_nt(left, right):
    return lax.dot_general(
        left, right, (((1,), (1,)), ((), ())), preferred_element_type=jnp.float32
    )


def sigmoid(value):
    return 0.5 * jnp.tanh(0.5 * value) + 0.5


def call(kernel, out_shape, operands, flops, scratch=(), scalars=2, away=0, limit=24):
    vmem = pl.BlockSpec(memory_space=pltpu.VMEM)
    smem = pl.BlockSpec(memory_space=pltpu.SMEM)
    anywhere = pl.BlockSpec(memory_space=pltpu.HBM)
    moved = sum(math.prod(x.shape) * x.dtype.itemsize for x in operands)
    return pl.pallas_call(
        kernel,
        out_shape=out_shape,
        in_specs=[smem] * scalars
        + [anywhere] * away
        + [vmem] * (len(operands) - scalars - away),
        out_specs=jax.tree.map(lambda _: vmem, out_shape),
        scratch_shapes=scratch,
        compiler_params=pltpu.CompilerParams(vmem_limit_bytes=limit * MIB),
        cost_estimate=pl.CostEstimate(flops=flops, bytes_accessed=moved, transcendentals=0),
    )(*operands)


def assemble(whole_ref, blocks, first):
    count = len(blocks)
    rows = blocks[0].shape[0]
    for k, block in enumerate(blocks):
        place = lax.rem(first - k + count, count) * rows
        whole_ref[pl.ds(pl.multiple_of(place, rows), rows), :] = block[...]


def mine_of(ref, index, rows):
    return ref[pl.ds(pl.multiple_of(index * rows, rows), rows), :]


def weights_kernel(*refs):
    sources, refs = refs[:7], refs[7:]
    w_send, w_recv, w_out, feats, w_send_t, w_recv_t, w_msg_t, w_node_v_t, w_node_a_t, w_out_t = refs[:10]
    w_msg, w_node_v, w_node_a, w_out_all, turned, sems = refs[10:]
    mine = lax.axis_index("ch")
    hid = w_send.shape[0]
    targets = (feats, w_send, w_recv, w_msg, w_node_v, w_node_a, w_out_all)
    copies = []
    for k, (source, target) in enumerate(zip(sources, targets)):
        if k in (1, 2):
            source = source.at[pl.ds(pl.multiple_of(mine * hid, hid), hid), :]
        copies.append(pltpu.make_async_copy(source, target, sems.at[k]))
    for copy in copies:
        copy.start()
    for copy in copies:
        copy.wait()
    w_send_t[...] = w_send[...].T
    w_recv_t[...] = w_recv[...].T
    turned[...] = w_msg[...].T
    w_msg_t[...] = mine_of(turned, mine, hid)
    turned[...] = w_node_v[...].T
    w_node_v_t[...] = mine_of(turned, mine, w_node_v_t.shape[0])
    w_node_a_t[...] = w_node_a[...].T
    w_out_t[...] = w_out_all[...].T
    w_out[...] = mine_of(w_out_all, mine, w_out.shape[0])


def edges_kernel(tiles, senders, in_degree, low_cols, high_cols, low_rows, high_rows):
    degree, nodes = senders.shape
    lane = lax.broadcasted_iota(jnp.int32, (degree, nodes), 1)
    row = lax.broadcasted_iota(jnp.int32, (degree, nodes), 0)
    valid = (row < in_degree[...]) & (lane < tiles[0] * TILE)
    ids = senders[...]
    low = (ids & (CHUNK - 1)).astype(jnp.float32)
    high = jnp.where(valid, ids // CHUNK, NO_CHUNK).astype(jnp.float32)
    for m in range(degree):
        shape = (PACK, nodes)
        low_rows[m] = jnp.broadcast_to(low[m : m + 1], shape).astype(jnp.bfloat16)
        high_rows[m] = jnp.broadcast_to(high[m : m + 1], shape).astype(jnp.bfloat16)
    fill = jnp.zeros((PACK - degree, nodes), jnp.float32)
    depth = 2 * PACK
    both = jnp.concatenate([low, fill, high, fill], axis=0).T.astype(jnp.bfloat16)
    width = degree * LANES
    spot = lax.broadcasted_iota(jnp.int32, (depth, width), 0)
    group = lax.broadcasted_iota(jnp.int32, (depth, width), 1) // LANES
    for first, out in ((0, low_cols), (PACK, high_cols)):
        pick = (spot == group + first).astype(jnp.bfloat16)
        spread = dot(both, pick).astype(jnp.bfloat16)
        for m in range(degree):
            out[m] = spread[:, m * LANES : (m + 1) * LANES]


def project_kernel(count, tiles, picks, bias, *refs):
    blocks = refs[:count]
    w_send, w_recv, feats, proj, base, upper, lower, beside = refs[count:]
    mine, sub = lax.axis_index("ch"), lax.axis_index("sub")
    first = tiles[0] // 2
    assemble(feats, blocks, mine)
    whole = feats[...]
    hid = proj.shape[1]
    proj[...] = (0.5 * dot(w_send[...], whole).T).astype(jnp.bfloat16)
    rows = upper.shape[0] - PACK
    upper[:rows, :] = proj[pl.ds(pl.multiple_of(first * TILE, TILE), rows), :]
    lower[:rows, :] = proj[:rows, :]
    spot = lax.broadcasted_iota(jnp.int32, (PACK, hid), 0)
    _, per_slot, slots = picks.shape
    half = slots // 2
    for start, out, lift in ((0, upper, first), (half, lower, 0)):
        marks = jnp.zeros((PACK, hid), jnp.float32)
        for k in range(half * per_slot):
            rel = picks[0, k % per_slot, start + k // per_slot] - lift
            marks = jnp.where(spot == k, rel.astype(jnp.float32), marks)
        out[rows:, :] = marks.astype(jnp.bfloat16)

    @pl.when(sub == 0)
    def _():
        beside[...] = upper[...]

    @pl.when(sub != 0)
    def _():
        beside[...] = lower[...]

    my_bias = jnp.zeros((1, hid), jnp.float32)
    for k in range(count):
        my_bias += jnp.where(mine == k, bias[:, k * hid : (k + 1) * hid], 0.0)
    recv = dot(w_recv[...], whole).T
    base[...] = 0.5 * (recv.astype(jnp.bfloat16).astype(jnp.float32) + my_bias)


def prepare_kernel(count, tiles, *refs):
    blocks = refs[:count]
    feats, w_node_v, bias, w_out_t, cots, pre, grad_hidden = refs[count:]
    assemble(cots, blocks, lax.axis_index("ch"))
    column = jnp.broadcast_to(bias[...], (8, bias.shape[1])).T[:, :1]
    pre[...] = dot(w_node_v[...], feats[...]) + column
    lane = lax.broadcasted_iota(jnp.int32, (1, cots.shape[1]), 1)
    active = (lane < tiles[0] * TILE).astype(jnp.bfloat16)
    grad_hidden[...] = dot(w_out_t[...], cots[...] * active)


def chunk_of(place, first, shape):
    on_zero, on_one = (float(first + slot) for slot in SLOT_OF[place])
    chunk = jnp.where(lax.axis_index("sub") == 0, on_zero, on_one)
    return jnp.full(shape, chunk, jnp.float32).astype(jnp.bfloat16)


def picks_of(block, place):
    marks = block[CHUNK : CHUNK + PACK, :].astype(jnp.float32)
    per_slot = CHUNK // TILE
    half = len(SLOT_OF) // 2
    starts = [slot % half * per_slot for slot in SLOT_OF[place]]
    sub = lax.axis_index("sub")
    return [
        jnp.where(
            sub == 0,
            marks[starts[0] + t : starts[0] + t + 1],
            marks[starts[1] + t : starts[1] + t + 1],
        )
        for t in range(per_slot)
    ]


def fill(ext, start, block, place):
    for t, pick in enumerate(picks_of(block, place)):
        ext[start + t * TILE : start + (t + 1) * TILE, :] = jnp.where(
            pick > 0.5, block[TILE : 2 * TILE, :], block[:TILE, :]
        )


def pick_rows(low, high, chunks, ext):
    one = jnp.bfloat16(1.0)
    zero = jnp.bfloat16(0.0)
    lane = lax.broadcasted_iota(jnp.int32, low.shape, 1)
    marks = [
        jnp.where(low == (lane + half * LANES).astype(jnp.bfloat16), one, zero)
        for half in range(CHUNK // LANES)
    ]
    picker = jnp.concatenate(
        [jnp.where(high == chunk, mark, zero) for chunk in chunks for mark in marks], axis=1
    )
    return dot(picker, ext[...])


def near_kernel(low, high, proj, beside, part, ext):
    own = proj.shape[0]
    ext[:own, :] = proj[...]
    fill(ext, own, beside, 0)
    first = own // CHUNK
    chunks = [jnp.bfloat16(chunk) for chunk in range(first)]
    chunks.append(chunk_of(0, first, low.shape[1:]))

    def step(m, carry):
        part[m] = pick_rows(low[m], high[m], chunks, ext).astype(jnp.bfloat16)
        return carry

    lax.fori_loop(0, low.shape[0], step, 0, unroll=True)


def line_kernel(low, high, before, west, east, part, ext):
    first = low.shape[1] // CHUNK
    chunks = []
    for index, (place, block) in enumerate(((1, west), (2, east))):
        fill(ext, index * CHUNK, block, place)
        chunks.append(jnp.bfloat16(first + SLOT_OF[place][0]))

    def step(m, carry):
        more = pick_rows(low[m], high[m], chunks, ext)
        part[m] = (before[m].astype(jnp.float32) + more).astype(jnp.bfloat16)
        return carry

    lax.fori_loop(0, low.shape[0], step, 0, unroll=True)


def message_kernel(
    start, low, high, base, in_degree, part, cross, west, east, message, slope, ext, total
):
    nodes = low.shape[1]
    degree, rows, hid = slope.shape
    first = nodes // CHUNK
    together = nodes // rows
    span = slice(start, start + rows)
    chunks = []
    for index, (place, block) in enumerate(((3, cross), (4, west), (5, east))):
        fill(ext, index * CHUNK, block, place)
        chunks.append(chunk_of(place, first, (nodes, LANES)))
    total[...] = jnp.zeros_like(total)

    def rows_of(ref, k):
        return jnp.concatenate([ref[k * together + i, span, :] for i in range(together)], axis=0)

    def step(k, carry):
        low_k, high_k = rows_of(low, k), rows_of(high, k)
        half = pick_rows(low_k, high_k, chunks, ext) + rows_of(part, k).astype(jnp.float32)
        half += jnp.concatenate([base[span, :]] * together, axis=0)
        wide = jnp.concatenate([high_k] * pl.cdiv(hid, LANES), axis=1)[:, :hid]
        half = jnp.where(wide.astype(jnp.float32) < NO_CHUNK, half, OFF)
        twice = jnp.tanh(half) + 1.0
        act = half * twice
        grad = (twice + act * (2.0 - twice)).astype(jnp.bfloat16)
        terms = 0.0
        for i in range(together):
            terms += act[i * rows : (i + 1) * rows]
            slope[k * together + i] = grad[i * rows : (i + 1) * rows]
        total[...] += terms
        return carry

    lax.fori_loop(0, degree // together, step, 0, unroll=True)
    count = in_degree[:, span].astype(jnp.float32)
    message[...] = (total[...].T / count).astype(jnp.bfloat16)


def node_kernel(count, start, in_degree, *refs):
    blocks = refs[:count]
    w_msg, w_node_a, w_node_a_t, w_msg_t, pre, grad_hidden = refs[count : count + 6]
    hidden, grad_pre, scale, messages = refs[count + 6 :]
    assemble(messages, blocks, lax.axis_index("ch"))
    span = slice(start, start + hidden.shape[1])
    agg = dot(w_msg[...], messages[...])
    half = 0.5 * (pre[:, span] + dot(w_node_a[...], agg.astype(jnp.bfloat16)))
    twice = jnp.tanh(half) + 1.0
    act = half * twice
    hidden[...] = act.astype(jnp.bfloat16)
    slope = 0.5 * (twice + act * (2.0 - twice))
    low_grad = (grad_hidden[:, span] * slope).astype(jnp.bfloat16)
    grad_pre[...] = low_grad
    grad_agg = dot(w_node_a_t[...], low_grad).astype(jnp.bfloat16)
    grad_msg = dot(w_msg_t[...], grad_agg).astype(jnp.bfloat16).astype(jnp.float32)
    scale[...] = (grad_msg * (0.5 / in_degree[:, span].astype(jnp.float32))).T


def scatter(low, high, edges, chunks, total):
    one = jnp.bfloat16(1.0)
    zero = jnp.bfloat16(0.0)
    groups = CHUNK // PACK
    for step in edges:
        width = sum(rows for _, _, rows, _ in step)
        place = lax.broadcasted_iota(jnp.int32, (groups, PACK, width), 0) * PACK
        place = place + lax.broadcasted_iota(jnp.int32, (groups, PACK, width), 1)
        low_k = jnp.concatenate([low[m, :, s : s + r] for m, s, r, _ in step], axis=1)
        high_k = jnp.concatenate([high[m, :, s : s + r] for m, s, r, _ in step], axis=1)
        grads = jnp.concatenate([grad() for _, _, _, grad in step], axis=0)
        mark = jnp.where(low_k[None] == place.astype(jnp.bfloat16), one, zero)
        picker = jnp.concatenate(
            [jnp.where(high_k[None] == chunk, mark, zero) for chunk in chunks], axis=0
        ).reshape(len(chunks) * CHUNK, width)
        total[...] += dot(picker, grads)


def pairs(start, ref, nodes, grad_of):
    degree, rows, _ = ref.shape
    together = nodes // rows
    return [
        [
            (m, start, rows, functools.partial(grad_of, ref, m))
            for m in range(k * together, (k + 1) * together)
        ]
        for k in range(degree // together)
    ]


def fold(block, place, index, total):
    picks = picks_of(block, place)
    halves = []
    for half in range(len(picks)):
        terms = 0.0
        for t, pick in enumerate(picks):
            start = index * CHUNK + t * TILE
            hit = jnp.abs(pick - half) < 0.5
            terms += jnp.where(hit, total[start : start + TILE, :], 0.0)
        halves.append(terms)
    return jnp.concatenate(halves, axis=0).astype(jnp.bfloat16)


def early_kernel(start, low, high, slope, scale, *refs):
    if start:
        before, beside, cross, west, east, to_cross, to_beside, grads, total = refs
        total[...] = before[...]
    else:
        grads, total = refs
        total[...] = jnp.zeros_like(total)
    nodes = low.shape[2]
    first = nodes // CHUNK

    def grad_of(ref, m):
        grads[m] = (ref[m].astype(jnp.float32) * scale[...]).astype(jnp.bfloat16)
        return grads[m]

    chunks = [chunk_of(place, first, (1, PACK, nodes)) for place in EARLY]
    scatter(low, high, pairs(start, slope, nodes, grad_of), chunks, total)
    if start:
        to_beside[0] = fold(beside, 0, 0, total)
        to_cross[...] = fold(cross, 3, 1, total)
        to_beside[1] = fold(west, 4, 2, total)
        to_beside[2] = fold(east, 5, 3, total)


def all_pairs(parts, nodes):
    start, steps = 0, []
    for part in parts:
        steps += pairs(start, part, nodes, lambda ref, m: ref[m])
        start += part.shape[1]
    return steps


def late_kernel(low, high, *refs):
    *parts, west, east, to_west, to_east, total = refs
    nodes = low.shape[2]
    first = nodes // CHUNK
    chunks = [jnp.bfloat16(first + SLOT_OF[place][0]) for place in LATE]
    total[...] = jnp.zeros_like(total)
    scatter(low, high, all_pairs(parts, nodes), chunks, total)
    to_west[...] = fold(west, 1, 0, total)
    to_east[...] = fold(east, 2, 1, total)


def own_kernel(low, high, *refs):
    *parts, total, recv = refs
    nodes = low.shape[2]
    chunks = [jnp.bfloat16(chunk) for chunk in range(nodes // CHUNK)]
    total[...] = jnp.zeros_like(total)
    scatter(low, high, all_pairs(parts, nodes), chunks, total)
    start = 0
    for part in parts:
        degree, rows, _ = part.shape
        terms = 0.0
        for m in range(degree):
            terms += part[m].astype(jnp.float32)
        recv[:, start : start + rows] = terms.T.astype(jnp.bfloat16)
        start += rows


def output_kernel(tiles, feats, cots, w_out, w_node_v_t, *refs):
    *parts, updated, direct = refs
    count = len(parts) // 2
    rows = parts[0].shape[1]
    for k in range(count):
        hidden, grad_pre = parts[k], parts[count + k]
        span = slice(k * rows, (k + 1) * rows)
        lane = lax.broadcasted_iota(jnp.int32, (1, rows), 1) + k * rows
        active = (lane < tiles[0] * TILE).astype(jnp.float32)
        node_out = dot(w_out[...], hidden[...])
        new = feats[:, span].astype(jnp.float32) + active * node_out
        updated[:, span] = new.astype(jnp.bfloat16)
        direct[:, span] = cots[:, span].astype(jnp.float32) + dot(w_node_v_t[...], grad_pre[...])


def add_kernel(left, more, right, across, west, east):
    sub = lax.axis_index("sub")
    other = across[...].astype(jnp.float32)
    to_west = left[...].astype(jnp.float32) + more[1].astype(jnp.float32)
    to_east = right[...].astype(jnp.float32) + more[2].astype(jnp.float32)
    west[...] = (to_west + jnp.where(sub == 0, 0.0, other)).astype(jnp.bfloat16)
    east[...] = (to_east + jnp.where(sub == 0, other, 0.0)).astype(jnp.bfloat16)


def back_kernel(start, inv_root, tiles, own, beside, feats, upper, *refs):
    *refs, total = refs
    sub = lax.axis_index("sub")
    offset = pl.multiple_of(tiles[0] // 2 * TILE, TILE)
    total[...] = own[...]
    near = beside[0].astype(jnp.float32)
    block = upper[...].astype(jnp.float32) + jnp.where(sub == 0, near, 0.0)
    total[pl.ds(offset, block.shape[0]), :] += block
    if start:
        grad_send, weight = refs
    else:
        lower, before, grad_send, w_mine, w_beside, weight = refs
        block = lower[...].astype(jnp.float32) + jnp.where(sub == 0, 0.0, near)
        total[: block.shape[0], :] += block
    rows = grad_send.shape[0]
    grad_send[...] = total[start : start + rows, :].astype(jnp.bfloat16)
    terms = dot(feats[:, start : start + rows], grad_send[...])
    if start:
        weight[...] = terms
        return
    weight[...] = (before[...] + terms) * inv_root
    lon = lax.axis_index("lon")
    lons, columns, _ = w_mine.shape
    for k in range(lons):
        band = lax.rem(lon + k, lons) * 2
        for out, core in ((w_mine, sub), (w_beside, 1 - sub)):
            spot = pl.multiple_of((band + core) * columns, columns)
            out[k] = weight[pl.ds(spot, columns), :].astype(out.dtype)


def terms_kernel(start, grad_send, recv, direct, w_send_t, w_recv_t, kept, sent, terms):
    span = slice(start, start + grad_send.shape[0])
    mine = lax.axis_index("ch")
    chans = kept.shape[0]
    grad_send_t = grad_send[...].astype(jnp.float32).T.astype(jnp.bfloat16)
    terms[...] = dot(w_send_t[...], grad_send_t) + dot(w_recv_t[...], recv[:, span])
    kept[...] = direct[:, span] + mine_of(terms, mine, chans)
    count = sent.shape[0] + 1
    for k in range(1, count):
        sent[k - 1] = mine_of(terms, lax.rem(mine + k, count), chans).astype(jnp.bfloat16)


def finish_kernel(*refs):
    *parts, out = refs
    rows = out.shape[1] // 2
    count = len(parts) // 2
    for k in range(2):
        kept, *others = parts[k * count : (k + 1) * count]
        total = kept[...]
        for other in others:
            total += other[...].astype(jnp.float32)
        out[:, k * rows : (k + 1) * rows] = total.astype(jnp.bfloat16)


def sum_kernel(w_mine, w_beside, near, sent):
    near[...] = w_mine[0] + w_beside[0].astype(jnp.float32)
    for k in range(sent.shape[0]):
        sent[k] = (w_mine[k + 1] + w_beside[k + 1].astype(jnp.float32)).astype(jnp.bfloat16)


def weight_kernel(near, *refs):
    out = refs[-1]
    total = near[...]
    for ref in refs[:-1]:
        total += ref[...].astype(jnp.float32)
    out[...] = total


def shards(
    features,
    cotangent,
    senders,
    in_degree,
    tile_count,
    send_tiles,
    w_send,
    w_recv,
    bias_edge,
    w_msg,
    w_node_v,
    w_node_a,
    bias_node,
    w_out,
):
    chans, nodes = features.shape
    count = lax.axis_size("ch")
    lons = lax.axis_size("lon")
    hidden_all, chans_all = w_send.shape
    hid = hidden_all // count
    cycle = ("lon", "sub")
    shard_count = lax.axis_size(cycle)
    total_nodes = nodes * shard_count
    degree = senders.shape[0]
    slots = send_tiles.shape[1]
    slot_rows = send_tiles.shape[2] * TILE
    ext_len = nodes + slots * slot_rows
    bf16, f32 = jnp.bfloat16, jnp.float32
    shape = jax.ShapeDtypeStruct

    across_route = [(i, (i + (1 if i % 2 else -1)) % shard_count) for i in range(shard_count)]
    across = lambda block: lax.ppermute(block, cycle, across_route)
    degrees = in_degree[None, :]
    picks = jnp.transpose(send_tiles, (0, 2, 1))
    sub = lax.axis_index("sub")

    feat_blocks = gathered(features, "ch")
    cot_blocks = gathered(cotangent, "ch")

    whole_w = pltpu.VMEM((chans_all, hidden_all), bf16)
    (
        w_send_my,
        w_recv_my,
        w_out_my,
        features_held,
        w_send_t,
        w_recv_t,
        w_msg_t,
        w_node_v_t,
        w_node_a_t,
        w_out_t,
    ) = call(
        weights_kernel,
        (
            shape((hid, chans_all), bf16),
            shape((hid, chans_all), bf16),
            shape((chans, hidden_all), bf16),
            shape((chans, nodes), bf16),
            shape((chans_all, hid), bf16),
            shape((chans_all, hid), bf16),
            shape((hid, chans_all), bf16),
            shape((chans, hidden_all), bf16),
            shape((chans_all, hidden_all), bf16),
            shape((hidden_all, chans_all), bf16),
        ),
        [features, w_send, w_recv, w_msg, w_node_v, w_node_a, w_out],
        flops=4 * hidden_all * chans_all * nodes,
        away=7,
        scalars=0,
        scratch=[whole_w] * 5 + [pltpu.SemaphoreType.DMA((7,))],
        limit=WEIGHTS_LIMIT,
    )
    feat_blocks[0] = features_held
    low_cols, high_cols, low_rows, high_rows = call(
        edges_kernel,
        (
            shape((degree, nodes, LANES), bf16),
            shape((degree, nodes, LANES), bf16),
            shape((degree, PACK, nodes), bf16),
            shape((degree, PACK, nodes), bf16),
        ),
        [tile_count, senders, degrees],
        flops=2 * hidden_all * chans_all * nodes,
        scalars=1,
    )

    block = shape((slot_rows + PACK, hid), bf16)
    feats, proj, base, upper, lower, beside = call(
        functools.partial(project_kernel, count),
        (
            shape((chans_all, nodes), bf16),
            shape((nodes, hid), bf16),
            shape((nodes, hid), f32),
            block,
            block,
            block,
        ),
        [tile_count, picks, bias_edge[None, :]] + feat_blocks + [w_send_my, w_recv_my],
        flops=4 * hid * chans_all * nodes,
    )
    west = shifted(upper, "lon", 1)
    east = shifted(lower, "lon", -1)
    beside = shifted(beside, "sub", 1)
    cots, pre, grad_hidden = call(
        functools.partial(prepare_kernel, count),
        (
            shape((chans_all, nodes), bf16),
            shape((hidden_all, nodes), f32),
            shape((hidden_all, nodes), f32),
        ),
        [tile_count] + cot_blocks + [feats, w_node_v, bias_node[None, :], w_out_t],
        flops=4 * hidden_all * chans_all * nodes,
        scalars=1,
    )

    part_shape = shape((degree, nodes, hid), bf16)
    part = call(
        near_kernel,
        part_shape,
        [low_cols, high_cols, proj, beside],
        flops=2 * degree * nodes * (nodes + slot_rows) * hid,
        scratch=[pltpu.VMEM((nodes + slot_rows, hid), bf16)],
        scalars=0,
    )
    west, east, part = lax.optimization_barrier((west, east, part))
    west_too = shifted(west, "sub", 1)
    east_too = shifted(east, "sub", 1)
    cross = across(jnp.where(sub == 0, east, west))
    part, pre = lax.optimization_barrier((part, pre))
    part = call(
        line_kernel,
        part_shape,
        [low_cols, high_cols, part, west, east],
        flops=2 * degree * nodes * 2 * slot_rows * hid,
        scratch=[pltpu.VMEM((2 * slot_rows, hid), bf16)],
        scalars=0,
    )
    halves = 2
    rows = nodes // halves
    slopes, messages, hiddens, grad_pres, grads = [], [], [], [], []
    for k in range(halves):
        message, slope = call(
            functools.partial(message_kernel, k * rows),
            (shape((hid, rows), bf16), shape((degree, rows, hid), bf16)),
            [low_cols, high_cols, base, degrees, part, cross, west_too, east_too],
            flops=2 * degree * rows * 3 * slot_rows * hid,
            scratch=[pltpu.VMEM((3 * slot_rows, hid), bf16), pltpu.VMEM((rows, hid), f32)],
            scalars=0,
        )
        slopes.append(slope)
        messages.append(gathered(message, "ch"))

    block = shape((slot_rows, hid), bf16)
    sums = shape((len(EARLY) * slot_rows, hid), f32)
    grad_shape = shape((degree, rows, hid), bf16)
    for k in range(halves):
        hidden, grad_pre, scale = call(
            functools.partial(node_kernel, count, k * rows),
            (
                shape((hidden_all, rows), bf16),
                shape((hidden_all, rows), bf16),
                shape((rows, hid), f32),
            ),
            [degrees] + messages[k] + [w_msg, w_node_a, w_node_a_t, w_msg_t, pre, grad_hidden],
            flops=6 * hidden_all * chans_all * rows,
            scratch=[pltpu.VMEM((hidden_all, rows), bf16)],
            scalars=0,
        )
        hiddens.append(hidden)
        grad_pres.append(grad_pre)
        operands = [low_rows, high_rows, slopes[k], scale]
        flops = 2 * degree * rows * len(EARLY) * slot_rows * hid
        kernel = functools.partial(early_kernel, k * rows)
        if k == 0:
            grad, before = call(kernel, (grad_shape, sums), operands, flops=flops, scalars=0)
        else:
            to_cross, to_beside, grad = call(
                kernel,
                (block, shape((3, slot_rows, hid), bf16), grad_shape),
                operands + [before, beside, cross, west_too, east_too],
                flops=flops,
                scratch=[pltpu.VMEM(sums.shape, f32)],
                scalars=0,
            )
        grads.append(grad)

    from_beside = shifted(to_beside, "sub", 1)
    from_cross = across(to_cross)
    to_west, to_east = call(
        late_kernel,
        (block, block),
        [low_rows, high_rows] + grads + [west, east],
        flops=2 * degree * nodes * len(LATE) * slot_rows * hid,
        scratch=[pltpu.VMEM((len(LATE) * slot_rows, hid), f32)],
        scalars=0,
    )
    to_west, to_east = call(
        add_kernel,
        (block, block),
        [to_west, from_beside, to_east, from_cross],
        flops=0,
        scalars=0,
    )
    from_upper = shifted(to_west, "lon", -1)
    from_lower = shifted(to_east, "lon", 1)

    own, grad_recv = call(
        own_kernel,
        (shape((nodes, hid), f32), shape((hid, nodes), bf16)),
        [low_rows, high_rows] + grads,
        flops=2 * degree * nodes * nodes * hid,
        scalars=0,
    )
    updated, direct = call(
        output_kernel,
        (shape((chans, nodes), bf16), shape((chans, nodes), f32)),
        [tile_count, features_held, cotangent, w_out_my, w_node_v_t] + hiddens + grad_pres,
        flops=4 * hidden_all * chans * nodes,
        scalars=1,
    )

    columns = chans_all // shard_count
    inv_root = 1.0 / math.sqrt(total_nodes)
    inputs = [tile_count, own, from_beside, feats, from_upper]
    weight_shape = shape((chans_all, hid), f32)
    grad_shape = shape((rows, hid), bf16)
    finals = [None] * halves
    for k in reversed(range(halves)):
        kernel = functools.partial(back_kernel, k * rows, inv_root)
        flops = 2 * hid * chans_all * rows
        if k:
            grad_send, weight = call(
                kernel,
                (grad_shape, weight_shape),
                inputs,
                flops=flops,
                scratch=[pltpu.VMEM((nodes, hid), f32)],
                scalars=1,
            )
        else:
            grad_send, w_mine, w_beside = call(
                kernel,
                (
                    grad_shape,
                    shape((lons, columns, hid), f32),
                    shape((lons, columns, hid), bf16),
                ),
                inputs + [from_lower, weight],
                flops=flops,
                scratch=[pltpu.VMEM(weight_shape.shape, f32), pltpu.VMEM((nodes, hid), f32)],
                scalars=1,
            )
            w_beside = shifted(w_beside, "sub", 1)
        kept, sent = call(
            functools.partial(terms_kernel, k * rows),
            (shape((chans, rows), f32), shape((count - 1, chans, rows), bf16)),
            [grad_send, grad_recv, direct, w_send_t, w_recv_t],
            flops=4 * hid * chans_all * rows,
            scratch=[pltpu.VMEM((chans_all, rows), f32)],
            scalars=0,
        )
        finals[k] = [kept] + [shifted(sent[i - 1], "ch", i) for i in range(1, count)]
    grad_features = call(
        finish_kernel, shape((chans, nodes), bf16), sum(finals, []), flops=0, scalars=0
    )

    near, w_sent = call(
        sum_kernel,
        (shape((columns, hid), f32), shape((lons - 1, columns, hid), bf16)),
        [w_mine, w_beside],
        flops=0,
        scalars=0,
    )
    w_terms = [shifted(w_sent[k - 1], "lon", k) for k in range(1, lons)]
    grad_w_send = call(
        weight_kernel, shape((columns, hid), f32), [near] + w_terms, flops=0, scalars=0
    )
    return (updated, grad_features, grad_w_send.T)


def solution(mesh):
    nodes_last = P("ch", ("parts", "lon", "sub"))
    spread = ("parts", "lon", "sub")
    placed = (nodes_last, nodes_last, P(None, spread), P(spread), P(spread), P(spread, None, None))
    return jax.shard_map(
        shards,
        mesh=mesh,
        in_specs=placed + (P(),) * 8,
        out_specs=(nodes_last, nodes_last, P(("parts", "ch"), ("lon", "sub"))),
        check_vma=False,
    )
```

```python
import functools
import math

import jax
import jax.numpy as jnp
from jax import lax
from jax.experimental import pallas as pl
from jax.experimental.pallas import tpu as pltpu
from jax.sharding import PartitionSpec as P

TILE = 128
CHUNK = 256
LANES = 128
PACK = 16
MIB = 1 << 20
WEIGHTS_LIMIT = 52
NO_CHUNK = 64
SLOT_OF = ((3, 0), (1, 1), (4, 4), (2, 5), (0, 2), (5, 3))
EARLY, LATE = (0, 3, 4, 5), (1, 2)
OFF = -1e4


def shifted(block, axis, distance):
    size = lax.axis_size(axis)
    route = [((i - distance) % size, i) for i in range(size)]
    return lax.ppermute(block, axis, route)


def gathered(block, axis):
    return [block] + [shifted(block, axis, k) for k in range(1, lax.axis_size(axis))]


def dot(left, right):
    return jnp.dot(left, right, preferred_element_type=jnp.float32)


def dot_nt(left, right):
    return lax.dot_general(
        left, right, (((1,), (1,)), ((), ())), preferred_element_type=jnp.float32
    )


def sigmoid(value):
    return 0.5 * jnp.tanh(0.5 * value) + 0.5


def call(kernel, out_shape, operands, flops, scratch=(), scalars=2, away=0, limit=24):
    vmem = pl.BlockSpec(memory_space=pltpu.VMEM)
    smem = pl.BlockSpec(memory_space=pltpu.SMEM)
    anywhere = pl.BlockSpec(memory_space=pltpu.HBM)
    moved = sum(math.prod(x.shape) * x.dtype.itemsize for x in operands)
    return pl.pallas_call(
        kernel,
        out_shape=out_shape,
        in_specs=[smem] * scalars
        + [anywhere] * away
        + [vmem] * (len(operands) - scalars - away),
        out_specs=jax.tree.map(lambda _: vmem, out_shape),
        scratch_shapes=scratch,
        compiler_params=pltpu.CompilerParams(vmem_limit_bytes=limit * MIB),
        cost_estimate=pl.CostEstimate(flops=flops, bytes_accessed=moved, transcendentals=0),
    )(*operands)


def assemble(whole_ref, blocks, first):
    count = len(blocks)
    rows = blocks[0].shape[0]
    for k, block in enumerate(blocks):
        place = lax.rem(first - k + count, count) * rows
        whole_ref[pl.ds(pl.multiple_of(place, rows), rows), :] = block[...]


def mine_of(ref, index, rows):
    return ref[pl.ds(pl.multiple_of(index * rows, rows), rows), :]


def weights_kernel(*refs):
    sources, refs = refs[:7], refs[7:]
    w_send, w_recv, w_out, feats, w_send_t, w_recv_t, w_msg_t, w_node_v_t, w_node_a_t, w_out_t = refs[:10]
    w_msg, w_node_v, w_node_a, w_out_all, turned, sems = refs[10:]
    mine = lax.axis_index("ch")
    hid = w_send.shape[0]
    targets = (feats, w_send, w_recv, w_msg, w_node_v, w_node_a, w_out_all)
    copies = []
    for k, (source, target) in enumerate(zip(sources, targets)):
        if k in (1, 2):
            source = source.at[pl.ds(pl.multiple_of(mine * hid, hid), hid), :]
        copies.append(pltpu.make_async_copy(source, target, sems.at[k]))
    for copy in copies:
        copy.start()
    for copy in copies:
        copy.wait()
    w_send_t[...] = w_send[...].T
    w_recv_t[...] = w_recv[...].T
    turned[...] = w_msg[...].T
    w_msg_t[...] = mine_of(turned, mine, hid)
    turned[...] = w_node_v[...].T
    w_node_v_t[...] = mine_of(turned, mine, w_node_v_t.shape[0])
    w_node_a_t[...] = w_node_a[...].T
    w_out_t[...] = w_out_all[...].T
    w_out[...] = mine_of(w_out_all, mine, w_out.shape[0])


def edges_kernel(tiles, senders, in_degree, low_cols, high_cols, low_rows, high_rows):
    degree, nodes = senders.shape
    lane = lax.broadcasted_iota(jnp.int32, (degree, nodes), 1)
    row = lax.broadcasted_iota(jnp.int32, (degree, nodes), 0)
    valid = (row < in_degree[...]) & (lane < tiles[0] * TILE)
    ids = senders[...]
    low = (ids & (CHUNK - 1)).astype(jnp.float32)
    high = jnp.where(valid, ids // CHUNK, NO_CHUNK).astype(jnp.float32)
    for m in range(degree):
        shape = (PACK, nodes)
        low_rows[m] = jnp.broadcast_to(low[m : m + 1], shape).astype(jnp.bfloat16)
        high_rows[m] = jnp.broadcast_to(high[m : m + 1], shape).astype(jnp.bfloat16)
    fill = jnp.zeros((PACK - degree, nodes), jnp.float32)
    depth = 2 * PACK
    both = jnp.concatenate([low, fill, high, fill], axis=0).T.astype(jnp.bfloat16)
    width = degree * LANES
    spot = lax.broadcasted_iota(jnp.int32, (depth, width), 0)
    group = lax.broadcasted_iota(jnp.int32, (depth, width), 1) // LANES
    for first, out in ((0, low_cols), (PACK, high_cols)):
        pick = (spot == group + first).astype(jnp.bfloat16)
        spread = dot(both, pick).astype(jnp.bfloat16)
        for m in range(degree):
            out[m] = spread[:, m * LANES : (m + 1) * LANES]


def project_kernel(count, tiles, picks, *refs):
    blocks = refs[:count]
    w_send, feats, proj, upper, lower, beside, cross = refs[count:]
    mine, sub = lax.axis_index("ch"), lax.axis_index("sub")
    first = tiles[0] // 2
    assemble(feats, blocks, mine)
    whole = feats[...]
    hid = proj.shape[1]
    proj[...] = (0.5 * dot(w_send[...], whole).T).astype(jnp.bfloat16)
    rows = upper.shape[0] - PACK
    upper[:rows, :] = proj[pl.ds(pl.multiple_of(first * TILE, TILE), rows), :]
    lower[:rows, :] = proj[:rows, :]
    spot = lax.broadcasted_iota(jnp.int32, (PACK, hid), 0)
    _, per_slot, slots = picks.shape
    half = slots // 2
    for start, out, lift in ((0, upper, first), (half, lower, 0)):
        marks = jnp.zeros((PACK, hid), jnp.float32)
        for k in range(half * per_slot):
            rel = picks[0, k % per_slot, start + k // per_slot] - lift
            marks = jnp.where(spot == k, rel.astype(jnp.float32), marks)
        out[rows:, :] = marks.astype(jnp.bfloat16)

    @pl.when(sub == 0)
    def _():
        beside[...] = upper[...]
        cross[...] = lower[...]

    @pl.when(sub != 0)
    def _():
        beside[...] = lower[...]
        cross[...] = upper[...]


def receive_kernel(bias, feats, w_recv, base):
    hid = base.shape[1]
    mine = lax.axis_index("ch")
    my_bias = jnp.zeros((1, hid), jnp.float32)
    for k in range(bias.shape[1] // hid):
        my_bias += jnp.where(mine == k, bias[:, k * hid : (k + 1) * hid], 0.0)
    recv = dot(w_recv[...], feats[...]).T
    base[...] = 0.5 * (recv.astype(jnp.bfloat16).astype(jnp.float32) + my_bias)


def prepare_kernel(count, tiles, *refs):
    blocks = refs[:count]
    feats, w_node_v, bias, w_out_t, cots, pre, grad_hidden = refs[count:]
    assemble(cots, blocks, lax.axis_index("ch"))
    column = jnp.broadcast_to(bias[...], (8, bias.shape[1])).T[:, :1]
    pre[...] = dot(w_node_v[...], feats[...]) + column
    lane = lax.broadcasted_iota(jnp.int32, (1, cots.shape[1]), 1)
    active = (lane < tiles[0] * TILE).astype(jnp.bfloat16)
    grad_hidden[...] = dot(w_out_t[...], cots[...] * active)


def chunk_of(place, first, shape):
    on_zero, on_one = (float(first + slot) for slot in SLOT_OF[place])
    chunk = jnp.where(lax.axis_index("sub") == 0, on_zero, on_one)
    return jnp.full(shape, chunk, jnp.float32).astype(jnp.bfloat16)


def picks_of(block, place):
    marks = block[CHUNK : CHUNK + PACK, :].astype(jnp.float32)
    per_slot = CHUNK // TILE
    half = len(SLOT_OF) // 2
    starts = [slot % half * per_slot for slot in SLOT_OF[place]]
    sub = lax.axis_index("sub")
    return [
        jnp.where(
            sub == 0,
            marks[starts[0] + t : starts[0] + t + 1],
            marks[starts[1] + t : starts[1] + t + 1],
        )
        for t in range(per_slot)
    ]


def fill(ext, start, block, place):
    for t, pick in enumerate(picks_of(block, place)):
        ext[start + t * TILE : start + (t + 1) * TILE, :] = jnp.where(
            pick > 0.5, block[TILE : 2 * TILE, :], block[:TILE, :]
        )


def pick_rows(low, high, chunks, ext):
    one = jnp.bfloat16(1.0)
    zero = jnp.bfloat16(0.0)
    lane = lax.broadcasted_iota(jnp.int32, low.shape, 1)
    marks = [
        jnp.where(low == (lane + half * LANES).astype(jnp.bfloat16), one, zero)
        for half in range(CHUNK // LANES)
    ]
    picker = jnp.concatenate(
        [jnp.where(high == chunk, mark, zero) for chunk in chunks for mark in marks], axis=1
    )
    return dot(picker, ext[...])


def near_kernel(low, high, proj, beside, part, ext):
    own = proj.shape[0]
    ext[:own, :] = proj[...]
    fill(ext, own, beside, 0)
    first = own // CHUNK
    chunks = [jnp.bfloat16(chunk) for chunk in range(first)]
    chunks.append(chunk_of(0, first, low.shape[1:]))

    def step(m, carry):
        part[m] = pick_rows(low[m], high[m], chunks, ext).astype(jnp.bfloat16)
        return carry

    lax.fori_loop(0, low.shape[0], step, 0, unroll=True)


def line_kernel(low, high, before, west, east, part, ext):
    first = low.shape[1] // CHUNK
    chunks = []
    for index, (place, block) in enumerate(((1, west), (2, east))):
        fill(ext, index * CHUNK, block, place)
        chunks.append(jnp.bfloat16(first + SLOT_OF[place][0]))

    def step(m, carry):
        more = pick_rows(low[m], high[m], chunks, ext)
        part[m] = (before[m].astype(jnp.float32) + more).astype(jnp.bfloat16)
        return carry

    lax.fori_loop(0, low.shape[0], step, 0, unroll=True)


def message_kernel(
    start, low, high, base, in_degree, part, cross, west, east, message, slope, ext, total
):
    nodes = low.shape[1]
    degree, rows, hid = slope.shape
    first = nodes // CHUNK
    together = nodes // rows
    span = slice(start, start + rows)
    chunks = []
    for index, (place, block) in enumerate(((3, cross), (4, west), (5, east))):
        fill(ext, index * CHUNK, block, place)
        chunks.append(chunk_of(place, first, (nodes, LANES)))
    total[...] = jnp.zeros_like(total)

    def rows_of(ref, k):
        return jnp.concatenate([ref[k * together + i, span, :] for i in range(together)], axis=0)

    def step(k, carry):
        low_k, high_k = rows_of(low, k), rows_of(high, k)
        half = pick_rows(low_k, high_k, chunks, ext) + rows_of(part, k).astype(jnp.float32)
        half += jnp.concatenate([base[span, :]] * together, axis=0)
        wide = jnp.concatenate([high_k] * pl.cdiv(hid, LANES), axis=1)[:, :hid]
        half = jnp.where(wide.astype(jnp.float32) < NO_CHUNK, half, OFF)
        twice = jnp.tanh(half) + 1.0
        act = half * twice
        grad = (twice + act * (2.0 - twice)).astype(jnp.bfloat16)
        terms = 0.0
        for i in range(together):
            terms += act[i * rows : (i + 1) * rows]
            slope[k * together + i] = grad[i * rows : (i + 1) * rows]
        total[...] += terms
        return carry

    lax.fori_loop(0, degree // together, step, 0, unroll=True)
    count = in_degree[:, span].astype(jnp.float32)
    message[...] = (total[...].T / count).astype(jnp.bfloat16)


def node_kernel(count, start, in_degree, *refs):
    blocks = refs[:count]
    w_msg, w_node_a, w_node_a_t, w_msg_t, pre, grad_hidden = refs[count : count + 6]
    hidden, grad_pre, scale, messages = refs[count + 6 :]
    assemble(messages, blocks, lax.axis_index("ch"))
    span = slice(start, start + hidden.shape[1])
    agg = dot(w_msg[...], messages[...])
    half = 0.5 * (pre[:, span] + dot(w_node_a[...], agg.astype(jnp.bfloat16)))
    twice = jnp.tanh(half) + 1.0
    act = half * twice
    hidden[...] = act.astype(jnp.bfloat16)
    slope = 0.5 * (twice + act * (2.0 - twice))
    low_grad = (grad_hidden[:, span] * slope).astype(jnp.bfloat16)
    grad_pre[...] = low_grad
    grad_agg = dot(w_node_a_t[...], low_grad).astype(jnp.bfloat16)
    grad_msg = dot(w_msg_t[...], grad_agg).astype(jnp.bfloat16).astype(jnp.float32)
    scale[...] = (grad_msg * (0.5 / in_degree[:, span].astype(jnp.float32))).T


def scatter(low, high, edges, chunks, total):
    one = jnp.bfloat16(1.0)
    zero = jnp.bfloat16(0.0)
    groups = CHUNK // PACK
    for step in edges:
        width = sum(rows for _, _, rows, _ in step)
        place = lax.broadcasted_iota(jnp.int32, (groups, PACK, width), 0) * PACK
        place = place + lax.broadcasted_iota(jnp.int32, (groups, PACK, width), 1)
        low_k = jnp.concatenate([low[m, :, s : s + r] for m, s, r, _ in step], axis=1)
        high_k = jnp.concatenate([high[m, :, s : s + r] for m, s, r, _ in step], axis=1)
        grads = jnp.concatenate([grad() for _, _, _, grad in step], axis=0)
        mark = jnp.where(low_k[None] == place.astype(jnp.bfloat16), one, zero)
        picker = jnp.concatenate(
            [jnp.where(high_k[None] == chunk, mark, zero) for chunk in chunks], axis=0
        ).reshape(len(chunks) * CHUNK, width)
        total[...] += dot(picker, grads)


def pairs(start, ref, nodes, grad_of):
    degree, rows, _ = ref.shape
    together = nodes // rows
    return [
        [
            (m, start, rows, functools.partial(grad_of, ref, m))
            for m in range(k * together, (k + 1) * together)
        ]
        for k in range(degree // together)
    ]


def fold(block, place, index, total):
    picks = picks_of(block, place)
    halves = []
    for half in range(len(picks)):
        terms = 0.0
        for t, pick in enumerate(picks):
            start = index * CHUNK + t * TILE
            hit = jnp.abs(pick - half) < 0.5
            terms += jnp.where(hit, total[start : start + TILE, :], 0.0)
        halves.append(terms)
    return jnp.concatenate(halves, axis=0).astype(jnp.bfloat16)


def early_kernel(start, low, high, slope, scale, *refs):
    if start:
        before, beside, cross, west, east, to_cross, to_beside, grads, total = refs
        total[...] = before[...]
    else:
        grads, total = refs
        total[...] = jnp.zeros_like(total)
    nodes = low.shape[2]
    first = nodes // CHUNK

    def grad_of(ref, m):
        grads[m] = (ref[m].astype(jnp.float32) * scale[...]).astype(jnp.bfloat16)
        return grads[m]

    chunks = [chunk_of(place, first, (1, PACK, nodes)) for place in EARLY]
    scatter(low, high, pairs(start, slope, nodes, grad_of), chunks, total)
    if start:
        to_beside[0] = fold(beside, 0, 0, total)
        to_cross[...] = fold(cross, 3, 1, total)
        to_beside[1] = fold(west, 4, 2, total)
        to_beside[2] = fold(east, 5, 3, total)


def all_pairs(parts, nodes):
    start, steps = 0, []
    for part in parts:
        steps += pairs(start, part, nodes, lambda ref, m: ref[m])
        start += part.shape[1]
    return steps


def late_kernel(low, high, *refs):
    *parts, west, east, to_west, to_east, total = refs
    nodes = low.shape[2]
    first = nodes // CHUNK
    chunks = [jnp.bfloat16(first + SLOT_OF[place][0]) for place in LATE]
    total[...] = jnp.zeros_like(total)
    scatter(low, high, all_pairs(parts, nodes), chunks, total)
    to_west[...] = fold(west, 1, 0, total)
    to_east[...] = fold(east, 2, 1, total)


def own_kernel(low, high, *refs):
    *parts, total, recv = refs
    nodes = low.shape[2]
    chunks = [jnp.bfloat16(chunk) for chunk in range(nodes // CHUNK)]
    total[...] = jnp.zeros_like(total)
    scatter(low, high, all_pairs(parts, nodes), chunks, total)
    start = 0
    for part in parts:
        degree, rows, _ = part.shape
        terms = 0.0
        for m in range(degree):
            terms += part[m].astype(jnp.float32)
        recv[:, start : start + rows] = terms.T.astype(jnp.bfloat16)
        start += rows


def output_kernel(tiles, feats, cots, w_out, w_node_v_t, *refs):
    *parts, updated, direct = refs
    count = len(parts) // 2
    rows = parts[0].shape[1]
    for k in range(count):
        hidden, grad_pre = parts[k], parts[count + k]
        span = slice(k * rows, (k + 1) * rows)
        lane = lax.broadcasted_iota(jnp.int32, (1, rows), 1) + k * rows
        active = (lane < tiles[0] * TILE).astype(jnp.float32)
        node_out = dot(w_out[...], hidden[...])
        new = feats[:, span].astype(jnp.float32) + active * node_out
        updated[:, span] = new.astype(jnp.bfloat16)
        direct[:, span] = cots[:, span].astype(jnp.float32) + dot(w_node_v_t[...], grad_pre[...])


def add_kernel(left, more, right, across, west, east):
    sub = lax.axis_index("sub")
    other = across[...].astype(jnp.float32)
    to_west = left[...].astype(jnp.float32) + more[1].astype(jnp.float32)
    to_east = right[...].astype(jnp.float32) + more[2].astype(jnp.float32)
    west[...] = (to_west + jnp.where(sub == 0, 0.0, other)).astype(jnp.bfloat16)
    east[...] = (to_east + jnp.where(sub == 0, other, 0.0)).astype(jnp.bfloat16)


def back_kernel(start, inv_root, tiles, own, beside, feats, upper, *refs):
    *refs, total = refs
    sub = lax.axis_index("sub")
    offset = pl.multiple_of(tiles[0] // 2 * TILE, TILE)
    total[...] = own[...]
    near = beside[0].astype(jnp.float32)
    block = upper[...].astype(jnp.float32) + jnp.where(sub == 0, near, 0.0)
    total[pl.ds(offset, block.shape[0]), :] += block
    if start:
        grad_send, weight = refs
    else:
        lower, before, grad_send, w_mine, w_beside, weight = refs
        block = lower[...].astype(jnp.float32) + jnp.where(sub == 0, 0.0, near)
        total[: block.shape[0], :] += block
    rows = grad_send.shape[0]
    grad_send[...] = total[start : start + rows, :].astype(jnp.bfloat16)
    terms = dot(feats[:, start : start + rows], grad_send[...])
    if start:
        weight[...] = terms
        return
    weight[...] = (before[...] + terms) * inv_root
    lon = lax.axis_index("lon")
    lons, columns, _ = w_mine.shape
    for k in range(lons):
        band = lax.rem(lon + k, lons) * 2
        for out, core in ((w_mine, sub), (w_beside, 1 - sub)):
            spot = pl.multiple_of((band + core) * columns, columns)
            out[k] = weight[pl.ds(spot, columns), :].astype(out.dtype)


def terms_kernel(start, grad_send, recv, direct, w_send_t, w_recv_t, kept, sent, terms):
    span = slice(start, start + grad_send.shape[0])
    mine = lax.axis_index("ch")
    chans = kept.shape[0]
    grad_send_t = grad_send[...].astype(jnp.float32).T.astype(jnp.bfloat16)
    terms[...] = dot(w_send_t[...], grad_send_t) + dot(w_recv_t[...], recv[:, span])
    kept[...] = direct[:, span] + mine_of(terms, mine, chans)
    count = sent.shape[0] + 1
    for k in range(1, count):
        sent[k - 1] = mine_of(terms, lax.rem(mine + k, count), chans).astype(jnp.bfloat16)


def finish_kernel(*refs):
    *parts, out = refs
    rows = out.shape[1] // 2
    count = len(parts) // 2
    for k in range(2):
        kept, *others = parts[k * count : (k + 1) * count]
        total = kept[...]
        for other in others:
            total += other[...].astype(jnp.float32)
        out[:, k * rows : (k + 1) * rows] = total.astype(jnp.bfloat16)


def sum_kernel(w_mine, w_beside, near, sent):
    near[...] = w_mine[0] + w_beside[0].astype(jnp.float32)
    for k in range(sent.shape[0]):
        sent[k] = (w_mine[k + 1] + w_beside[k + 1].astype(jnp.float32)).astype(jnp.bfloat16)


def weight_kernel(near, *refs):
    out = refs[-1]
    total = near[...]
    for ref in refs[:-1]:
        total += ref[...].astype(jnp.float32)
    out[...] = total


def shards(
    features,
    cotangent,
    senders,
    in_degree,
    tile_count,
    send_tiles,
    w_send,
    w_recv,
    bias_edge,
    w_msg,
    w_node_v,
    w_node_a,
    bias_node,
    w_out,
):
    chans, nodes = features.shape
    count = lax.axis_size("ch")
    lons = lax.axis_size("lon")
    hidden_all, chans_all = w_send.shape
    hid = hidden_all // count
    cycle = ("lon", "sub")
    shard_count = lax.axis_size(cycle)
    total_nodes = nodes * shard_count
    degree = senders.shape[0]
    slots = send_tiles.shape[1]
    slot_rows = send_tiles.shape[2] * TILE
    ext_len = nodes + slots * slot_rows
    bf16, f32 = jnp.bfloat16, jnp.float32
    shape = jax.ShapeDtypeStruct

    far_route = [(i, (i + (3 if i % 2 else -3)) % shard_count) for i in range(shard_count)]
    across_route = [(i, (i + (1 if i % 2 else -1)) % shard_count) for i in range(shard_count)]
    across = lambda block: lax.ppermute(block, cycle, across_route)
    degrees = in_degree[None, :]
    picks = jnp.transpose(send_tiles, (0, 2, 1))
    sub = lax.axis_index("sub")

    feat_blocks = gathered(features, "ch")
    cot_later, feat_blocks[-1] = lax.optimization_barrier((cotangent, feat_blocks[-1]))
    cot_blocks = gathered(cot_later, "ch")

    whole_w = pltpu.VMEM((chans_all, hidden_all), bf16)
    (
        w_send_my,
        w_recv_my,
        w_out_my,
        features_held,
        w_send_t,
        w_recv_t,
        w_msg_t,
        w_node_v_t,
        w_node_a_t,
        w_out_t,
    ) = call(
        weights_kernel,
        (
            shape((hid, chans_all), bf16),
            shape((hid, chans_all), bf16),
            shape((chans, hidden_all), bf16),
            shape((chans, nodes), bf16),
            shape((chans_all, hid), bf16),
            shape((chans_all, hid), bf16),
            shape((hid, chans_all), bf16),
            shape((chans, hidden_all), bf16),
            shape((chans_all, hidden_all), bf16),
            shape((hidden_all, chans_all), bf16),
        ),
        [features, w_send, w_recv, w_msg, w_node_v, w_node_a, w_out],
        flops=4 * hidden_all * chans_all * nodes,
        away=7,
        scalars=0,
        scratch=[whole_w] * 5 + [pltpu.SemaphoreType.DMA((7,))],
        limit=WEIGHTS_LIMIT,
    )
    low_cols, high_cols, low_rows, high_rows = call(
        edges_kernel,
        (
            shape((degree, nodes, LANES), bf16),
            shape((degree, nodes, LANES), bf16),
            shape((degree, PACK, nodes), bf16),
            shape((degree, PACK, nodes), bf16),
        ),
        [tile_count, senders, degrees],
        flops=2 * hidden_all * chans_all * nodes,
        scalars=1,
    )
    feat_blocks[0], low_cols, high_cols, low_rows, high_rows = lax.optimization_barrier(
        (features_held, low_cols, high_cols, low_rows, high_rows)
    )

    block = shape((slot_rows + PACK, hid), bf16)
    feats, proj, upper, lower, beside, cross = call(
        functools.partial(project_kernel, count),
        (
            shape((chans_all, nodes), bf16),
            shape((nodes, hid), bf16),
            block,
            block,
            block,
            block,
        ),
        [tile_count, picks] + feat_blocks + [w_send_my],
        flops=2 * hid * chans_all * nodes,
    )
    base = call(
        receive_kernel,
        shape((nodes, hid), f32),
        [bias_edge[None, :], feats, w_recv_my],
        flops=2 * hid * chans_all * nodes,
        scalars=0,
    )
    west = shifted(upper, "lon", 1)
    east = shifted(lower, "lon", -1)
    beside = shifted(beside, "sub", 1)
    cross = lax.ppermute(cross, cycle, far_route)
    cots, pre, grad_hidden = call(
        functools.partial(prepare_kernel, count),
        (
            shape((chans_all, nodes), bf16),
            shape((hidden_all, nodes), f32),
            shape((hidden_all, nodes), f32),
        ),
        [tile_count] + cot_blocks + [feats, w_node_v, bias_node[None, :], w_out_t],
        flops=4 * hidden_all * chans_all * nodes,
        scalars=1,
    )

    part_shape = shape((degree, nodes, hid), bf16)
    part = call(
        near_kernel,
        part_shape,
        [low_cols, high_cols, proj, beside],
        flops=2 * degree * nodes * (nodes + slot_rows) * hid,
        scratch=[pltpu.VMEM((nodes + slot_rows, hid), bf16)],
        scalars=0,
    )
    west, east, part = lax.optimization_barrier((west, east, part))
    west_too = shifted(west, "sub", 1)
    east_too = shifted(east, "sub", 1)
    part, pre = lax.optimization_barrier((part, pre))
    part = call(
        line_kernel,
        part_shape,
        [low_cols, high_cols, part, west, east],
        flops=2 * degree * nodes * 2 * slot_rows * hid,
        scratch=[pltpu.VMEM((2 * slot_rows, hid), bf16)],
        scalars=0,
    )
    halves = 2
    rows = nodes // halves
    slopes, messages, hiddens, grad_pres, grads = [], [], [], [], []
    for k in range(halves):
        message, slope = call(
            functools.partial(message_kernel, k * rows),
            (shape((hid, rows), bf16), shape((degree, rows, hid), bf16)),
            [low_cols, high_cols, base, degrees, part, cross, west_too, east_too],
            flops=2 * degree * rows * 3 * slot_rows * hid,
            scratch=[pltpu.VMEM((3 * slot_rows, hid), bf16), pltpu.VMEM((rows, hid), f32)],
            scalars=0,
        )
        slopes.append(slope)
        messages.append(gathered(message, "ch"))

    block = shape((slot_rows, hid), bf16)
    sums = shape((len(EARLY) * slot_rows, hid), f32)
    grad_shape = shape((degree, rows, hid), bf16)
    for k in range(halves):
        hidden, grad_pre, scale = call(
            functools.partial(node_kernel, count, k * rows),
            (
                shape((hidden_all, rows), bf16),
                shape((hidden_all, rows), bf16),
                shape((rows, hid), f32),
            ),
            [degrees] + messages[k] + [w_msg, w_node_a, w_node_a_t, w_msg_t, pre, grad_hidden],
            flops=6 * hidden_all * chans_all * rows,
            scratch=[pltpu.VMEM((hidden_all, rows), bf16)],
            scalars=0,
        )
        hiddens.append(hidden)
        grad_pres.append(grad_pre)
        operands = [low_rows, high_rows, slopes[k], scale]
        flops = 2 * degree * rows * len(EARLY) * slot_rows * hid
        kernel = functools.partial(early_kernel, k * rows)
        if k == 0:
            grad, before = call(kernel, (grad_shape, sums), operands, flops=flops, scalars=0)
        else:
            to_cross, to_beside, grad = call(
                kernel,
                (block, shape((3, slot_rows, hid), bf16), grad_shape),
                operands + [before, beside, cross, west_too, east_too],
                flops=flops,
                scratch=[pltpu.VMEM(sums.shape, f32)],
                scalars=0,
            )
        grads.append(grad)

    from_beside = shifted(to_beside, "sub", 1)
    from_cross = across(to_cross)
    to_west, to_east = call(
        late_kernel,
        (block, block),
        [low_rows, high_rows] + grads + [west, east],
        flops=2 * degree * nodes * len(LATE) * slot_rows * hid,
        scratch=[pltpu.VMEM((len(LATE) * slot_rows, hid), f32)],
        scalars=0,
    )
    updated, direct = call(
        output_kernel,
        (shape((chans, nodes), bf16), shape((chans, nodes), f32)),
        [tile_count, features_held, cotangent, w_out_my, w_node_v_t] + hiddens + grad_pres,
        flops=4 * hidden_all * chans * nodes,
        scalars=1,
    )
    to_west, direct = lax.optimization_barrier((to_west, direct))
    to_west, to_east = call(
        add_kernel,
        (block, block),
        [to_west, from_beside, to_east, from_cross],
        flops=0,
        scalars=0,
    )
    from_upper = shifted(to_west, "lon", -1)
    from_lower = shifted(to_east, "lon", 1)

    own, grad_recv = call(
        own_kernel,
        (shape((nodes, hid), f32), shape((hid, nodes), bf16)),
        [low_rows, high_rows] + grads,
        flops=2 * degree * nodes * nodes * hid,
        scalars=0,
    )
    columns = chans_all // shard_count
    inv_root = 1.0 / math.sqrt(total_nodes)
    inputs = [tile_count, own, from_beside, feats, from_upper]
    weight_shape = shape((chans_all, hid), f32)
    grad_shape = shape((rows, hid), bf16)
    finals = [None] * halves
    for k in reversed(range(halves)):
        kernel = functools.partial(back_kernel, k * rows, inv_root)
        flops = 2 * hid * chans_all * rows
        if k:
            grad_send, weight = call(
                kernel,
                (grad_shape, weight_shape),
                inputs,
                flops=flops,
                scratch=[pltpu.VMEM((nodes, hid), f32)],
                scalars=1,
            )
        else:
            grad_send, w_mine, w_beside = call(
                kernel,
                (
                    grad_shape,
                    shape((lons, columns, hid), f32),
                    shape((lons, columns, hid), bf16),
                ),
                inputs + [from_lower, weight],
                flops=flops,
                scratch=[pltpu.VMEM(weight_shape.shape, f32), pltpu.VMEM((nodes, hid), f32)],
                scalars=1,
            )
            w_beside = shifted(w_beside, "sub", 1)
        kept, sent = call(
            functools.partial(terms_kernel, k * rows),
            (shape((chans, rows), f32), shape((count - 1, chans, rows), bf16)),
            [grad_send, grad_recv, direct, w_send_t, w_recv_t],
            flops=4 * hid * chans_all * rows,
            scratch=[pltpu.VMEM((chans_all, rows), f32)],
            scalars=0,
        )
        finals[k] = [kept] + [shifted(sent[i - 1], "ch", i) for i in range(1, count)]
    grad_features = call(
        finish_kernel, shape((chans, nodes), bf16), sum(finals, []), flops=0, scalars=0
    )

    near, w_sent = call(
        sum_kernel,
        (shape((columns, hid), f32), shape((lons - 1, columns, hid), bf16)),
        [w_mine, w_beside],
        flops=0,
        scalars=0,
    )
    w_terms = [shifted(w_sent[k - 1], "lon", k) for k in range(1, lons)]
    grad_w_send = call(
        weight_kernel, shape((columns, hid), f32), [near] + w_terms, flops=0, scalars=0
    )
    return (updated, grad_features, grad_w_send.T)


def solution(mesh):
    nodes_last = P("ch", ("parts", "lon", "sub"))
    spread = ("parts", "lon", "sub")
    placed = (nodes_last, nodes_last, P(None, spread), P(spread), P(spread), P(spread, None, None))
    return jax.shard_map(
        shards,
        mesh=mesh,
        in_specs=placed + (P(),) * 8,
        out_specs=(nodes_last, nodes_last, P(("parts", "ch"), ("lon", "sub"))),
        check_vma=False,
    )
```

```python
import functools
import math

import jax
import jax.numpy as jnp
from jax import lax
from jax.experimental import pallas as pl
from jax.experimental.pallas import tpu as pltpu
from jax.sharding import PartitionSpec as P

TILE = 128
CHUNK = 256
LANES = 128
PACK = 16
MIB = 1 << 20
WEIGHTS_LIMIT = 52
NO_CHUNK = 64
SLOT_OF = ((3, 0), (1, 1), (4, 4), (2, 5), (0, 2), (5, 3))
EARLY, LATE = (3, 4, 5), (1, 2, 0)
OFF = -1e4


def shifted(block, axis, distance):
    size = lax.axis_size(axis)
    route = [((i - distance) % size, i) for i in range(size)]
    return lax.ppermute(block, axis, route)


def gathered(block, axis):
    return [block] + [shifted(block, axis, k) for k in range(1, lax.axis_size(axis))]


def dot(left, right):
    return jnp.dot(left, right, preferred_element_type=jnp.float32)


def dot_nt(left, right):
    return lax.dot_general(
        left, right, (((1,), (1,)), ((), ())), preferred_element_type=jnp.float32
    )


def sigmoid(value):
    return 0.5 * jnp.tanh(0.5 * value) + 0.5


def call(kernel, out_shape, operands, scratch=(), scalars=2, away=0, limit=24):
    vmem = pl.BlockSpec(memory_space=pltpu.VMEM)
    smem = pl.BlockSpec(memory_space=pltpu.SMEM)
    anywhere = pl.BlockSpec(memory_space=pltpu.HBM)
    return pl.pallas_call(
        kernel,
        out_shape=out_shape,
        in_specs=[smem] * scalars
        + [anywhere] * away
        + [vmem] * (len(operands) - scalars - away),
        out_specs=jax.tree.map(lambda _: vmem, out_shape),
        scratch_shapes=scratch,
        compiler_params=pltpu.CompilerParams(vmem_limit_bytes=limit * MIB),
        cost_estimate=pl.CostEstimate(flops=1024, bytes_accessed=1024, transcendentals=0),
    )(*operands)


def assemble(whole_ref, blocks, first):
    count = len(blocks)
    rows = blocks[0].shape[0]
    for k, block in enumerate(blocks):
        place = lax.rem(first - k + count, count) * rows
        whole_ref[pl.ds(pl.multiple_of(place, rows), rows), :] = block[...]


def mine_of(ref, index, rows):
    return ref[pl.ds(pl.multiple_of(index * rows, rows), rows), :]


def weights_kernel(*refs):
    sources, refs = refs[:7], refs[7:]
    w_send, w_recv, w_out, feats, w_send_t, w_recv_t, w_both_t, w_node_v_t, w_both, w_out_t = refs[:10]
    w_msg, w_node_v, w_node_a, w_out_all, turned, sems = refs[10:]
    mine = lax.axis_index("ch")
    hid = w_send.shape[0]
    targets = (w_msg, w_node_a, feats, w_send, w_recv, w_node_v, w_out_all)
    copies = []
    for k, (source, target) in enumerate(zip(sources, targets)):
        if k in (3, 4):
            source = source.at[pl.ds(pl.multiple_of(mine * hid, hid), hid), :]
        copies.append(pltpu.make_async_copy(source, target, sems.at[k]))
    for copy in copies:
        copy.start()
    for copy in copies[:2]:
        copy.wait()
    w_both[...] = dot(w_node_a[...], w_msg[...]).astype(jnp.bfloat16)
    turned[...] = w_both[...].T
    w_both_t[...] = mine_of(turned, mine, hid)
    for copy in copies[2:]:
        copy.wait()
    w_send_t[...] = w_send[...].T
    w_recv_t[...] = w_recv[...].T
    turned[...] = w_node_v[...].T
    w_node_v_t[...] = mine_of(turned, mine, w_node_v_t.shape[0])
    w_out_t[...] = w_out_all[...].T
    w_out[...] = mine_of(w_out_all, mine, w_out.shape[0])


def edges_kernel(tiles, senders, in_degree, low_cols, high_cols, low_rows, high_rows):
    degree, nodes = senders.shape
    lane = lax.broadcasted_iota(jnp.int32, (degree, nodes), 1)
    row = lax.broadcasted_iota(jnp.int32, (degree, nodes), 0)
    valid = (row < in_degree[...]) & (lane < tiles[0] * TILE)
    ids = senders[...]
    low = (ids & (CHUNK - 1)).astype(jnp.float32)
    high = jnp.where(valid, ids // CHUNK, NO_CHUNK).astype(jnp.float32)
    for m in range(degree):
        shape = (PACK, nodes)
        low_rows[m] = jnp.broadcast_to(low[m : m + 1], shape).astype(jnp.bfloat16)
        high_rows[m] = jnp.broadcast_to(high[m : m + 1], shape).astype(jnp.bfloat16)
    fill = jnp.zeros((PACK - degree, nodes), jnp.float32)
    depth = 2 * PACK
    both = jnp.concatenate([low, fill, high, fill], axis=0).T.astype(jnp.bfloat16)
    width = degree * LANES
    spot = lax.broadcasted_iota(jnp.int32, (depth, width), 0)
    group = lax.broadcasted_iota(jnp.int32, (depth, width), 1) // LANES
    for first, out in ((0, low_cols), (PACK, high_cols)):
        pick = (spot == group + first).astype(jnp.bfloat16)
        spread = dot(both, pick).astype(jnp.bfloat16)
        for m in range(degree):
            out[m] = spread[:, m * LANES : (m + 1) * LANES]


def project_kernel(count, tiles, picks, *refs):
    blocks = refs[:count]
    w_send, feats, proj, upper, lower, beside, cross = refs[count:]
    mine, sub = lax.axis_index("ch"), lax.axis_index("sub")
    first = tiles[0] // 2
    assemble(feats, blocks, mine)
    whole = feats[...]
    hid = proj.shape[1]
    proj[...] = (0.5 * dot(w_send[...], whole).T).astype(jnp.bfloat16)
    rows = upper.shape[0] - PACK
    upper[:rows, :] = proj[pl.ds(pl.multiple_of(first * TILE, TILE), rows), :]
    lower[:rows, :] = proj[:rows, :]
    spot = lax.broadcasted_iota(jnp.int32, (PACK, hid), 0)
    _, per_slot, slots = picks.shape
    half = slots // 2
    for start, out, lift in ((0, upper, first), (half, lower, 0)):
        marks = jnp.zeros((PACK, hid), jnp.float32)
        for k in range(half * per_slot):
            rel = picks[0, k % per_slot, start + k // per_slot] - lift
            marks = jnp.where(spot == k, rel.astype(jnp.float32), marks)
        out[rows:, :] = marks.astype(jnp.bfloat16)

    @pl.when(sub == 0)
    def _():
        beside[...] = upper[...]
        cross[...] = lower[...]

    @pl.when(sub != 0)
    def _():
        beside[...] = lower[...]
        cross[...] = upper[...]


def receive_kernel(bias, feats, w_recv, base):
    hid = base.shape[1]
    mine = lax.axis_index("ch")
    my_bias = jnp.zeros((1, hid), jnp.float32)
    for k in range(bias.shape[1] // hid):
        my_bias += jnp.where(mine == k, bias[:, k * hid : (k + 1) * hid], 0.0)
    recv = dot(w_recv[...], feats[...]).T
    base[...] = 0.5 * (recv.astype(jnp.bfloat16).astype(jnp.float32) + my_bias)


def prepare_kernel(count, tiles, *refs):
    blocks = refs[:count]
    feats, w_node_v, bias, w_out_t, cots, pre, grad_hidden = refs[count:]
    assemble(cots, blocks, lax.axis_index("ch"))
    column = jnp.broadcast_to(bias[...], (8, bias.shape[1])).T[:, :1]
    pre[...] = dot(w_node_v[...], feats[...]) + column
    lane = lax.broadcasted_iota(jnp.int32, (1, cots.shape[1]), 1)
    active = (lane < tiles[0] * TILE).astype(jnp.bfloat16)
    grad_hidden[...] = dot(w_out_t[...], cots[...] * active)


def chunk_of(place, first, shape):
    on_zero, on_one = (float(first + slot) for slot in SLOT_OF[place])
    chunk = jnp.where(lax.axis_index("sub") == 0, on_zero, on_one)
    return jnp.full(shape, chunk, jnp.float32).astype(jnp.bfloat16)


def picks_of(block, place):
    marks = block[CHUNK : CHUNK + PACK, :].astype(jnp.float32)
    per_slot = CHUNK // TILE
    half = len(SLOT_OF) // 2
    starts = [slot % half * per_slot for slot in SLOT_OF[place]]
    sub = lax.axis_index("sub")
    return [
        jnp.where(
            sub == 0,
            marks[starts[0] + t : starts[0] + t + 1],
            marks[starts[1] + t : starts[1] + t + 1],
        )
        for t in range(per_slot)
    ]


def fill(ext, start, block, place):
    for t, pick in enumerate(picks_of(block, place)):
        ext[start + t * TILE : start + (t + 1) * TILE, :] = jnp.where(
            pick > 0.5, block[TILE : 2 * TILE, :], block[:TILE, :]
        )


def pick_rows(low, high, chunks, ext):
    one = jnp.bfloat16(1.0)
    zero = jnp.bfloat16(0.0)
    lane = lax.broadcasted_iota(jnp.int32, low.shape, 1)
    marks = [
        jnp.where(low == (lane + half * LANES).astype(jnp.bfloat16), one, zero)
        for half in range(CHUNK // LANES)
    ]
    picker = jnp.concatenate(
        [jnp.where(high == chunk, mark, zero) for chunk in chunks for mark in marks], axis=1
    )
    return dot(picker, ext[...])


def near_kernel(low, high, proj, beside, part, ext):
    own = proj.shape[0]
    ext[:own, :] = proj[...]
    fill(ext, own, beside, 0)
    first = own // CHUNK
    chunks = [jnp.bfloat16(chunk) for chunk in range(first)]
    chunks.append(chunk_of(0, first, low.shape[1:]))

    def step(m, carry):
        part[m] = pick_rows(low[m], high[m], chunks, ext).astype(jnp.bfloat16)
        return carry

    lax.fori_loop(0, low.shape[0], step, 0, unroll=True)


def line_kernel(low, high, before, west, east, part, ext):
    first = low.shape[1] // CHUNK
    chunks = []
    for index, (place, block) in enumerate(((1, west), (2, east))):
        fill(ext, index * CHUNK, block, place)
        chunks.append(jnp.bfloat16(first + SLOT_OF[place][0]))

    def step(m, carry):
        more = pick_rows(low[m], high[m], chunks, ext)
        part[m] = (before[m].astype(jnp.float32) + more).astype(jnp.bfloat16)
        return carry

    lax.fori_loop(0, low.shape[0], step, 0, unroll=True)


def message_kernel(
    start, low, high, base, in_degree, part, cross, west, east, message, slope, ext, total
):
    nodes = low.shape[1]
    degree, rows, hid = slope.shape
    first = nodes // CHUNK
    together = nodes // rows
    span = slice(start, start + rows)
    chunks = []
    for index, (place, block) in enumerate(((3, cross), (4, west), (5, east))):
        fill(ext, index * CHUNK, block, place)
        chunks.append(chunk_of(place, first, (nodes, LANES)))
    total[...] = jnp.zeros_like(total)

    def rows_of(ref, k):
        return jnp.concatenate([ref[k * together + i, span, :] for i in range(together)], axis=0)

    def step(k, carry):
        low_k, high_k = rows_of(low, k), rows_of(high, k)
        half = pick_rows(low_k, high_k, chunks, ext) + rows_of(part, k).astype(jnp.float32)
        half += jnp.concatenate([base[span, :]] * together, axis=0)
        wide = jnp.concatenate([high_k] * pl.cdiv(hid, LANES), axis=1)[:, :hid]
        half = jnp.where(wide.astype(jnp.float32) < NO_CHUNK, half, OFF)
        twice = jnp.tanh(half) + 1.0
        act = half * twice
        grad = (twice + act * (2.0 - twice)).astype(jnp.bfloat16)
        terms = 0.0
        for i in range(together):
            terms += act[i * rows : (i + 1) * rows]
            slope[k * together + i] = grad[i * rows : (i + 1) * rows]
        total[...] += terms
        return carry

    lax.fori_loop(0, degree // together, step, 0, unroll=True)
    count = in_degree[:, span].astype(jnp.float32)
    message[...] = (total[...].T / count).astype(jnp.bfloat16)


def node_kernel(count, start, in_degree, *refs):
    blocks = refs[:count]
    w_both, w_both_t, pre, grad_hidden = refs[count : count + 4]
    hidden, grad_pre, scale, messages = refs[count + 4 :]
    assemble(messages, blocks, lax.axis_index("ch"))
    span = slice(start, start + hidden.shape[1])
    half = 0.5 * (pre[:, span] + dot(w_both[...], messages[...]))
    twice = jnp.tanh(half) + 1.0
    act = half * twice
    hidden[...] = act.astype(jnp.bfloat16)
    slope = 0.5 * (twice + act * (2.0 - twice))
    low_grad = (grad_hidden[:, span] * slope).astype(jnp.bfloat16)
    grad_pre[...] = low_grad
    grad_msg = dot(w_both_t[...], low_grad).astype(jnp.bfloat16).astype(jnp.float32)
    scale[...] = (grad_msg * (0.5 / in_degree[:, span].astype(jnp.float32))).T


def scatter(low, high, edges, chunks, total):
    one = jnp.bfloat16(1.0)
    zero = jnp.bfloat16(0.0)
    groups = CHUNK // PACK
    for step in edges:
        width = sum(rows for _, _, rows, _ in step)
        place = lax.broadcasted_iota(jnp.int32, (groups, PACK, width), 0) * PACK
        place = place + lax.broadcasted_iota(jnp.int32, (groups, PACK, width), 1)
        low_k = jnp.concatenate([low[m, :, s : s + r] for m, s, r, _ in step], axis=1)
        high_k = jnp.concatenate([high[m, :, s : s + r] for m, s, r, _ in step], axis=1)
        grads = jnp.concatenate([grad() for _, _, _, grad in step], axis=0)
        mark = jnp.where(low_k[None] == place.astype(jnp.bfloat16), one, zero)
        picker = jnp.concatenate(
            [jnp.where(high_k[None] == chunk, mark, zero) for chunk in chunks], axis=0
        ).reshape(len(chunks) * CHUNK, width)
        total[...] += dot(picker, grads)


def pairs(start, ref, nodes, grad_of):
    degree, rows, _ = ref.shape
    together = nodes // rows
    return [
        [
            (m, start, rows, functools.partial(grad_of, ref, m))
            for m in range(k * together, (k + 1) * together)
        ]
        for k in range(degree // together)
    ]


def fold(block, place, index, total):
    picks = picks_of(block, place)
    halves = []
    for half in range(len(picks)):
        terms = 0.0
        for t, pick in enumerate(picks):
            start = index * CHUNK + t * TILE
            hit = jnp.abs(pick - half) < 0.5
            terms += jnp.where(hit, total[start : start + TILE, :], 0.0)
        halves.append(terms)
    return jnp.concatenate(halves, axis=0).astype(jnp.bfloat16)


def early_kernel(start, low, high, slope, scale, *refs):
    if start:
        before, cross, west, east, to_cross, to_other, grads, total = refs
        total[...] = before[...]
    else:
        grads, total = refs
        total[...] = jnp.zeros_like(total)
    nodes = low.shape[2]
    first = nodes // CHUNK

    def grad_of(ref, m):
        grads[m] = (ref[m].astype(jnp.float32) * scale[...]).astype(jnp.bfloat16)
        return grads[m]

    chunks = [chunk_of(place, first, (1, PACK, nodes)) for place in EARLY]
    scatter(low, high, pairs(start, slope, nodes, grad_of), chunks, total)
    if start:
        to_cross[...] = fold(cross, 3, 0, total)
        to_other[0] = fold(west, 4, 1, total)
        to_other[1] = fold(east, 5, 2, total)


def all_pairs(parts, nodes):
    start, steps = 0, []
    for part in parts:
        steps += pairs(start, part, nodes, lambda ref, m: ref[m])
        start += part.shape[1]
    return steps


def late_kernel(low, high, *refs):
    *parts, west, east, beside, to_west, to_east, to_beside, total = refs
    nodes = low.shape[2]
    first = nodes // CHUNK
    chunks = [chunk_of(place, first, (1, PACK, nodes)) for place in LATE]
    total[...] = jnp.zeros_like(total)
    scatter(low, high, all_pairs(parts, nodes), chunks, total)
    to_west[...] = fold(west, 1, 0, total)
    to_east[...] = fold(east, 2, 1, total)
    to_beside[...] = fold(beside, 0, 2, total)


def own_kernel(low, high, *refs):
    *parts, total, recv = refs
    nodes = low.shape[2]
    chunks = [jnp.bfloat16(chunk) for chunk in range(nodes // CHUNK)]
    total[...] = jnp.zeros_like(total)
    scatter(low, high, all_pairs(parts, nodes), chunks, total)
    start = 0
    for part in parts:
        degree, rows, _ = part.shape
        terms = 0.0
        for m in range(degree):
            terms += part[m].astype(jnp.float32)
        recv[:, start : start + rows] = terms.T.astype(jnp.bfloat16)
        start += rows


def output_kernel(tiles, feats, cots, w_out, w_node_v_t, *refs):
    *parts, updated, direct = refs
    count = len(parts) // 2
    rows = parts[0].shape[1]
    for k in range(count):
        hidden, grad_pre = parts[k], parts[count + k]
        span = slice(k * rows, (k + 1) * rows)
        lane = lax.broadcasted_iota(jnp.int32, (1, rows), 1) + k * rows
        active = (lane < tiles[0] * TILE).astype(jnp.float32)
        node_out = dot(w_out[...], hidden[...])
        new = feats[:, span].astype(jnp.float32) + active * node_out
        updated[:, span] = new.astype(jnp.bfloat16)
        direct[:, span] = cots[:, span].astype(jnp.float32) + dot(w_node_v_t[...], grad_pre[...])


def add_kernel(left, more, right, across, west, east):
    sub = lax.axis_index("sub")
    other = across[...].astype(jnp.float32)
    to_west = left[...].astype(jnp.float32) + more[0].astype(jnp.float32)
    to_east = right[...].astype(jnp.float32) + more[1].astype(jnp.float32)
    west[...] = (to_west + jnp.where(sub == 0, 0.0, other)).astype(jnp.bfloat16)
    east[...] = (to_east + jnp.where(sub == 0, other, 0.0)).astype(jnp.bfloat16)


def back_kernel(start, inv_root, tiles, own, beside, feats, upper, *refs):
    *refs, total = refs
    sub = lax.axis_index("sub")
    offset = pl.multiple_of(tiles[0] // 2 * TILE, TILE)
    total[...] = own[...]
    near = beside[...].astype(jnp.float32)
    block = upper[...].astype(jnp.float32) + jnp.where(sub == 0, near, 0.0)
    total[pl.ds(offset, block.shape[0]), :] += block
    if start:
        grad_send, weight = refs
    else:
        lower, before, grad_send, w_mine, w_beside, weight = refs
        block = lower[...].astype(jnp.float32) + jnp.where(sub == 0, 0.0, near)
        total[: block.shape[0], :] += block
    rows = grad_send.shape[0]
    grad_send[...] = total[start : start + rows, :].astype(jnp.bfloat16)
    terms = dot(feats[:, start : start + rows], grad_send[...])
    if start:
        weight[...] = terms
        return
    weight[...] = (before[...] + terms) * inv_root
    lon = lax.axis_index("lon")
    lons, columns, _ = w_mine.shape
    for k in range(lons):
        band = lax.rem(lon + k, lons) * 2
        for out, core in ((w_mine, sub), (w_beside, 1 - sub)):
            spot = pl.multiple_of((band + core) * columns, columns)
            out[k] = weight[pl.ds(spot, columns), :].astype(out.dtype)


def terms_kernel(start, grad_send, recv, direct, w_send_t, w_recv_t, kept, sent, terms):
    span = slice(start, start + grad_send.shape[0])
    mine = lax.axis_index("ch")
    chans = kept.shape[0]
    grad_send_t = grad_send[...].astype(jnp.float32).T.astype(jnp.bfloat16)
    terms[...] = dot(w_send_t[...], grad_send_t) + dot(w_recv_t[...], recv[:, span])
    kept[...] = direct[:, span] + mine_of(terms, mine, chans)
    count = sent.shape[0] + 1
    for k in range(1, count):
        sent[k - 1] = mine_of(terms, lax.rem(mine + k, count), chans).astype(jnp.bfloat16)


def finish_kernel(count, *refs):
    kept, *others = refs[: count]
    *done, out = refs[count:]
    total = kept[...]
    for other in others:
        total += other[...].astype(jnp.float32)
    out[:, : kept.shape[1]] = total.astype(jnp.bfloat16)
    start = kept.shape[1]
    for part in done:
        out[:, start : start + part.shape[1]] = part[...]
        start += part.shape[1]


def sum_kernel(w_mine, w_beside, near, sent):
    near[...] = w_mine[0] + w_beside[0].astype(jnp.float32)
    for k in range(sent.shape[0]):
        sent[k] = (w_mine[k + 1] + w_beside[k + 1].astype(jnp.float32)).astype(jnp.bfloat16)


def weight_kernel(near, *refs):
    out = refs[-1]
    total = near[...]
    for ref in refs[:-1]:
        total += ref[...].astype(jnp.float32)
    out[...] = total


def shards(
    features,
    cotangent,
    senders,
    in_degree,
    tile_count,
    send_tiles,
    w_send,
    w_recv,
    bias_edge,
    w_msg,
    w_node_v,
    w_node_a,
    bias_node,
    w_out,
):
    chans, nodes = features.shape
    count = lax.axis_size("ch")
    lons = lax.axis_size("lon")
    hidden_all, chans_all = w_send.shape
    hid = hidden_all // count
    cycle = ("lon", "sub")
    shard_count = lax.axis_size(cycle)
    total_nodes = nodes * shard_count
    degree = senders.shape[0]
    slots = send_tiles.shape[1]
    slot_rows = send_tiles.shape[2] * TILE
    ext_len = nodes + slots * slot_rows
    bf16, f32 = jnp.bfloat16, jnp.float32
    shape = jax.ShapeDtypeStruct

    far_route = [(i, (i + (3 if i % 2 else -3)) % shard_count) for i in range(shard_count)]
    across_route = [(i, (i + (1 if i % 2 else -1)) % shard_count) for i in range(shard_count)]
    across = lambda block: lax.ppermute(block, cycle, across_route)
    degrees = in_degree[None, :]
    picks = jnp.transpose(send_tiles, (0, 2, 1))
    sub = lax.axis_index("sub")

    feat_blocks = gathered(features, "ch")

    whole_w = pltpu.VMEM((chans_all, hidden_all), bf16)
    (
        w_send_my,
        w_recv_my,
        w_out_my,
        features_held,
        w_send_t,
        w_recv_t,
        w_both_t,
        w_node_v_t,
        w_both,
        w_out_t,
    ) = call(
        weights_kernel,
        (
            shape((hid, chans_all), bf16),
            shape((hid, chans_all), bf16),
            shape((chans, hidden_all), bf16),
            shape((chans, nodes), bf16),
            shape((chans_all, hid), bf16),
            shape((chans_all, hid), bf16),
            shape((hid, hidden_all), bf16),
            shape((chans, hidden_all), bf16),
            shape((hidden_all, hidden_all), bf16),
            shape((hidden_all, chans_all), bf16),
        ),
        [w_msg, w_node_a, features, w_send, w_recv, w_node_v, w_out],
        away=7,
        scalars=0,
        scratch=[whole_w] * 5 + [pltpu.SemaphoreType.DMA((7,))],
        limit=WEIGHTS_LIMIT,
    )
    feat_blocks[0] = features_held

    block = shape((slot_rows + PACK, hid), bf16)
    feats, proj, upper, lower, beside, cross = call(
        functools.partial(project_kernel, count),
        (
            shape((chans_all, nodes), bf16),
            shape((nodes, hid), bf16),
            block,
            block,
            block,
            block,
        ),
        [tile_count, picks] + feat_blocks + [w_send_my],
    )
    west = shifted(upper, "lon", 1)
    east = shifted(lower, "lon", -1)
    cross = lax.ppermute(cross, cycle, far_route)
    base = call(
        receive_kernel,
        shape((nodes, hid), f32),
        [bias_edge[None, :], feats, w_recv_my],
        scalars=0,
    )
    base, senders, cotangent_late = lax.optimization_barrier((base, senders, cotangent))
    beside = shifted(beside, "sub", 1)
    cot_blocks = gathered(cotangent_late, "ch")
    low_cols, high_cols, low_rows, high_rows = call(
        edges_kernel,
        (
            shape((degree, nodes, LANES), bf16),
            shape((degree, nodes, LANES), bf16),
            shape((degree, PACK, nodes), bf16),
            shape((degree, PACK, nodes), bf16),
        ),
        [tile_count, senders, degrees],
        scalars=1,
    )
    cots, pre, grad_hidden = call(
        functools.partial(prepare_kernel, count),
        (
            shape((chans_all, nodes), bf16),
            shape((hidden_all, nodes), f32),
            shape((hidden_all, nodes), f32),
        ),
        [tile_count] + cot_blocks + [feats, w_node_v, bias_node[None, :], w_out_t],
        scalars=1,
    )

    part_shape = shape((degree, nodes, hid), bf16)
    part = call(
        near_kernel,
        part_shape,
        [low_cols, high_cols, proj, beside],
        scratch=[pltpu.VMEM((nodes + slot_rows, hid), bf16)],
        scalars=0,
    )
    west, east, part = lax.optimization_barrier((west, east, part))
    west_too = shifted(west, "sub", 1)
    east_too = shifted(east, "sub", 1)
    part, pre = lax.optimization_barrier((part, pre))
    part = call(
        line_kernel,
        part_shape,
        [low_cols, high_cols, part, west, east],
        scratch=[pltpu.VMEM((2 * slot_rows, hid), bf16)],
        scalars=0,
    )
    halves = 2
    rows = nodes // halves
    slopes, messages, hiddens, grad_pres, grads = [], [], [], [], []
    for k in range(halves):
        message, slope = call(
            functools.partial(message_kernel, k * rows),
            (shape((hid, rows), bf16), shape((degree, rows, hid), bf16)),
            [low_cols, high_cols, base, degrees, part, cross, west_too, east_too],
            scratch=[pltpu.VMEM((3 * slot_rows, hid), bf16), pltpu.VMEM((rows, hid), f32)],
            scalars=0,
        )
        slopes.append(slope)
        messages.append(gathered(message, "ch"))

    block = shape((slot_rows, hid), bf16)
    sums = shape((len(EARLY) * slot_rows, hid), f32)
    grad_shape = shape((degree, rows, hid), bf16)
    for k in range(halves):
        hidden, grad_pre, scale = call(
            functools.partial(node_kernel, count, k * rows),
            (
                shape((hidden_all, rows), bf16),
                shape((hidden_all, rows), bf16),
                shape((rows, hid), f32),
            ),
            [degrees] + messages[k] + [w_both, w_both_t, pre, grad_hidden],
            scratch=[pltpu.VMEM((hidden_all, rows), bf16)],
            scalars=0,
        )
        hiddens.append(hidden)
        grad_pres.append(grad_pre)
        operands = [low_rows, high_rows, slopes[k], scale]
        kernel = functools.partial(early_kernel, k * rows)
        if k == 0:
            grad, before = call(kernel, (grad_shape, sums), operands, scalars=0)
        else:
            to_cross, to_other, grad = call(
                kernel,
                (block, shape((2, slot_rows, hid), bf16), grad_shape),
                operands + [before, cross, west_too, east_too],
                scratch=[pltpu.VMEM(sums.shape, f32)],
                scalars=0,
            )
        grads.append(grad)

    from_other = shifted(to_other, "sub", 1)
    from_cross = across(to_cross)
    to_west, to_east, to_beside = call(
        late_kernel,
        (block, block, block),
        [low_rows, high_rows] + grads + [west, east, beside],
        scratch=[pltpu.VMEM((len(LATE) * slot_rows, hid), f32)],
        scalars=0,
    )
    updated, direct = call(
        output_kernel,
        (shape((chans, nodes), bf16), shape((chans, nodes), f32)),
        [tile_count, features_held, cotangent, w_out_my, w_node_v_t] + hiddens + grad_pres,
        scalars=1,
    )
    to_west, direct = lax.optimization_barrier((to_west, direct))
    to_west, to_east = call(
        add_kernel,
        (block, block),
        [to_west, from_other, to_east, from_cross],
        scalars=0,
    )
    from_upper = shifted(to_west, "lon", -1)
    from_lower = shifted(to_east, "lon", 1)
    from_beside = shifted(to_beside, "sub", 1)

    own, grad_recv = call(
        own_kernel,
        (shape((nodes, hid), f32), shape((hid, nodes), bf16)),
        [low_rows, high_rows] + grads,
        scalars=0,
    )
    columns = chans_all // shard_count
    inv_root = 1.0 / math.sqrt(total_nodes)
    inputs = [tile_count, own, from_beside, feats, from_upper]
    weight_shape = shape((chans_all, hid), f32)
    grad_shape = shape((rows, hid), bf16)
    finals = []
    for k in reversed(range(halves)):
        kernel = functools.partial(back_kernel, k * rows, inv_root)
        if k:
            grad_send, weight = call(
                kernel,
                (grad_shape, weight_shape),
                inputs,
                scratch=[pltpu.VMEM((nodes, hid), f32)],
                scalars=1,
            )
        else:
            grad_send, w_mine, w_beside = call(
                kernel,
                (
                    grad_shape,
                    shape((lons, columns, hid), f32),
                    shape((lons, columns, hid), bf16),
                ),
                inputs + [from_lower, weight],
                scratch=[pltpu.VMEM(weight_shape.shape, f32), pltpu.VMEM((nodes, hid), f32)],
                scalars=1,
            )
            w_beside = shifted(w_beside, "sub", 1)
            w_beside, *finals = lax.optimization_barrier((w_beside, *finals))
        kept, sent = call(
            functools.partial(terms_kernel, k * rows),
            (shape((chans, rows), f32), shape((count - 1, chans, rows), bf16)),
            [grad_send, grad_recv, direct, w_send_t, w_recv_t],
            scratch=[pltpu.VMEM((chans_all, rows), f32)],
            scalars=0,
        )
        if k:
            weight, kept = lax.optimization_barrier((weight, kept))
        parts = [kept] + [shifted(sent[i - 1], "ch", i) for i in range(1, count)]
        grad_features = call(
            functools.partial(finish_kernel, count),
            shape((chans, nodes - k * rows), bf16),
            parts + finals,
            scalars=0,
        )
        finals = [grad_features]

    near, w_sent = call(
        sum_kernel,
        (shape((columns, hid), f32), shape((lons - 1, columns, hid), bf16)),
        [w_mine, w_beside],
        scalars=0,
    )
    w_terms = [shifted(w_sent[k - 1], "lon", k) for k in range(1, lons)]
    grad_w_send = call(
        weight_kernel, shape((columns, hid), f32), [near] + w_terms, scalars=0
    )
    return (updated, grad_features, grad_w_send.T)


def solution(mesh):
    nodes_last = P("ch", ("parts", "lon", "sub"))
    spread = ("parts", "lon", "sub")
    placed = (nodes_last, nodes_last, P(None, spread), P(spread), P(spread), P(spread, None, None))
    return jax.shard_map(
        shards,
        mesh=mesh,
        in_specs=placed + (P(),) * 8,
        out_specs=(nodes_last, nodes_last, P(("parts", "ch"), ("lon", "sub"))),
        check_vma=False,
    )
```

```python
import functools
import math

import jax
import jax.numpy as jnp
from jax import lax
from jax.experimental import pallas as pl
from jax.experimental.pallas import tpu as pltpu
from jax.sharding import PartitionSpec as P

TILE = 128
CHUNK = 256
LANES = 128
PACK = 16
MIB = 1 << 20
WEIGHTS_LIMIT = 52
NO_CHUNK = 64
SLOT_OF = ((3, 0), (1, 1), (4, 4), (2, 5), (0, 2), (5, 3))
EARLY, LATE = (3, 4, 5), (1, 2, 0)
OFF = -1e4


def shifted(block, axis, distance):
    size = lax.axis_size(axis)
    route = [((i - distance) % size, i) for i in range(size)]
    return lax.ppermute(block, axis, route)


def gathered(block, axis):
    return [block] + [shifted(block, axis, k) for k in range(1, lax.axis_size(axis))]


def dot(left, right):
    return jnp.dot(left, right, preferred_element_type=jnp.float32)


def dot_nt(left, right):
    return lax.dot_general(
        left, right, (((1,), (1,)), ((), ())), preferred_element_type=jnp.float32
    )


def sigmoid(value):
    return 0.5 * jnp.tanh(0.5 * value) + 0.5


def call(kernel, out_shape, operands, scratch=(), scalars=2, away=0, limit=24, flops=1024):
    vmem = pl.BlockSpec(memory_space=pltpu.VMEM)
    smem = pl.BlockSpec(memory_space=pltpu.SMEM)
    anywhere = pl.BlockSpec(memory_space=pltpu.HBM)
    return pl.pallas_call(
        kernel,
        out_shape=out_shape,
        in_specs=[smem] * scalars
        + [anywhere] * away
        + [vmem] * (len(operands) - scalars - away),
        out_specs=jax.tree.map(lambda _: vmem, out_shape),
        scratch_shapes=scratch,
        compiler_params=pltpu.CompilerParams(vmem_limit_bytes=limit * MIB),
        cost_estimate=pl.CostEstimate(flops=flops, bytes_accessed=1024, transcendentals=0),
    )(*operands)


def assemble(whole_ref, blocks, first):
    count = len(blocks)
    rows = blocks[0].shape[0]
    for k, block in enumerate(blocks):
        place = lax.rem(first - k + count, count) * rows
        whole_ref[pl.ds(pl.multiple_of(place, rows), rows), :] = block[...]


def mine_of(ref, index, rows):
    return ref[pl.ds(pl.multiple_of(index * rows, rows), rows), :]


def weights_kernel(*refs):
    sources, refs = refs[:7], refs[7:]
    w_send, w_recv, w_out, feats, w_send_t, w_recv_t, w_both_t, w_node_v_t, w_both, w_out_t = refs[:10]
    w_msg, w_node_v, w_node_a, w_out_all, turned, sems = refs[10:]
    mine = lax.axis_index("ch")
    hid = w_send.shape[0]
    targets = (w_msg, w_node_a, feats, w_send, w_recv, w_node_v, w_out_all)
    copies = []
    for k, (source, target) in enumerate(zip(sources, targets)):
        if k in (3, 4):
            source = source.at[pl.ds(pl.multiple_of(mine * hid, hid), hid), :]
        copies.append(pltpu.make_async_copy(source, target, sems.at[k]))
    for copy in copies:
        copy.start()
    for copy in copies[:2]:
        copy.wait()
    w_both[...] = dot(w_node_a[...], w_msg[...]).astype(jnp.bfloat16)
    turned[...] = w_both[...].T
    w_both_t[...] = mine_of(turned, mine, hid)
    for copy in copies[2:]:
        copy.wait()
    w_send_t[...] = w_send[...].T
    w_recv_t[...] = w_recv[...].T
    turned[...] = w_node_v[...].T
    w_node_v_t[...] = mine_of(turned, mine, w_node_v_t.shape[0])
    w_out_t[...] = w_out_all[...].T
    w_out[...] = mine_of(w_out_all, mine, w_out.shape[0])


def edges_kernel(tiles, senders, in_degree, low_cols, high_cols, low_rows, high_rows):
    degree, nodes = senders.shape
    lane = lax.broadcasted_iota(jnp.int32, (degree, nodes), 1)
    row = lax.broadcasted_iota(jnp.int32, (degree, nodes), 0)
    valid = (row < in_degree[...]) & (lane < tiles[0] * TILE)
    ids = senders[...]
    low = (ids & (CHUNK - 1)).astype(jnp.float32)
    high = jnp.where(valid, ids // CHUNK, NO_CHUNK).astype(jnp.float32)
    for m in range(degree):
        shape = (PACK, nodes)
        low_rows[m] = jnp.broadcast_to(low[m : m + 1], shape).astype(jnp.bfloat16)
        high_rows[m] = jnp.broadcast_to(high[m : m + 1], shape).astype(jnp.bfloat16)
    fill = jnp.zeros((PACK - degree, nodes), jnp.float32)
    depth = 2 * PACK
    both = jnp.concatenate([low, fill, high, fill], axis=0).T.astype(jnp.bfloat16)
    width = degree * LANES
    spot = lax.broadcasted_iota(jnp.int32, (depth, width), 0)
    group = lax.broadcasted_iota(jnp.int32, (depth, width), 1) // LANES
    for first, out in ((0, low_cols), (PACK, high_cols)):
        pick = (spot == group + first).astype(jnp.bfloat16)
        spread = dot(both, pick).astype(jnp.bfloat16)
        for m in range(degree):
            out[m] = spread[:, m * LANES : (m + 1) * LANES]


def project_kernel(count, tiles, picks, *refs):
    blocks = refs[:count]
    w_send, feats, proj, upper, lower, beside, cross = refs[count:]
    mine, sub = lax.axis_index("ch"), lax.axis_index("sub")
    first = tiles[0] // 2
    assemble(feats, blocks, mine)
    whole = feats[...]
    hid = proj.shape[1]
    proj[...] = (0.5 * dot(w_send[...], whole).T).astype(jnp.bfloat16)
    rows = upper.shape[0] - PACK
    upper[:rows, :] = proj[pl.ds(pl.multiple_of(first * TILE, TILE), rows), :]
    lower[:rows, :] = proj[:rows, :]
    spot = lax.broadcasted_iota(jnp.int32, (PACK, hid), 0)
    _, per_slot, slots = picks.shape
    half = slots // 2
    for start, out, lift in ((0, upper, first), (half, lower, 0)):
        marks = jnp.zeros((PACK, hid), jnp.float32)
        for k in range(half * per_slot):
            rel = picks[0, k % per_slot, start + k // per_slot] - lift
            marks = jnp.where(spot == k, rel.astype(jnp.float32), marks)
        out[rows:, :] = marks.astype(jnp.bfloat16)

    @pl.when(sub == 0)
    def _():
        beside[...] = upper[...]
        cross[...] = lower[...]

    @pl.when(sub != 0)
    def _():
        beside[...] = lower[...]
        cross[...] = upper[...]


def receive_kernel(bias, feats, w_recv, base):
    hid = base.shape[1]
    mine = lax.axis_index("ch")
    my_bias = jnp.zeros((1, hid), jnp.float32)
    for k in range(bias.shape[1] // hid):
        my_bias += jnp.where(mine == k, bias[:, k * hid : (k + 1) * hid], 0.0)
    recv = dot(w_recv[...], feats[...]).T
    base[...] = 0.5 * (recv.astype(jnp.bfloat16).astype(jnp.float32) + my_bias)


def prepare_kernel(count, tiles, *refs):
    blocks = refs[:count]
    feats, w_node_v, bias, w_out_t, cots, pre, grad_hidden = refs[count:]
    assemble(cots, blocks, lax.axis_index("ch"))
    column = jnp.broadcast_to(bias[...], (8, bias.shape[1])).T[:, :1]
    pre[...] = dot(w_node_v[...], feats[...]) + column
    lane = lax.broadcasted_iota(jnp.int32, (1, cots.shape[1]), 1)
    active = (lane < tiles[0] * TILE).astype(jnp.bfloat16)
    grad_hidden[...] = dot(w_out_t[...], cots[...] * active)


def chunk_of(place, first, shape):
    on_zero, on_one = (float(first + slot) for slot in SLOT_OF[place])
    chunk = jnp.where(lax.axis_index("sub") == 0, on_zero, on_one)
    return jnp.full(shape, chunk, jnp.float32).astype(jnp.bfloat16)


def picks_of(block, place):
    marks = block[CHUNK : CHUNK + PACK, :].astype(jnp.float32)
    per_slot = CHUNK // TILE
    half = len(SLOT_OF) // 2
    starts = [slot % half * per_slot for slot in SLOT_OF[place]]
    sub = lax.axis_index("sub")
    return [
        jnp.where(
            sub == 0,
            marks[starts[0] + t : starts[0] + t + 1],
            marks[starts[1] + t : starts[1] + t + 1],
        )
        for t in range(per_slot)
    ]


def fill(ext, start, block, place):
    for t, pick in enumerate(picks_of(block, place)):
        ext[start + t * TILE : start + (t + 1) * TILE, :] = jnp.where(
            pick > 0.5, block[TILE : 2 * TILE, :], block[:TILE, :]
        )


def pick_rows(low, high, chunks, ext):
    one = jnp.bfloat16(1.0)
    zero = jnp.bfloat16(0.0)
    lane = lax.broadcasted_iota(jnp.int32, low.shape, 1)
    marks = [
        jnp.where(low == (lane + half * LANES).astype(jnp.bfloat16), one, zero)
        for half in range(CHUNK // LANES)
    ]
    picker = jnp.concatenate(
        [jnp.where(high == chunk, mark, zero) for chunk in chunks for mark in marks], axis=1
    )
    return dot(picker, ext[...])


def near_kernel(low, high, proj, beside, part, ext):
    own = proj.shape[0]
    ext[:own, :] = proj[...]
    fill(ext, own, beside, 0)
    first = own // CHUNK
    chunks = [jnp.bfloat16(chunk) for chunk in range(first)]
    chunks.append(chunk_of(0, first, low.shape[1:]))

    def step(m, carry):
        part[m] = pick_rows(low[m], high[m], chunks, ext).astype(jnp.bfloat16)
        return carry

    lax.fori_loop(0, low.shape[0], step, 0, unroll=True)


def line_kernel(low, high, before, west, east, part, ext):
    first = low.shape[1] // CHUNK
    chunks = []
    for index, (place, block) in enumerate(((1, west), (2, east))):
        fill(ext, index * CHUNK, block, place)
        chunks.append(jnp.bfloat16(first + SLOT_OF[place][0]))

    def step(m, carry):
        more = pick_rows(low[m], high[m], chunks, ext)
        part[m] = (before[m].astype(jnp.float32) + more).astype(jnp.bfloat16)
        return carry

    lax.fori_loop(0, low.shape[0], step, 0, unroll=True)


def cross_rows_kernel(block, rows):
    fill(rows, 0, block, 3)


def message_kernel(
    start, low, high, base, in_degree, part, cross, west, east, message, slope, ext, total
):
    nodes = low.shape[1]
    degree, rows, hid = slope.shape
    first = nodes // CHUNK
    together = nodes // rows
    span = slice(start, start + rows)
    chunks = []
    ext[:CHUNK, :] = cross[...]
    for index, (place, block) in enumerate(((4, west), (5, east))):
        fill(ext, (index + 1) * CHUNK, block, place)
    for place in (3, 4, 5):
        chunks.append(chunk_of(place, first, (nodes, LANES)))
    total[...] = jnp.zeros_like(total)

    def rows_of(ref, k):
        return jnp.concatenate([ref[k * together + i, span, :] for i in range(together)], axis=0)

    def step(k, carry):
        low_k, high_k = rows_of(low, k), rows_of(high, k)
        half = pick_rows(low_k, high_k, chunks, ext) + rows_of(part, k).astype(jnp.float32)
        half += jnp.concatenate([base[span, :]] * together, axis=0)
        wide = jnp.concatenate([high_k] * pl.cdiv(hid, LANES), axis=1)[:, :hid]
        half = jnp.where(wide.astype(jnp.float32) < NO_CHUNK, half, OFF)
        twice = jnp.tanh(half) + 1.0
        act = half * twice
        grad = (twice + act * (2.0 - twice)).astype(jnp.bfloat16)
        terms = 0.0
        for i in range(together):
            terms += act[i * rows : (i + 1) * rows]
            slope[k * together + i] = grad[i * rows : (i + 1) * rows]
        total[...] += terms
        return carry

    lax.fori_loop(0, degree // together, step, 0, unroll=True)
    count = in_degree[:, span].astype(jnp.float32)
    message[...] = (total[...].T / count).astype(jnp.bfloat16)


def node_kernel(count, start, in_degree, *refs):
    blocks = refs[:count]
    w_both, w_both_t, pre, grad_hidden = refs[count : count + 4]
    hidden, grad_pre, scale, messages = refs[count + 4 :]
    assemble(messages, blocks, lax.axis_index("ch"))
    span = slice(start, start + hidden.shape[1])
    half = 0.5 * (pre[:, span] + dot(w_both[...], messages[...]))
    twice = jnp.tanh(half) + 1.0
    act = half * twice
    hidden[...] = act.astype(jnp.bfloat16)
    slope = 0.5 * (twice + act * (2.0 - twice))
    low_grad = (grad_hidden[:, span] * slope).astype(jnp.bfloat16)
    grad_pre[...] = low_grad
    grad_msg = dot(w_both_t[...], low_grad).astype(jnp.bfloat16).astype(jnp.float32)
    scale[...] = (grad_msg * (0.5 / in_degree[:, span].astype(jnp.float32))).T


def scatter(low, high, edges, chunks, total):
    one = jnp.bfloat16(1.0)
    zero = jnp.bfloat16(0.0)
    groups = CHUNK // PACK
    for step in edges:
        width = sum(rows for _, _, rows, _ in step)
        place = lax.broadcasted_iota(jnp.int32, (groups, PACK, width), 0) * PACK
        place = place + lax.broadcasted_iota(jnp.int32, (groups, PACK, width), 1)
        low_k = jnp.concatenate([low[m, :, s : s + r] for m, s, r, _ in step], axis=1)
        high_k = jnp.concatenate([high[m, :, s : s + r] for m, s, r, _ in step], axis=1)
        grads = jnp.concatenate([grad() for _, _, _, grad in step], axis=0)
        mark = jnp.where(low_k[None] == place.astype(jnp.bfloat16), one, zero)
        picker = jnp.concatenate(
            [jnp.where(high_k[None] == chunk, mark, zero) for chunk in chunks], axis=0
        ).reshape(len(chunks) * CHUNK, width)
        total[...] += dot(picker, grads)


def pairs(start, ref, nodes, grad_of):
    degree, rows, _ = ref.shape
    together = nodes // rows
    return [
        [
            (m, start, rows, functools.partial(grad_of, ref, m))
            for m in range(k * together, (k + 1) * together)
        ]
        for k in range(degree // together)
    ]


def fold(block, place, index, total):
    picks = picks_of(block, place)
    halves = []
    for half in range(len(picks)):
        terms = 0.0
        for t, pick in enumerate(picks):
            start = index * CHUNK + t * TILE
            hit = jnp.abs(pick - half) < 0.5
            terms += jnp.where(hit, total[start : start + TILE, :], 0.0)
        halves.append(terms)
    return jnp.concatenate(halves, axis=0).astype(jnp.bfloat16)


def early_kernel(low, high, slope, scale, grads, total):
    nodes = low.shape[2]

    def grad_of(ref, m):
        grads[m] = (ref[m].astype(jnp.float32) * scale[...]).astype(jnp.bfloat16)
        return grads[m]

    chunks = [chunk_of(place, nodes // CHUNK, (1, PACK, nodes)) for place in EARLY]
    total[...] = jnp.zeros_like(total)
    scatter(low, high, pairs(0, slope, nodes, grad_of), chunks, total)


def cross_kernel(start, low, high, slope, scale, before, cross, to_cross, grads, total):
    nodes = low.shape[2]

    def grad_of(ref, m):
        grads[m] = (ref[m].astype(jnp.float32) * scale[...]).astype(jnp.bfloat16)
        return grads[m]

    chunks = [chunk_of(EARLY[0], nodes // CHUNK, (1, PACK, nodes))]
    total[...] = before[:CHUNK, :]
    scatter(low, high, pairs(start, slope, nodes, grad_of), chunks, total)
    to_cross[...] = fold(cross, EARLY[0], 0, total)


def other_kernel(start, low, high, grads, before, west, east, to_other, total):
    nodes = low.shape[2]
    chunks = [chunk_of(place, nodes // CHUNK, (1, PACK, nodes)) for place in EARLY[1:]]
    total[...] = before[CHUNK:, :]
    scatter(low, high, pairs(start, grads, nodes, lambda ref, m: ref[m]), chunks, total)
    to_other[0] = fold(west, EARLY[1], 0, total)
    to_other[1] = fold(east, EARLY[2], 1, total)


def all_pairs(parts, nodes):
    start, steps = 0, []
    for part in parts:
        steps += pairs(start, part, nodes, lambda ref, m: ref[m])
        start += part.shape[1]
    return steps


def late_kernel(low, high, *refs):
    *parts, west, east, beside, to_west, to_east, to_beside, total = refs
    nodes = low.shape[2]
    first = nodes // CHUNK
    chunks = [chunk_of(place, first, (1, PACK, nodes)) for place in LATE]
    total[...] = jnp.zeros_like(total)
    scatter(low, high, all_pairs(parts, nodes), chunks, total)
    to_west[...] = fold(west, 1, 0, total)
    to_east[...] = fold(east, 2, 1, total)
    to_beside[...] = fold(beside, 0, 2, total)


def own_kernel(low, high, *refs):
    *parts, total, recv = refs
    nodes = low.shape[2]
    chunks = [jnp.bfloat16(chunk) for chunk in range(nodes // CHUNK)]
    total[...] = jnp.zeros_like(total)
    scatter(low, high, all_pairs(parts, nodes), chunks, total)
    start = 0
    for part in parts:
        degree, rows, _ = part.shape
        terms = 0.0
        for m in range(degree):
            terms += part[m].astype(jnp.float32)
        recv[:, start : start + rows] = terms.T.astype(jnp.bfloat16)
        start += rows


def output_kernel(tiles, feats, cots, w_out, w_node_v_t, *refs):
    *parts, updated, direct = refs
    count = len(parts) // 2
    rows = parts[0].shape[1]
    for k in range(count):
        hidden, grad_pre = parts[k], parts[count + k]
        span = slice(k * rows, (k + 1) * rows)
        lane = lax.broadcasted_iota(jnp.int32, (1, rows), 1) + k * rows
        active = (lane < tiles[0] * TILE).astype(jnp.float32)
        node_out = dot(w_out[...], hidden[...])
        new = feats[:, span].astype(jnp.float32) + active * node_out
        updated[:, span] = new.astype(jnp.bfloat16)
        direct[:, span] = cots[:, span].astype(jnp.float32) + dot(w_node_v_t[...], grad_pre[...])


def across_kernel(left, right, across, west, east):
    sub = lax.axis_index("sub")
    other = across[...].astype(jnp.float32)
    to_west = left[...].astype(jnp.float32) + jnp.where(sub == 0, 0.0, other)
    to_east = right[...].astype(jnp.float32) + jnp.where(sub == 0, other, 0.0)
    west[...] = to_west.astype(west.dtype)
    east[...] = to_east.astype(east.dtype)


def add_kernel(left, right, more, west, east):
    west[...] = (left[...] + more[0].astype(jnp.float32)).astype(jnp.bfloat16)
    east[...] = (right[...] + more[1].astype(jnp.float32)).astype(jnp.bfloat16)


def back_kernel(start, inv_root, tiles, own, beside, feats, upper, *refs):
    *refs, total = refs
    sub = lax.axis_index("sub")
    offset = pl.multiple_of(tiles[0] // 2 * TILE, TILE)
    total[...] = own[...]
    near = beside[...].astype(jnp.float32)
    block = upper[...].astype(jnp.float32) + jnp.where(sub == 0, near, 0.0)
    total[pl.ds(offset, block.shape[0]), :] += block
    if start:
        grad_send, weight = refs
    else:
        lower, before, grad_send, w_mine, w_beside, weight = refs
        block = lower[...].astype(jnp.float32) + jnp.where(sub == 0, 0.0, near)
        total[: block.shape[0], :] += block
    rows = grad_send.shape[0]
    grad_send[...] = total[start : start + rows, :].astype(jnp.bfloat16)
    terms = dot(feats[:, start : start + rows], grad_send[...])
    if start:
        weight[...] = terms
        return
    weight[...] = (before[...] + terms) * inv_root
    lon = lax.axis_index("lon")
    lons, columns, _ = w_mine.shape
    for k in range(lons):
        band = lax.rem(lon + k, lons) * 2
        for out, core in ((w_mine, sub), (w_beside, 1 - sub)):
            spot = pl.multiple_of((band + core) * columns, columns)
            out[k] = weight[pl.ds(spot, columns), :].astype(out.dtype)


def terms_kernel(start, grad_send, recv, direct, w_send_t, w_recv_t, kept, sent, terms):
    span = slice(start, start + grad_send.shape[0])
    mine = lax.axis_index("ch")
    chans = kept.shape[0]
    grad_send_t = grad_send[...].astype(jnp.float32).T.astype(jnp.bfloat16)
    terms[...] = dot(w_send_t[...], grad_send_t) + dot(w_recv_t[...], recv[:, span])
    kept[...] = direct[:, span] + mine_of(terms, mine, chans)
    count = sent.shape[0] + 1
    for k in range(1, count):
        sent[k - 1] = mine_of(terms, lax.rem(mine + k, count), chans).astype(jnp.bfloat16)


def finish_kernel(count, *refs):
    kept, *others = refs[: count]
    *done, out = refs[count:]
    total = kept[...]
    for other in others:
        total += other[...].astype(jnp.float32)
    out[:, : kept.shape[1]] = total.astype(jnp.bfloat16)
    start = kept.shape[1]
    for part in done:
        out[:, start : start + part.shape[1]] = part[...]
        start += part.shape[1]


def sum_kernel(w_mine, w_beside, near, sent):
    near[...] = w_mine[0] + w_beside[0].astype(jnp.float32)
    for k in range(sent.shape[0]):
        sent[k] = (w_mine[k + 1] + w_beside[k + 1].astype(jnp.float32)).astype(jnp.bfloat16)


def weight_kernel(near, *refs):
    out = refs[-1]
    total = near[...]
    for ref in refs[:-1]:
        total += ref[...].astype(jnp.float32)
    out[...] = total


def shards(
    features,
    cotangent,
    senders,
    in_degree,
    tile_count,
    send_tiles,
    w_send,
    w_recv,
    bias_edge,
    w_msg,
    w_node_v,
    w_node_a,
    bias_node,
    w_out,
):
    chans, nodes = features.shape
    count = lax.axis_size("ch")
    lons = lax.axis_size("lon")
    hidden_all, chans_all = w_send.shape
    hid = hidden_all // count
    cycle = ("lon", "sub")
    shard_count = lax.axis_size(cycle)
    total_nodes = nodes * shard_count
    degree = senders.shape[0]
    slots = send_tiles.shape[1]
    slot_rows = send_tiles.shape[2] * TILE
    ext_len = nodes + slots * slot_rows
    bf16, f32 = jnp.bfloat16, jnp.float32
    shape = jax.ShapeDtypeStruct

    far_route = [(i, (i + (3 if i % 2 else -3)) % shard_count) for i in range(shard_count)]
    across_route = [(i, (i + (1 if i % 2 else -1)) % shard_count) for i in range(shard_count)]
    across = lambda block: lax.ppermute(block, cycle, across_route)
    degrees = in_degree[None, :]
    picks = jnp.transpose(send_tiles, (0, 2, 1))
    sub = lax.axis_index("sub")

    feat_blocks = gathered(features, "ch")

    whole_w = pltpu.VMEM((chans_all, hidden_all), bf16)
    (
        w_send_my,
        w_recv_my,
        w_out_my,
        features_held,
        w_send_t,
        w_recv_t,
        w_both_t,
        w_node_v_t,
        w_both,
        w_out_t,
    ) = call(
        weights_kernel,
        (
            shape((hid, chans_all), bf16),
            shape((hid, chans_all), bf16),
            shape((chans, hidden_all), bf16),
            shape((chans, nodes), bf16),
            shape((chans_all, hid), bf16),
            shape((chans_all, hid), bf16),
            shape((hid, hidden_all), bf16),
            shape((chans, hidden_all), bf16),
            shape((hidden_all, hidden_all), bf16),
            shape((hidden_all, chans_all), bf16),
        ),
        [w_msg, w_node_a, features, w_send, w_recv, w_node_v, w_out],
        away=7,
        scalars=0,
        scratch=[whole_w] * 5 + [pltpu.SemaphoreType.DMA((7,))],
        limit=WEIGHTS_LIMIT,
    )
    feat_blocks[0] = features_held

    block = shape((slot_rows + PACK, hid), bf16)
    feats, proj, upper, lower, beside, cross = call(
        functools.partial(project_kernel, count),
        (
            shape((chans_all, nodes), bf16),
            shape((nodes, hid), bf16),
            block,
            block,
            block,
            block,
        ),
        [tile_count, picks] + feat_blocks + [w_send_my],
    )
    west = shifted(upper, "lon", 1)
    east = shifted(lower, "lon", -1)
    cross = lax.ppermute(cross, cycle, far_route)
    base = call(
        receive_kernel,
        shape((nodes, hid), f32),
        [bias_edge[None, :], feats, w_recv_my],
        scalars=0,
    )
    base, senders, cotangent_late = lax.optimization_barrier((base, senders, cotangent))
    beside = shifted(beside, "sub", 1)
    cot_blocks = gathered(cotangent_late, "ch")
    low_cols, high_cols, low_rows, high_rows = call(
        edges_kernel,
        (
            shape((degree, nodes, LANES), bf16),
            shape((degree, nodes, LANES), bf16),
            shape((degree, PACK, nodes), bf16),
            shape((degree, PACK, nodes), bf16),
        ),
        [tile_count, senders, degrees],
        scalars=1,
    )
    cots, pre, grad_hidden = call(
        functools.partial(prepare_kernel, count),
        (
            shape((chans_all, nodes), bf16),
            shape((hidden_all, nodes), f32),
            shape((hidden_all, nodes), f32),
        ),
        [tile_count] + cot_blocks + [feats, w_node_v, bias_node[None, :], w_out_t],
        scalars=1,
    )

    part_shape = shape((degree, nodes, hid), bf16)
    part = call(
        near_kernel,
        part_shape,
        [low_cols, high_cols, proj, beside],
        scratch=[pltpu.VMEM((nodes + slot_rows, hid), bf16)],
        scalars=0,
    )
    west, east, part = lax.optimization_barrier((west, east, part))
    west_too = shifted(west, "sub", 1)
    east_too = shifted(east, "sub", 1)
    part, pre = lax.optimization_barrier((part, pre))
    part = call(
        line_kernel,
        part_shape,
        [low_cols, high_cols, part, west, east],
        scratch=[pltpu.VMEM((2 * slot_rows, hid), bf16)],
        scalars=0,
    )
    part, cross = lax.optimization_barrier((part, cross))
    cross_rows = call(
        cross_rows_kernel, shape((slot_rows, hid), bf16), [cross], scalars=0
    )
    halves = 2
    rows = nodes // halves
    slopes, messages, hiddens, grad_pres, grads = [], [], [], [], []
    for k in range(halves):
        message, slope = call(
            functools.partial(message_kernel, k * rows),
            (shape((hid, rows), bf16), shape((degree, rows, hid), bf16)),
            [low_cols, high_cols, base, degrees, part, cross_rows, west_too, east_too],
            scratch=[pltpu.VMEM((3 * slot_rows, hid), bf16), pltpu.VMEM((rows, hid), f32)],
            scalars=0,
        )
        slopes.append(slope)
        messages.append(gathered(message, "ch"))

    block = shape((slot_rows, hid), bf16)
    sums = shape((len(EARLY) * slot_rows, hid), f32)
    grad_shape = shape((degree, rows, hid), bf16)
    for k in range(halves):
        hidden, grad_pre, scale = call(
            functools.partial(node_kernel, count, k * rows),
            (
                shape((hidden_all, rows), bf16),
                shape((hidden_all, rows), bf16),
                shape((rows, hid), f32),
            ),
            [degrees] + messages[k] + [w_both, w_both_t, pre, grad_hidden],
            scratch=[pltpu.VMEM((hidden_all, rows), bf16)],
            scalars=0,
        )
        hiddens.append(hidden)
        grad_pres.append(grad_pre)
        operands = [low_rows, high_rows, slopes[k], scale]
        if k == 0:
            grad, before = call(early_kernel, (grad_shape, sums), operands, scalars=0)
        else:
            to_cross, grad = call(
                functools.partial(cross_kernel, k * rows),
                (block, grad_shape),
                operands + [before, cross],
                scratch=[pltpu.VMEM((slot_rows, hid), f32)],
                scalars=0,
            )
            to_other = call(
                functools.partial(other_kernel, k * rows),
                shape((2, slot_rows, hid), bf16),
                [low_rows, high_rows, grad, before, west_too, east_too],
                scratch=[pltpu.VMEM((2 * slot_rows, hid), f32)],
                scalars=0,
            )
        grads.append(grad)

    grads[0], to_other = lax.optimization_barrier((grads[0], to_other))
    from_other = shifted(to_other, "sub", 1)
    from_cross = across(to_cross)
    to_west, to_east, to_beside = call(
        late_kernel,
        (block, block, block),
        [low_rows, high_rows] + grads + [west, east, beside],
        scratch=[pltpu.VMEM((len(LATE) * slot_rows, hid), f32)],
        scalars=0,
    )
    wide = shape((slot_rows, hid), f32)
    to_west, to_east = call(
        across_kernel, (wide, wide), [to_west, to_east, from_cross], scalars=0, flops=15 * 10**8
    )
    to_west, to_east = call(add_kernel, (block, block), [to_west, to_east, from_other], scalars=0)
    from_upper = shifted(to_west, "lon", -1)
    from_lower = shifted(to_east, "lon", 1)
    from_beside = shifted(to_beside, "sub", 1)
    to_west, grads[0] = lax.optimization_barrier((to_west, grads[0]))

    own, grad_recv = call(
        own_kernel,
        (shape((nodes, hid), f32), shape((hid, nodes), bf16)),
        [low_rows, high_rows] + grads,
        scalars=0,
    )
    own, hiddens[0] = lax.optimization_barrier((own, hiddens[0]))
    updated, direct = call(
        output_kernel,
        (shape((chans, nodes), bf16), shape((chans, nodes), f32)),
        [tile_count, features_held, cotangent, w_out_my, w_node_v_t] + hiddens + grad_pres,
        scalars=1,
    )
    columns = chans_all // shard_count
    inv_root = 1.0 / math.sqrt(total_nodes)
    inputs = [tile_count, own, from_beside, feats, from_upper]
    weight_shape = shape((chans_all, hid), f32)
    grad_shape = shape((rows, hid), bf16)
    finals = []
    for k in reversed(range(halves)):
        kernel = functools.partial(back_kernel, k * rows, inv_root)
        if k:
            grad_send, weight = call(
                kernel,
                (grad_shape, weight_shape),
                inputs,
                scratch=[pltpu.VMEM((nodes, hid), f32)],
                scalars=1,
            )
        else:
            grad_send, w_mine, w_beside = call(
                kernel,
                (
                    grad_shape,
                    shape((lons, columns, hid), f32),
                    shape((lons, columns, hid), bf16),
                ),
                inputs + [from_lower, weight],
                scratch=[pltpu.VMEM(weight_shape.shape, f32), pltpu.VMEM((nodes, hid), f32)],
                scalars=1,
            )
            w_beside = shifted(w_beside, "sub", 1)
            w_beside, *finals = lax.optimization_barrier((w_beside, *finals))
        kept, sent = call(
            functools.partial(terms_kernel, k * rows),
            (shape((chans, rows), f32), shape((count - 1, chans, rows), bf16)),
            [grad_send, grad_recv, direct, w_send_t, w_recv_t],
            scratch=[pltpu.VMEM((chans_all, rows), f32)],
            scalars=0,
        )
        if k:
            weight, kept = lax.optimization_barrier((weight, kept))
        parts = [kept] + [shifted(sent[i - 1], "ch", i) for i in range(1, count)]
        grad_features = call(
            functools.partial(finish_kernel, count),
            shape((chans, nodes - k * rows), bf16),
            parts + finals,
            scalars=0,
        )
        finals = [grad_features]

    near, w_sent = call(
        sum_kernel,
        (shape((columns, hid), f32), shape((lons - 1, columns, hid), bf16)),
        [w_mine, w_beside],
        scalars=0,
    )
    w_terms = [shifted(w_sent[k - 1], "lon", k) for k in range(1, lons)]
    grad_w_send = call(
        weight_kernel, shape((columns, hid), f32), [near] + w_terms, scalars=0
    )
    return (updated, grad_features, grad_w_send.T)


def solution(mesh):
    nodes_last = P("ch", ("parts", "lon", "sub"))
    spread = ("parts", "lon", "sub")
    placed = (nodes_last, nodes_last, P(None, spread), P(spread), P(spread), P(spread, None, None))
    return jax.shard_map(
        shards,
        mesh=mesh,
        in_specs=placed + (P(),) * 8,
        out_specs=(nodes_last, nodes_last, P(("parts", "ch"), ("lon", "sub"))),
        check_vma=False,
    )
```

```python
import functools
import math

import jax
import jax.numpy as jnp
from jax import lax
from jax.experimental import pallas as pl
from jax.experimental.pallas import tpu as pltpu
from jax.sharding import PartitionSpec as P

TILE = 128
CHUNK = 256
LANES = 128
PACK = 16
MIB = 1 << 20
WEIGHTS_LIMIT = 52
NO_CHUNK = 64
SLOT_OF = ((3, 0), (1, 1), (4, 4), (2, 5), (0, 2), (5, 3))
EARLY, LATE = (3, 4, 5), (1, 2, 0)
OFF = -1e4


def shifted(block, axis, distance):
    size = lax.axis_size(axis)
    route = [((i - distance) % size, i) for i in range(size)]
    return lax.ppermute(block, axis, route)


def gathered(block, axis):
    return [block] + [shifted(block, axis, k) for k in range(1, lax.axis_size(axis))]


def dot(left, right):
    return jnp.dot(left, right, preferred_element_type=jnp.float32)


def dot_nt(left, right):
    return lax.dot_general(
        left, right, (((1,), (1,)), ((), ())), preferred_element_type=jnp.float32
    )


def sigmoid(value):
    return 0.5 * jnp.tanh(0.5 * value) + 0.5


def call(kernel, out_shape, operands, scratch=(), scalars=2, away=0, limit=24, flops=1024):
    vmem = pl.BlockSpec(memory_space=pltpu.VMEM)
    smem = pl.BlockSpec(memory_space=pltpu.SMEM)
    anywhere = pl.BlockSpec(memory_space=pltpu.HBM)
    return pl.pallas_call(
        kernel,
        out_shape=out_shape,
        in_specs=[smem] * scalars
        + [anywhere] * away
        + [vmem] * (len(operands) - scalars - away),
        out_specs=jax.tree.map(lambda _: vmem, out_shape),
        scratch_shapes=scratch,
        compiler_params=pltpu.CompilerParams(vmem_limit_bytes=limit * MIB),
        cost_estimate=pl.CostEstimate(flops=flops, bytes_accessed=1024, transcendentals=0),
    )(*operands)


def assemble(whole_ref, blocks, first):
    count = len(blocks)
    rows = blocks[0].shape[0]
    for k, block in enumerate(blocks):
        place = lax.rem(first - k + count, count) * rows
        whole_ref[pl.ds(pl.multiple_of(place, rows), rows), :] = block[...]


def mine_of(ref, index, rows):
    return ref[pl.ds(pl.multiple_of(index * rows, rows), rows), :]


def weights_kernel(*refs):
    sources, refs = refs[:7], refs[7:]
    w_send, w_recv, w_out, feats, w_send_t, w_recv_t, w_both_t, w_node_v_t, w_both, w_out_t = refs[:10]
    w_msg, w_node_v, w_node_a, w_out_all, turned, sems = refs[10:]
    mine = lax.axis_index("ch")
    hid = w_send.shape[0]
    targets = (w_msg, w_node_a, feats, w_send, w_recv, w_node_v, w_out_all)
    copies = []
    for k, (source, target) in enumerate(zip(sources, targets)):
        if k in (3, 4):
            source = source.at[pl.ds(pl.multiple_of(mine * hid, hid), hid), :]
        copies.append(pltpu.make_async_copy(source, target, sems.at[k]))
    for copy in copies:
        copy.start()
    for copy in copies[:2]:
        copy.wait()
    w_both[...] = dot(w_node_a[...], w_msg[...]).astype(jnp.bfloat16)
    turned[...] = w_both[...].T
    w_both_t[...] = mine_of(turned, mine, hid)
    for copy in copies[2:]:
        copy.wait()
    w_send_t[...] = w_send[...].T
    w_recv_t[...] = w_recv[...].T
    turned[...] = w_node_v[...].T
    w_node_v_t[...] = mine_of(turned, mine, w_node_v_t.shape[0])
    w_out_t[...] = w_out_all[...].T
    w_out[...] = mine_of(w_out_all, mine, w_out.shape[0])


def edges_kernel(tiles, senders, in_degree, low_cols, high_cols, low_rows, high_rows):
    degree, nodes = senders.shape
    lane = lax.broadcasted_iota(jnp.int32, (degree, nodes), 1)
    row = lax.broadcasted_iota(jnp.int32, (degree, nodes), 0)
    valid = (row < in_degree[...]) & (lane < tiles[0] * TILE)
    ids = senders[...]
    low = (ids & (CHUNK - 1)).astype(jnp.float32)
    high = jnp.where(valid, ids // CHUNK, NO_CHUNK).astype(jnp.float32)
    for m in range(degree):
        shape = (PACK, nodes)
        low_rows[m] = jnp.broadcast_to(low[m : m + 1], shape).astype(jnp.bfloat16)
        high_rows[m] = jnp.broadcast_to(high[m : m + 1], shape).astype(jnp.bfloat16)
    fill = jnp.zeros((PACK - degree, nodes), jnp.float32)
    depth = 2 * PACK
    both = jnp.concatenate([low, fill, high, fill], axis=0).T.astype(jnp.bfloat16)
    width = degree * LANES
    spot = lax.broadcasted_iota(jnp.int32, (depth, width), 0)
    group = lax.broadcasted_iota(jnp.int32, (depth, width), 1) // LANES
    for first, out in ((0, low_cols), (PACK, high_cols)):
        pick = (spot == group + first).astype(jnp.bfloat16)
        spread = dot(both, pick).astype(jnp.bfloat16)
        for m in range(degree):
            out[m] = spread[:, m * LANES : (m + 1) * LANES]


def project_kernel(count, tiles, picks, *refs):
    blocks = refs[:count]
    w_send, feats, proj, upper, lower, beside, cross = refs[count:]
    mine, sub = lax.axis_index("ch"), lax.axis_index("sub")
    first = tiles[0] // 2
    assemble(feats, blocks, mine)
    whole = feats[...]
    hid = proj.shape[1]
    proj[...] = (0.5 * dot(w_send[...], whole).T).astype(jnp.bfloat16)
    rows = upper.shape[0] - PACK
    upper[:rows, :] = proj[pl.ds(pl.multiple_of(first * TILE, TILE), rows), :]
    lower[:rows, :] = proj[:rows, :]
    spot = lax.broadcasted_iota(jnp.int32, (PACK, hid), 0)
    _, per_slot, slots = picks.shape
    half = slots // 2
    for start, out, lift in ((0, upper, first), (half, lower, 0)):
        marks = jnp.zeros((PACK, hid), jnp.float32)
        for k in range(half * per_slot):
            rel = picks[0, k % per_slot, start + k // per_slot] - lift
            marks = jnp.where(spot == k, rel.astype(jnp.float32), marks)
        out[rows:, :] = marks.astype(jnp.bfloat16)

    @pl.when(sub == 0)
    def _():
        beside[...] = upper[...]
        cross[...] = lower[...]

    @pl.when(sub != 0)
    def _():
        beside[...] = lower[...]
        cross[...] = upper[...]


def receive_kernel(bias, feats, w_recv, base):
    hid = base.shape[1]
    mine = lax.axis_index("ch")
    my_bias = jnp.zeros((1, hid), jnp.float32)
    for k in range(bias.shape[1] // hid):
        my_bias += jnp.where(mine == k, bias[:, k * hid : (k + 1) * hid], 0.0)
    recv = dot(w_recv[...], feats[...]).T
    base[...] = 0.5 * (recv.astype(jnp.bfloat16).astype(jnp.float32) + my_bias)


def prepare_kernel(count, tiles, *refs):
    blocks = refs[:count]
    feats, w_node_v, bias, w_out_t, cots, pre, grad_hidden = refs[count:]
    assemble(cots, blocks, lax.axis_index("ch"))
    column = jnp.broadcast_to(bias[...], (8, bias.shape[1])).T[:, :1]
    pre[...] = dot(w_node_v[...], feats[...]) + column
    lane = lax.broadcasted_iota(jnp.int32, (1, cots.shape[1]), 1)
    active = (lane < tiles[0] * TILE).astype(jnp.bfloat16)
    grad_hidden[...] = dot(w_out_t[...], cots[...] * active)


def chunk_of(place, first, shape):
    on_zero, on_one = (float(first + slot) for slot in SLOT_OF[place])
    chunk = jnp.where(lax.axis_index("sub") == 0, on_zero, on_one)
    return jnp.full(shape, chunk, jnp.float32).astype(jnp.bfloat16)


def picks_of(block, place):
    marks = block[CHUNK : CHUNK + PACK, :].astype(jnp.float32)
    per_slot = CHUNK // TILE
    half = len(SLOT_OF) // 2
    starts = [slot % half * per_slot for slot in SLOT_OF[place]]
    sub = lax.axis_index("sub")
    return [
        jnp.where(
            sub == 0,
            marks[starts[0] + t : starts[0] + t + 1],
            marks[starts[1] + t : starts[1] + t + 1],
        )
        for t in range(per_slot)
    ]


def fill(ext, start, block, place):
    for t, pick in enumerate(picks_of(block, place)):
        ext[start + t * TILE : start + (t + 1) * TILE, :] = jnp.where(
            pick > 0.5, block[TILE : 2 * TILE, :], block[:TILE, :]
        )


def pick_rows(low, high, chunks, ext):
    one = jnp.bfloat16(1.0)
    zero = jnp.bfloat16(0.0)
    lane = lax.broadcasted_iota(jnp.int32, low.shape, 1)
    marks = [
        jnp.where(low == (lane + half * LANES).astype(jnp.bfloat16), one, zero)
        for half in range(CHUNK // LANES)
    ]
    picker = jnp.concatenate(
        [jnp.where(high == chunk, mark, zero) for chunk in chunks for mark in marks], axis=1
    )
    return dot(picker, ext[...])


def near_kernel(low, high, proj, beside, part, ext):
    own = proj.shape[0]
    ext[:own, :] = proj[...]
    fill(ext, own, beside, 0)
    first = own // CHUNK
    chunks = [jnp.bfloat16(chunk) for chunk in range(first)]
    chunks.append(chunk_of(0, first, low.shape[1:]))

    def step(m, carry):
        part[m] = pick_rows(low[m], high[m], chunks, ext).astype(jnp.bfloat16)
        return carry

    lax.fori_loop(0, low.shape[0], step, 0, unroll=True)


def line_kernel(low, high, before, west, east, part, ext):
    first = low.shape[1] // CHUNK
    chunks = []
    for index, (place, block) in enumerate(((1, west), (2, east))):
        fill(ext, index * CHUNK, block, place)
        chunks.append(jnp.bfloat16(first + SLOT_OF[place][0]))

    def step(m, carry):
        more = pick_rows(low[m], high[m], chunks, ext)
        part[m] = (before[m].astype(jnp.float32) + more).astype(jnp.bfloat16)
        return carry

    lax.fori_loop(0, low.shape[0], step, 0, unroll=True)


def cross_rows_kernel(block, rows):
    fill(rows, 0, block, 3)


def message_kernel(
    start, low, high, base, in_degree, part, cross, west, east, message, slope, ext, total
):
    nodes = low.shape[1]
    degree, rows, hid = slope.shape
    first = nodes // CHUNK
    together = nodes // rows
    span = slice(start, start + rows)
    chunks = []
    ext[:CHUNK, :] = cross[...]
    for index, (place, block) in enumerate(((4, west), (5, east))):
        fill(ext, (index + 1) * CHUNK, block, place)
    for place in (3, 4, 5):
        chunks.append(chunk_of(place, first, (nodes, LANES)))
    total[...] = jnp.zeros_like(total)

    def rows_of(ref, k):
        return jnp.concatenate([ref[k * together + i, span, :] for i in range(together)], axis=0)

    def step(k, carry):
        low_k, high_k = rows_of(low, k), rows_of(high, k)
        half = pick_rows(low_k, high_k, chunks, ext) + rows_of(part, k).astype(jnp.float32)
        half += jnp.concatenate([base[span, :]] * together, axis=0)
        wide = jnp.concatenate([high_k] * pl.cdiv(hid, LANES), axis=1)[:, :hid]
        half = jnp.where(wide.astype(jnp.float32) < NO_CHUNK, half, OFF)
        twice = jnp.tanh(half) + 1.0
        act = half * twice
        grad = (twice + act * (2.0 - twice)).astype(jnp.bfloat16)
        terms = 0.0
        for i in range(together):
            terms += act[i * rows : (i + 1) * rows]
            slope[k * together + i] = grad[i * rows : (i + 1) * rows]
        total[...] += terms
        return carry

    lax.fori_loop(0, degree // together, step, 0, unroll=True)
    count = in_degree[:, span].astype(jnp.float32)
    message[...] = (total[...].T / count).astype(jnp.bfloat16)


def node_kernel(count, start, in_degree, *refs):
    blocks = refs[:count]
    w_both, w_both_t, pre, grad_hidden = refs[count : count + 4]
    hidden, grad_pre, scale, messages = refs[count + 4 :]
    assemble(messages, blocks, lax.axis_index("ch"))
    span = slice(start, start + hidden.shape[1])
    half = 0.5 * (pre[:, span] + dot(w_both[...], messages[...]))
    twice = jnp.tanh(half) + 1.0
    act = half * twice
    hidden[...] = act.astype(jnp.bfloat16)
    slope = 0.5 * (twice + act * (2.0 - twice))
    low_grad = (grad_hidden[:, span] * slope).astype(jnp.bfloat16)
    grad_pre[...] = low_grad
    grad_msg = dot(w_both_t[...], low_grad).astype(jnp.bfloat16).astype(jnp.float32)
    scale[...] = (grad_msg * (0.5 / in_degree[:, span].astype(jnp.float32))).T


def scatter(low, high, edges, chunks, total):
    one = jnp.bfloat16(1.0)
    zero = jnp.bfloat16(0.0)
    groups = CHUNK // PACK
    for step in edges:
        width = sum(rows for _, _, rows, _ in step)
        place = lax.broadcasted_iota(jnp.int32, (groups, PACK, width), 0) * PACK
        place = place + lax.broadcasted_iota(jnp.int32, (groups, PACK, width), 1)
        low_k = jnp.concatenate([low[m, :, s : s + r] for m, s, r, _ in step], axis=1)
        high_k = jnp.concatenate([high[m, :, s : s + r] for m, s, r, _ in step], axis=1)
        grads = jnp.concatenate([grad() for _, _, _, grad in step], axis=0)
        mark = jnp.where(low_k[None] == place.astype(jnp.bfloat16), one, zero)
        picker = jnp.concatenate(
            [jnp.where(high_k[None] == chunk, mark, zero) for chunk in chunks], axis=0
        ).reshape(len(chunks) * CHUNK, width)
        total[...] += dot(picker, grads)


def pairs(start, ref, nodes, grad_of):
    degree, rows, _ = ref.shape
    together = nodes // rows
    return [
        [
            (m, start, rows, functools.partial(grad_of, ref, m))
            for m in range(k * together, (k + 1) * together)
        ]
        for k in range(degree // together)
    ]


def fold(block, place, index, total):
    picks = picks_of(block, place)
    halves = []
    for half in range(len(picks)):
        terms = 0.0
        for t, pick in enumerate(picks):
            start = index * CHUNK + t * TILE
            hit = jnp.abs(pick - half) < 0.5
            terms += jnp.where(hit, total[start : start + TILE, :], 0.0)
        halves.append(terms)
    return jnp.concatenate(halves, axis=0).astype(jnp.bfloat16)


def early_kernel(low, high, slope, scale, grads, total):
    nodes = low.shape[2]

    def grad_of(ref, m):
        grads[m] = (ref[m].astype(jnp.float32) * scale[...]).astype(jnp.bfloat16)
        return grads[m]

    chunks = [chunk_of(place, nodes // CHUNK, (1, PACK, nodes)) for place in EARLY]
    total[...] = jnp.zeros_like(total)
    scatter(low, high, pairs(0, slope, nodes, grad_of), chunks, total)


def cross_kernel(start, low, high, slope, scale, before, cross, to_cross, grads, total):
    nodes = low.shape[2]

    def grad_of(ref, m):
        grads[m] = (ref[m].astype(jnp.float32) * scale[...]).astype(jnp.bfloat16)
        return grads[m]

    chunks = [chunk_of(EARLY[0], nodes // CHUNK, (1, PACK, nodes))]
    total[...] = before[:CHUNK, :]
    scatter(low, high, pairs(start, slope, nodes, grad_of), chunks, total)
    to_cross[...] = fold(cross, EARLY[0], 0, total)


def other_kernel(start, low, high, grads, before, west, east, to_other, total):
    nodes = low.shape[2]
    chunks = [chunk_of(place, nodes // CHUNK, (1, PACK, nodes)) for place in EARLY[1:]]
    total[...] = before[CHUNK:, :]
    scatter(low, high, pairs(start, grads, nodes, lambda ref, m: ref[m]), chunks, total)
    to_other[0] = fold(west, EARLY[1], 0, total)
    to_other[1] = fold(east, EARLY[2], 1, total)


def all_pairs(parts, nodes):
    start, steps = 0, []
    for part in parts:
        steps += pairs(start, part, nodes, lambda ref, m: ref[m])
        start += part.shape[1]
    return steps


def late_kernel(low, high, *refs):
    *parts, west, east, beside, to_west, to_east, to_beside, total = refs
    nodes = low.shape[2]
    first = nodes // CHUNK
    chunks = [chunk_of(place, first, (1, PACK, nodes)) for place in LATE]
    total[...] = jnp.zeros_like(total)
    scatter(low, high, all_pairs(parts, nodes), chunks, total)
    to_west[...] = fold(west, 1, 0, total)
    to_east[...] = fold(east, 2, 1, total)
    to_beside[...] = fold(beside, 0, 2, total)


def own_kernel(low, high, *refs):
    *parts, total, recv = refs
    nodes = low.shape[2]
    chunks = [jnp.bfloat16(chunk) for chunk in range(nodes // CHUNK)]
    total[...] = jnp.zeros_like(total)
    scatter(low, high, all_pairs(parts, nodes), chunks, total)
    start = 0
    for part in parts:
        degree, rows, _ = part.shape
        terms = 0.0
        for m in range(degree):
            terms += part[m].astype(jnp.float32)
        recv[:, start : start + rows] = terms.T.astype(jnp.bfloat16)
        start += rows


def output_kernel(tiles, feats, cots, w_out, w_node_v_t, *refs):
    *parts, updated, direct = refs
    count = len(parts) // 2
    rows = parts[0].shape[1]
    for k in range(count):
        hidden, grad_pre = parts[k], parts[count + k]
        span = slice(k * rows, (k + 1) * rows)
        lane = lax.broadcasted_iota(jnp.int32, (1, rows), 1) + k * rows
        active = (lane < tiles[0] * TILE).astype(jnp.float32)
        node_out = dot(w_out[...], hidden[...])
        new = feats[:, span].astype(jnp.float32) + active * node_out
        updated[:, span] = new.astype(jnp.bfloat16)
        direct[:, span] = cots[:, span].astype(jnp.float32) + dot(w_node_v_t[...], grad_pre[...])


def across_kernel(left, right, across, west, east):
    sub = lax.axis_index("sub")
    other = across[...].astype(jnp.float32)
    to_west = left[...].astype(jnp.float32) + jnp.where(sub == 0, 0.0, other)
    to_east = right[...].astype(jnp.float32) + jnp.where(sub == 0, other, 0.0)
    west[...] = to_west.astype(west.dtype)
    east[...] = to_east.astype(east.dtype)


def add_kernel(left, right, more, west, east):
    west[...] = (left[...] + more[0].astype(jnp.float32)).astype(jnp.bfloat16)
    east[...] = (right[...] + more[1].astype(jnp.float32)).astype(jnp.bfloat16)


def back_kernel(start, inv_root, tiles, own, beside, feats, upper, *refs):
    *refs, total = refs
    sub = lax.axis_index("sub")
    offset = pl.multiple_of(tiles[0] // 2 * TILE, TILE)
    total[...] = own[...]
    near = beside[...].astype(jnp.float32)
    block = upper[...].astype(jnp.float32) + jnp.where(sub == 0, near, 0.0)
    total[pl.ds(offset, block.shape[0]), :] += block
    if start:
        grad_send, weight = refs
    else:
        lower, before, grad_send, w_mine, w_beside, weight = refs
        block = lower[...].astype(jnp.float32) + jnp.where(sub == 0, 0.0, near)
        total[: block.shape[0], :] += block
    rows = grad_send.shape[0]
    grad_send[...] = total[start : start + rows, :].astype(jnp.bfloat16)
    terms = dot(feats[:, start : start + rows], grad_send[...])
    if start:
        weight[...] = terms
        return
    weight[...] = (before[...] + terms) * inv_root
    lon = lax.axis_index("lon")
    lons, columns, _ = w_mine.shape
    for k in range(lons):
        band = (lon ^ k) * 2
        for out, core in ((w_mine, sub), (w_beside, 1 - sub)):
            spot = pl.multiple_of((band + core) * columns, columns)
            out[k] = weight[pl.ds(spot, columns), :].astype(out.dtype)


def terms_kernel(start, grad_send, recv, direct, w_send_t, w_recv_t, kept, sent, terms):
    span = slice(start, start + grad_send.shape[0])
    mine = lax.axis_index("ch")
    chans = kept.shape[0]
    grad_send_t = grad_send[...].astype(jnp.float32).T.astype(jnp.bfloat16)
    terms[...] = dot(w_send_t[...], grad_send_t) + dot(w_recv_t[...], recv[:, span])
    kept[...] = direct[:, span] + mine_of(terms, mine, chans)
    count = sent.shape[0] + 1
    for k in range(1, count):
        sent[k - 1] = mine_of(terms, lax.rem(mine + k, count), chans).astype(jnp.bfloat16)


def finish_kernel(count, *refs):
    kept, *others = refs[: count]
    *done, out = refs[count:]
    total = kept[...]
    for other in others:
        total += other[...].astype(jnp.float32)
    out[:, : kept.shape[1]] = total.astype(jnp.bfloat16)
    start = kept.shape[1]
    for part in done:
        out[:, start : start + part.shape[1]] = part[...]
        start += part.shape[1]


def sum_kernel(held, received, near, sent):
    half = near.shape[0]
    near[...] = held[:half] + received[:half].astype(jnp.float32)
    sent[...] = (held[half:] + received[half:].astype(jnp.float32)).astype(jnp.bfloat16)


def weight_kernel(held, received, out):
    out[...] = held[0] + received[0].astype(jnp.float32)


def shards(
    features,
    cotangent,
    senders,
    in_degree,
    tile_count,
    send_tiles,
    w_send,
    w_recv,
    bias_edge,
    w_msg,
    w_node_v,
    w_node_a,
    bias_node,
    w_out,
):
    chans, nodes = features.shape
    count = lax.axis_size("ch")
    lons = lax.axis_size("lon")
    hidden_all, chans_all = w_send.shape
    hid = hidden_all // count
    cycle = ("lon", "sub")
    shard_count = lax.axis_size(cycle)
    total_nodes = nodes * shard_count
    degree = senders.shape[0]
    slots = send_tiles.shape[1]
    slot_rows = send_tiles.shape[2] * TILE
    ext_len = nodes + slots * slot_rows
    bf16, f32 = jnp.bfloat16, jnp.float32
    shape = jax.ShapeDtypeStruct

    far_route = [(i, (i + (3 if i % 2 else -3)) % shard_count) for i in range(shard_count)]
    across_route = [(i, (i + (1 if i % 2 else -1)) % shard_count) for i in range(shard_count)]
    across = lambda block: lax.ppermute(block, cycle, across_route)
    degrees = in_degree[None, :]
    picks = jnp.transpose(send_tiles, (0, 2, 1))
    sub = lax.axis_index("sub")

    feat_blocks = gathered(features, "ch")

    whole_w = pltpu.VMEM((chans_all, hidden_all), bf16)
    (
        w_send_my,
        w_recv_my,
        w_out_my,
        features_held,
        w_send_t,
        w_recv_t,
        w_both_t,
        w_node_v_t,
        w_both,
        w_out_t,
    ) = call(
        weights_kernel,
        (
            shape((hid, chans_all), bf16),
            shape((hid, chans_all), bf16),
            shape((chans, hidden_all), bf16),
            shape((chans, nodes), bf16),
            shape((chans_all, hid), bf16),
            shape((chans_all, hid), bf16),
            shape((hid, hidden_all), bf16),
            shape((chans, hidden_all), bf16),
            shape((hidden_all, hidden_all), bf16),
            shape((hidden_all, chans_all), bf16),
        ),
        [w_msg, w_node_a, features, w_send, w_recv, w_node_v, w_out],
        away=7,
        scalars=0,
        scratch=[whole_w] * 5 + [pltpu.SemaphoreType.DMA((7,))],
        limit=WEIGHTS_LIMIT,
    )
    feat_blocks[0] = features_held

    block = shape((slot_rows + PACK, hid), bf16)
    feats, proj, upper, lower, beside, cross = call(
        functools.partial(project_kernel, count),
        (
            shape((chans_all, nodes), bf16),
            shape((nodes, hid), bf16),
            block,
            block,
            block,
            block,
        ),
        [tile_count, picks] + feat_blocks + [w_send_my],
    )
    west = shifted(upper, "lon", 1)
    east = shifted(lower, "lon", -1)
    cross = lax.ppermute(cross, cycle, far_route)
    base = call(
        receive_kernel,
        shape((nodes, hid), f32),
        [bias_edge[None, :], feats, w_recv_my],
        scalars=0,
    )
    base, senders, cotangent_late = lax.optimization_barrier((base, senders, cotangent))
    beside = shifted(beside, "sub", 1)
    cot_blocks = gathered(cotangent_late, "ch")
    low_cols, high_cols, low_rows, high_rows = call(
        edges_kernel,
        (
            shape((degree, nodes, LANES), bf16),
            shape((degree, nodes, LANES), bf16),
            shape((degree, PACK, nodes), bf16),
            shape((degree, PACK, nodes), bf16),
        ),
        [tile_count, senders, degrees],
        scalars=1,
    )
    cots, pre, grad_hidden = call(
        functools.partial(prepare_kernel, count),
        (
            shape((chans_all, nodes), bf16),
            shape((hidden_all, nodes), f32),
            shape((hidden_all, nodes), f32),
        ),
        [tile_count] + cot_blocks + [feats, w_node_v, bias_node[None, :], w_out_t],
        scalars=1,
    )

    part_shape = shape((degree, nodes, hid), bf16)
    part = call(
        near_kernel,
        part_shape,
        [low_cols, high_cols, proj, beside],
        scratch=[pltpu.VMEM((nodes + slot_rows, hid), bf16)],
        scalars=0,
    )
    west, east, part = lax.optimization_barrier((west, east, part))
    west_too = shifted(west, "sub", 1)
    east_too = shifted(east, "sub", 1)
    part, pre = lax.optimization_barrier((part, pre))
    part = call(
        line_kernel,
        part_shape,
        [low_cols, high_cols, part, west, east],
        scratch=[pltpu.VMEM((2 * slot_rows, hid), bf16)],
        scalars=0,
    )
    part, cross = lax.optimization_barrier((part, cross))
    cross_rows = call(
        cross_rows_kernel, shape((slot_rows, hid), bf16), [cross], scalars=0
    )
    halves = 2
    rows = nodes // halves
    slopes, messages, hiddens, grad_pres, grads = [], [], [], [], []
    for k in range(halves):
        message, slope = call(
            functools.partial(message_kernel, k * rows),
            (shape((hid, rows), bf16), shape((degree, rows, hid), bf16)),
            [low_cols, high_cols, base, degrees, part, cross_rows, west_too, east_too],
            scratch=[pltpu.VMEM((3 * slot_rows, hid), bf16), pltpu.VMEM((rows, hid), f32)],
            scalars=0,
        )
        slopes.append(slope)
        messages.append(gathered(message, "ch"))

    block = shape((slot_rows, hid), bf16)
    sums = shape((len(EARLY) * slot_rows, hid), f32)
    grad_shape = shape((degree, rows, hid), bf16)
    for k in range(halves):
        hidden, grad_pre, scale = call(
            functools.partial(node_kernel, count, k * rows),
            (
                shape((hidden_all, rows), bf16),
                shape((hidden_all, rows), bf16),
                shape((rows, hid), f32),
            ),
            [degrees] + messages[k] + [w_both, w_both_t, pre, grad_hidden],
            scratch=[pltpu.VMEM((hidden_all, rows), bf16)],
            scalars=0,
        )
        hiddens.append(hidden)
        grad_pres.append(grad_pre)
        operands = [low_rows, high_rows, slopes[k], scale]
        if k == 0:
            grad, before = call(early_kernel, (grad_shape, sums), operands, scalars=0)
        else:
            to_cross, grad = call(
                functools.partial(cross_kernel, k * rows),
                (block, grad_shape),
                operands + [before, cross],
                scratch=[pltpu.VMEM((slot_rows, hid), f32)],
                scalars=0,
            )
            to_other = call(
                functools.partial(other_kernel, k * rows),
                shape((2, slot_rows, hid), bf16),
                [low_rows, high_rows, grad, before, west_too, east_too],
                scratch=[pltpu.VMEM((2 * slot_rows, hid), f32)],
                scalars=0,
            )
        grads.append(grad)

    grads[0], to_other = lax.optimization_barrier((grads[0], to_other))
    from_other = shifted(to_other, "sub", 1)
    from_cross = across(to_cross)
    to_west, to_east, to_beside = call(
        late_kernel,
        (block, block, block),
        [low_rows, high_rows] + grads + [west, east, beside],
        scratch=[pltpu.VMEM((len(LATE) * slot_rows, hid), f32)],
        scalars=0,
    )
    wide = shape((slot_rows, hid), f32)
    to_west, to_east = call(
        across_kernel, (wide, wide), [to_west, to_east, from_cross], scalars=0, flops=15 * 10**8
    )
    to_west, to_east = call(add_kernel, (block, block), [to_west, to_east, from_other], scalars=0)
    from_upper = shifted(to_west, "lon", -1)
    from_lower = shifted(to_east, "lon", 1)
    from_beside = shifted(to_beside, "sub", 1)
    to_west, grads[0] = lax.optimization_barrier((to_west, grads[0]))

    own, grad_recv = call(
        own_kernel,
        (shape((nodes, hid), f32), shape((hid, nodes), bf16)),
        [low_rows, high_rows] + grads,
        scalars=0,
    )
    own, hiddens[0] = lax.optimization_barrier((own, hiddens[0]))
    updated, direct = call(
        output_kernel,
        (shape((chans, nodes), bf16), shape((chans, nodes), f32)),
        [tile_count, features_held, cotangent, w_out_my, w_node_v_t] + hiddens + grad_pres,
        scalars=1,
    )
    columns = chans_all // shard_count
    inv_root = 1.0 / math.sqrt(total_nodes)
    inputs = [tile_count, own, from_beside, feats, from_upper]
    weight_shape = shape((chans_all, hid), f32)
    grad_shape = shape((rows, hid), bf16)
    finals = []
    for k in reversed(range(halves)):
        kernel = functools.partial(back_kernel, k * rows, inv_root)
        if k:
            grad_send, weight = call(
                kernel,
                (grad_shape, weight_shape),
                inputs,
                scratch=[pltpu.VMEM((nodes, hid), f32)],
                scalars=1,
            )
        else:
            grad_send, w_mine, w_beside = call(
                kernel,
                (
                    grad_shape,
                    shape((lons, columns, hid), f32),
                    shape((lons, columns, hid), bf16),
                ),
                inputs + [from_lower, weight],
                scratch=[pltpu.VMEM(weight_shape.shape, f32), pltpu.VMEM((nodes, hid), f32)],
                scalars=1,
            )
            w_beside = shifted(w_beside, "sub", 1)
            w_beside, *finals = lax.optimization_barrier((w_beside, *finals))
        kept, sent = call(
            functools.partial(terms_kernel, k * rows),
            (shape((chans, rows), f32), shape((count - 1, chans, rows), bf16)),
            [grad_send, grad_recv, direct, w_send_t, w_recv_t],
            scratch=[pltpu.VMEM((chans_all, rows), f32)],
            scalars=0,
        )
        if k:
            weight, kept = lax.optimization_barrier((weight, kept))
        parts = [kept] + [shifted(sent[i - 1], "ch", i) for i in range(1, count)]
        grad_features = call(
            functools.partial(finish_kernel, count),
            shape((chans, nodes - k * rows), bf16),
            parts + finals,
            scalars=0,
        )
        finals = [grad_features]

    span = lons
    while span > 1:
        span //= 2
        w_mine, w_sent = call(
            sum_kernel,
            (shape((span, columns, hid), f32), shape((span, columns, hid), bf16)),
            [w_mine, w_beside],
            scalars=0,
        )
        w_beside = lax.ppermute(w_sent, "lon", [(i, i ^ span) for i in range(lons)])
    grad_w_send = call(
        weight_kernel, shape((columns, hid), f32), [w_mine, w_beside], scalars=0
    )
    return (updated, grad_features, grad_w_send.T)


def solution(mesh):
    nodes_last = P("ch", ("parts", "lon", "sub"))
    spread = ("parts", "lon", "sub")
    placed = (nodes_last, nodes_last, P(None, spread), P(spread), P(spread), P(spread, None, None))
    return jax.shard_map(
        shards,
        mesh=mesh,
        in_specs=placed + (P(),) * 8,
        out_specs=(nodes_last, nodes_last, P(("parts", "ch"), ("lon", "sub"))),
        check_vma=False,
    )
```

```python
import functools
import math

import jax
import jax.numpy as jnp
from jax import lax
from jax.experimental import pallas as pl
from jax.experimental.pallas import tpu as pltpu
from jax.sharding import PartitionSpec as P

TILE = 128
CHUNK = 256
LANES = 128
PACK = 16
MIB = 1 << 20
WEIGHTS_LIMIT = 52
LINE_FLOPS = 10**9
NO_CHUNK = 64
SLOT_OF = ((3, 0), (1, 1), (4, 4), (2, 5), (0, 2), (5, 3))
EARLY, LATE = (3, 4, 5), (1, 2, 0)
OFF = -1e4


def shifted(block, axis, distance):
    size = lax.axis_size(axis)
    route = [((i - distance) % size, i) for i in range(size)]
    return lax.ppermute(block, axis, route)


def gathered(block, axis):
    return [block] + [shifted(block, axis, k) for k in range(1, lax.axis_size(axis))]


def dot(left, right):
    return jnp.dot(left, right, preferred_element_type=jnp.float32)


def dot_nt(left, right):
    return lax.dot_general(
        left, right, (((1,), (1,)), ((), ())), preferred_element_type=jnp.float32
    )


def sigmoid(value):
    return 0.5 * jnp.tanh(0.5 * value) + 0.5


def call(kernel, out_shape, operands, scratch=(), scalars=2, away=0, limit=24, flops=1024):
    vmem = pl.BlockSpec(memory_space=pltpu.VMEM)
    smem = pl.BlockSpec(memory_space=pltpu.SMEM)
    anywhere = pl.BlockSpec(memory_space=pltpu.HBM)
    return pl.pallas_call(
        kernel,
        out_shape=out_shape,
        in_specs=[smem] * scalars
        + [anywhere] * away
        + [vmem] * (len(operands) - scalars - away),
        out_specs=jax.tree.map(lambda _: vmem, out_shape),
        scratch_shapes=scratch,
        compiler_params=pltpu.CompilerParams(vmem_limit_bytes=limit * MIB),
        cost_estimate=pl.CostEstimate(flops=flops, bytes_accessed=1024, transcendentals=0),
    )(*operands)


def assemble(whole_ref, blocks, first):
    count = len(blocks)
    rows = blocks[0].shape[0]
    for k, block in enumerate(blocks):
        place = lax.rem(first - k + count, count) * rows
        whole_ref[pl.ds(pl.multiple_of(place, rows), rows), :] = block[...]


def mine_of(ref, index, rows):
    return ref[pl.ds(pl.multiple_of(index * rows, rows), rows), :]


def weights_kernel(*refs):
    sources, refs = refs[:6], refs[6:]
    w_send, w_recv, w_out, w_send_t, w_recv_t, w_both_t, w_node_v_t, w_both, w_out_t = refs[:9]
    w_msg, w_node_v, w_node_a, w_out_all, turned, sems = refs[9:]
    mine = lax.axis_index("ch")
    hid = w_send.shape[0]
    targets = (w_msg, w_node_a, w_send, w_recv, w_node_v, w_out_all)
    copies = []
    for k, (source, target) in enumerate(zip(sources, targets)):
        if k in (2, 3):
            source = source.at[pl.ds(pl.multiple_of(mine * hid, hid), hid), :]
        copies.append(pltpu.make_async_copy(source, target, sems.at[k]))
    for copy in copies:
        copy.start()
    for copy in copies[:2]:
        copy.wait()
    w_both[...] = dot(w_node_a[...], w_msg[...]).astype(jnp.bfloat16)
    turned[...] = w_both[...].T
    w_both_t[...] = mine_of(turned, mine, hid)
    for copy in copies[2:]:
        copy.wait()
    w_send_t[...] = w_send[...].T
    w_recv_t[...] = w_recv[...].T
    turned[...] = w_node_v[...].T
    w_node_v_t[...] = mine_of(turned, mine, w_node_v_t.shape[0])
    w_out_t[...] = w_out_all[...].T
    w_out[...] = mine_of(w_out_all, mine, w_out.shape[0])


def edges_kernel(tiles, senders, in_degree, low_cols, high_cols, low_rows, high_rows):
    degree, nodes = senders.shape
    lane = lax.broadcasted_iota(jnp.int32, (degree, nodes), 1)
    row = lax.broadcasted_iota(jnp.int32, (degree, nodes), 0)
    valid = (row < in_degree[...]) & (lane < tiles[0] * TILE)
    ids = senders[...]
    low = (ids & (CHUNK - 1)).astype(jnp.float32)
    high = jnp.where(valid, ids // CHUNK, NO_CHUNK).astype(jnp.float32)
    for m in range(degree):
        shape = (PACK, nodes)
        low_rows[m] = jnp.broadcast_to(low[m : m + 1], shape).astype(jnp.bfloat16)
        high_rows[m] = jnp.broadcast_to(high[m : m + 1], shape).astype(jnp.bfloat16)
    fill = jnp.zeros((PACK - degree, nodes), jnp.float32)
    depth = 2 * PACK
    both = jnp.concatenate([low, fill, high, fill], axis=0).T.astype(jnp.bfloat16)
    width = degree * LANES
    spot = lax.broadcasted_iota(jnp.int32, (depth, width), 0)
    group = lax.broadcasted_iota(jnp.int32, (depth, width), 1) // LANES
    for first, out in ((0, low_cols), (PACK, high_cols)):
        pick = (spot == group + first).astype(jnp.bfloat16)
        spread = dot(both, pick).astype(jnp.bfloat16)
        for m in range(degree):
            out[m] = spread[:, m * LANES : (m + 1) * LANES]


def put_marks(picks, start, lift, out):
    _, per_slot, slots = picks.shape
    hid = out.shape[1]
    spot = lax.broadcasted_iota(jnp.int32, (PACK, hid), 0)
    marks = jnp.zeros((PACK, hid), jnp.float32)
    for k in range(slots // 2 * per_slot):
        rel = picks[0, k % per_slot, start + k // per_slot] - lift
        marks = jnp.where(spot == k, rel.astype(jnp.float32), marks)
    out[out.shape[0] - PACK :, :] = marks.astype(jnp.bfloat16)


def project_half(blocks, w_send, feats, proj):
    assemble(feats, blocks, lax.axis_index("ch"))
    proj[...] = (0.5 * dot(w_send[...], feats[...]).T).astype(jnp.bfloat16)


def lower_kernel(count, picks, *refs):
    blocks, (w_send, feats, proj, lower) = refs[:count], refs[count:]
    project_half(blocks, w_send, feats, proj)
    lower[: proj.shape[0], :] = proj[...]
    put_marks(picks, picks.shape[2] // 2, 0, lower)


def upper_kernel(count, tiles, picks, *refs):
    blocks = refs[:count]
    w_send, below, lower, feats, proj, upper, beside, cross, both = refs[count:]
    sub = lax.axis_index("sub")
    first = tiles[0] // 2
    project_half(blocks, w_send, feats, proj)
    rows = proj.shape[0]
    both[:rows, :] = below[...]
    both[rows:, :] = proj[...]
    upper[:rows, :] = both[pl.ds(pl.multiple_of(first * TILE, TILE), rows), :]
    put_marks(picks, 0, first, upper)

    @pl.when(sub == 0)
    def _():
        beside[...] = upper[...]
        cross[...] = lower[...]

    @pl.when(sub != 0)
    def _():
        beside[...] = lower[...]
        cross[...] = upper[...]


def receive_kernel(bias, below, above, w_recv, base):
    hid = base.shape[1]
    mine = lax.axis_index("ch")
    my_bias = jnp.zeros((1, hid), jnp.float32)
    for k in range(bias.shape[1] // hid):
        my_bias += jnp.where(mine == k, bias[:, k * hid : (k + 1) * hid], 0.0)
    rows = below.shape[1]
    for k, feats in enumerate((below, above)):
        recv = dot(w_recv[...], feats[...]).T.astype(jnp.bfloat16).astype(jnp.float32)
        base[k * rows : (k + 1) * rows, :] = 0.5 * (recv + my_bias)


def prepare_kernel(count, tiles, *refs):
    blocks = refs[:count]
    below, above, w_node_v, bias, w_out_t, cots, pre, grad_hidden = refs[count:]
    assemble(cots, blocks, lax.axis_index("ch"))
    column = jnp.broadcast_to(bias[...], (8, bias.shape[1])).T[:, :1]
    rows = below.shape[1]
    pre[:, :rows] = dot(w_node_v[...], below[...]) + column
    pre[:, rows:] = dot(w_node_v[...], above[...]) + column
    lane = lax.broadcasted_iota(jnp.int32, (1, cots.shape[1]), 1)
    active = (lane < tiles[0] * TILE).astype(jnp.bfloat16)
    grad_hidden[...] = dot(w_out_t[...], cots[...] * active)


def chunk_of(place, first, shape):
    on_zero, on_one = (float(first + slot) for slot in SLOT_OF[place])
    chunk = jnp.where(lax.axis_index("sub") == 0, on_zero, on_one)
    return jnp.full(shape, chunk, jnp.float32).astype(jnp.bfloat16)


def picks_of(block, place):
    marks = block[CHUNK : CHUNK + PACK, :].astype(jnp.float32)
    per_slot = CHUNK // TILE
    half = len(SLOT_OF) // 2
    starts = [slot % half * per_slot for slot in SLOT_OF[place]]
    sub = lax.axis_index("sub")
    return [
        jnp.where(
            sub == 0,
            marks[starts[0] + t : starts[0] + t + 1],
            marks[starts[1] + t : starts[1] + t + 1],
        )
        for t in range(per_slot)
    ]


def fill(ext, start, block, place):
    for t, pick in enumerate(picks_of(block, place)):
        ext[start + t * TILE : start + (t + 1) * TILE, :] = jnp.where(
            pick > 0.5, block[TILE : 2 * TILE, :], block[:TILE, :]
        )


def pick_rows(low, high, chunks, ext):
    one = jnp.bfloat16(1.0)
    zero = jnp.bfloat16(0.0)
    lane = lax.broadcasted_iota(jnp.int32, low.shape, 1)
    marks = [
        jnp.where(low == (lane + half * LANES).astype(jnp.bfloat16), one, zero)
        for half in range(CHUNK // LANES)
    ]
    picker = jnp.concatenate(
        [jnp.where(high == chunk, mark, zero) for chunk in chunks for mark in marks], axis=1
    )
    return dot(picker, ext[...])


def near_kernel(low, high, before, below, above, beside, part, ext):
    rows = below.shape[0]
    own = 2 * rows
    ext[:rows, :] = below[...]
    ext[rows:own, :] = above[...]
    fill(ext, own, beside, 0)
    first = own // CHUNK
    chunks = [jnp.bfloat16(chunk) for chunk in range(first)]
    chunks.append(chunk_of(0, first, low.shape[1:]))

    def step(m, carry):
        more = pick_rows(low[m], high[m], chunks, ext)
        part[m] = (before[m].astype(jnp.float32) + more).astype(jnp.bfloat16)
        return carry

    lax.fori_loop(0, low.shape[0], step, 0, unroll=True)


def line_kernel(place, low, high, block, *refs):
    *before, part, ext = refs
    fill(ext, 0, block, place)
    chunks = [jnp.bfloat16(low.shape[1] // CHUNK + SLOT_OF[place][0])]

    def step(m, carry):
        rows = pick_rows(low[m], high[m], chunks, ext)
        for ref in before:
            rows += ref[m].astype(jnp.float32)
        part[m] = rows.astype(jnp.bfloat16)
        return carry

    lax.fori_loop(0, low.shape[0], step, 0, unroll=True)


def cross_rows_kernel(block, rows):
    fill(rows, 0, block, 3)


def message_kernel(
    start, low, high, base, in_degree, part, cross, west, east, message, slope, ext, total
):
    nodes = low.shape[1]
    degree, rows, hid = slope.shape
    first = nodes // CHUNK
    together = nodes // rows
    span = slice(start, start + rows)
    chunks = []
    ext[:CHUNK, :] = cross[...]
    for index, (place, block) in enumerate(((4, west), (5, east))):
        fill(ext, (index + 1) * CHUNK, block, place)
    for place in (3, 4, 5):
        chunks.append(chunk_of(place, first, (nodes, LANES)))
    total[...] = jnp.zeros_like(total)

    def rows_of(ref, k):
        return jnp.concatenate([ref[k * together + i, span, :] for i in range(together)], axis=0)

    def step(k, carry):
        low_k, high_k = rows_of(low, k), rows_of(high, k)
        half = pick_rows(low_k, high_k, chunks, ext) + rows_of(part, k).astype(jnp.float32)
        half += jnp.concatenate([base[span, :]] * together, axis=0)
        wide = jnp.concatenate([high_k] * pl.cdiv(hid, LANES), axis=1)[:, :hid]
        half = jnp.where(wide.astype(jnp.float32) < NO_CHUNK, half, OFF)
        twice = jnp.tanh(half) + 1.0
        act = half * twice
        grad = (twice + act * (2.0 - twice)).astype(jnp.bfloat16)
        terms = 0.0
        for i in range(together):
            terms += act[i * rows : (i + 1) * rows]
            slope[k * together + i] = grad[i * rows : (i + 1) * rows]
        total[...] += terms
        return carry

    lax.fori_loop(0, degree // together, step, 0, unroll=True)
    count = in_degree[:, span].astype(jnp.float32)
    message[...] = (total[...].T / count).astype(jnp.bfloat16)


def node_kernel(count, start, in_degree, *refs):
    blocks = refs[:count]
    w_both, w_both_t, pre, grad_hidden = refs[count : count + 4]
    hidden, grad_pre, scale, messages = refs[count + 4 :]
    assemble(messages, blocks, lax.axis_index("ch"))
    span = slice(start, start + hidden.shape[1])
    half = 0.5 * (pre[:, span] + dot(w_both[...], messages[...]))
    twice = jnp.tanh(half) + 1.0
    act = half * twice
    hidden[...] = act.astype(jnp.bfloat16)
    slope = 0.5 * (twice + act * (2.0 - twice))
    low_grad = (grad_hidden[:, span] * slope).astype(jnp.bfloat16)
    grad_pre[...] = low_grad
    grad_msg = dot(w_both_t[...], low_grad).astype(jnp.bfloat16).astype(jnp.float32)
    scale[...] = (grad_msg * (0.5 / in_degree[:, span].astype(jnp.float32))).T


def scatter(low, high, edges, chunks, total):
    one = jnp.bfloat16(1.0)
    zero = jnp.bfloat16(0.0)
    groups = CHUNK // PACK
    for step in edges:
        width = sum(rows for _, _, rows, _ in step)
        place = lax.broadcasted_iota(jnp.int32, (groups, PACK, width), 0) * PACK
        place = place + lax.broadcasted_iota(jnp.int32, (groups, PACK, width), 1)
        low_k = jnp.concatenate([low[m, :, s : s + r] for m, s, r, _ in step], axis=1)
        high_k = jnp.concatenate([high[m, :, s : s + r] for m, s, r, _ in step], axis=1)
        grads = jnp.concatenate([grad() for _, _, _, grad in step], axis=0)
        mark = jnp.where(low_k[None] == place.astype(jnp.bfloat16), one, zero)
        picker = jnp.concatenate(
            [jnp.where(high_k[None] == chunk, mark, zero) for chunk in chunks], axis=0
        ).reshape(len(chunks) * CHUNK, width)
        total[...] += dot(picker, grads)


def pairs(start, ref, nodes, grad_of):
    degree, rows, _ = ref.shape
    together = nodes // rows
    return [
        [
            (m, start, rows, functools.partial(grad_of, ref, m))
            for m in range(k * together, (k + 1) * together)
        ]
        for k in range(degree // together)
    ]


def fold(block, place, index, total):
    picks = picks_of(block, place)
    halves = []
    for half in range(len(picks)):
        terms = 0.0
        for t, pick in enumerate(picks):
            start = index * CHUNK + t * TILE
            hit = jnp.abs(pick - half) < 0.5
            terms += jnp.where(hit, total[start : start + TILE, :], 0.0)
        halves.append(terms)
    return jnp.concatenate(halves, axis=0).astype(jnp.bfloat16)


def early_kernel(low, high, slope, scale, grads, total):
    nodes = low.shape[2]

    def grad_of(ref, m):
        grads[m] = (ref[m].astype(jnp.float32) * scale[...]).astype(jnp.bfloat16)
        return grads[m]

    chunks = [chunk_of(place, nodes // CHUNK, (1, PACK, nodes)) for place in EARLY]
    total[...] = jnp.zeros_like(total)
    scatter(low, high, pairs(0, slope, nodes, grad_of), chunks, total)


def cross_kernel(start, low, high, slope, scale, before, cross, to_cross, grads, total):
    nodes = low.shape[2]

    def grad_of(ref, m):
        grads[m] = (ref[m].astype(jnp.float32) * scale[...]).astype(jnp.bfloat16)
        return grads[m]

    chunks = [chunk_of(EARLY[0], nodes // CHUNK, (1, PACK, nodes))]
    total[...] = before[:CHUNK, :]
    scatter(low, high, pairs(start, slope, nodes, grad_of), chunks, total)
    to_cross[...] = fold(cross, EARLY[0], 0, total)


def other_kernel(start, low, high, grads, before, west, east, to_other, total):
    nodes = low.shape[2]
    chunks = [chunk_of(place, nodes // CHUNK, (1, PACK, nodes)) for place in EARLY[1:]]
    total[...] = before[CHUNK:, :]
    scatter(low, high, pairs(start, grads, nodes, lambda ref, m: ref[m]), chunks, total)
    to_other[0] = fold(west, EARLY[1], 0, total)
    to_other[1] = fold(east, EARLY[2], 1, total)


def all_pairs(parts, nodes):
    start, steps = 0, []
    for part in parts:
        steps += pairs(start, part, nodes, lambda ref, m: ref[m])
        start += part.shape[1]
    return steps


def late_kernel(low, high, *refs):
    *parts, west, east, beside, to_west, to_east, to_beside, total = refs
    nodes = low.shape[2]
    first = nodes // CHUNK
    chunks = [chunk_of(place, first, (1, PACK, nodes)) for place in LATE]
    total[...] = jnp.zeros_like(total)
    scatter(low, high, all_pairs(parts, nodes), chunks, total)
    to_west[...] = fold(west, 1, 0, total)
    to_east[...] = fold(east, 2, 1, total)
    to_beside[...] = fold(beside, 0, 2, total)


def own_kernel(low, high, *refs):
    *parts, total, recv = refs
    nodes = low.shape[2]
    chunks = [jnp.bfloat16(chunk) for chunk in range(nodes // CHUNK)]
    total[...] = jnp.zeros_like(total)
    scatter(low, high, all_pairs(parts, nodes), chunks, total)
    start = 0
    for part in parts:
        degree, rows, _ = part.shape
        terms = 0.0
        for m in range(degree):
            terms += part[m].astype(jnp.float32)
        recv[:, start : start + rows] = terms.T.astype(jnp.bfloat16)
        start += rows


def output_kernel(tiles, feats, cots, w_out, w_node_v_t, *refs):
    *parts, updated, direct = refs
    count = len(parts) // 2
    rows = parts[0].shape[1]
    for k in range(count):
        hidden, grad_pre = parts[k], parts[count + k]
        span = slice(k * rows, (k + 1) * rows)
        lane = lax.broadcasted_iota(jnp.int32, (1, rows), 1) + k * rows
        active = (lane < tiles[0] * TILE).astype(jnp.float32)
        node_out = dot(w_out[...], hidden[...])
        new = feats[:, span].astype(jnp.float32) + active * node_out
        updated[:, span] = new.astype(jnp.bfloat16)
        direct[:, span] = cots[:, span].astype(jnp.float32) + dot(w_node_v_t[...], grad_pre[...])


def across_kernel(left, right, across, west, east):
    sub = lax.axis_index("sub")
    other = across[...].astype(jnp.float32)
    to_west = left[...].astype(jnp.float32) + jnp.where(sub == 0, 0.0, other)
    to_east = right[...].astype(jnp.float32) + jnp.where(sub == 0, other, 0.0)
    west[...] = to_west.astype(west.dtype)
    east[...] = to_east.astype(east.dtype)


def add_kernel(left, right, more, west, east):
    west[...] = (left[...] + more[0].astype(jnp.float32)).astype(jnp.bfloat16)
    east[...] = (right[...] + more[1].astype(jnp.float32)).astype(jnp.bfloat16)


def band_bits(place, lons):
    bits, weight = 0, 1
    while weight < lons:
        bits += weight if place * weight * 2 // lons % 2 else 0
        weight *= 2
    return bits


def back_kernel(start, inv_root, tiles, feats, own, beside, upper, *refs):
    *refs, total = refs
    sub = lax.axis_index("sub")
    offset = pl.multiple_of(tiles[0] // 2 * TILE, TILE)
    total[...] = own[...]
    near = beside[...].astype(jnp.float32)
    block = upper[...].astype(jnp.float32) + jnp.where(sub == 0, near, 0.0)
    total[pl.ds(offset, block.shape[0]), :] += block
    if start:
        grad_send, weight = refs
    else:
        lower, before, grad_send, w_mine, w_beside, weight = refs
        block = lower[...].astype(jnp.float32) + jnp.where(sub == 0, 0.0, near)
        total[: block.shape[0], :] += block
    rows = grad_send.shape[0]
    grad_send[...] = total[start : start + rows, :].astype(jnp.bfloat16)
    terms = dot(feats[...], grad_send[...])
    if start:
        weight[...] = terms
        return
    weight[...] = (before[...] + terms) * inv_root
    lon = lax.axis_index("lon")
    lons, columns, _ = w_mine.shape
    for k in range(lons):
        band = (lon ^ band_bits(k, lons)) * 2
        for out, core in ((w_mine, sub), (w_beside, 1 - sub)):
            spot = pl.multiple_of((band + core) * columns, columns)
            out[k] = weight[pl.ds(spot, columns), :].astype(out.dtype)


def terms_kernel(start, grad_send, recv, direct, w_send_t, w_recv_t, kept, sent, terms):
    span = slice(start, start + grad_send.shape[0])
    mine = lax.axis_index("ch")
    chans = kept.shape[0]
    grad_send_t = grad_send[...].astype(jnp.float32).T.astype(jnp.bfloat16)
    terms[...] = dot(w_send_t[...], grad_send_t) + dot(w_recv_t[...], recv[:, span])
    kept[...] = direct[:, span] + mine_of(terms, mine, chans)
    count = sent.shape[0] + 1
    for k in range(1, count):
        sent[k - 1] = mine_of(terms, lax.rem(mine + k, count), chans).astype(jnp.bfloat16)


def finish_kernel(count, *refs):
    kept, *others = refs[: count]
    *done, out = refs[count:]
    total = kept[...]
    for other in others:
        total += other[...].astype(jnp.float32)
    out[:, : kept.shape[1]] = total.astype(jnp.bfloat16)
    start = kept.shape[1]
    for part in done:
        out[:, start : start + part.shape[1]] = part[...]
        start += part.shape[1]


def sum_kernel(held, received, near, sent):
    half = near.shape[0]
    near[...] = held[:half] + received[:half].astype(jnp.float32)
    sent[...] = (held[half:] + received[half:].astype(jnp.float32)).astype(jnp.bfloat16)


def weight_kernel(held, received, out):
    out[...] = held[0] + received[0].astype(jnp.float32)


def shards(
    features,
    cotangent,
    senders,
    in_degree,
    tile_count,
    send_tiles,
    w_send,
    w_recv,
    bias_edge,
    w_msg,
    w_node_v,
    w_node_a,
    bias_node,
    w_out,
):
    chans, nodes = features.shape
    count = lax.axis_size("ch")
    lons = lax.axis_size("lon")
    hidden_all, chans_all = w_send.shape
    hid = hidden_all // count
    cycle = ("lon", "sub")
    shard_count = lax.axis_size(cycle)
    total_nodes = nodes * shard_count
    degree = senders.shape[0]
    slots = send_tiles.shape[1]
    slot_rows = send_tiles.shape[2] * TILE
    ext_len = nodes + slots * slot_rows
    bf16, f32 = jnp.bfloat16, jnp.float32
    shape = jax.ShapeDtypeStruct

    far_route = [(i, (i + (3 if i % 2 else -3)) % shard_count) for i in range(shard_count)]
    across_route = [(i, (i + (1 if i % 2 else -1)) % shard_count) for i in range(shard_count)]
    across = lambda block: lax.ppermute(block, cycle, across_route)
    degrees = in_degree[None, :]
    picks = jnp.transpose(send_tiles, (0, 2, 1))
    sub = lax.axis_index("sub")

    halves = 2
    rows = nodes // halves
    below_blocks = gathered(features[:, :rows], "ch")

    whole_w = pltpu.VMEM((chans_all, hidden_all), bf16)
    (
        w_send_my,
        w_recv_my,
        w_out_my,
        w_send_t,
        w_recv_t,
        w_both_t,
        w_node_v_t,
        w_both,
        w_out_t,
    ) = call(
        weights_kernel,
        (
            shape((hid, chans_all), bf16),
            shape((hid, chans_all), bf16),
            shape((chans, hidden_all), bf16),
            shape((chans_all, hid), bf16),
            shape((chans_all, hid), bf16),
            shape((hid, hidden_all), bf16),
            shape((chans, hidden_all), bf16),
            shape((hidden_all, hidden_all), bf16),
            shape((hidden_all, chans_all), bf16),
        ),
        [w_msg, w_node_a, w_send, w_recv, w_node_v, w_out],
        away=6,
        scalars=0,
        scratch=[whole_w] * 5 + [pltpu.SemaphoreType.DMA((6,))],
        limit=WEIGHTS_LIMIT,
    )
    block = shape((slot_rows + PACK, hid), bf16)
    w_send_my, above = lax.optimization_barrier((w_send_my, features[:, rows:]))
    above_blocks = gathered(above, "ch")
    feat_shape, proj_shape = shape((chans_all, rows), bf16), shape((rows, hid), bf16)
    feats_below, proj_below, lower = call(
        functools.partial(lower_kernel, count),
        (feat_shape, proj_shape, block),
        [picks] + below_blocks + [w_send_my],
        scalars=1,
    )
    east = shifted(lower, "lon", -1)
    proj_below, senders = lax.optimization_barrier((proj_below, senders))
    low_cols, high_cols, low_rows, high_rows = call(
        edges_kernel,
        (
            shape((degree, nodes, LANES), bf16),
            shape((degree, nodes, LANES), bf16),
            shape((degree, PACK, nodes), bf16),
            shape((degree, PACK, nodes), bf16),
        ),
        [tile_count, senders, degrees],
        scalars=1,
    )
    above_blocks[-1], low_cols = lax.optimization_barrier((above_blocks[-1], low_cols))
    feats_above, proj_above, upper, beside, cross = call(
        functools.partial(upper_kernel, count),
        (feat_shape, proj_shape, block, block, block),
        [tile_count, picks] + above_blocks + [w_send_my, proj_below, lower],
        scratch=[pltpu.VMEM((nodes, hid), bf16)],
    )
    west = shifted(upper, "lon", 1)
    cross = lax.ppermute(cross, cycle, far_route)
    base = call(
        receive_kernel,
        shape((nodes, hid), f32),
        [bias_edge[None, :], feats_below, feats_above, w_recv_my],
        scalars=0,
    )
    base, cotangent_late = lax.optimization_barrier((base, cotangent))
    beside = shifted(beside, "sub", 1)
    cot_blocks = gathered(cotangent_late, "ch")
    cots, pre, grad_hidden = call(
        functools.partial(prepare_kernel, count),
        (
            shape((chans_all, nodes), bf16),
            shape((hidden_all, nodes), f32),
            shape((hidden_all, nodes), f32),
        ),
        [tile_count] + cot_blocks + [feats_below, feats_above, w_node_v, bias_node[None, :], w_out_t],
        scalars=1,
    )

    part_shape = shape((degree, nodes, hid), bf16)
    def line(block, place, before, flops=1024):
        return call(
            functools.partial(line_kernel, place),
            part_shape,
            [low_cols, high_cols, block] + before,
            scratch=[pltpu.VMEM((slot_rows, hid), bf16)],
            scalars=0,
            flops=flops,
        )

    east_too = shifted(east, "sub", 1)
    part = line(east, 2, [], LINE_FLOPS)
    part, beside = lax.optimization_barrier((part, beside))
    part = call(
        near_kernel,
        part_shape,
        [low_cols, high_cols, part, proj_below, proj_above, beside],
        scratch=[pltpu.VMEM((nodes + slot_rows, hid), bf16)],
        scalars=0,
    )
    west, part = lax.optimization_barrier((west, part))
    west_too = shifted(west, "sub", 1)
    part, pre = lax.optimization_barrier((part, pre))
    part = line(west, 1, [part])
    part, cross = lax.optimization_barrier((part, cross))
    cross_rows = call(
        cross_rows_kernel, shape((slot_rows, hid), bf16), [cross], scalars=0
    )
    slopes, messages, hiddens, grad_pres, grads = [], [], [], [], []
    for k in range(halves):
        message, slope = call(
            functools.partial(message_kernel, k * rows),
            (shape((hid, rows), bf16), shape((degree, rows, hid), bf16)),
            [low_cols, high_cols, base, degrees, part, cross_rows, west_too, east_too],
            scratch=[pltpu.VMEM((3 * slot_rows, hid), bf16), pltpu.VMEM((rows, hid), f32)],
            scalars=0,
        )
        slopes.append(slope)
        messages.append(gathered(message, "ch"))

    block = shape((slot_rows, hid), bf16)
    sums = shape((len(EARLY) * slot_rows, hid), f32)
    grad_shape = shape((degree, rows, hid), bf16)
    for k in range(halves):
        hidden, grad_pre, scale = call(
            functools.partial(node_kernel, count, k * rows),
            (
                shape((hidden_all, rows), bf16),
                shape((hidden_all, rows), bf16),
                shape((rows, hid), f32),
            ),
            [degrees] + messages[k] + [w_both, w_both_t, pre, grad_hidden],
            scratch=[pltpu.VMEM((hidden_all, rows), bf16)],
            scalars=0,
        )
        hiddens.append(hidden)
        grad_pres.append(grad_pre)
        operands = [low_rows, high_rows, slopes[k], scale]
        if k == 0:
            grad, before = call(early_kernel, (grad_shape, sums), operands, scalars=0)
        else:
            to_cross, grad = call(
                functools.partial(cross_kernel, k * rows),
                (block, grad_shape),
                operands + [before, cross],
                scratch=[pltpu.VMEM((slot_rows, hid), f32)],
                scalars=0,
            )
            to_other = call(
                functools.partial(other_kernel, k * rows),
                shape((2, slot_rows, hid), bf16),
                [low_rows, high_rows, grad, before, west_too, east_too],
                scratch=[pltpu.VMEM((2 * slot_rows, hid), f32)],
                scalars=0,
            )
        grads.append(grad)

    grads[0], to_other = lax.optimization_barrier((grads[0], to_other))
    from_other = shifted(to_other, "sub", 1)
    from_cross = across(to_cross)
    to_west, to_east, to_beside = call(
        late_kernel,
        (block, block, block),
        [low_rows, high_rows] + grads + [west, east, beside],
        scratch=[pltpu.VMEM((len(LATE) * slot_rows, hid), f32)],
        scalars=0,
    )
    wide = shape((slot_rows, hid), f32)
    to_west, to_east = call(
        across_kernel, (wide, wide), [to_west, to_east, from_cross], scalars=0, flops=15 * 10**8
    )
    to_west, to_east = call(add_kernel, (block, block), [to_west, to_east, from_other], scalars=0)
    from_upper = shifted(to_west, "lon", -1)
    from_lower = shifted(to_east, "lon", 1)
    from_beside = shifted(to_beside, "sub", 1)
    to_west, grads[0] = lax.optimization_barrier((to_west, grads[0]))

    own, grad_recv = call(
        own_kernel,
        (shape((nodes, hid), f32), shape((hid, nodes), bf16)),
        [low_rows, high_rows] + grads,
        scalars=0,
    )
    own, hiddens[0] = lax.optimization_barrier((own, hiddens[0]))
    updated, direct = call(
        output_kernel,
        (shape((chans, nodes), bf16), shape((chans, nodes), f32)),
        [tile_count, features, cotangent, w_out_my, w_node_v_t] + hiddens + grad_pres,
        scalars=1,
    )
    columns = chans_all // shard_count
    inv_root = 1.0 / math.sqrt(total_nodes)
    feats_of = [feats_below, feats_above]
    weight_shape = shape((chans_all, hid), f32)
    grad_shape = shape((rows, hid), bf16)
    finals = []
    for k in reversed(range(halves)):
        kernel = functools.partial(back_kernel, k * rows, inv_root)
        inputs = [tile_count, feats_of[k], own, from_beside, from_upper]
        if k:
            grad_send, weight = call(
                kernel,
                (grad_shape, weight_shape),
                inputs,
                scratch=[pltpu.VMEM((nodes, hid), f32)],
                scalars=1,
            )
        else:
            grad_send, w_mine, w_beside = call(
                kernel,
                (
                    grad_shape,
                    shape((lons, columns, hid), f32),
                    shape((lons, columns, hid), bf16),
                ),
                inputs + [from_lower, weight],
                scratch=[pltpu.VMEM(weight_shape.shape, f32), pltpu.VMEM((nodes, hid), f32)],
                scalars=1,
            )
            w_beside = shifted(w_beside, "sub", 1)
            w_beside, *finals = lax.optimization_barrier((w_beside, *finals))
        kept, sent = call(
            functools.partial(terms_kernel, k * rows),
            (shape((chans, rows), f32), shape((count - 1, chans, rows), bf16)),
            [grad_send, grad_recv, direct, w_send_t, w_recv_t],
            scratch=[pltpu.VMEM((chans_all, rows), f32)],
            scalars=0,
        )
        if k:
            weight, kept = lax.optimization_barrier((weight, kept))
        parts = [kept] + [shifted(sent[i - 1], "ch", i) for i in range(1, count)]
        grad_features = call(
            functools.partial(finish_kernel, count),
            shape((chans, nodes - k * rows), bf16),
            parts + finals,
            scalars=0,
        )
        finals = [grad_features]

    span = lons
    while span > 1:
        span //= 2
        w_mine, w_sent = call(
            sum_kernel,
            (shape((span, columns, hid), f32), shape((span, columns, hid), bf16)),
            [w_mine, w_beside],
            scalars=0,
        )
        apart = lons // span // 2
        w_beside = lax.ppermute(w_sent, "lon", [(i, i ^ apart) for i in range(lons)])
    grad_w_send = call(
        weight_kernel, shape((columns, hid), f32), [w_mine, w_beside], scalars=0
    )
    return (updated, grad_features, grad_w_send.T)


def solution(mesh):
    nodes_last = P("ch", ("parts", "lon", "sub"))
    spread = ("parts", "lon", "sub")
    placed = (nodes_last, nodes_last, P(None, spread), P(spread), P(spread), P(spread, None, None))
    return jax.shard_map(
        shards,
        mesh=mesh,
        in_specs=placed + (P(),) * 8,
        out_specs=(nodes_last, nodes_last, P(("parts", "ch"), ("lon", "sub"))),
        check_vma=False,
    )
```

```python
import functools
import math

import jax
import jax.numpy as jnp
from jax import lax
from jax.experimental import pallas as pl
from jax.experimental.pallas import tpu as pltpu
from jax.sharding import PartitionSpec as P

TILE = 128
CHUNK = 256
LANES = 128
PACK = 16
MIB = 1 << 20
WEIGHTS_LIMIT = 52
WEIGHT_FLOPS = 3 * 10**9
CROSS_FLOPS = 2 * 10**9
NO_CHUNK = 64
SLOT_OF = ((3, 0), (1, 1), (4, 4), (2, 5), (0, 2), (5, 3))
EARLY, LATE = (3, 4, 5), (1, 2, 0)
OFF = -1e4


def shifted(block, axis, distance):
    size = lax.axis_size(axis)
    route = [((i - distance) % size, i) for i in range(size)]
    return lax.ppermute(block, axis, route)


def gathered(block, axis):
    return [block] + [shifted(block, axis, k) for k in range(1, lax.axis_size(axis))]


def dot(left, right):
    return jnp.dot(left, right, preferred_element_type=jnp.float32)


def dot_nt(left, right):
    return lax.dot_general(
        left, right, (((1,), (1,)), ((), ())), preferred_element_type=jnp.float32
    )


def sigmoid(value):
    return 0.5 * jnp.tanh(0.5 * value) + 0.5


def call(kernel, out_shape, operands, scratch=(), scalars=2, away=0, limit=24, flops=1024):
    vmem = pl.BlockSpec(memory_space=pltpu.VMEM)
    smem = pl.BlockSpec(memory_space=pltpu.SMEM)
    anywhere = pl.BlockSpec(memory_space=pltpu.HBM)
    return pl.pallas_call(
        kernel,
        out_shape=out_shape,
        in_specs=[smem] * scalars
        + [anywhere] * away
        + [vmem] * (len(operands) - scalars - away),
        out_specs=jax.tree.map(lambda _: vmem, out_shape),
        scratch_shapes=scratch,
        compiler_params=pltpu.CompilerParams(vmem_limit_bytes=limit * MIB),
        cost_estimate=pl.CostEstimate(flops=flops, bytes_accessed=1024, transcendentals=0),
    )(*operands)


def assemble(whole_ref, blocks, first):
    count = len(blocks)
    rows = blocks[0].shape[0]
    for k, block in enumerate(blocks):
        place = lax.rem(first - k + count, count) * rows
        whole_ref[pl.ds(pl.multiple_of(place, rows), rows), :] = block[...]


def mine_of(ref, index, rows):
    return ref[pl.ds(pl.multiple_of(index * rows, rows), rows), :]


def weights_kernel(*refs):
    sources, refs = refs[:7], refs[7:]
    w_send, w_recv, w_out, feats, w_send_t, w_recv_t, w_both_t, w_node_v_t, w_both, w_out_t = refs[:10]
    w_msg, w_node_v, w_node_a, w_out_all, turned, sems = refs[10:]
    mine = lax.axis_index("ch")
    hid = w_send.shape[0]
    targets = (w_msg, w_node_a, feats, w_send, w_recv, w_node_v, w_out_all)
    copies = []
    for k, (source, target) in enumerate(zip(sources, targets)):
        if k in (3, 4):
            source = source.at[pl.ds(pl.multiple_of(mine * hid, hid), hid), :]
        copies.append(pltpu.make_async_copy(source, target, sems.at[k]))
    for copy in copies:
        copy.start()
    for copy in copies[:2]:
        copy.wait()
    w_both[...] = dot(w_node_a[...], w_msg[...]).astype(jnp.bfloat16)
    turned[...] = w_both[...].T
    w_both_t[...] = mine_of(turned, mine, hid)
    for copy in copies[2:]:
        copy.wait()
    w_send_t[...] = w_send[...].T
    w_recv_t[...] = w_recv[...].T
    turned[...] = w_node_v[...].T
    w_node_v_t[...] = mine_of(turned, mine, w_node_v_t.shape[0])
    w_out_t[...] = w_out_all[...].T
    w_out[...] = mine_of(w_out_all, mine, w_out.shape[0])


def edges_kernel(tiles, senders, in_degree, low_cols, high_cols, low_rows, high_rows):
    degree, nodes = senders.shape
    lane = lax.broadcasted_iota(jnp.int32, (degree, nodes), 1)
    row = lax.broadcasted_iota(jnp.int32, (degree, nodes), 0)
    valid = (row < in_degree[...]) & (lane < tiles[0] * TILE)
    ids = senders[...]
    low = (ids & (CHUNK - 1)).astype(jnp.float32)
    high = jnp.where(valid, ids // CHUNK, NO_CHUNK).astype(jnp.float32)
    for m in range(degree):
        shape = (PACK, nodes)
        low_rows[m] = jnp.broadcast_to(low[m : m + 1], shape).astype(jnp.bfloat16)
        high_rows[m] = jnp.broadcast_to(high[m : m + 1], shape).astype(jnp.bfloat16)
    fill = jnp.zeros((PACK - degree, nodes), jnp.float32)
    depth = 2 * PACK
    both = jnp.concatenate([low, fill, high, fill], axis=0).T.astype(jnp.bfloat16)
    width = degree * LANES
    spot = lax.broadcasted_iota(jnp.int32, (depth, width), 0)
    group = lax.broadcasted_iota(jnp.int32, (depth, width), 1) // LANES
    for first, out in ((0, low_cols), (PACK, high_cols)):
        pick = (spot == group + first).astype(jnp.bfloat16)
        spread = dot(both, pick).astype(jnp.bfloat16)
        for m in range(degree):
            out[m] = spread[:, m * LANES : (m + 1) * LANES]


def project_kernel(count, tiles, picks, *refs):
    blocks = refs[:count]
    w_send, feats, proj, upper, lower, beside, cross = refs[count:]
    mine, sub = lax.axis_index("ch"), lax.axis_index("sub")
    first = tiles[0] // 2
    assemble(feats, blocks, mine)
    whole = feats[...]
    hid = proj.shape[1]
    proj[...] = (0.5 * dot(w_send[...], whole).T).astype(jnp.bfloat16)
    rows = upper.shape[0] - PACK
    upper[:rows, :] = proj[pl.ds(pl.multiple_of(first * TILE, TILE), rows), :]
    lower[:rows, :] = proj[:rows, :]
    spot = lax.broadcasted_iota(jnp.int32, (PACK, hid), 0)
    _, per_slot, slots = picks.shape
    half = slots // 2
    for start, out, lift in ((0, upper, first), (half, lower, 0)):
        marks = jnp.zeros((PACK, hid), jnp.float32)
        for k in range(half * per_slot):
            rel = picks[0, k % per_slot, start + k // per_slot] - lift
            marks = jnp.where(spot == k, rel.astype(jnp.float32), marks)
        out[rows:, :] = marks.astype(jnp.bfloat16)

    @pl.when(sub == 0)
    def _():
        beside[...] = upper[...]
        cross[...] = lower[...]

    @pl.when(sub != 0)
    def _():
        beside[...] = lower[...]
        cross[...] = upper[...]


def receive_kernel(bias, feats, w_recv, base):
    hid = base.shape[1]
    mine = lax.axis_index("ch")
    my_bias = jnp.zeros((1, hid), jnp.float32)
    for k in range(bias.shape[1] // hid):
        my_bias += jnp.where(mine == k, bias[:, k * hid : (k + 1) * hid], 0.0)
    recv = dot(w_recv[...], feats[...]).T
    base[...] = 0.5 * (recv.astype(jnp.bfloat16).astype(jnp.float32) + my_bias)


def prepare_kernel(count, tiles, *refs):
    blocks = refs[:count]
    feats, w_node_v, bias, w_out_t, cots, pre, grad_hidden = refs[count:]
    assemble(cots, blocks, lax.axis_index("ch"))
    column = jnp.broadcast_to(bias[...], (8, bias.shape[1])).T[:, :1]
    pre[...] = dot(w_node_v[...], feats[...]) + column
    lane = lax.broadcasted_iota(jnp.int32, (1, cots.shape[1]), 1)
    active = (lane < tiles[0] * TILE).astype(jnp.bfloat16)
    grad_hidden[...] = dot(w_out_t[...], cots[...] * active)


def chunk_of(place, first, shape):
    on_zero, on_one = (float(first + slot) for slot in SLOT_OF[place])
    chunk = jnp.where(lax.axis_index("sub") == 0, on_zero, on_one)
    return jnp.full(shape, chunk, jnp.float32).astype(jnp.bfloat16)


def picks_of(block, place):
    marks = block[CHUNK : CHUNK + PACK, :].astype(jnp.float32)
    per_slot = CHUNK // TILE
    half = len(SLOT_OF) // 2
    starts = [slot % half * per_slot for slot in SLOT_OF[place]]
    sub = lax.axis_index("sub")
    return [
        jnp.where(
            sub == 0,
            marks[starts[0] + t : starts[0] + t + 1],
            marks[starts[1] + t : starts[1] + t + 1],
        )
        for t in range(per_slot)
    ]


def fill(ext, start, block, place):
    for t, pick in enumerate(picks_of(block, place)):
        ext[start + t * TILE : start + (t + 1) * TILE, :] = jnp.where(
            pick > 0.5, block[TILE : 2 * TILE, :], block[:TILE, :]
        )


def pick_rows(low, high, chunks, ext):
    one = jnp.bfloat16(1.0)
    zero = jnp.bfloat16(0.0)
    lane = lax.broadcasted_iota(jnp.int32, low.shape, 1)
    marks = [
        jnp.where(low == (lane + half * LANES).astype(jnp.bfloat16), one, zero)
        for half in range(CHUNK // LANES)
    ]
    picker = jnp.concatenate(
        [jnp.where(high == chunk, mark, zero) for chunk in chunks for mark in marks], axis=1
    )
    return dot(picker, ext[...])


def near_kernel(low, high, proj, beside, part, ext):
    own = proj.shape[0]
    ext[:own, :] = proj[...]
    fill(ext, own, beside, 0)
    first = own // CHUNK
    chunks = [jnp.bfloat16(chunk) for chunk in range(first)]
    chunks.append(chunk_of(0, first, low.shape[1:]))

    def step(m, carry):
        part[m] = pick_rows(low[m], high[m], chunks, ext).astype(jnp.bfloat16)
        return carry

    lax.fori_loop(0, low.shape[0], step, 0, unroll=True)


def line_kernel(low, high, before, west, east, part, ext):
    first = low.shape[1] // CHUNK
    chunks = []
    for index, (place, block) in enumerate(((1, west), (2, east))):
        fill(ext, index * CHUNK, block, place)
        chunks.append(jnp.bfloat16(first + SLOT_OF[place][0]))

    def step(m, carry):
        more = pick_rows(low[m], high[m], chunks, ext)
        part[m] = (before[m].astype(jnp.float32) + more).astype(jnp.bfloat16)
        return carry

    lax.fori_loop(0, low.shape[0], step, 0, unroll=True)


def cross_rows_kernel(block, rows):
    fill(rows, 0, block, 3)


def message_kernel(
    start, low, high, base, in_degree, part, cross, west, east, message, slope, ext, total
):
    nodes = low.shape[1]
    degree, rows, hid = slope.shape
    first = nodes // CHUNK
    together = nodes // rows
    span = slice(start, start + rows)
    chunks = []
    ext[:CHUNK, :] = cross[...]
    for index, (place, block) in enumerate(((4, west), (5, east))):
        fill(ext, (index + 1) * CHUNK, block, place)
    for place in (3, 4, 5):
        chunks.append(chunk_of(place, first, (nodes, LANES)))
    total[...] = jnp.zeros_like(total)

    def rows_of(ref, k):
        return jnp.concatenate([ref[k * together + i, span, :] for i in range(together)], axis=0)

    def step(k, carry):
        low_k, high_k = rows_of(low, k), rows_of(high, k)
        half = pick_rows(low_k, high_k, chunks, ext) + rows_of(part, k).astype(jnp.float32)
        half += jnp.concatenate([base[span, :]] * together, axis=0)
        wide = jnp.concatenate([high_k] * pl.cdiv(hid, LANES), axis=1)[:, :hid]
        half = jnp.where(wide.astype(jnp.float32) < NO_CHUNK, half, OFF)
        twice = jnp.tanh(half) + 1.0
        act = half * twice
        grad = (twice + act * (2.0 - twice)).astype(jnp.bfloat16)
        terms = 0.0
        for i in range(together):
            terms += act[i * rows : (i + 1) * rows]
            slope[k * together + i] = grad[i * rows : (i + 1) * rows]
        total[...] += terms
        return carry

    lax.fori_loop(0, degree // together, step, 0, unroll=True)
    count = in_degree[:, span].astype(jnp.float32)
    message[...] = (total[...].T / count).astype(jnp.bfloat16)


def node_kernel(count, start, in_degree, *refs):
    blocks = refs[:count]
    w_both, w_both_t, pre, grad_hidden = refs[count : count + 4]
    hidden, grad_pre, scale, messages = refs[count + 4 :]
    assemble(messages, blocks, lax.axis_index("ch"))
    span = slice(start, start + hidden.shape[1])
    half = 0.5 * (pre[:, span] + dot(w_both[...], messages[...]))
    twice = jnp.tanh(half) + 1.0
    act = half * twice
    hidden[...] = act.astype(jnp.bfloat16)
    slope = 0.5 * (twice + act * (2.0 - twice))
    low_grad = (grad_hidden[:, span] * slope).astype(jnp.bfloat16)
    grad_pre[...] = low_grad
    grad_msg = dot(w_both_t[...], low_grad).astype(jnp.bfloat16).astype(jnp.float32)
    scale[...] = (grad_msg * (0.5 / in_degree[:, span].astype(jnp.float32))).T


def scatter(low, high, edges, chunks, total):
    one = jnp.bfloat16(1.0)
    zero = jnp.bfloat16(0.0)
    groups = CHUNK // PACK
    for step in edges:
        width = sum(rows for _, _, rows, _ in step)
        place = lax.broadcasted_iota(jnp.int32, (groups, PACK, width), 0) * PACK
        place = place + lax.broadcasted_iota(jnp.int32, (groups, PACK, width), 1)
        low_k = jnp.concatenate([low[m, :, s : s + r] for m, s, r, _ in step], axis=1)
        high_k = jnp.concatenate([high[m, :, s : s + r] for m, s, r, _ in step], axis=1)
        grads = jnp.concatenate([grad() for _, _, _, grad in step], axis=0)
        mark = jnp.where(low_k[None] == place.astype(jnp.bfloat16), one, zero)
        picker = jnp.concatenate(
            [jnp.where(high_k[None] == chunk, mark, zero) for chunk in chunks], axis=0
        ).reshape(len(chunks) * CHUNK, width)
        total[...] += dot(picker, grads)


def pairs(start, ref, nodes, grad_of):
    degree, rows, _ = ref.shape
    together = nodes // rows
    return [
        [
            (m, start, rows, functools.partial(grad_of, ref, m))
            for m in range(k * together, (k + 1) * together)
        ]
        for k in range(degree // together)
    ]


def fold(block, place, index, total):
    picks = picks_of(block, place)
    halves = []
    for half in range(len(picks)):
        terms = 0.0
        for t, pick in enumerate(picks):
            start = index * CHUNK + t * TILE
            hit = jnp.abs(pick - half) < 0.5
            terms += jnp.where(hit, total[start : start + TILE, :], 0.0)
        halves.append(terms)
    return jnp.concatenate(halves, axis=0).astype(jnp.bfloat16)


def early_kernel(low, high, slope, scale, grads, total):
    nodes = low.shape[2]

    def grad_of(ref, m):
        grads[m] = (ref[m].astype(jnp.float32) * scale[...]).astype(jnp.bfloat16)
        return grads[m]

    chunks = [chunk_of(place, nodes // CHUNK, (1, PACK, nodes)) for place in EARLY]
    total[...] = jnp.zeros_like(total)
    scatter(low, high, pairs(0, slope, nodes, grad_of), chunks, total)


def cross_kernel(start, low, high, slope, scale, before, cross, to_cross, grads, total):
    nodes = low.shape[2]

    def grad_of(ref, m):
        grads[m] = (ref[m].astype(jnp.float32) * scale[...]).astype(jnp.bfloat16)
        return grads[m]

    chunks = [chunk_of(EARLY[0], nodes // CHUNK, (1, PACK, nodes))]
    total[...] = before[:CHUNK, :]
    scatter(low, high, pairs(start, slope, nodes, grad_of), chunks, total)
    to_cross[...] = fold(cross, EARLY[0], 0, total)


def other_kernel(start, low, high, grads, before, west, east, to_other, total):
    nodes = low.shape[2]
    chunks = [chunk_of(place, nodes // CHUNK, (1, PACK, nodes)) for place in EARLY[1:]]
    total[...] = before[CHUNK:, :]
    scatter(low, high, pairs(start, grads, nodes, lambda ref, m: ref[m]), chunks, total)
    to_other[0] = fold(west, EARLY[1], 0, total)
    to_other[1] = fold(east, EARLY[2], 1, total)


def all_pairs(parts, nodes):
    start, steps = 0, []
    for part in parts:
        steps += pairs(start, part, nodes, lambda ref, m: ref[m])
        start += part.shape[1]
    return steps


def late_kernel(low, high, *refs):
    *parts, west, east, beside, to_west, to_east, to_beside, total = refs
    nodes = low.shape[2]
    first = nodes // CHUNK
    chunks = [chunk_of(place, first, (1, PACK, nodes)) for place in LATE]
    total[...] = jnp.zeros_like(total)
    scatter(low, high, all_pairs(parts, nodes), chunks, total)
    to_west[...] = fold(west, 1, 0, total)
    to_east[...] = fold(east, 2, 1, total)
    to_beside[...] = fold(beside, 0, 2, total)


def own_kernel(low, high, *refs):
    *parts, total, recv = refs
    nodes = low.shape[2]
    chunks = [jnp.bfloat16(chunk) for chunk in range(nodes // CHUNK)]
    total[...] = jnp.zeros_like(total)
    scatter(low, high, all_pairs(parts, nodes), chunks, total)
    start = 0
    for part in parts:
        degree, rows, _ = part.shape
        terms = 0.0
        for m in range(degree):
            terms += part[m].astype(jnp.float32)
        recv[:, start : start + rows] = terms.T.astype(jnp.bfloat16)
        start += rows


def output_kernel(tiles, feats, cots, w_out, w_node_v_t, *refs):
    *parts, updated, direct = refs
    count = len(parts) // 2
    rows = parts[0].shape[1]
    for k in range(count):
        hidden, grad_pre = parts[k], parts[count + k]
        span = slice(k * rows, (k + 1) * rows)
        lane = lax.broadcasted_iota(jnp.int32, (1, rows), 1) + k * rows
        active = (lane < tiles[0] * TILE).astype(jnp.float32)
        node_out = dot(w_out[...], hidden[...])
        new = feats[:, span].astype(jnp.float32) + active * node_out
        updated[:, span] = new.astype(jnp.bfloat16)
        direct[:, span] = cots[:, span].astype(jnp.float32) + dot(w_node_v_t[...], grad_pre[...])


def across_kernel(left, right, across, west, east):
    sub = lax.axis_index("sub")
    other = across[...].astype(jnp.float32)
    to_west = left[...].astype(jnp.float32) + jnp.where(sub == 0, 0.0, other)
    to_east = right[...].astype(jnp.float32) + jnp.where(sub == 0, other, 0.0)
    west[...] = to_west.astype(west.dtype)
    east[...] = to_east.astype(east.dtype)


def add_kernel(left, right, more, west, east):
    west[...] = (left[...] + more[0].astype(jnp.float32)).astype(jnp.bfloat16)
    east[...] = (right[...] + more[1].astype(jnp.float32)).astype(jnp.bfloat16)


def band_bits(place, lons):
    bits, weight = 0, 1
    while weight < lons:
        bits += weight if place * weight * 2 // lons % 2 else 0
        weight *= 2
    return bits


def back_kernel(start, inv_root, tiles, own, beside, feats, upper, *refs):
    *refs, total = refs
    sub = lax.axis_index("sub")
    offset = pl.multiple_of(tiles[0] // 2 * TILE, TILE)
    total[...] = own[...]
    near = beside[...].astype(jnp.float32)
    block = upper[...].astype(jnp.float32) + jnp.where(sub == 0, near, 0.0)
    total[pl.ds(offset, block.shape[0]), :] += block
    if start:
        grad_send, weight = refs
    else:
        lower, before, grad_send, w_mine, w_beside, weight = refs
        block = lower[...].astype(jnp.float32) + jnp.where(sub == 0, 0.0, near)
        total[: block.shape[0], :] += block
    rows = grad_send.shape[0]
    grad_send[...] = total[start : start + rows, :].astype(jnp.bfloat16)
    terms = dot(feats[:, start : start + rows], grad_send[...])
    if start:
        weight[...] = terms
        return
    weight[...] = (before[...] + terms) * inv_root
    lon = lax.axis_index("lon")
    lons, columns, _ = w_mine.shape
    for k in range(lons):
        band = (lon ^ band_bits(k, lons)) * 2
        for out, core in ((w_mine, sub), (w_beside, 1 - sub)):
            spot = pl.multiple_of((band + core) * columns, columns)
            out[k] = weight[pl.ds(spot, columns), :].astype(out.dtype)


def terms_kernel(start, grad_send, recv, direct, w_send_t, w_recv_t, kept, sent, terms):
    span = slice(start, start + grad_send.shape[0])
    mine = lax.axis_index("ch")
    chans = kept.shape[0]
    grad_send_t = grad_send[...].astype(jnp.float32).T.astype(jnp.bfloat16)
    terms[...] = dot(w_send_t[...], grad_send_t) + dot(w_recv_t[...], recv[:, span])
    kept[...] = direct[:, span] + mine_of(terms, mine, chans)
    count = sent.shape[0] + 1
    for k in range(1, count):
        sent[k - 1] = mine_of(terms, lax.rem(mine + k, count), chans).astype(jnp.bfloat16)


def finish_kernel(count, *refs):
    kept, *others = refs[: count]
    *done, out = refs[count:]
    total = kept[...]
    for other in others:
        total += other[...].astype(jnp.float32)
    out[:, : kept.shape[1]] = total.astype(jnp.bfloat16)
    start = kept.shape[1]
    for part in done:
        out[:, start : start + part.shape[1]] = part[...]
        start += part.shape[1]


def sum_kernel(held, received, near, sent):
    half = near.shape[0]
    near[...] = held[:half] + received[:half].astype(jnp.float32)
    sent[...] = (held[half:] + received[half:].astype(jnp.float32)).astype(jnp.bfloat16)


def weight_kernel(held, received, out):
    out[...] = held[0] + received[0].astype(jnp.float32)


def shards(
    features,
    cotangent,
    senders,
    in_degree,
    tile_count,
    send_tiles,
    w_send,
    w_recv,
    bias_edge,
    w_msg,
    w_node_v,
    w_node_a,
    bias_node,
    w_out,
):
    chans, nodes = features.shape
    count = lax.axis_size("ch")
    lons = lax.axis_size("lon")
    hidden_all, chans_all = w_send.shape
    hid = hidden_all // count
    cycle = ("lon", "sub")
    shard_count = lax.axis_size(cycle)
    total_nodes = nodes * shard_count
    degree = senders.shape[0]
    slots = send_tiles.shape[1]
    slot_rows = send_tiles.shape[2] * TILE
    ext_len = nodes + slots * slot_rows
    bf16, f32 = jnp.bfloat16, jnp.float32
    shape = jax.ShapeDtypeStruct

    far_route = [(i, (i + (3 if i % 2 else -3)) % shard_count) for i in range(shard_count)]
    across_route = [(i, (i + (1 if i % 2 else -1)) % shard_count) for i in range(shard_count)]
    across = lambda block: lax.ppermute(block, cycle, across_route)
    degrees = in_degree[None, :]
    picks = jnp.transpose(send_tiles, (0, 2, 1))
    sub = lax.axis_index("sub")

    feat_blocks = gathered(features, "ch")

    whole_w = pltpu.VMEM((chans_all, hidden_all), bf16)
    (
        w_send_my,
        w_recv_my,
        w_out_my,
        features_held,
        w_send_t,
        w_recv_t,
        w_both_t,
        w_node_v_t,
        w_both,
        w_out_t,
    ) = call(
        weights_kernel,
        (
            shape((hid, chans_all), bf16),
            shape((hid, chans_all), bf16),
            shape((chans, hidden_all), bf16),
            shape((chans, nodes), bf16),
            shape((chans_all, hid), bf16),
            shape((chans_all, hid), bf16),
            shape((hid, hidden_all), bf16),
            shape((chans, hidden_all), bf16),
            shape((hidden_all, hidden_all), bf16),
            shape((hidden_all, chans_all), bf16),
        ),
        [w_msg, w_node_a, features, w_send, w_recv, w_node_v, w_out],
        away=7,
        scalars=0,
        scratch=[whole_w] * 5 + [pltpu.SemaphoreType.DMA((7,))],
        limit=WEIGHTS_LIMIT,
    )
    feat_blocks[0] = features_held

    block = shape((slot_rows + PACK, hid), bf16)
    feats, proj, upper, lower, beside, cross = call(
        functools.partial(project_kernel, count),
        (
            shape((chans_all, nodes), bf16),
            shape((nodes, hid), bf16),
            block,
            block,
            block,
            block,
        ),
        [tile_count, picks] + feat_blocks + [w_send_my],
    )
    west = shifted(upper, "lon", 1)
    east = shifted(lower, "lon", -1)
    cross = lax.ppermute(cross, cycle, far_route)
    base = call(
        receive_kernel,
        shape((nodes, hid), f32),
        [bias_edge[None, :], feats, w_recv_my],
        scalars=0,
    )
    base, senders = lax.optimization_barrier((base, senders))
    beside = shifted(beside, "sub", 1)
    low_cols, high_cols, low_rows, high_rows = call(
        edges_kernel,
        (
            shape((degree, nodes, LANES), bf16),
            shape((degree, nodes, LANES), bf16),
            shape((degree, PACK, nodes), bf16),
            shape((degree, PACK, nodes), bf16),
        ),
        [tile_count, senders, degrees],
        scalars=1,
    )
    part_shape = shape((degree, nodes, hid), bf16)
    part = call(
        near_kernel,
        part_shape,
        [low_cols, high_cols, proj, beside],
        scratch=[pltpu.VMEM((nodes + slot_rows, hid), bf16)],
        scalars=0,
    )
    west, east, part = lax.optimization_barrier((west, east, part))
    west_too = shifted(west, "sub", 1)
    east_too = shifted(east, "sub", 1)
    west, cotangent_late = lax.optimization_barrier((west, cotangent))
    cot_blocks = gathered(cotangent_late, "ch")
    part = call(
        line_kernel,
        part_shape,
        [low_cols, high_cols, part, west, east],
        scratch=[pltpu.VMEM((2 * slot_rows, hid), bf16)],
        scalars=0,
    )
    part, cross = lax.optimization_barrier((part, cross))
    cross_rows = call(
        cross_rows_kernel, shape((slot_rows, hid), bf16), [cross], scalars=0, flops=CROSS_FLOPS
    )
    halves = 2
    rows = nodes // halves
    slopes, messages, hiddens, grad_pres, grads = [], [], [], [], []
    for k in range(halves):
        message, slope = call(
            functools.partial(message_kernel, k * rows),
            (shape((hid, rows), bf16), shape((degree, rows, hid), bf16)),
            [low_cols, high_cols, base, degrees, part, cross_rows, west_too, east_too],
            scratch=[pltpu.VMEM((3 * slot_rows, hid), bf16), pltpu.VMEM((rows, hid), f32)],
            scalars=0,
        )
        if k == halves - 1:
            message, cot_blocks[-1] = lax.optimization_barrier((message, cot_blocks[-1]))
        slopes.append(slope)
        messages.append(gathered(message, "ch"))

    cots, pre, grad_hidden = call(
        functools.partial(prepare_kernel, count),
        (
            shape((chans_all, nodes), bf16),
            shape((hidden_all, nodes), f32),
            shape((hidden_all, nodes), f32),
        ),
        [tile_count] + cot_blocks + [feats, w_node_v, bias_node[None, :], w_out_t],
        scalars=1,
    )

    block = shape((slot_rows, hid), bf16)
    sums = shape((len(EARLY) * slot_rows, hid), f32)
    grad_shape = shape((degree, rows, hid), bf16)
    for k in range(halves):
        hidden, grad_pre, scale = call(
            functools.partial(node_kernel, count, k * rows),
            (
                shape((hidden_all, rows), bf16),
                shape((hidden_all, rows), bf16),
                shape((rows, hid), f32),
            ),
            [degrees] + messages[k] + [w_both, w_both_t, pre, grad_hidden],
            scratch=[pltpu.VMEM((hidden_all, rows), bf16)],
            scalars=0,
        )
        hiddens.append(hidden)
        grad_pres.append(grad_pre)
        operands = [low_rows, high_rows, slopes[k], scale]
        if k == 0:
            grad, before = call(early_kernel, (grad_shape, sums), operands, scalars=0)
        else:
            to_cross, grad = call(
                functools.partial(cross_kernel, k * rows),
                (block, grad_shape),
                operands + [before, cross],
                scratch=[pltpu.VMEM((slot_rows, hid), f32)],
                scalars=0,
            )
            to_other = call(
                functools.partial(other_kernel, k * rows),
                shape((2, slot_rows, hid), bf16),
                [low_rows, high_rows, grad, before, west_too, east_too],
                scratch=[pltpu.VMEM((2 * slot_rows, hid), f32)],
                scalars=0,
            )
        grads.append(grad)

    grads[0], to_other = lax.optimization_barrier((grads[0], to_other))
    from_other = shifted(to_other, "sub", 1)
    from_cross = across(to_cross)
    to_west, to_east, to_beside = call(
        late_kernel,
        (block, block, block),
        [low_rows, high_rows] + grads + [west, east, beside],
        scratch=[pltpu.VMEM((len(LATE) * slot_rows, hid), f32)],
        scalars=0,
    )
    wide = shape((slot_rows, hid), f32)
    to_west, to_east = call(
        across_kernel, (wide, wide), [to_west, to_east, from_cross], scalars=0, flops=15 * 10**8
    )
    to_west, to_east = call(add_kernel, (block, block), [to_west, to_east, from_other], scalars=0)
    from_upper = shifted(to_west, "lon", -1)
    from_lower = shifted(to_east, "lon", 1)
    from_beside = shifted(to_beside, "sub", 1)
    to_west, grads[0] = lax.optimization_barrier((to_west, grads[0]))

    own, grad_recv = call(
        own_kernel,
        (shape((nodes, hid), f32), shape((hid, nodes), bf16)),
        [low_rows, high_rows] + grads,
        scalars=0,
    )
    own, hiddens[0] = lax.optimization_barrier((own, hiddens[0]))
    updated, direct = call(
        output_kernel,
        (shape((chans, nodes), bf16), shape((chans, nodes), f32)),
        [tile_count, features_held, cotangent, w_out_my, w_node_v_t] + hiddens + grad_pres,
        scalars=1,
    )
    columns = chans_all // shard_count
    inv_root = 1.0 / math.sqrt(total_nodes)
    inputs = [tile_count, own, from_beside, feats, from_upper]
    weight_shape = shape((chans_all, hid), f32)
    grad_shape = shape((rows, hid), bf16)
    def finish(k, grad_send, done):
        kept, sent = call(
            functools.partial(terms_kernel, k * rows),
            (shape((chans, rows), f32), shape((count - 1, chans, rows), bf16)),
            [grad_send, grad_recv, direct, w_send_t, w_recv_t],
            scratch=[pltpu.VMEM((chans_all, rows), f32)],
            scalars=0,
        )
        parts = [kept] + [shifted(sent[i - 1], "ch", i) for i in range(1, count)]
        out = call(
            functools.partial(finish_kernel, count),
            shape((chans, nodes - k * rows), bf16),
            parts + done,
            scalars=0,
        )
        return kept, out

    grad_send, weight = call(
        functools.partial(back_kernel, rows, inv_root),
        (grad_shape, weight_shape),
        inputs,
        scratch=[pltpu.VMEM((nodes, hid), f32)],
        scalars=1,
    )
    kept, upper_out = finish(1, grad_send, [])
    weight, kept = lax.optimization_barrier((weight, kept))
    grad_send, w_mine, w_beside = call(
        functools.partial(back_kernel, 0, inv_root),
        (grad_shape, shape((lons, columns, hid), f32), shape((lons, columns, hid), bf16)),
        inputs + [from_lower, weight],
        scratch=[pltpu.VMEM(weight_shape.shape, f32), pltpu.VMEM((nodes, hid), f32)],
        scalars=1,
    )
    w_beside = shifted(w_beside, "sub", 1)
    w_beside, upper_out = lax.optimization_barrier((w_beside, upper_out))
    span = lons
    while span > 1:
        span //= 2
        w_mine, w_sent = call(
            sum_kernel,
            (shape((span, columns, hid), f32), shape((span, columns, hid), bf16)),
            [w_mine, w_beside],
            scalars=0,
        )
        if span == 1:
            w_sent, grad_send = lax.optimization_barrier((w_sent, grad_send))
        apart = lons // span // 2
        w_beside = lax.ppermute(w_sent, "lon", [(i, i ^ apart) for i in range(lons)])
    grad_w_send = call(
        weight_kernel, shape((columns, hid), f32), [w_mine, w_beside], scalars=0, flops=WEIGHT_FLOPS
    )
    _, grad_features = finish(0, grad_send, [upper_out])
    return (updated, grad_features, grad_w_send.T)


def solution(mesh):
    nodes_last = P("ch", ("parts", "lon", "sub"))
    spread = ("parts", "lon", "sub")
    placed = (nodes_last, nodes_last, P(None, spread), P(spread), P(spread), P(spread, None, None))
    return jax.shard_map(
        shards,
        mesh=mesh,
        in_specs=placed + (P(),) * 8,
        out_specs=(nodes_last, nodes_last, P(("parts", "ch"), ("lon", "sub"))),
        check_vma=False,
    )
```

```python
import functools
import math

import jax
import jax.numpy as jnp
from jax import lax
from jax.experimental import pallas as pl
from jax.experimental.pallas import tpu as pltpu
from jax.sharding import PartitionSpec as P

TILE = 128
CHUNK = 256
LANES = 128
PACK = 16
MIB = 1 << 20
WEIGHTS_LIMIT = 52
NO_CHUNK = 64
SLOT_OF = ((3, 0), (1, 1), (4, 4), (2, 5), (0, 2), (5, 3))
EARLY, LATE = (3, 4, 5), (1, 2, 0)
OFF = -1e4


def shifted(block, axis, distance):
    size = lax.axis_size(axis)
    route = [((i - distance) % size, i) for i in range(size)]
    return lax.ppermute(block, axis, route)


def gathered(block, axis):
    return [block] + [shifted(block, axis, k) for k in range(1, lax.axis_size(axis))]


def dot(left, right):
    return jnp.dot(left, right, preferred_element_type=jnp.float32)


def dot_nt(left, right):
    return lax.dot_general(
        left, right, (((1,), (1,)), ((), ())), preferred_element_type=jnp.float32
    )


def sigmoid(value):
    return 0.5 * jnp.tanh(0.5 * value) + 0.5


def call(kernel, out_shape, operands, scratch=(), scalars=2, away=0, limit=24, flops=1024):
    vmem = pl.BlockSpec(memory_space=pltpu.VMEM)
    smem = pl.BlockSpec(memory_space=pltpu.SMEM)
    anywhere = pl.BlockSpec(memory_space=pltpu.HBM)
    return pl.pallas_call(
        kernel,
        out_shape=out_shape,
        in_specs=[smem] * scalars
        + [anywhere] * away
        + [vmem] * (len(operands) - scalars - away),
        out_specs=jax.tree.map(lambda _: vmem, out_shape),
        scratch_shapes=scratch,
        compiler_params=pltpu.CompilerParams(vmem_limit_bytes=limit * MIB),
        cost_estimate=pl.CostEstimate(flops=flops, bytes_accessed=1024, transcendentals=0),
    )(*operands)


def assemble(whole_ref, blocks, first):
    count = len(blocks)
    rows = blocks[0].shape[0]
    for k, block in enumerate(blocks):
        place = lax.rem(first - k + count, count) * rows
        whole_ref[pl.ds(pl.multiple_of(place, rows), rows), :] = block[...]


def mine_of(ref, index, rows):
    return ref[pl.ds(pl.multiple_of(index * rows, rows), rows), :]


def weights_kernel(*refs):
    sources, refs = refs[:7], refs[7:]
    w_send, w_recv, w_out, feats, w_send_t, w_recv_t, w_both_t, w_node_v_t, w_both, w_out_t = refs[:10]
    w_msg, w_node_v, w_node_a, w_out_all, turned, sems = refs[10:]
    mine = lax.axis_index("ch")
    hid = w_send.shape[0]
    targets = (w_msg, w_node_a, feats, w_send, w_recv, w_node_v, w_out_all)
    copies = []
    for k, (source, target) in enumerate(zip(sources, targets)):
        if k in (3, 4):
            source = source.at[pl.ds(pl.multiple_of(mine * hid, hid), hid), :]
        copies.append(pltpu.make_async_copy(source, target, sems.at[k]))
    for copy in copies:
        copy.start()
    for copy in copies[:2]:
        copy.wait()
    w_both[...] = dot(w_node_a[...], w_msg[...]).astype(jnp.bfloat16)
    turned[...] = w_both[...].T
    w_both_t[...] = mine_of(turned, mine, hid)
    for copy in copies[2:]:
        copy.wait()
    w_send_t[...] = w_send[...].T
    w_recv_t[...] = w_recv[...].T
    turned[...] = w_node_v[...].T
    w_node_v_t[...] = mine_of(turned, mine, w_node_v_t.shape[0])
    w_out_t[...] = w_out_all[...].T
    w_out[...] = mine_of(w_out_all, mine, w_out.shape[0])


def edges_kernel(tiles, senders, in_degree, low_cols, high_cols, low_rows, high_rows):
    degree, nodes = senders.shape
    lane = lax.broadcasted_iota(jnp.int32, (degree, nodes), 1)
    row = lax.broadcasted_iota(jnp.int32, (degree, nodes), 0)
    valid = (row < in_degree[...]) & (lane < tiles[0] * TILE)
    ids = senders[...]
    low = (ids & (CHUNK - 1)).astype(jnp.float32)
    high = jnp.where(valid, ids // CHUNK, NO_CHUNK).astype(jnp.float32)
    for m in range(degree):
        shape = (PACK, nodes)
        low_rows[m] = jnp.broadcast_to(low[m : m + 1], shape).astype(jnp.bfloat16)
        high_rows[m] = jnp.broadcast_to(high[m : m + 1], shape).astype(jnp.bfloat16)
    fill = jnp.zeros((PACK - degree, nodes), jnp.float32)
    depth = 2 * PACK
    both = jnp.concatenate([low, fill, high, fill], axis=0).T.astype(jnp.bfloat16)
    width = degree * LANES
    spot = lax.broadcasted_iota(jnp.int32, (depth, width), 0)
    group = lax.broadcasted_iota(jnp.int32, (depth, width), 1) // LANES
    for first, out in ((0, low_cols), (PACK, high_cols)):
        pick = (spot == group + first).astype(jnp.bfloat16)
        spread = dot(both, pick).astype(jnp.bfloat16)
        for m in range(degree):
            out[m] = spread[:, m * LANES : (m + 1) * LANES]


def project_kernel(count, tiles, picks, *refs):
    blocks = refs[:count]
    w_send, feats, proj, upper, lower, beside, cross = refs[count:]
    mine, sub = lax.axis_index("ch"), lax.axis_index("sub")
    first = tiles[0] // 2
    assemble(feats, blocks, mine)
    whole = feats[...]
    hid = proj.shape[1]
    proj[...] = (0.5 * dot(w_send[...], whole).T).astype(jnp.bfloat16)
    rows = upper.shape[0] - PACK
    upper[:rows, :] = proj[pl.ds(pl.multiple_of(first * TILE, TILE), rows), :]
    lower[:rows, :] = proj[:rows, :]
    spot = lax.broadcasted_iota(jnp.int32, (PACK, hid), 0)
    _, per_slot, slots = picks.shape
    half = slots // 2
    for start, out, lift in ((0, upper, first), (half, lower, 0)):
        marks = jnp.zeros((PACK, hid), jnp.float32)
        for k in range(half * per_slot):
            rel = picks[0, k % per_slot, start + k // per_slot] - lift
            marks = jnp.where(spot == k, rel.astype(jnp.float32), marks)
        out[rows:, :] = marks.astype(jnp.bfloat16)

    @pl.when(sub == 0)
    def _():
        beside[...] = upper[...]
        cross[...] = lower[...]

    @pl.when(sub != 0)
    def _():
        beside[...] = lower[...]
        cross[...] = upper[...]


def receive_kernel(bias, feats, w_recv, base):
    hid = base.shape[1]
    mine = lax.axis_index("ch")
    my_bias = jnp.zeros((1, hid), jnp.float32)
    for k in range(bias.shape[1] // hid):
        my_bias += jnp.where(mine == k, bias[:, k * hid : (k + 1) * hid], 0.0)
    recv = dot(w_recv[...], feats[...]).T
    base[...] = 0.5 * (recv.astype(jnp.bfloat16).astype(jnp.float32) + my_bias)


def prepare_kernel(count, tiles, *refs):
    blocks = refs[:count]
    feats, w_node_v, bias, w_out_t, cots, pre, grad_hidden = refs[count:]
    assemble(cots, blocks, lax.axis_index("ch"))
    column = jnp.broadcast_to(bias[...], (8, bias.shape[1])).T[:, :1]
    pre[...] = dot(w_node_v[...], feats[...]) + column
    lane = lax.broadcasted_iota(jnp.int32, (1, cots.shape[1]), 1)
    active = (lane < tiles[0] * TILE).astype(jnp.bfloat16)
    grad_hidden[...] = dot(w_out_t[...], cots[...] * active)


def chunk_of(place, first, shape):
    on_zero, on_one = (float(first + slot) for slot in SLOT_OF[place])
    chunk = jnp.where(lax.axis_index("sub") == 0, on_zero, on_one)
    return jnp.full(shape, chunk, jnp.float32).astype(jnp.bfloat16)


def picks_of(block, place):
    marks = block[CHUNK : CHUNK + PACK, :].astype(jnp.float32)
    per_slot = CHUNK // TILE
    half = len(SLOT_OF) // 2
    starts = [slot % half * per_slot for slot in SLOT_OF[place]]
    sub = lax.axis_index("sub")
    return [
        jnp.where(
            sub == 0,
            marks[starts[0] + t : starts[0] + t + 1],
            marks[starts[1] + t : starts[1] + t + 1],
        )
        for t in range(per_slot)
    ]


def fill(ext, start, block, place):
    for t, pick in enumerate(picks_of(block, place)):
        ext[start + t * TILE : start + (t + 1) * TILE, :] = jnp.where(
            pick > 0.5, block[TILE : 2 * TILE, :], block[:TILE, :]
        )


def pick_rows(low, high, chunks, ext):
    one = jnp.bfloat16(1.0)
    zero = jnp.bfloat16(0.0)
    lane = lax.broadcasted_iota(jnp.int32, low.shape, 1)
    marks = [
        jnp.where(low == (lane + half * LANES).astype(jnp.bfloat16), one, zero)
        for half in range(CHUNK // LANES)
    ]
    picker = jnp.concatenate(
        [jnp.where(high == chunk, mark, zero) for chunk in chunks for mark in marks], axis=1
    )
    return dot(picker, ext[...])


def near_kernel(low, high, proj, beside, part, ext):
    own = proj.shape[0]
    ext[:own, :] = proj[...]
    fill(ext, own, beside, 0)
    first = own // CHUNK
    chunks = [jnp.bfloat16(chunk) for chunk in range(first)]
    chunks.append(chunk_of(0, first, low.shape[1:]))

    def step(m, carry):
        part[m] = pick_rows(low[m], high[m], chunks, ext).astype(jnp.bfloat16)
        return carry

    lax.fori_loop(0, low.shape[0], step, 0, unroll=True)


def line_kernel(low, high, before, west, east, part, ext):
    first = low.shape[1] // CHUNK
    chunks = []
    for index, (place, block) in enumerate(((1, west), (2, east))):
        fill(ext, index * CHUNK, block, place)
        chunks.append(jnp.bfloat16(first + SLOT_OF[place][0]))

    def step(m, carry):
        more = pick_rows(low[m], high[m], chunks, ext)
        part[m] = (before[m].astype(jnp.float32) + more).astype(jnp.bfloat16)
        return carry

    lax.fori_loop(0, low.shape[0], step, 0, unroll=True)


def cross_rows_kernel(block, rows):
    fill(rows, 0, block, 3)


def message_kernel(
    start, low, high, base, in_degree, part, cross, west, east, message, slope, ext, total
):
    nodes = low.shape[1]
    degree, rows, hid = slope.shape
    first = nodes // CHUNK
    together = nodes // rows
    span = slice(start, start + rows)
    chunks = []
    ext[:CHUNK, :] = cross[...]
    for index, (place, block) in enumerate(((4, west), (5, east))):
        fill(ext, (index + 1) * CHUNK, block, place)
    for place in (3, 4, 5):
        chunks.append(chunk_of(place, first, (nodes, LANES)))
    total[...] = jnp.zeros_like(total)

    def rows_of(ref, k):
        return jnp.concatenate([ref[k * together + i, span, :] for i in range(together)], axis=0)

    def step(k, carry):
        low_k, high_k = rows_of(low, k), rows_of(high, k)
        half = pick_rows(low_k, high_k, chunks, ext) + rows_of(part, k).astype(jnp.float32)
        half += jnp.concatenate([base[span, :]] * together, axis=0)
        wide = jnp.concatenate([high_k] * pl.cdiv(hid, LANES), axis=1)[:, :hid]
        half = jnp.where(wide.astype(jnp.float32) < NO_CHUNK, half, OFF)
        twice = jnp.tanh(half) + 1.0
        act = half * twice
        grad = (twice + act * (2.0 - twice)).astype(jnp.bfloat16)
        terms = 0.0
        for i in range(together):
            terms += act[i * rows : (i + 1) * rows]
            slope[k * together + i] = grad[i * rows : (i + 1) * rows]
        total[...] += terms
        return carry

    lax.fori_loop(0, degree // together, step, 0, unroll=True)
    count = in_degree[:, span].astype(jnp.float32)
    message[...] = (total[...].T / count).astype(jnp.bfloat16)


def node_kernel(count, start, in_degree, *refs):
    blocks = refs[:count]
    w_both, w_both_t, pre, grad_hidden = refs[count : count + 4]
    hidden, grad_pre, scale, messages = refs[count + 4 :]
    assemble(messages, blocks, lax.axis_index("ch"))
    span = slice(start, start + hidden.shape[1])
    half = 0.5 * (pre[:, span] + dot(w_both[...], messages[...]))
    twice = jnp.tanh(half) + 1.0
    act = half * twice
    hidden[...] = act.astype(jnp.bfloat16)
    slope = 0.5 * (twice + act * (2.0 - twice))
    low_grad = (grad_hidden[:, span] * slope).astype(jnp.bfloat16)
    grad_pre[...] = low_grad
    grad_msg = dot(w_both_t[...], low_grad).astype(jnp.bfloat16).astype(jnp.float32)
    scale[...] = (grad_msg * (0.5 / in_degree[:, span].astype(jnp.float32))).T


def scatter(low, high, edges, chunks, total):
    one = jnp.bfloat16(1.0)
    zero = jnp.bfloat16(0.0)
    groups = CHUNK // PACK
    for step in edges:
        width = sum(rows for _, _, rows, _ in step)
        place = lax.broadcasted_iota(jnp.int32, (groups, PACK, width), 0) * PACK
        place = place + lax.broadcasted_iota(jnp.int32, (groups, PACK, width), 1)
        low_k = jnp.concatenate([low[m, :, s : s + r] for m, s, r, _ in step], axis=1)
        high_k = jnp.concatenate([high[m, :, s : s + r] for m, s, r, _ in step], axis=1)
        grads = jnp.concatenate([grad() for _, _, _, grad in step], axis=0)
        mark = jnp.where(low_k[None] == place.astype(jnp.bfloat16), one, zero)
        picker = jnp.concatenate(
            [jnp.where(high_k[None] == chunk, mark, zero) for chunk in chunks], axis=0
        ).reshape(len(chunks) * CHUNK, width)
        total[...] += dot(picker, grads)


def pairs(start, ref, nodes, grad_of):
    degree, rows, _ = ref.shape
    together = nodes // rows
    return [
        [
            (m, start, rows, functools.partial(grad_of, ref, m))
            for m in range(k * together, (k + 1) * together)
        ]
        for k in range(degree // together)
    ]


def fold(block, place, index, total):
    picks = picks_of(block, place)
    halves = []
    for half in range(len(picks)):
        terms = 0.0
        for t, pick in enumerate(picks):
            start = index * CHUNK + t * TILE
            hit = jnp.abs(pick - half) < 0.5
            terms += jnp.where(hit, total[start : start + TILE, :], 0.0)
        halves.append(terms)
    return jnp.concatenate(halves, axis=0).astype(jnp.bfloat16)


def early_kernel(low, high, slope, scale, grads, total):
    nodes = low.shape[2]

    def grad_of(ref, m):
        grads[m] = (ref[m].astype(jnp.float32) * scale[...]).astype(jnp.bfloat16)
        return grads[m]

    chunks = [chunk_of(place, nodes // CHUNK, (1, PACK, nodes)) for place in EARLY]
    total[...] = jnp.zeros_like(total)
    scatter(low, high, pairs(0, slope, nodes, grad_of), chunks, total)


def cross_kernel(start, low, high, slope, scale, before, cross, to_cross, grads, total):
    nodes = low.shape[2]

    def grad_of(ref, m):
        grads[m] = (ref[m].astype(jnp.float32) * scale[...]).astype(jnp.bfloat16)
        return grads[m]

    chunks = [chunk_of(EARLY[0], nodes // CHUNK, (1, PACK, nodes))]
    total[...] = before[:CHUNK, :]
    scatter(low, high, pairs(start, slope, nodes, grad_of), chunks, total)
    to_cross[...] = fold(cross, EARLY[0], 0, total)


def other_kernel(start, low, high, grads, before, west, east, to_other, total):
    nodes = low.shape[2]
    chunks = [chunk_of(place, nodes // CHUNK, (1, PACK, nodes)) for place in EARLY[1:]]
    total[...] = before[CHUNK:, :]
    scatter(low, high, pairs(start, grads, nodes, lambda ref, m: ref[m]), chunks, total)
    to_other[0] = fold(west, EARLY[1], 0, total)
    to_other[1] = fold(east, EARLY[2], 1, total)


def all_pairs(parts, nodes):
    start, steps = 0, []
    for part in parts:
        steps += pairs(start, part, nodes, lambda ref, m: ref[m])
        start += part.shape[1]
    return steps


def late_kernel(low, high, *refs):
    *parts, west, east, beside, to_west, to_east, to_beside, total = refs
    nodes = low.shape[2]
    first = nodes // CHUNK
    chunks = [chunk_of(place, first, (1, PACK, nodes)) for place in LATE]
    total[...] = jnp.zeros_like(total)
    scatter(low, high, all_pairs(parts, nodes), chunks, total)
    to_west[...] = fold(west, 1, 0, total)
    to_east[...] = fold(east, 2, 1, total)
    to_beside[...] = fold(beside, 0, 2, total)


def own_kernel(low, high, *refs):
    *parts, total, recv = refs
    nodes = low.shape[2]
    chunks = [jnp.bfloat16(chunk) for chunk in range(nodes // CHUNK)]
    total[...] = jnp.zeros_like(total)
    scatter(low, high, all_pairs(parts, nodes), chunks, total)
    start = 0
    for part in parts:
        degree, rows, _ = part.shape
        terms = 0.0
        for m in range(degree):
            terms += part[m].astype(jnp.float32)
        recv[:, start : start + rows] = terms.T.astype(jnp.bfloat16)
        start += rows


def output_kernel(tiles, feats, cots, w_out, w_node_v_t, *refs):
    *parts, updated, direct = refs
    count = len(parts) // 2
    rows = parts[0].shape[1]
    for k in range(count):
        hidden, grad_pre = parts[k], parts[count + k]
        span = slice(k * rows, (k + 1) * rows)
        lane = lax.broadcasted_iota(jnp.int32, (1, rows), 1) + k * rows
        active = (lane < tiles[0] * TILE).astype(jnp.float32)
        node_out = dot(w_out[...], hidden[...])
        new = feats[:, span].astype(jnp.float32) + active * node_out
        updated[:, span] = new.astype(jnp.bfloat16)
        direct[:, span] = cots[:, span].astype(jnp.float32) + dot(w_node_v_t[...], grad_pre[...])


def across_kernel(left, right, across, west, east):
    sub = lax.axis_index("sub")
    other = across[...].astype(jnp.float32)
    to_west = left[...].astype(jnp.float32) + jnp.where(sub == 0, 0.0, other)
    to_east = right[...].astype(jnp.float32) + jnp.where(sub == 0, other, 0.0)
    west[...] = to_west.astype(west.dtype)
    east[...] = to_east.astype(east.dtype)


def add_kernel(left, right, more, west, east):
    west[...] = (left[...] + more[0].astype(jnp.float32)).astype(jnp.bfloat16)
    east[...] = (right[...] + more[1].astype(jnp.float32)).astype(jnp.bfloat16)


def back_kernel(start, inv_root, tiles, own, beside, feats, upper, *refs):
    *refs, total = refs
    sub = lax.axis_index("sub")
    offset = pl.multiple_of(tiles[0] // 2 * TILE, TILE)
    total[...] = own[...]
    near = beside[...].astype(jnp.float32)
    block = upper[...].astype(jnp.float32) + jnp.where(sub == 0, near, 0.0)
    total[pl.ds(offset, block.shape[0]), :] += block
    if start:
        grad_send, weight = refs
    else:
        lower, before, grad_send, w_mine, w_beside, weight = refs
        block = lower[...].astype(jnp.float32) + jnp.where(sub == 0, 0.0, near)
        total[: block.shape[0], :] += block
    rows = grad_send.shape[0]
    grad_send[...] = total[start : start + rows, :].astype(jnp.bfloat16)
    terms = dot(feats[:, start : start + rows], grad_send[...])
    if start:
        weight[...] = terms
        return
    weight[...] = (before[...] + terms) * inv_root
    lon = lax.axis_index("lon")
    lons, columns, _ = w_mine.shape
    for k in range(lons):
        band = (lon ^ k) * 2
        for out, core in ((w_mine, sub), (w_beside, 1 - sub)):
            spot = pl.multiple_of((band + core) * columns, columns)
            out[k] = weight[pl.ds(spot, columns), :].astype(out.dtype)


def terms_kernel(start, grad_send, recv, direct, w_send_t, w_recv_t, kept, sent, terms):
    span = slice(start, start + grad_send.shape[0])
    mine = lax.axis_index("ch")
    chans = kept.shape[0]
    grad_send_t = grad_send[...].astype(jnp.float32).T.astype(jnp.bfloat16)
    terms[...] = dot(w_send_t[...], grad_send_t) + dot(w_recv_t[...], recv[:, span])
    kept[...] = direct[:, span] + mine_of(terms, mine, chans)
    count = sent.shape[0] + 1
    for k in range(1, count):
        sent[k - 1] = mine_of(terms, lax.rem(mine + k, count), chans).astype(jnp.bfloat16)


def finish_kernel(count, *refs):
    kept, *others = refs[: count]
    *done, out = refs[count:]
    total = kept[...]
    for other in others:
        total += other[...].astype(jnp.float32)
    out[:, : kept.shape[1]] = total.astype(jnp.bfloat16)
    start = kept.shape[1]
    for part in done:
        out[:, start : start + part.shape[1]] = part[...]
        start += part.shape[1]


def sum_kernel(held, received, near, sent):
    near[...] = held[0] + received[0].astype(jnp.float32)
    sent[...] = (held[1:] + received[1:].astype(jnp.float32)).astype(jnp.bfloat16)


def weight_kernel(near, *refs):
    *terms, out = refs
    total = near[...]
    for term in terms:
        total += term[...].astype(jnp.float32)
    out[...] = total


def shards(
    features,
    cotangent,
    senders,
    in_degree,
    tile_count,
    send_tiles,
    w_send,
    w_recv,
    bias_edge,
    w_msg,
    w_node_v,
    w_node_a,
    bias_node,
    w_out,
):
    chans, nodes = features.shape
    count = lax.axis_size("ch")
    lons = lax.axis_size("lon")
    hidden_all, chans_all = w_send.shape
    hid = hidden_all // count
    cycle = ("lon", "sub")
    shard_count = lax.axis_size(cycle)
    total_nodes = nodes * shard_count
    degree = senders.shape[0]
    slots = send_tiles.shape[1]
    slot_rows = send_tiles.shape[2] * TILE
    ext_len = nodes + slots * slot_rows
    bf16, f32 = jnp.bfloat16, jnp.float32
    shape = jax.ShapeDtypeStruct

    far_route = [(i, (i + (3 if i % 2 else -3)) % shard_count) for i in range(shard_count)]
    across_route = [(i, (i + (1 if i % 2 else -1)) % shard_count) for i in range(shard_count)]
    across = lambda block: lax.ppermute(block, cycle, across_route)
    degrees = in_degree[None, :]
    picks = jnp.transpose(send_tiles, (0, 2, 1))
    sub = lax.axis_index("sub")

    feat_blocks = gathered(features, "ch")

    whole_w = pltpu.VMEM((chans_all, hidden_all), bf16)
    (
        w_send_my,
        w_recv_my,
        w_out_my,
        features_held,
        w_send_t,
        w_recv_t,
        w_both_t,
        w_node_v_t,
        w_both,
        w_out_t,
    ) = call(
        weights_kernel,
        (
            shape((hid, chans_all), bf16),
            shape((hid, chans_all), bf16),
            shape((chans, hidden_all), bf16),
            shape((chans, nodes), bf16),
            shape((chans_all, hid), bf16),
            shape((chans_all, hid), bf16),
            shape((hid, hidden_all), bf16),
            shape((chans, hidden_all), bf16),
            shape((hidden_all, hidden_all), bf16),
            shape((hidden_all, chans_all), bf16),
        ),
        [w_msg, w_node_a, features, w_send, w_recv, w_node_v, w_out],
        away=7,
        scalars=0,
        scratch=[whole_w] * 5 + [pltpu.SemaphoreType.DMA((7,))],
        limit=WEIGHTS_LIMIT,
    )
    feat_blocks[0] = features_held

    block = shape((slot_rows + PACK, hid), bf16)
    feats, proj, upper, lower, beside, cross = call(
        functools.partial(project_kernel, count),
        (
            shape((chans_all, nodes), bf16),
            shape((nodes, hid), bf16),
            block,
            block,
            block,
            block,
        ),
        [tile_count, picks] + feat_blocks + [w_send_my],
    )
    west = shifted(upper, "lon", 1)
    east = shifted(lower, "lon", -1)
    cross = lax.ppermute(cross, cycle, far_route)
    base = call(
        receive_kernel,
        shape((nodes, hid), f32),
        [bias_edge[None, :], feats, w_recv_my],
        scalars=0,
    )
    base, senders, cotangent_late = lax.optimization_barrier((base, senders, cotangent))
    beside = shifted(beside, "sub", 1)
    cot_blocks = gathered(cotangent_late, "ch")
    low_cols, high_cols, low_rows, high_rows = call(
        edges_kernel,
        (
            shape((degree, nodes, LANES), bf16),
            shape((degree, nodes, LANES), bf16),
            shape((degree, PACK, nodes), bf16),
            shape((degree, PACK, nodes), bf16),
        ),
        [tile_count, senders, degrees],
        scalars=1,
    )
    cots, pre, grad_hidden = call(
        functools.partial(prepare_kernel, count),
        (
            shape((chans_all, nodes), bf16),
            shape((hidden_all, nodes), f32),
            shape((hidden_all, nodes), f32),
        ),
        [tile_count] + cot_blocks + [feats, w_node_v, bias_node[None, :], w_out_t],
        scalars=1,
    )

    part_shape = shape((degree, nodes, hid), bf16)
    part = call(
        near_kernel,
        part_shape,
        [low_cols, high_cols, proj, beside],
        scratch=[pltpu.VMEM((nodes + slot_rows, hid), bf16)],
        scalars=0,
    )
    west, east, part = lax.optimization_barrier((west, east, part))
    west_too = shifted(west, "sub", 1)
    east_too = shifted(east, "sub", 1)
    part, pre = lax.optimization_barrier((part, pre))
    part = call(
        line_kernel,
        part_shape,
        [low_cols, high_cols, part, west, east],
        scratch=[pltpu.VMEM((2 * slot_rows, hid), bf16)],
        scalars=0,
    )
    part, cross = lax.optimization_barrier((part, cross))
    cross_rows = call(
        cross_rows_kernel, shape((slot_rows, hid), bf16), [cross], scalars=0
    )
    halves = 2
    rows = nodes // halves
    slopes, messages, hiddens, grad_pres, grads = [], [], [], [], []
    for k in range(halves):
        message, slope = call(
            functools.partial(message_kernel, k * rows),
            (shape((hid, rows), bf16), shape((degree, rows, hid), bf16)),
            [low_cols, high_cols, base, degrees, part, cross_rows, west_too, east_too],
            scratch=[pltpu.VMEM((3 * slot_rows, hid), bf16), pltpu.VMEM((rows, hid), f32)],
            scalars=0,
        )
        slopes.append(slope)
        messages.append(gathered(message, "ch"))

    block = shape((slot_rows, hid), bf16)
    sums = shape((len(EARLY) * slot_rows, hid), f32)
    grad_shape = shape((degree, rows, hid), bf16)
    for k in range(halves):
        hidden, grad_pre, scale = call(
            functools.partial(node_kernel, count, k * rows),
            (
                shape((hidden_all, rows), bf16),
                shape((hidden_all, rows), bf16),
                shape((rows, hid), f32),
            ),
            [degrees] + messages[k] + [w_both, w_both_t, pre, grad_hidden],
            scratch=[pltpu.VMEM((hidden_all, rows), bf16)],
            scalars=0,
        )
        hiddens.append(hidden)
        grad_pres.append(grad_pre)
        operands = [low_rows, high_rows, slopes[k], scale]
        if k == 0:
            grad, before = call(early_kernel, (grad_shape, sums), operands, scalars=0)
        else:
            to_cross, grad = call(
                functools.partial(cross_kernel, k * rows),
                (block, grad_shape),
                operands + [before, cross],
                scratch=[pltpu.VMEM((slot_rows, hid), f32)],
                scalars=0,
            )
            to_other = call(
                functools.partial(other_kernel, k * rows),
                shape((2, slot_rows, hid), bf16),
                [low_rows, high_rows, grad, before, west_too, east_too],
                scratch=[pltpu.VMEM((2 * slot_rows, hid), f32)],
                scalars=0,
            )
        grads.append(grad)

    grads[0], to_other = lax.optimization_barrier((grads[0], to_other))
    from_other = shifted(to_other, "sub", 1)
    from_cross = across(to_cross)
    to_west, to_east, to_beside = call(
        late_kernel,
        (block, block, block),
        [low_rows, high_rows] + grads + [west, east, beside],
        scratch=[pltpu.VMEM((len(LATE) * slot_rows, hid), f32)],
        scalars=0,
    )
    wide = shape((slot_rows, hid), f32)
    to_west, to_east = call(
        across_kernel, (wide, wide), [to_west, to_east, from_cross], scalars=0, flops=15 * 10**8
    )
    to_west, to_east = call(add_kernel, (block, block), [to_west, to_east, from_other], scalars=0)
    from_upper = shifted(to_west, "lon", -1)
    from_lower = shifted(to_east, "lon", 1)
    from_beside = shifted(to_beside, "sub", 1)
    to_west, grads[0] = lax.optimization_barrier((to_west, grads[0]))

    own, grad_recv = call(
        own_kernel,
        (shape((nodes, hid), f32), shape((hid, nodes), bf16)),
        [low_rows, high_rows] + grads,
        scalars=0,
    )
    own, hiddens[0] = lax.optimization_barrier((own, hiddens[0]))
    updated, direct = call(
        output_kernel,
        (shape((chans, nodes), bf16), shape((chans, nodes), f32)),
        [tile_count, features_held, cotangent, w_out_my, w_node_v_t] + hiddens + grad_pres,
        scalars=1,
    )
    columns = chans_all // shard_count
    inv_root = 1.0 / math.sqrt(total_nodes)
    inputs = [tile_count, own, from_beside, feats, from_upper]
    weight_shape = shape((chans_all, hid), f32)
    grad_shape = shape((rows, hid), bf16)
    finals = []
    for k in reversed(range(halves)):
        kernel = functools.partial(back_kernel, k * rows, inv_root)
        if k:
            grad_send, weight = call(
                kernel,
                (grad_shape, weight_shape),
                inputs,
                scratch=[pltpu.VMEM((nodes, hid), f32)],
                scalars=1,
            )
        else:
            grad_send, w_mine, w_beside = call(
                kernel,
                (
                    grad_shape,
                    shape((lons, columns, hid), f32),
                    shape((lons, columns, hid), bf16),
                ),
                inputs + [from_lower, weight],
                scratch=[pltpu.VMEM(weight_shape.shape, f32), pltpu.VMEM((nodes, hid), f32)],
                scalars=1,
            )
            w_beside = shifted(w_beside, "sub", 1)
            w_beside, *finals = lax.optimization_barrier((w_beside, *finals))
        kept, sent = call(
            functools.partial(terms_kernel, k * rows),
            (shape((chans, rows), f32), shape((count - 1, chans, rows), bf16)),
            [grad_send, grad_recv, direct, w_send_t, w_recv_t],
            scratch=[pltpu.VMEM((chans_all, rows), f32)],
            scalars=0,
        )
        if k:
            weight, kept = lax.optimization_barrier((weight, kept))
        parts = [kept] + [shifted(sent[i - 1], "ch", i) for i in range(1, count)]
        grad_features = call(
            functools.partial(finish_kernel, count),
            shape((chans, nodes - k * rows), bf16),
            parts + finals,
            scalars=0,
        )
        finals = [grad_features]

    near, w_sent = call(
        sum_kernel,
        (shape((columns, hid), f32), shape((lons - 1, columns, hid), bf16)),
        [w_mine, w_beside],
        scalars=0,
    )
    w_terms = [
        lax.ppermute(w_sent[k - 1], "lon", [(i, i ^ k) for i in range(lons)])
        for k in range(1, lons)
    ]
    grad_w_send = call(weight_kernel, shape((columns, hid), f32), [near] + w_terms, scalars=0)
    return (updated, grad_features, grad_w_send.T)


def solution(mesh):
    nodes_last = P("ch", ("parts", "lon", "sub"))
    spread = ("parts", "lon", "sub")
    placed = (nodes_last, nodes_last, P(None, spread), P(spread), P(spread), P(spread, None, None))
    return jax.shard_map(
        shards,
        mesh=mesh,
        in_specs=placed + (P(),) * 8,
        out_specs=(nodes_last, nodes_last, P(("parts", "ch"), ("lon", "sub"))),
        check_vma=False,
    )
```

```python
import functools
import math

import jax
import jax.numpy as jnp
from jax import lax
from jax.experimental import pallas as pl
from jax.experimental.pallas import tpu as pltpu
from jax.sharding import PartitionSpec as P

TILE = 128
CHUNK = 256
LANES = 128
PACK = 16
MIB = 1 << 20
WEIGHTS_LIMIT = 52
WEIGHT_FLOPS = 3 * 10**9
NO_CHUNK = 64
SLOT_OF = ((3, 0), (1, 1), (4, 4), (2, 5), (0, 2), (5, 3))
EARLY, LATE = (3, 4, 5), (1, 2, 0)
OFF = -1e4


def shifted(block, axis, distance):
    size = lax.axis_size(axis)
    route = [((i - distance) % size, i) for i in range(size)]
    return lax.ppermute(block, axis, route)


def gathered(block, axis):
    return [block] + [shifted(block, axis, k) for k in range(1, lax.axis_size(axis))]


def dot(left, right):
    return jnp.dot(left, right, preferred_element_type=jnp.float32)


def dot_nt(left, right):
    return lax.dot_general(
        left, right, (((1,), (1,)), ((), ())), preferred_element_type=jnp.float32
    )


def sigmoid(value):
    return 0.5 * jnp.tanh(0.5 * value) + 0.5


def call(kernel, out_shape, operands, scratch=(), scalars=2, away=0, limit=24, flops=1024):
    vmem = pl.BlockSpec(memory_space=pltpu.VMEM)
    smem = pl.BlockSpec(memory_space=pltpu.SMEM)
    anywhere = pl.BlockSpec(memory_space=pltpu.HBM)
    return pl.pallas_call(
        kernel,
        out_shape=out_shape,
        in_specs=[smem] * scalars
        + [anywhere] * away
        + [vmem] * (len(operands) - scalars - away),
        out_specs=jax.tree.map(lambda _: vmem, out_shape),
        scratch_shapes=scratch,
        compiler_params=pltpu.CompilerParams(vmem_limit_bytes=limit * MIB),
        cost_estimate=pl.CostEstimate(flops=flops, bytes_accessed=1024, transcendentals=0),
    )(*operands)


def assemble(whole_ref, blocks, first):
    count = len(blocks)
    rows = blocks[0].shape[0]
    for k, block in enumerate(blocks):
        place = lax.rem(first - k + count, count) * rows
        whole_ref[pl.ds(pl.multiple_of(place, rows), rows), :] = block[...]


def mine_of(ref, index, rows):
    return ref[pl.ds(pl.multiple_of(index * rows, rows), rows), :]


def weights_kernel(*refs):
    sources, refs = refs[:7], refs[7:]
    w_send, w_recv, w_out, feats, w_send_t, w_recv_t, w_both_t, w_node_v_t, w_both, w_out_t = refs[:10]
    w_msg, w_node_v, w_node_a, w_out_all, turned, sems = refs[10:]
    mine = lax.axis_index("ch")
    hid = w_send.shape[0]
    targets = (w_msg, w_node_a, feats, w_send, w_recv, w_node_v, w_out_all)
    copies = []
    for k, (source, target) in enumerate(zip(sources, targets)):
        if k in (3, 4):
            source = source.at[pl.ds(pl.multiple_of(mine * hid, hid), hid), :]
        copies.append(pltpu.make_async_copy(source, target, sems.at[k]))
    for copy in copies:
        copy.start()
    for copy in copies[:2]:
        copy.wait()
    w_both[...] = dot(w_node_a[...], w_msg[...]).astype(jnp.bfloat16)
    turned[...] = w_both[...].T
    w_both_t[...] = mine_of(turned, mine, hid)
    for copy in copies[2:]:
        copy.wait()
    w_send_t[...] = w_send[...].T
    w_recv_t[...] = w_recv[...].T
    turned[...] = w_node_v[...].T
    w_node_v_t[...] = mine_of(turned, mine, w_node_v_t.shape[0])
    w_out_t[...] = w_out_all[...].T
    w_out[...] = mine_of(w_out_all, mine, w_out.shape[0])


def edges_kernel(tiles, senders, in_degree, low_cols, high_cols, low_rows, high_rows):
    degree, nodes = senders.shape
    lane = lax.broadcasted_iota(jnp.int32, (degree, nodes), 1)
    row = lax.broadcasted_iota(jnp.int32, (degree, nodes), 0)
    valid = (row < in_degree[...]) & (lane < tiles[0] * TILE)
    ids = senders[...]
    low = (ids & (CHUNK - 1)).astype(jnp.float32)
    high = jnp.where(valid, ids // CHUNK, NO_CHUNK).astype(jnp.float32)
    for m in range(degree):
        shape = (PACK, nodes)
        low_rows[m] = jnp.broadcast_to(low[m : m + 1], shape).astype(jnp.bfloat16)
        high_rows[m] = jnp.broadcast_to(high[m : m + 1], shape).astype(jnp.bfloat16)
    fill = jnp.zeros((PACK - degree, nodes), jnp.float32)
    depth = 2 * PACK
    both = jnp.concatenate([low, fill, high, fill], axis=0).T.astype(jnp.bfloat16)
    width = degree * LANES
    spot = lax.broadcasted_iota(jnp.int32, (depth, width), 0)
    group = lax.broadcasted_iota(jnp.int32, (depth, width), 1) // LANES
    for first, out in ((0, low_cols), (PACK, high_cols)):
        pick = (spot == group + first).astype(jnp.bfloat16)
        spread = dot(both, pick).astype(jnp.bfloat16)
        for m in range(degree):
            out[m] = spread[:, m * LANES : (m + 1) * LANES]


def project_kernel(count, tiles, picks, *refs):
    blocks = refs[:count]
    w_send, feats, proj, upper, lower, beside, cross = refs[count:]
    mine, sub = lax.axis_index("ch"), lax.axis_index("sub")
    first = tiles[0] // 2
    assemble(feats, blocks, mine)
    whole = feats[...]
    hid = proj.shape[1]
    proj[...] = (0.5 * dot(w_send[...], whole).T).astype(jnp.bfloat16)
    rows = upper.shape[0] - PACK
    upper[:rows, :] = proj[pl.ds(pl.multiple_of(first * TILE, TILE), rows), :]
    lower[:rows, :] = proj[:rows, :]
    spot = lax.broadcasted_iota(jnp.int32, (PACK, hid), 0)
    _, per_slot, slots = picks.shape
    half = slots // 2
    for start, out, lift in ((0, upper, first), (half, lower, 0)):
        marks = jnp.zeros((PACK, hid), jnp.float32)
        for k in range(half * per_slot):
            rel = picks[0, k % per_slot, start + k // per_slot] - lift
            marks = jnp.where(spot == k, rel.astype(jnp.float32), marks)
        out[rows:, :] = marks.astype(jnp.bfloat16)

    @pl.when(sub == 0)
    def _():
        beside[...] = upper[...]
        cross[...] = lower[...]

    @pl.when(sub != 0)
    def _():
        beside[...] = lower[...]
        cross[...] = upper[...]


def receive_kernel(bias, feats, w_recv, base):
    hid = base.shape[1]
    mine = lax.axis_index("ch")
    my_bias = jnp.zeros((1, hid), jnp.float32)
    for k in range(bias.shape[1] // hid):
        my_bias += jnp.where(mine == k, bias[:, k * hid : (k + 1) * hid], 0.0)
    recv = dot(w_recv[...], feats[...]).T
    base[...] = 0.5 * (recv.astype(jnp.bfloat16).astype(jnp.float32) + my_bias)


def prepare_kernel(count, tiles, *refs):
    blocks = refs[:count]
    feats, w_node_v, bias, w_out_t, cots, pre, grad_hidden = refs[count:]
    assemble(cots, blocks, lax.axis_index("ch"))
    column = jnp.broadcast_to(bias[...], (8, bias.shape[1])).T[:, :1]
    pre[...] = dot(w_node_v[...], feats[...]) + column
    lane = lax.broadcasted_iota(jnp.int32, (1, cots.shape[1]), 1)
    active = (lane < tiles[0] * TILE).astype(jnp.bfloat16)
    grad_hidden[...] = dot(w_out_t[...], cots[...] * active)


def chunk_of(place, first, shape):
    on_zero, on_one = (float(first + slot) for slot in SLOT_OF[place])
    chunk = jnp.where(lax.axis_index("sub") == 0, on_zero, on_one)
    return jnp.full(shape, chunk, jnp.float32).astype(jnp.bfloat16)


def picks_of(block, place):
    marks = block[CHUNK : CHUNK + PACK, :].astype(jnp.float32)
    per_slot = CHUNK // TILE
    half = len(SLOT_OF) // 2
    starts = [slot % half * per_slot for slot in SLOT_OF[place]]
    sub = lax.axis_index("sub")
    return [
        jnp.where(
            sub == 0,
            marks[starts[0] + t : starts[0] + t + 1],
            marks[starts[1] + t : starts[1] + t + 1],
        )
        for t in range(per_slot)
    ]


def fill(ext, start, block, place):
    for t, pick in enumerate(picks_of(block, place)):
        ext[start + t * TILE : start + (t + 1) * TILE, :] = jnp.where(
            pick > 0.5, block[TILE : 2 * TILE, :], block[:TILE, :]
        )


def pick_rows(low, high, chunks, ext):
    one = jnp.bfloat16(1.0)
    zero = jnp.bfloat16(0.0)
    lane = lax.broadcasted_iota(jnp.int32, low.shape, 1)
    marks = [
        jnp.where(low == (lane + half * LANES).astype(jnp.bfloat16), one, zero)
        for half in range(CHUNK // LANES)
    ]
    picker = jnp.concatenate(
        [jnp.where(high == chunk, mark, zero) for chunk in chunks for mark in marks], axis=1
    )
    return dot(picker, ext[...])


def near_kernel(low, high, proj, beside, part, ext):
    own = proj.shape[0]
    ext[:own, :] = proj[...]
    fill(ext, own, beside, 0)
    first = own // CHUNK
    chunks = [jnp.bfloat16(chunk) for chunk in range(first)]
    chunks.append(chunk_of(0, first, low.shape[1:]))

    def step(m, carry):
        part[m] = pick_rows(low[m], high[m], chunks, ext).astype(jnp.bfloat16)
        return carry

    lax.fori_loop(0, low.shape[0], step, 0, unroll=True)


def line_kernel(low, high, before, west, east, part, ext):
    first = low.shape[1] // CHUNK
    chunks = []
    for index, (place, block) in enumerate(((1, west), (2, east))):
        fill(ext, index * CHUNK, block, place)
        chunks.append(jnp.bfloat16(first + SLOT_OF[place][0]))

    def step(m, carry):
        more = pick_rows(low[m], high[m], chunks, ext)
        part[m] = (before[m].astype(jnp.float32) + more).astype(jnp.bfloat16)
        return carry

    lax.fori_loop(0, low.shape[0], step, 0, unroll=True)


def cross_rows_kernel(block, rows):
    fill(rows, 0, block, 3)


def message_kernel(
    start, low, high, base, in_degree, part, cross, west, east, message, slope, ext, total
):
    nodes = low.shape[1]
    degree, rows, hid = slope.shape
    first = nodes // CHUNK
    together = nodes // rows
    span = slice(start, start + rows)
    chunks = []
    ext[:CHUNK, :] = cross[...]
    for index, (place, block) in enumerate(((4, west), (5, east))):
        fill(ext, (index + 1) * CHUNK, block, place)
    for place in (3, 4, 5):
        chunks.append(chunk_of(place, first, (nodes, LANES)))
    total[...] = jnp.zeros_like(total)

    def rows_of(ref, k):
        return jnp.concatenate([ref[k * together + i, span, :] for i in range(together)], axis=0)

    def step(k, carry):
        low_k, high_k = rows_of(low, k), rows_of(high, k)
        half = pick_rows(low_k, high_k, chunks, ext) + rows_of(part, k).astype(jnp.float32)
        half += jnp.concatenate([base[span, :]] * together, axis=0)
        wide = jnp.concatenate([high_k] * pl.cdiv(hid, LANES), axis=1)[:, :hid]
        half = jnp.where(wide.astype(jnp.float32) < NO_CHUNK, half, OFF)
        twice = jnp.tanh(half) + 1.0
        act = half * twice
        grad = (twice + act * (2.0 - twice)).astype(jnp.bfloat16)
        terms = 0.0
        for i in range(together):
            terms += act[i * rows : (i + 1) * rows]
            slope[k * together + i] = grad[i * rows : (i + 1) * rows]
        total[...] += terms
        return carry

    lax.fori_loop(0, degree // together, step, 0, unroll=True)
    count = in_degree[:, span].astype(jnp.float32)
    message[...] = (total[...].T / count).astype(jnp.bfloat16)


def node_kernel(count, start, in_degree, *refs):
    blocks = refs[:count]
    w_both, w_both_t, pre, grad_hidden = refs[count : count + 4]
    hidden, grad_pre, scale, messages = refs[count + 4 :]
    assemble(messages, blocks, lax.axis_index("ch"))
    span = slice(start, start + hidden.shape[1])
    half = 0.5 * (pre[:, span] + dot(w_both[...], messages[...]))
    twice = jnp.tanh(half) + 1.0
    act = half * twice
    hidden[...] = act.astype(jnp.bfloat16)
    slope = 0.5 * (twice + act * (2.0 - twice))
    low_grad = (grad_hidden[:, span] * slope).astype(jnp.bfloat16)
    grad_pre[...] = low_grad
    grad_msg = dot(w_both_t[...], low_grad).astype(jnp.bfloat16).astype(jnp.float32)
    scale[...] = (grad_msg * (0.5 / in_degree[:, span].astype(jnp.float32))).T


def scatter(low, high, edges, chunks, total):
    one = jnp.bfloat16(1.0)
    zero = jnp.bfloat16(0.0)
    groups = CHUNK // PACK
    for step in edges:
        width = sum(rows for _, _, rows, _ in step)
        place = lax.broadcasted_iota(jnp.int32, (groups, PACK, width), 0) * PACK
        place = place + lax.broadcasted_iota(jnp.int32, (groups, PACK, width), 1)
        low_k = jnp.concatenate([low[m, :, s : s + r] for m, s, r, _ in step], axis=1)
        high_k = jnp.concatenate([high[m, :, s : s + r] for m, s, r, _ in step], axis=1)
        grads = jnp.concatenate([grad() for _, _, _, grad in step], axis=0)
        mark = jnp.where(low_k[None] == place.astype(jnp.bfloat16), one, zero)
        picker = jnp.concatenate(
            [jnp.where(high_k[None] == chunk, mark, zero) for chunk in chunks], axis=0
        ).reshape(len(chunks) * CHUNK, width)
        total[...] += dot(picker, grads)


def pairs(start, ref, nodes, grad_of):
    degree, rows, _ = ref.shape
    together = nodes // rows
    return [
        [
            (m, start, rows, functools.partial(grad_of, ref, m))
            for m in range(k * together, (k + 1) * together)
        ]
        for k in range(degree // together)
    ]


def fold(block, place, index, total):
    picks = picks_of(block, place)
    halves = []
    for half in range(len(picks)):
        terms = 0.0
        for t, pick in enumerate(picks):
            start = index * CHUNK + t * TILE
            hit = jnp.abs(pick - half) < 0.5
            terms += jnp.where(hit, total[start : start + TILE, :], 0.0)
        halves.append(terms)
    return jnp.concatenate(halves, axis=0).astype(jnp.bfloat16)


def early_kernel(low, high, slope, scale, grads, total):
    nodes = low.shape[2]

    def grad_of(ref, m):
        grads[m] = (ref[m].astype(jnp.float32) * scale[...]).astype(jnp.bfloat16)
        return grads[m]

    chunks = [chunk_of(place, nodes // CHUNK, (1, PACK, nodes)) for place in EARLY]
    total[...] = jnp.zeros_like(total)
    scatter(low, high, pairs(0, slope, nodes, grad_of), chunks, total)


def cross_kernel(start, low, high, slope, scale, before, cross, to_cross, grads, total):
    nodes = low.shape[2]

    def grad_of(ref, m):
        grads[m] = (ref[m].astype(jnp.float32) * scale[...]).astype(jnp.bfloat16)
        return grads[m]

    chunks = [chunk_of(EARLY[0], nodes // CHUNK, (1, PACK, nodes))]
    total[...] = before[:CHUNK, :]
    scatter(low, high, pairs(start, slope, nodes, grad_of), chunks, total)
    to_cross[...] = fold(cross, EARLY[0], 0, total)


def other_kernel(start, low, high, grads, before, west, east, to_other, total):
    nodes = low.shape[2]
    chunks = [chunk_of(place, nodes // CHUNK, (1, PACK, nodes)) for place in EARLY[1:]]
    total[...] = before[CHUNK:, :]
    scatter(low, high, pairs(start, grads, nodes, lambda ref, m: ref[m]), chunks, total)
    to_other[0] = fold(west, EARLY[1], 0, total)
    to_other[1] = fold(east, EARLY[2], 1, total)


def all_pairs(parts, nodes):
    start, steps = 0, []
    for part in parts:
        steps += pairs(start, part, nodes, lambda ref, m: ref[m])
        start += part.shape[1]
    return steps


def late_kernel(low, high, *refs):
    *parts, west, east, beside, to_west, to_east, to_beside, total = refs
    nodes = low.shape[2]
    first = nodes // CHUNK
    chunks = [chunk_of(place, first, (1, PACK, nodes)) for place in LATE]
    total[...] = jnp.zeros_like(total)
    scatter(low, high, all_pairs(parts, nodes), chunks, total)
    to_west[...] = fold(west, 1, 0, total)
    to_east[...] = fold(east, 2, 1, total)
    to_beside[...] = fold(beside, 0, 2, total)


def own_kernel(low, high, *refs):
    *parts, total, recv = refs
    nodes = low.shape[2]
    chunks = [jnp.bfloat16(chunk) for chunk in range(nodes // CHUNK)]
    total[...] = jnp.zeros_like(total)
    scatter(low, high, all_pairs(parts, nodes), chunks, total)
    start = 0
    for part in parts:
        degree, rows, _ = part.shape
        terms = 0.0
        for m in range(degree):
            terms += part[m].astype(jnp.float32)
        recv[:, start : start + rows] = terms.T.astype(jnp.bfloat16)
        start += rows


def output_kernel(tiles, feats, cots, w_out, w_node_v_t, *refs):
    *parts, updated, direct = refs
    count = len(parts) // 2
    rows = parts[0].shape[1]
    for k in range(count):
        hidden, grad_pre = parts[k], parts[count + k]
        span = slice(k * rows, (k + 1) * rows)
        lane = lax.broadcasted_iota(jnp.int32, (1, rows), 1) + k * rows
        active = (lane < tiles[0] * TILE).astype(jnp.float32)
        node_out = dot(w_out[...], hidden[...])
        new = feats[:, span].astype(jnp.float32) + active * node_out
        updated[:, span] = new.astype(jnp.bfloat16)
        direct[:, span] = cots[:, span].astype(jnp.float32) + dot(w_node_v_t[...], grad_pre[...])


def across_kernel(left, right, across, west, east):
    sub = lax.axis_index("sub")
    other = across[...].astype(jnp.float32)
    to_west = left[...].astype(jnp.float32) + jnp.where(sub == 0, 0.0, other)
    to_east = right[...].astype(jnp.float32) + jnp.where(sub == 0, other, 0.0)
    west[...] = to_west.astype(west.dtype)
    east[...] = to_east.astype(east.dtype)


def add_kernel(left, right, more, west, east):
    west[...] = (left[...] + more[0].astype(jnp.float32)).astype(jnp.bfloat16)
    east[...] = (right[...] + more[1].astype(jnp.float32)).astype(jnp.bfloat16)


def back_kernel(start, inv_root, tiles, own, beside, feats, upper, *refs):
    *refs, total = refs
    sub = lax.axis_index("sub")
    offset = pl.multiple_of(tiles[0] // 2 * TILE, TILE)
    total[...] = own[...]
    near = beside[...].astype(jnp.float32)
    block = upper[...].astype(jnp.float32) + jnp.where(sub == 0, near, 0.0)
    total[pl.ds(offset, block.shape[0]), :] += block
    if start:
        grad_send, weight = refs
    else:
        lower, before, grad_send, w_mine, w_beside, weight = refs
        block = lower[...].astype(jnp.float32) + jnp.where(sub == 0, 0.0, near)
        total[: block.shape[0], :] += block
    rows = grad_send.shape[0]
    grad_send[...] = total[start : start + rows, :].astype(jnp.bfloat16)
    terms = dot(feats[:, start : start + rows], grad_send[...])
    if start:
        weight[...] = terms
        return
    weight[...] = (before[...] + terms) * inv_root
    lon = lax.axis_index("lon")
    lons, columns, _ = w_mine.shape
    for k in range(lons):
        band = (lon ^ k) * 2
        for out, core in ((w_mine, sub), (w_beside, 1 - sub)):
            spot = pl.multiple_of((band + core) * columns, columns)
            out[k] = weight[pl.ds(spot, columns), :].astype(out.dtype)


def terms_kernel(start, grad_send, recv, direct, w_send_t, w_recv_t, kept, sent, terms):
    span = slice(start, start + grad_send.shape[0])
    mine = lax.axis_index("ch")
    chans = kept.shape[0]
    grad_send_t = grad_send[...].astype(jnp.float32).T.astype(jnp.bfloat16)
    terms[...] = dot(w_send_t[...], grad_send_t) + dot(w_recv_t[...], recv[:, span])
    kept[...] = direct[:, span] + mine_of(terms, mine, chans)
    count = sent.shape[0] + 1
    for k in range(1, count):
        sent[k - 1] = mine_of(terms, lax.rem(mine + k, count), chans).astype(jnp.bfloat16)


def finish_kernel(count, *refs):
    kept, *others = refs[: count]
    *done, out = refs[count:]
    total = kept[...]
    for other in others:
        total += other[...].astype(jnp.float32)
    out[:, : kept.shape[1]] = total.astype(jnp.bfloat16)
    start = kept.shape[1]
    for part in done:
        out[:, start : start + part.shape[1]] = part[...]
        start += part.shape[1]


def sum_kernel(held, received, near, sent):
    near[...] = held[0] + received[0].astype(jnp.float32)
    sent[...] = (held[1:] + received[1:].astype(jnp.float32)).astype(jnp.bfloat16)


def weight_kernel(near, *refs):
    *terms, out = refs
    total = near[...]
    for term in terms:
        total += term[...].astype(jnp.float32)
    out[...] = total


def shards(
    features,
    cotangent,
    senders,
    in_degree,
    tile_count,
    send_tiles,
    w_send,
    w_recv,
    bias_edge,
    w_msg,
    w_node_v,
    w_node_a,
    bias_node,
    w_out,
):
    chans, nodes = features.shape
    count = lax.axis_size("ch")
    lons = lax.axis_size("lon")
    hidden_all, chans_all = w_send.shape
    hid = hidden_all // count
    cycle = ("lon", "sub")
    shard_count = lax.axis_size(cycle)
    total_nodes = nodes * shard_count
    degree = senders.shape[0]
    slots = send_tiles.shape[1]
    slot_rows = send_tiles.shape[2] * TILE
    ext_len = nodes + slots * slot_rows
    bf16, f32 = jnp.bfloat16, jnp.float32
    shape = jax.ShapeDtypeStruct

    far_route = [(i, (i + (3 if i % 2 else -3)) % shard_count) for i in range(shard_count)]
    across_route = [(i, (i + (1 if i % 2 else -1)) % shard_count) for i in range(shard_count)]
    across = lambda block: lax.ppermute(block, cycle, across_route)
    degrees = in_degree[None, :]
    picks = jnp.transpose(send_tiles, (0, 2, 1))
    sub = lax.axis_index("sub")

    feat_blocks = gathered(features, "ch")

    whole_w = pltpu.VMEM((chans_all, hidden_all), bf16)
    (
        w_send_my,
        w_recv_my,
        w_out_my,
        features_held,
        w_send_t,
        w_recv_t,
        w_both_t,
        w_node_v_t,
        w_both,
        w_out_t,
    ) = call(
        weights_kernel,
        (
            shape((hid, chans_all), bf16),
            shape((hid, chans_all), bf16),
            shape((chans, hidden_all), bf16),
            shape((chans, nodes), bf16),
            shape((chans_all, hid), bf16),
            shape((chans_all, hid), bf16),
            shape((hid, hidden_all), bf16),
            shape((chans, hidden_all), bf16),
            shape((hidden_all, hidden_all), bf16),
            shape((hidden_all, chans_all), bf16),
        ),
        [w_msg, w_node_a, features, w_send, w_recv, w_node_v, w_out],
        away=7,
        scalars=0,
        scratch=[whole_w] * 5 + [pltpu.SemaphoreType.DMA((7,))],
        limit=WEIGHTS_LIMIT,
    )
    feat_blocks[0] = features_held

    block = shape((slot_rows + PACK, hid), bf16)
    feats, proj, upper, lower, beside, cross = call(
        functools.partial(project_kernel, count),
        (
            shape((chans_all, nodes), bf16),
            shape((nodes, hid), bf16),
            block,
            block,
            block,
            block,
        ),
        [tile_count, picks] + feat_blocks + [w_send_my],
    )
    west = shifted(upper, "lon", 1)
    east = shifted(lower, "lon", -1)
    cross = lax.ppermute(cross, cycle, far_route)
    base = call(
        receive_kernel,
        shape((nodes, hid), f32),
        [bias_edge[None, :], feats, w_recv_my],
        scalars=0,
    )
    base, senders, cotangent_late = lax.optimization_barrier((base, senders, cotangent))
    beside = shifted(beside, "sub", 1)
    cot_blocks = gathered(cotangent_late, "ch")
    low_cols, high_cols, low_rows, high_rows = call(
        edges_kernel,
        (
            shape((degree, nodes, LANES), bf16),
            shape((degree, nodes, LANES), bf16),
            shape((degree, PACK, nodes), bf16),
            shape((degree, PACK, nodes), bf16),
        ),
        [tile_count, senders, degrees],
        scalars=1,
    )
    cots, pre, grad_hidden = call(
        functools.partial(prepare_kernel, count),
        (
            shape((chans_all, nodes), bf16),
            shape((hidden_all, nodes), f32),
            shape((hidden_all, nodes), f32),
        ),
        [tile_count] + cot_blocks + [feats, w_node_v, bias_node[None, :], w_out_t],
        scalars=1,
    )

    part_shape = shape((degree, nodes, hid), bf16)
    part = call(
        near_kernel,
        part_shape,
        [low_cols, high_cols, proj, beside],
        scratch=[pltpu.VMEM((nodes + slot_rows, hid), bf16)],
        scalars=0,
    )
    west, east, part = lax.optimization_barrier((west, east, part))
    west_too = shifted(west, "sub", 1)
    east_too = shifted(east, "sub", 1)
    part, pre = lax.optimization_barrier((part, pre))
    part = call(
        line_kernel,
        part_shape,
        [low_cols, high_cols, part, west, east],
        scratch=[pltpu.VMEM((2 * slot_rows, hid), bf16)],
        scalars=0,
    )
    part, cross = lax.optimization_barrier((part, cross))
    cross_rows = call(
        cross_rows_kernel, shape((slot_rows, hid), bf16), [cross], scalars=0
    )
    halves = 2
    rows = nodes // halves
    slopes, messages, hiddens, grad_pres, grads = [], [], [], [], []
    for k in range(halves):
        message, slope = call(
            functools.partial(message_kernel, k * rows),
            (shape((hid, rows), bf16), shape((degree, rows, hid), bf16)),
            [low_cols, high_cols, base, degrees, part, cross_rows, west_too, east_too],
            scratch=[pltpu.VMEM((3 * slot_rows, hid), bf16), pltpu.VMEM((rows, hid), f32)],
            scalars=0,
        )
        slopes.append(slope)
        messages.append(gathered(message, "ch"))

    block = shape((slot_rows, hid), bf16)
    sums = shape((len(EARLY) * slot_rows, hid), f32)
    grad_shape = shape((degree, rows, hid), bf16)
    for k in range(halves):
        hidden, grad_pre, scale = call(
            functools.partial(node_kernel, count, k * rows),
            (
                shape((hidden_all, rows), bf16),
                shape((hidden_all, rows), bf16),
                shape((rows, hid), f32),
            ),
            [degrees] + messages[k] + [w_both, w_both_t, pre, grad_hidden],
            scratch=[pltpu.VMEM((hidden_all, rows), bf16)],
            scalars=0,
        )
        hiddens.append(hidden)
        grad_pres.append(grad_pre)
        operands = [low_rows, high_rows, slopes[k], scale]
        if k == 0:
            grad, before = call(early_kernel, (grad_shape, sums), operands, scalars=0)
        else:
            to_cross, grad = call(
                functools.partial(cross_kernel, k * rows),
                (block, grad_shape),
                operands + [before, cross],
                scratch=[pltpu.VMEM((slot_rows, hid), f32)],
                scalars=0,
            )
            to_other = call(
                functools.partial(other_kernel, k * rows),
                shape((2, slot_rows, hid), bf16),
                [low_rows, high_rows, grad, before, west_too, east_too],
                scratch=[pltpu.VMEM((2 * slot_rows, hid), f32)],
                scalars=0,
            )
        grads.append(grad)

    grads[0], to_other = lax.optimization_barrier((grads[0], to_other))
    from_other = shifted(to_other, "sub", 1)
    from_cross = across(to_cross)
    to_west, to_east, to_beside = call(
        late_kernel,
        (block, block, block),
        [low_rows, high_rows] + grads + [west, east, beside],
        scratch=[pltpu.VMEM((len(LATE) * slot_rows, hid), f32)],
        scalars=0,
    )
    wide = shape((slot_rows, hid), f32)
    to_west, to_east = call(
        across_kernel, (wide, wide), [to_west, to_east, from_cross], scalars=0, flops=15 * 10**8
    )
    to_west, to_east = call(add_kernel, (block, block), [to_west, to_east, from_other], scalars=0)
    from_upper = shifted(to_west, "lon", -1)
    from_lower = shifted(to_east, "lon", 1)
    from_beside = shifted(to_beside, "sub", 1)
    to_west, grads[0] = lax.optimization_barrier((to_west, grads[0]))

    own, grad_recv = call(
        own_kernel,
        (shape((nodes, hid), f32), shape((hid, nodes), bf16)),
        [low_rows, high_rows] + grads,
        scalars=0,
    )
    own, hiddens[0] = lax.optimization_barrier((own, hiddens[0]))
    updated, direct = call(
        output_kernel,
        (shape((chans, nodes), bf16), shape((chans, nodes), f32)),
        [tile_count, features_held, cotangent, w_out_my, w_node_v_t] + hiddens + grad_pres,
        scalars=1,
    )
    columns = chans_all // shard_count
    inv_root = 1.0 / math.sqrt(total_nodes)
    inputs = [tile_count, own, from_beside, feats, from_upper]
    weight_shape = shape((chans_all, hid), f32)
    grad_shape = shape((rows, hid), bf16)
    def finish(k, grad_send, done):
        kept, sent = call(
            functools.partial(terms_kernel, k * rows),
            (shape((chans, rows), f32), shape((count - 1, chans, rows), bf16)),
            [grad_send, grad_recv, direct, w_send_t, w_recv_t],
            scratch=[pltpu.VMEM((chans_all, rows), f32)],
            scalars=0,
        )
        parts = [kept] + [shifted(sent[i - 1], "ch", i) for i in range(1, count)]
        out = call(
            functools.partial(finish_kernel, count),
            shape((chans, nodes - k * rows), bf16),
            parts + done,
            scalars=0,
        )
        return kept, out

    grad_send, weight = call(
        functools.partial(back_kernel, rows, inv_root),
        (grad_shape, weight_shape),
        inputs,
        scratch=[pltpu.VMEM((nodes, hid), f32)],
        scalars=1,
    )
    kept, upper_out = finish(1, grad_send, [])
    weight, kept = lax.optimization_barrier((weight, kept))
    grad_send, w_mine, w_beside = call(
        functools.partial(back_kernel, 0, inv_root),
        (grad_shape, shape((lons, columns, hid), f32), shape((lons, columns, hid), bf16)),
        inputs + [from_lower, weight],
        scratch=[pltpu.VMEM(weight_shape.shape, f32), pltpu.VMEM((nodes, hid), f32)],
        scalars=1,
    )
    w_beside = shifted(w_beside, "sub", 1)
    w_beside, upper_out = lax.optimization_barrier((w_beside, upper_out))
    near, w_sent = call(
        sum_kernel,
        (shape((columns, hid), f32), shape((lons - 1, columns, hid), bf16)),
        [w_mine, w_beside],
        scalars=0,
    )
    w_sent, grad_send = lax.optimization_barrier((w_sent, grad_send))
    w_terms = [
        lax.ppermute(w_sent[k - 1], "lon", [(i, i ^ k) for i in range(lons)])
        for k in range(1, lons)
    ]
    grad_w_send = call(
        weight_kernel,
        shape((columns, hid), f32),
        [near] + w_terms,
        scalars=0,
        flops=WEIGHT_FLOPS,
    )
    _, grad_features = finish(0, grad_send, [upper_out])
    return (updated, grad_features, grad_w_send.T)


def solution(mesh):
    nodes_last = P("ch", ("parts", "lon", "sub"))
    spread = ("parts", "lon", "sub")
    placed = (nodes_last, nodes_last, P(None, spread), P(spread), P(spread), P(spread, None, None))
    return jax.shard_map(
        shards,
        mesh=mesh,
        in_specs=placed + (P(),) * 8,
        out_specs=(nodes_last, nodes_last, P(("parts", "ch"), ("lon", "sub"))),
        check_vma=False,
    )
```

```python
import functools
import math

import jax
import jax.numpy as jnp
from jax import lax
from jax.experimental import pallas as pl
from jax.experimental.pallas import tpu as pltpu
from jax.sharding import PartitionSpec as P

TILE = 128
CHUNK = 256
LANES = 128
PACK = 16
MIB = 1 << 20
WEIGHTS_LIMIT = 52
NO_CHUNK = 64
SLOT_OF = ((3, 0), (1, 1), (4, 4), (2, 5), (0, 2), (5, 3))
EARLY, LATE = (3, 4, 5), (1, 2, 0)
OFF = -1e4


def shifted(block, axis, distance):
    size = lax.axis_size(axis)
    route = [((i - distance) % size, i) for i in range(size)]
    return lax.ppermute(block, axis, route)


def gathered(block, axis):
    return [block] + [shifted(block, axis, k) for k in range(1, lax.axis_size(axis))]


def dot(left, right):
    return jnp.dot(left, right, preferred_element_type=jnp.float32)


def dot_nt(left, right):
    return lax.dot_general(
        left, right, (((1,), (1,)), ((), ())), preferred_element_type=jnp.float32
    )


def sigmoid(value):
    return 0.5 * jnp.tanh(0.5 * value) + 0.5


def call(kernel, out_shape, operands, scratch=(), scalars=2, away=0, limit=24, flops=1024):
    vmem = pl.BlockSpec(memory_space=pltpu.VMEM)
    smem = pl.BlockSpec(memory_space=pltpu.SMEM)
    anywhere = pl.BlockSpec(memory_space=pltpu.HBM)
    return pl.pallas_call(
        kernel,
        out_shape=out_shape,
        in_specs=[smem] * scalars
        + [anywhere] * away
        + [vmem] * (len(operands) - scalars - away),
        out_specs=jax.tree.map(lambda _: vmem, out_shape),
        scratch_shapes=scratch,
        compiler_params=pltpu.CompilerParams(vmem_limit_bytes=limit * MIB),
        cost_estimate=pl.CostEstimate(flops=flops, bytes_accessed=1024, transcendentals=0),
    )(*operands)


def assemble(whole_ref, blocks, first):
    count = len(blocks)
    rows = blocks[0].shape[0]
    for k, block in enumerate(blocks):
        place = lax.rem(first - k + count, count) * rows
        whole_ref[pl.ds(pl.multiple_of(place, rows), rows), :] = block[...]


def mine_of(ref, index, rows):
    return ref[pl.ds(pl.multiple_of(index * rows, rows), rows), :]


def weights_kernel(*refs):
    sources, refs = refs[:7], refs[7:]
    w_send, w_recv, w_out, feats, w_send_t, w_recv_t, w_both_t, w_node_v_t, w_both, w_out_t = refs[:10]
    w_msg, w_node_v, w_node_a, w_out_all, turned, sems = refs[10:]
    mine = lax.axis_index("ch")
    hid = w_send.shape[0]
    targets = (w_msg, w_node_a, feats, w_send, w_recv, w_node_v, w_out_all)
    copies = []
    for k, (source, target) in enumerate(zip(sources, targets)):
        if k in (3, 4):
            source = source.at[pl.ds(pl.multiple_of(mine * hid, hid), hid), :]
        copies.append(pltpu.make_async_copy(source, target, sems.at[k]))
    for copy in copies:
        copy.start()
    for copy in copies[:2]:
        copy.wait()
    w_both[...] = dot(w_node_a[...], w_msg[...]).astype(jnp.bfloat16)
    turned[...] = w_both[...].T
    w_both_t[...] = mine_of(turned, mine, hid)
    for copy in copies[2:]:
        copy.wait()
    w_send_t[...] = w_send[...].T
    w_recv_t[...] = w_recv[...].T
    turned[...] = w_node_v[...].T
    w_node_v_t[...] = mine_of(turned, mine, w_node_v_t.shape[0])
    w_out_t[...] = w_out_all[...].T
    w_out[...] = mine_of(w_out_all, mine, w_out.shape[0])


def edges_kernel(tiles, senders, in_degree, low_cols, high_cols, low_rows, high_rows):
    degree, nodes = senders.shape
    lane = lax.broadcasted_iota(jnp.int32, (degree, nodes), 1)
    row = lax.broadcasted_iota(jnp.int32, (degree, nodes), 0)
    valid = (row < in_degree[...]) & (lane < tiles[0] * TILE)
    ids = senders[...]
    low = (ids & (CHUNK - 1)).astype(jnp.float32)
    high = jnp.where(valid, ids // CHUNK, NO_CHUNK).astype(jnp.float32)
    for m in range(degree):
        shape = (PACK, nodes)
        low_rows[m] = jnp.broadcast_to(low[m : m + 1], shape).astype(jnp.bfloat16)
        high_rows[m] = jnp.broadcast_to(high[m : m + 1], shape).astype(jnp.bfloat16)
    fill = jnp.zeros((PACK - degree, nodes), jnp.float32)
    depth = 2 * PACK
    both = jnp.concatenate([low, fill, high, fill], axis=0).T.astype(jnp.bfloat16)
    width = degree * LANES
    spot = lax.broadcasted_iota(jnp.int32, (depth, width), 0)
    group = lax.broadcasted_iota(jnp.int32, (depth, width), 1) // LANES
    for first, out in ((0, low_cols), (PACK, high_cols)):
        pick = (spot == group + first).astype(jnp.bfloat16)
        spread = dot(both, pick).astype(jnp.bfloat16)
        for m in range(degree):
            out[m] = spread[:, m * LANES : (m + 1) * LANES]


def project_kernel(count, tiles, picks, *refs):
    blocks = refs[:count]
    w_send, feats, proj, upper, lower, beside, cross = refs[count:]
    mine, sub = lax.axis_index("ch"), lax.axis_index("sub")
    first = tiles[0] // 2
    assemble(feats, blocks, mine)
    whole = feats[...]
    hid = proj.shape[1]
    proj[...] = (0.5 * dot(w_send[...], whole).T).astype(jnp.bfloat16)
    rows = upper.shape[0] - PACK
    upper[:rows, :] = proj[pl.ds(pl.multiple_of(first * TILE, TILE), rows), :]
    lower[:rows, :] = proj[:rows, :]
    spot = lax.broadcasted_iota(jnp.int32, (PACK, hid), 0)
    _, per_slot, slots = picks.shape
    half = slots // 2
    for start, out, lift in ((0, upper, first), (half, lower, 0)):
        marks = jnp.zeros((PACK, hid), jnp.float32)
        for k in range(half * per_slot):
            rel = picks[0, k % per_slot, start + k // per_slot] - lift
            marks = jnp.where(spot == k, rel.astype(jnp.float32), marks)
        out[rows:, :] = marks.astype(jnp.bfloat16)

    @pl.when(sub == 0)
    def _():
        beside[...] = upper[...]
        cross[...] = lower[...]

    @pl.when(sub != 0)
    def _():
        beside[...] = lower[...]
        cross[...] = upper[...]


def receive_kernel(bias, feats, w_recv, base):
    hid = base.shape[1]
    mine = lax.axis_index("ch")
    my_bias = jnp.zeros((1, hid), jnp.float32)
    for k in range(bias.shape[1] // hid):
        my_bias += jnp.where(mine == k, bias[:, k * hid : (k + 1) * hid], 0.0)
    recv = dot(w_recv[...], feats[...]).T
    base[...] = 0.5 * (recv.astype(jnp.bfloat16).astype(jnp.float32) + my_bias)


def prepare_kernel(count, tiles, *refs):
    blocks = refs[:count]
    feats, w_node_v, bias, w_out_t, cots, pre, grad_hidden = refs[count:]
    assemble(cots, blocks, lax.axis_index("ch"))
    column = jnp.broadcast_to(bias[...], (8, bias.shape[1])).T[:, :1]
    pre[...] = dot(w_node_v[...], feats[...]) + column
    lane = lax.broadcasted_iota(jnp.int32, (1, cots.shape[1]), 1)
    active = (lane < tiles[0] * TILE).astype(jnp.bfloat16)
    grad_hidden[...] = dot(w_out_t[...], cots[...] * active)


def chunk_of(place, first, shape):
    on_zero, on_one = (float(first + slot) for slot in SLOT_OF[place])
    chunk = jnp.where(lax.axis_index("sub") == 0, on_zero, on_one)
    return jnp.full(shape, chunk, jnp.float32).astype(jnp.bfloat16)


def picks_of(block, place):
    marks = block[CHUNK : CHUNK + PACK, :].astype(jnp.float32)
    per_slot = CHUNK // TILE
    half = len(SLOT_OF) // 2
    starts = [slot % half * per_slot for slot in SLOT_OF[place]]
    sub = lax.axis_index("sub")
    return [
        jnp.where(
            sub == 0,
            marks[starts[0] + t : starts[0] + t + 1],
            marks[starts[1] + t : starts[1] + t + 1],
        )
        for t in range(per_slot)
    ]


def fill(ext, start, block, place):
    for t, pick in enumerate(picks_of(block, place)):
        ext[start + t * TILE : start + (t + 1) * TILE, :] = jnp.where(
            pick > 0.5, block[TILE : 2 * TILE, :], block[:TILE, :]
        )


def pick_rows(low, high, chunks, ext):
    one = jnp.bfloat16(1.0)
    zero = jnp.bfloat16(0.0)
    lane = lax.broadcasted_iota(jnp.int32, low.shape, 1)
    marks = [
        jnp.where(low == (lane + half * LANES).astype(jnp.bfloat16), one, zero)
        for half in range(CHUNK // LANES)
    ]
    picker = jnp.concatenate(
        [jnp.where(high == chunk, mark, zero) for chunk in chunks for mark in marks], axis=1
    )
    return dot(picker, ext[...])


def near_kernel(low, high, proj, beside, part, ext):
    own = proj.shape[0]
    ext[:own, :] = proj[...]
    fill(ext, own, beside, 0)
    first = own // CHUNK
    chunks = [jnp.bfloat16(chunk) for chunk in range(first)]
    chunks.append(chunk_of(0, first, low.shape[1:]))

    def step(m, carry):
        part[m] = pick_rows(low[m], high[m], chunks, ext).astype(jnp.bfloat16)
        return carry

    lax.fori_loop(0, low.shape[0], step, 0, unroll=True)


def line_kernel(low, high, before, west, east, part, ext):
    first = low.shape[1] // CHUNK
    chunks = []
    for index, (place, block) in enumerate(((1, west), (2, east))):
        fill(ext, index * CHUNK, block, place)
        chunks.append(jnp.bfloat16(first + SLOT_OF[place][0]))

    def step(m, carry):
        more = pick_rows(low[m], high[m], chunks, ext)
        part[m] = (before[m].astype(jnp.float32) + more).astype(jnp.bfloat16)
        return carry

    lax.fori_loop(0, low.shape[0], step, 0, unroll=True)


def cross_rows_kernel(block, rows):
    fill(rows, 0, block, 3)


def message_kernel(
    start, low, high, base, in_degree, part, cross, west, east, message, slope, ext, total
):
    nodes = low.shape[1]
    degree, rows, hid = slope.shape
    first = nodes // CHUNK
    together = nodes // rows
    span = slice(start, start + rows)
    chunks = []
    ext[:CHUNK, :] = cross[...]
    for index, (place, block) in enumerate(((4, west), (5, east))):
        fill(ext, (index + 1) * CHUNK, block, place)
    for place in (3, 4, 5):
        chunks.append(chunk_of(place, first, (nodes, LANES)))
    total[...] = jnp.zeros_like(total)

    def rows_of(ref, k):
        return jnp.concatenate([ref[k * together + i, span, :] for i in range(together)], axis=0)

    def step(k, carry):
        low_k, high_k = rows_of(low, k), rows_of(high, k)
        half = pick_rows(low_k, high_k, chunks, ext) + rows_of(part, k).astype(jnp.float32)
        half += jnp.concatenate([base[span, :]] * together, axis=0)
        wide = jnp.concatenate([high_k] * pl.cdiv(hid, LANES), axis=1)[:, :hid]
        half = jnp.where(wide.astype(jnp.float32) < NO_CHUNK, half, OFF)
        twice = jnp.tanh(half) + 1.0
        act = half * twice
        grad = (twice + act * (2.0 - twice)).astype(jnp.bfloat16)
        terms = 0.0
        for i in range(together):
            terms += act[i * rows : (i + 1) * rows]
            slope[k * together + i] = grad[i * rows : (i + 1) * rows]
        total[...] += terms
        return carry

    lax.fori_loop(0, degree // together, step, 0, unroll=True)
    count = in_degree[:, span].astype(jnp.float32)
    message[...] = (total[...].T / count).astype(jnp.bfloat16)


def node_kernel(count, start, in_degree, *refs):
    blocks = refs[:count]
    w_both, w_both_t, pre, grad_hidden = refs[count : count + 4]
    hidden, grad_pre, scale, messages = refs[count + 4 :]
    assemble(messages, blocks, lax.axis_index("ch"))
    span = slice(start, start + hidden.shape[1])
    half = 0.5 * (pre[:, span] + dot(w_both[...], messages[...]))
    twice = jnp.tanh(half) + 1.0
    act = half * twice
    hidden[...] = act.astype(jnp.bfloat16)
    slope = 0.5 * (twice + act * (2.0 - twice))
    low_grad = (grad_hidden[:, span] * slope).astype(jnp.bfloat16)
    grad_pre[...] = low_grad
    grad_msg = dot(w_both_t[...], low_grad).astype(jnp.bfloat16).astype(jnp.float32)
    scale[...] = (grad_msg * (0.5 / in_degree[:, span].astype(jnp.float32))).T


def scatter(low, high, edges, chunks, total):
    one = jnp.bfloat16(1.0)
    zero = jnp.bfloat16(0.0)
    groups = CHUNK // PACK
    for step in edges:
        width = sum(rows for _, _, rows, _ in step)
        place = lax.broadcasted_iota(jnp.int32, (groups, PACK, width), 0) * PACK
        place = place + lax.broadcasted_iota(jnp.int32, (groups, PACK, width), 1)
        low_k = jnp.concatenate([low[m, :, s : s + r] for m, s, r, _ in step], axis=1)
        high_k = jnp.concatenate([high[m, :, s : s + r] for m, s, r, _ in step], axis=1)
        grads = jnp.concatenate([grad() for _, _, _, grad in step], axis=0)
        mark = jnp.where(low_k[None] == place.astype(jnp.bfloat16), one, zero)
        picker = jnp.concatenate(
            [jnp.where(high_k[None] == chunk, mark, zero) for chunk in chunks], axis=0
        ).reshape(len(chunks) * CHUNK, width)
        total[...] += dot(picker, grads)


def pairs(start, ref, nodes, grad_of):
    degree, rows, _ = ref.shape
    together = nodes // rows
    return [
        [
            (m, start, rows, functools.partial(grad_of, ref, m))
            for m in range(k * together, (k + 1) * together)
        ]
        for k in range(degree // together)
    ]


def fold(block, place, index, total):
    picks = picks_of(block, place)
    halves = []
    for half in range(len(picks)):
        terms = 0.0
        for t, pick in enumerate(picks):
            start = index * CHUNK + t * TILE
            hit = jnp.abs(pick - half) < 0.5
            terms += jnp.where(hit, total[start : start + TILE, :], 0.0)
        halves.append(terms)
    return jnp.concatenate(halves, axis=0).astype(jnp.bfloat16)


def early_kernel(low, high, slope, scale, grads, total):
    nodes = low.shape[2]

    def grad_of(ref, m):
        grads[m] = (ref[m].astype(jnp.float32) * scale[...]).astype(jnp.bfloat16)
        return grads[m]

    chunks = [chunk_of(place, nodes // CHUNK, (1, PACK, nodes)) for place in EARLY + LATE]
    total[...] = jnp.zeros_like(total)
    scatter(low, high, pairs(0, slope, nodes, grad_of), chunks, total)


def cross_kernel(start, low, high, slope, scale, before, cross, to_cross, grads, total):
    nodes = low.shape[2]

    def grad_of(ref, m):
        grads[m] = (ref[m].astype(jnp.float32) * scale[...]).astype(jnp.bfloat16)
        return grads[m]

    chunks = [chunk_of(EARLY[0], nodes // CHUNK, (1, PACK, nodes))]
    total[...] = before[:CHUNK, :]
    scatter(low, high, pairs(start, slope, nodes, grad_of), chunks, total)
    to_cross[...] = fold(cross, EARLY[0], 0, total)


def other_kernel(start, low, high, grads, before, west, east, to_other, total):
    nodes = low.shape[2]
    chunks = [chunk_of(place, nodes // CHUNK, (1, PACK, nodes)) for place in EARLY[1:]]
    total[...] = before[CHUNK : len(EARLY) * CHUNK, :]
    scatter(low, high, pairs(start, grads, nodes, lambda ref, m: ref[m]), chunks, total)
    to_other[0] = fold(west, EARLY[1], 0, total)
    to_other[1] = fold(east, EARLY[2], 1, total)


def all_pairs(parts, nodes):
    start, steps = 0, []
    for part in parts:
        steps += pairs(start, part, nodes, lambda ref, m: ref[m])
        start += part.shape[1]
    return steps


def late_kernel(
    start, low, high, grads, before, west, east, beside, to_west, to_east, to_beside, total
):
    nodes = low.shape[2]
    chunks = [chunk_of(place, nodes // CHUNK, (1, PACK, nodes)) for place in LATE]
    total[...] = before[len(EARLY) * CHUNK :, :]
    scatter(low, high, pairs(start, grads, nodes, lambda ref, m: ref[m]), chunks, total)
    to_west[...] = fold(west, 1, 0, total)
    to_east[...] = fold(east, 2, 1, total)
    to_beside[...] = fold(beside, 0, 2, total)


def own_kernel(low, high, *refs):
    *parts, total, recv = refs
    nodes = low.shape[2]
    chunks = [jnp.bfloat16(chunk) for chunk in range(nodes // CHUNK)]
    total[...] = jnp.zeros_like(total)
    scatter(low, high, all_pairs(parts, nodes), chunks, total)
    start = 0
    for part in parts:
        degree, rows, _ = part.shape
        terms = 0.0
        for m in range(degree):
            terms += part[m].astype(jnp.float32)
        recv[:, start : start + rows] = terms.T.astype(jnp.bfloat16)
        start += rows


def output_kernel(tiles, feats, cots, w_out, w_node_v_t, *refs):
    *parts, updated, direct = refs
    count = len(parts) // 2
    rows = parts[0].shape[1]
    for k in range(count):
        hidden, grad_pre = parts[k], parts[count + k]
        span = slice(k * rows, (k + 1) * rows)
        lane = lax.broadcasted_iota(jnp.int32, (1, rows), 1) + k * rows
        active = (lane < tiles[0] * TILE).astype(jnp.float32)
        node_out = dot(w_out[...], hidden[...])
        new = feats[:, span].astype(jnp.float32) + active * node_out
        updated[:, span] = new.astype(jnp.bfloat16)
        direct[:, span] = cots[:, span].astype(jnp.float32) + dot(w_node_v_t[...], grad_pre[...])


def across_kernel(left, right, across, west, east):
    sub = lax.axis_index("sub")
    other = across[...].astype(jnp.float32)
    to_west = left[...].astype(jnp.float32) + jnp.where(sub == 0, 0.0, other)
    to_east = right[...].astype(jnp.float32) + jnp.where(sub == 0, other, 0.0)
    west[...] = to_west.astype(west.dtype)
    east[...] = to_east.astype(east.dtype)


def add_kernel(left, right, more, west, east):
    west[...] = (left[...] + more[0].astype(jnp.float32)).astype(jnp.bfloat16)
    east[...] = (right[...] + more[1].astype(jnp.float32)).astype(jnp.bfloat16)


def back_kernel(start, inv_root, tiles, own, beside, feats, upper, *refs):
    *refs, total = refs
    sub = lax.axis_index("sub")
    offset = pl.multiple_of(tiles[0] // 2 * TILE, TILE)
    total[...] = own[...]
    near = beside[...].astype(jnp.float32)
    block = upper[...].astype(jnp.float32) + jnp.where(sub == 0, near, 0.0)
    total[pl.ds(offset, block.shape[0]), :] += block
    if start:
        grad_send, weight = refs
    else:
        lower, before, grad_send, w_mine, w_beside, weight = refs
        block = lower[...].astype(jnp.float32) + jnp.where(sub == 0, 0.0, near)
        total[: block.shape[0], :] += block
    rows = grad_send.shape[0]
    grad_send[...] = total[start : start + rows, :].astype(jnp.bfloat16)
    terms = dot(feats[:, start : start + rows], grad_send[...])
    if start:
        weight[...] = terms
        return
    weight[...] = (before[...] + terms) * inv_root
    lon = lax.axis_index("lon")
    lons, columns, _ = w_mine.shape
    for k in range(lons):
        band = (lon ^ k) * 2
        for out, core in ((w_mine, sub), (w_beside, 1 - sub)):
            spot = pl.multiple_of((band + core) * columns, columns)
            out[k] = weight[pl.ds(spot, columns), :].astype(out.dtype)


def terms_kernel(start, grad_send, recv, direct, w_send_t, w_recv_t, kept, sent, terms):
    span = slice(start, start + grad_send.shape[0])
    mine = lax.axis_index("ch")
    chans = kept.shape[0]
    grad_send_t = grad_send[...].astype(jnp.float32).T.astype(jnp.bfloat16)
    terms[...] = dot(w_send_t[...], grad_send_t) + dot(w_recv_t[...], recv[:, span])
    kept[...] = direct[:, span] + mine_of(terms, mine, chans)
    count = sent.shape[0] + 1
    for k in range(1, count):
        sent[k - 1] = mine_of(terms, lax.rem(mine + k, count), chans).astype(jnp.bfloat16)


def finish_kernel(count, *refs):
    kept, *others = refs[: count]
    *done, out = refs[count:]
    total = kept[...]
    for other in others:
        total += other[...].astype(jnp.float32)
    out[:, : kept.shape[1]] = total.astype(jnp.bfloat16)
    start = kept.shape[1]
    for part in done:
        out[:, start : start + part.shape[1]] = part[...]
        start += part.shape[1]


def sum_kernel(held, received, near, sent):
    half = near.shape[0]
    near[...] = held[:half] + received[:half].astype(jnp.float32)
    sent[...] = (held[half:] + received[half:].astype(jnp.float32)).astype(jnp.bfloat16)


def weight_kernel(held, received, out):
    out[...] = held[0] + received[0].astype(jnp.float32)


def shards(
    features,
    cotangent,
    senders,
    in_degree,
    tile_count,
    send_tiles,
    w_send,
    w_recv,
    bias_edge,
    w_msg,
    w_node_v,
    w_node_a,
    bias_node,
    w_out,
):
    chans, nodes = features.shape
    count = lax.axis_size("ch")
    lons = lax.axis_size("lon")
    hidden_all, chans_all = w_send.shape
    hid = hidden_all // count
    cycle = ("lon", "sub")
    shard_count = lax.axis_size(cycle)
    total_nodes = nodes * shard_count
    degree = senders.shape[0]
    slots = send_tiles.shape[1]
    slot_rows = send_tiles.shape[2] * TILE
    ext_len = nodes + slots * slot_rows
    bf16, f32 = jnp.bfloat16, jnp.float32
    shape = jax.ShapeDtypeStruct

    far_route = [(i, (i + (3 if i % 2 else -3)) % shard_count) for i in range(shard_count)]
    across_route = [(i, (i + (1 if i % 2 else -1)) % shard_count) for i in range(shard_count)]
    across = lambda block: lax.ppermute(block, cycle, across_route)
    degrees = in_degree[None, :]
    picks = jnp.transpose(send_tiles, (0, 2, 1))
    sub = lax.axis_index("sub")

    feat_blocks = gathered(features, "ch")

    whole_w = pltpu.VMEM((chans_all, hidden_all), bf16)
    (
        w_send_my,
        w_recv_my,
        w_out_my,
        features_held,
        w_send_t,
        w_recv_t,
        w_both_t,
        w_node_v_t,
        w_both,
        w_out_t,
    ) = call(
        weights_kernel,
        (
            shape((hid, chans_all), bf16),
            shape((hid, chans_all), bf16),
            shape((chans, hidden_all), bf16),
            shape((chans, nodes), bf16),
            shape((chans_all, hid), bf16),
            shape((chans_all, hid), bf16),
            shape((hid, hidden_all), bf16),
            shape((chans, hidden_all), bf16),
            shape((hidden_all, hidden_all), bf16),
            shape((hidden_all, chans_all), bf16),
        ),
        [w_msg, w_node_a, features, w_send, w_recv, w_node_v, w_out],
        away=7,
        scalars=0,
        scratch=[whole_w] * 5 + [pltpu.SemaphoreType.DMA((7,))],
        limit=WEIGHTS_LIMIT,
    )
    feat_blocks[0] = features_held

    block = shape((slot_rows + PACK, hid), bf16)
    feats, proj, upper, lower, beside, cross = call(
        functools.partial(project_kernel, count),
        (
            shape((chans_all, nodes), bf16),
            shape((nodes, hid), bf16),
            block,
            block,
            block,
            block,
        ),
        [tile_count, picks] + feat_blocks + [w_send_my],
    )
    west = shifted(upper, "lon", 1)
    east = shifted(lower, "lon", -1)
    cross = lax.ppermute(cross, cycle, far_route)
    base = call(
        receive_kernel,
        shape((nodes, hid), f32),
        [bias_edge[None, :], feats, w_recv_my],
        scalars=0,
    )
    base, senders, cotangent_late = lax.optimization_barrier((base, senders, cotangent))
    beside = shifted(beside, "sub", 1)
    cot_blocks = gathered(cotangent_late, "ch")
    low_cols, high_cols, low_rows, high_rows = call(
        edges_kernel,
        (
            shape((degree, nodes, LANES), bf16),
            shape((degree, nodes, LANES), bf16),
            shape((degree, PACK, nodes), bf16),
            shape((degree, PACK, nodes), bf16),
        ),
        [tile_count, senders, degrees],
        scalars=1,
    )
    cots, pre, grad_hidden = call(
        functools.partial(prepare_kernel, count),
        (
            shape((chans_all, nodes), bf16),
            shape((hidden_all, nodes), f32),
            shape((hidden_all, nodes), f32),
        ),
        [tile_count] + cot_blocks + [feats, w_node_v, bias_node[None, :], w_out_t],
        scalars=1,
    )

    part_shape = shape((degree, nodes, hid), bf16)
    part = call(
        near_kernel,
        part_shape,
        [low_cols, high_cols, proj, beside],
        scratch=[pltpu.VMEM((nodes + slot_rows, hid), bf16)],
        scalars=0,
    )
    west, east, part = lax.optimization_barrier((west, east, part))
    west_too = shifted(west, "sub", 1)
    east_too = shifted(east, "sub", 1)
    part, pre = lax.optimization_barrier((part, pre))
    part = call(
        line_kernel,
        part_shape,
        [low_cols, high_cols, part, west, east],
        scratch=[pltpu.VMEM((2 * slot_rows, hid), bf16)],
        scalars=0,
    )
    part, cross = lax.optimization_barrier((part, cross))
    cross_rows = call(
        cross_rows_kernel, shape((slot_rows, hid), bf16), [cross], scalars=0
    )
    halves = 2
    rows = nodes // halves
    slopes, messages, hiddens, grad_pres, grads = [], [], [], [], []
    for k in range(halves):
        message, slope = call(
            functools.partial(message_kernel, k * rows),
            (shape((hid, rows), bf16), shape((degree, rows, hid), bf16)),
            [low_cols, high_cols, base, degrees, part, cross_rows, west_too, east_too],
            scratch=[pltpu.VMEM((3 * slot_rows, hid), bf16), pltpu.VMEM((rows, hid), f32)],
            scalars=0,
        )
        slopes.append(slope)
        messages.append(gathered(message, "ch"))

    block = shape((slot_rows, hid), bf16)
    sums = shape((slots * slot_rows, hid), f32)
    grad_shape = shape((degree, rows, hid), bf16)
    for k in range(halves):
        hidden, grad_pre, scale = call(
            functools.partial(node_kernel, count, k * rows),
            (
                shape((hidden_all, rows), bf16),
                shape((hidden_all, rows), bf16),
                shape((rows, hid), f32),
            ),
            [degrees] + messages[k] + [w_both, w_both_t, pre, grad_hidden],
            scratch=[pltpu.VMEM((hidden_all, rows), bf16)],
            scalars=0,
        )
        hiddens.append(hidden)
        grad_pres.append(grad_pre)
        operands = [low_rows, high_rows, slopes[k], scale]
        if k == 0:
            grad, before = call(early_kernel, (grad_shape, sums), operands, scalars=0)
        else:
            to_cross, grad = call(
                functools.partial(cross_kernel, k * rows),
                (block, grad_shape),
                operands + [before, cross],
                scratch=[pltpu.VMEM((slot_rows, hid), f32)],
                scalars=0,
            )
            to_other = call(
                functools.partial(other_kernel, k * rows),
                shape((2, slot_rows, hid), bf16),
                [low_rows, high_rows, grad, before, west_too, east_too],
                scratch=[pltpu.VMEM((2 * slot_rows, hid), f32)],
                scalars=0,
            )
        grads.append(grad)

    before, to_other = lax.optimization_barrier((before, to_other))
    from_other = shifted(to_other, "sub", 1)
    from_cross = across(to_cross)
    to_west, to_east, to_beside = call(
        functools.partial(late_kernel, nodes - rows),
        (block, block, block),
        [low_rows, high_rows, grads[-1], before, west, east, beside],
        scratch=[pltpu.VMEM((len(LATE) * slot_rows, hid), f32)],
        scalars=0,
    )
    wide = shape((slot_rows, hid), f32)
    to_west, to_east = call(
        across_kernel, (wide, wide), [to_west, to_east, from_cross], scalars=0, flops=15 * 10**8
    )
    to_west, to_east = call(add_kernel, (block, block), [to_west, to_east, from_other], scalars=0)
    from_upper = shifted(to_west, "lon", -1)
    from_lower = shifted(to_east, "lon", 1)
    from_beside = shifted(to_beside, "sub", 1)
    to_west, grads[0] = lax.optimization_barrier((to_west, grads[0]))

    own, grad_recv = call(
        own_kernel,
        (shape((nodes, hid), f32), shape((hid, nodes), bf16)),
        [low_rows, high_rows] + grads,
        scalars=0,
    )
    own, hiddens[0] = lax.optimization_barrier((own, hiddens[0]))
    updated, direct = call(
        output_kernel,
        (shape((chans, nodes), bf16), shape((chans, nodes), f32)),
        [tile_count, features_held, cotangent, w_out_my, w_node_v_t] + hiddens + grad_pres,
        scalars=1,
    )
    columns = chans_all // shard_count
    inv_root = 1.0 / math.sqrt(total_nodes)
    inputs = [tile_count, own, from_beside, feats, from_upper]
    weight_shape = shape((chans_all, hid), f32)
    grad_shape = shape((rows, hid), bf16)
    finals = []
    for k in reversed(range(halves)):
        kernel = functools.partial(back_kernel, k * rows, inv_root)
        if k:
            grad_send, weight = call(
                kernel,
                (grad_shape, weight_shape),
                inputs,
                scratch=[pltpu.VMEM((nodes, hid), f32)],
                scalars=1,
            )
        else:
            grad_send, w_mine, w_beside = call(
                kernel,
                (
                    grad_shape,
                    shape((lons, columns, hid), f32),
                    shape((lons, columns, hid), bf16),
                ),
                inputs + [from_lower, weight],
                scratch=[pltpu.VMEM(weight_shape.shape, f32), pltpu.VMEM((nodes, hid), f32)],
                scalars=1,
            )
            w_beside = shifted(w_beside, "sub", 1)
            w_beside, *finals = lax.optimization_barrier((w_beside, *finals))
        kept, sent = call(
            functools.partial(terms_kernel, k * rows),
            (shape((chans, rows), f32), shape((count - 1, chans, rows), bf16)),
            [grad_send, grad_recv, direct, w_send_t, w_recv_t],
            scratch=[pltpu.VMEM((chans_all, rows), f32)],
            scalars=0,
        )
        if k:
            weight, kept = lax.optimization_barrier((weight, kept))
        parts = [kept] + [shifted(sent[i - 1], "ch", i) for i in range(1, count)]
        grad_features = call(
            functools.partial(finish_kernel, count),
            shape((chans, nodes - k * rows), bf16),
            parts + finals,
            scalars=0,
        )
        finals = [grad_features]

    span = lons
    while span > 1:
        span //= 2
        w_mine, w_sent = call(
            sum_kernel,
            (shape((span, columns, hid), f32), shape((span, columns, hid), bf16)),
            [w_mine, w_beside],
            scalars=0,
        )
        w_beside = lax.ppermute(w_sent, "lon", [(i, i ^ span) for i in range(lons)])
    grad_w_send = call(
        weight_kernel, shape((columns, hid), f32), [w_mine, w_beside], scalars=0
    )
    return (updated, grad_features, grad_w_send.T)


def solution(mesh):
    nodes_last = P("ch", ("parts", "lon", "sub"))
    spread = ("parts", "lon", "sub")
    placed = (nodes_last, nodes_last, P(None, spread), P(spread), P(spread), P(spread, None, None))
    return jax.shard_map(
        shards,
        mesh=mesh,
        in_specs=placed + (P(),) * 8,
        out_specs=(nodes_last, nodes_last, P(("parts", "ch"), ("lon", "sub"))),
        check_vma=False,
    )
```

```python
import functools
import math

import jax
import jax.numpy as jnp
from jax import lax
from jax.experimental import pallas as pl
from jax.experimental.pallas import tpu as pltpu
from jax.sharding import PartitionSpec as P

TILE = 128
CHUNK = 256
LANES = 128
PACK = 16
MIB = 1 << 20
WEIGHTS_LIMIT = 52
NO_CHUNK = 64
SLOT_OF = ((3, 0), (1, 1), (4, 4), (2, 5), (0, 2), (5, 3))
EARLY, LATE = (3, 4, 5), (1, 2, 0)
OFF = -1e4


def shifted(block, axis, distance):
    size = lax.axis_size(axis)
    route = [((i - distance) % size, i) for i in range(size)]
    return lax.ppermute(block, axis, route)


def gathered(block, axis):
    return [block] + [shifted(block, axis, k) for k in range(1, lax.axis_size(axis))]


def dot(left, right):
    return jnp.dot(left, right, preferred_element_type=jnp.float32)


def dot_nt(left, right):
    return lax.dot_general(
        left, right, (((1,), (1,)), ((), ())), preferred_element_type=jnp.float32
    )


def sigmoid(value):
    return 0.5 * jnp.tanh(0.5 * value) + 0.5


def call(kernel, out_shape, operands, scratch=(), scalars=2, away=0, limit=24, flops=1024):
    vmem = pl.BlockSpec(memory_space=pltpu.VMEM)
    smem = pl.BlockSpec(memory_space=pltpu.SMEM)
    anywhere = pl.BlockSpec(memory_space=pltpu.HBM)
    return pl.pallas_call(
        kernel,
        out_shape=out_shape,
        in_specs=[smem] * scalars
        + [anywhere] * away
        + [vmem] * (len(operands) - scalars - away),
        out_specs=jax.tree.map(lambda _: vmem, out_shape),
        scratch_shapes=scratch,
        compiler_params=pltpu.CompilerParams(vmem_limit_bytes=limit * MIB),
        cost_estimate=pl.CostEstimate(flops=flops, bytes_accessed=1024, transcendentals=0),
    )(*operands)


def assemble(whole_ref, blocks, first):
    count = len(blocks)
    rows = blocks[0].shape[0]
    for k, block in enumerate(blocks):
        place = lax.rem(first - k + count, count) * rows
        whole_ref[pl.ds(pl.multiple_of(place, rows), rows), :] = block[...]


def mine_of(ref, index, rows):
    return ref[pl.ds(pl.multiple_of(index * rows, rows), rows), :]


def weights_kernel(*refs):
    sources, refs = refs[:7], refs[7:]
    w_send, w_recv, w_out, feats, w_send_t, w_recv_t, w_both_t, w_node_v_t, w_both, w_out_t = refs[:10]
    w_msg, w_node_v, w_node_a, w_out_all, turned, sems = refs[10:]
    mine = lax.axis_index("ch")
    hid = w_send.shape[0]
    targets = (w_msg, w_node_a, feats, w_send, w_recv, w_node_v, w_out_all)
    copies = []
    for k, (source, target) in enumerate(zip(sources, targets)):
        if k in (3, 4):
            source = source.at[pl.ds(pl.multiple_of(mine * hid, hid), hid), :]
        copies.append(pltpu.make_async_copy(source, target, sems.at[k]))
    for copy in copies:
        copy.start()
    for copy in copies[:2]:
        copy.wait()
    w_both[...] = dot(w_node_a[...], w_msg[...]).astype(jnp.bfloat16)
    turned[...] = w_both[...].T
    w_both_t[...] = mine_of(turned, mine, hid)
    for copy in copies[2:]:
        copy.wait()
    w_send_t[...] = w_send[...].T
    w_recv_t[...] = w_recv[...].T
    turned[...] = w_node_v[...].T
    w_node_v_t[...] = mine_of(turned, mine, w_node_v_t.shape[0])
    w_out_t[...] = w_out_all[...].T
    w_out[...] = mine_of(w_out_all, mine, w_out.shape[0])


def edges_kernel(tiles, senders, in_degree, low_cols, high_cols, low_rows, high_rows):
    degree, nodes = senders.shape
    lane = lax.broadcasted_iota(jnp.int32, (degree, nodes), 1)
    row = lax.broadcasted_iota(jnp.int32, (degree, nodes), 0)
    valid = (row < in_degree[...]) & (lane < tiles[0] * TILE)
    ids = senders[...]
    low = (ids & (CHUNK - 1)).astype(jnp.float32)
    high = jnp.where(valid, ids // CHUNK, NO_CHUNK).astype(jnp.float32)
    for m in range(degree):
        shape = (PACK, nodes)
        low_rows[m] = jnp.broadcast_to(low[m : m + 1], shape).astype(jnp.bfloat16)
        high_rows[m] = jnp.broadcast_to(high[m : m + 1], shape).astype(jnp.bfloat16)
    fill = jnp.zeros((PACK - degree, nodes), jnp.float32)
    depth = 2 * PACK
    both = jnp.concatenate([low, fill, high, fill], axis=0).T.astype(jnp.bfloat16)
    width = degree * LANES
    spot = lax.broadcasted_iota(jnp.int32, (depth, width), 0)
    group = lax.broadcasted_iota(jnp.int32, (depth, width), 1) // LANES
    for first, out in ((0, low_cols), (PACK, high_cols)):
        pick = (spot == group + first).astype(jnp.bfloat16)
        spread = dot(both, pick).astype(jnp.bfloat16)
        for m in range(degree):
            out[m] = spread[:, m * LANES : (m + 1) * LANES]


def project_kernel(count, tiles, picks, *refs):
    blocks = refs[:count]
    w_send, feats, proj, upper, lower, beside, cross = refs[count:]
    mine, sub = lax.axis_index("ch"), lax.axis_index("sub")
    first = tiles[0] // 2
    assemble(feats, blocks, mine)
    whole = feats[...]
    hid = proj.shape[1]
    proj[...] = (0.5 * dot(w_send[...], whole).T).astype(jnp.bfloat16)
    rows = upper.shape[0] - PACK
    upper[:rows, :] = proj[pl.ds(pl.multiple_of(first * TILE, TILE), rows), :]
    lower[:rows, :] = proj[:rows, :]
    spot = lax.broadcasted_iota(jnp.int32, (PACK, hid), 0)
    _, per_slot, slots = picks.shape
    half = slots // 2
    for start, out, lift in ((0, upper, first), (half, lower, 0)):
        marks = jnp.zeros((PACK, hid), jnp.float32)
        for k in range(half * per_slot):
            rel = picks[0, k % per_slot, start + k // per_slot] - lift
            marks = jnp.where(spot == k, rel.astype(jnp.float32), marks)
        out[rows:, :] = marks.astype(jnp.bfloat16)

    @pl.when(sub == 0)
    def _():
        beside[...] = upper[...]
        cross[...] = lower[...]

    @pl.when(sub != 0)
    def _():
        beside[...] = lower[...]
        cross[...] = upper[...]


def receive_kernel(bias, feats, w_recv, base):
    hid = base.shape[1]
    mine = lax.axis_index("ch")
    my_bias = jnp.zeros((1, hid), jnp.float32)
    for k in range(bias.shape[1] // hid):
        my_bias += jnp.where(mine == k, bias[:, k * hid : (k + 1) * hid], 0.0)
    recv = dot(w_recv[...], feats[...]).T
    base[...] = 0.5 * (recv.astype(jnp.bfloat16).astype(jnp.float32) + my_bias)


def prepare_kernel(count, tiles, *refs):
    blocks = refs[:count]
    feats, w_node_v, bias, w_out_t, cots, pre, grad_hidden = refs[count:]
    assemble(cots, blocks, lax.axis_index("ch"))
    column = jnp.broadcast_to(bias[...], (8, bias.shape[1])).T[:, :1]
    pre[...] = dot(w_node_v[...], feats[...]) + column
    lane = lax.broadcasted_iota(jnp.int32, (1, cots.shape[1]), 1)
    active = (lane < tiles[0] * TILE).astype(jnp.bfloat16)
    grad_hidden[...] = dot(w_out_t[...], cots[...] * active)


def chunk_of(place, first, shape):
    on_zero, on_one = (float(first + slot) for slot in SLOT_OF[place])
    chunk = jnp.where(lax.axis_index("sub") == 0, on_zero, on_one)
    return jnp.full(shape, chunk, jnp.float32).astype(jnp.bfloat16)


def picks_of(block, place):
    marks = block[CHUNK : CHUNK + PACK, :].astype(jnp.float32)
    per_slot = CHUNK // TILE
    half = len(SLOT_OF) // 2
    starts = [slot % half * per_slot for slot in SLOT_OF[place]]
    sub = lax.axis_index("sub")
    return [
        jnp.where(
            sub == 0,
            marks[starts[0] + t : starts[0] + t + 1],
            marks[starts[1] + t : starts[1] + t + 1],
        )
        for t in range(per_slot)
    ]


def fill(ext, start, block, place):
    for t, pick in enumerate(picks_of(block, place)):
        ext[start + t * TILE : start + (t + 1) * TILE, :] = jnp.where(
            pick > 0.5, block[TILE : 2 * TILE, :], block[:TILE, :]
        )


def pick_rows(low, high, chunks, ext):
    one = jnp.bfloat16(1.0)
    zero = jnp.bfloat16(0.0)
    lane = lax.broadcasted_iota(jnp.int32, low.shape, 1)
    marks = [
        jnp.where(low == (lane + half * LANES).astype(jnp.bfloat16), one, zero)
        for half in range(CHUNK // LANES)
    ]
    picker = jnp.concatenate(
        [jnp.where(high == chunk, mark, zero) for chunk in chunks for mark in marks], axis=1
    )
    return dot(picker, ext[...])


def near_kernel(low, high, proj, beside, part, ext):
    own = proj.shape[0]
    ext[:own, :] = proj[...]
    fill(ext, own, beside, 0)
    first = own // CHUNK
    chunks = [jnp.bfloat16(chunk) for chunk in range(first)]
    chunks.append(chunk_of(0, first, low.shape[1:]))

    def step(m, carry):
        part[m] = pick_rows(low[m], high[m], chunks, ext).astype(jnp.bfloat16)
        return carry

    lax.fori_loop(0, low.shape[0], step, 0, unroll=True)


def line_kernel(low, high, before, west, east, part, ext):
    first = low.shape[1] // CHUNK
    chunks = []
    for index, (place, block) in enumerate(((1, west), (2, east))):
        fill(ext, index * CHUNK, block, place)
        chunks.append(jnp.bfloat16(first + SLOT_OF[place][0]))

    def step(m, carry):
        more = pick_rows(low[m], high[m], chunks, ext)
        part[m] = (before[m].astype(jnp.float32) + more).astype(jnp.bfloat16)
        return carry

    lax.fori_loop(0, low.shape[0], step, 0, unroll=True)


def cross_rows_kernel(block, rows):
    fill(rows, 0, block, 3)


def message_kernel(
    start, low, high, base, in_degree, part, cross, west, east, message, slope, ext, total
):
    nodes = low.shape[1]
    degree, rows, hid = slope.shape
    first = nodes // CHUNK
    together = nodes // rows
    span = slice(start, start + rows)
    chunks = []
    ext[:CHUNK, :] = cross[...]
    for index, (place, block) in enumerate(((4, west), (5, east))):
        fill(ext, (index + 1) * CHUNK, block, place)
    for place in (3, 4, 5):
        chunks.append(chunk_of(place, first, (nodes, LANES)))
    total[...] = jnp.zeros_like(total)

    def rows_of(ref, k):
        return jnp.concatenate([ref[k * together + i, span, :] for i in range(together)], axis=0)

    def step(k, carry):
        low_k, high_k = rows_of(low, k), rows_of(high, k)
        half = pick_rows(low_k, high_k, chunks, ext) + rows_of(part, k).astype(jnp.float32)
        half += jnp.concatenate([base[span, :]] * together, axis=0)
        wide = jnp.concatenate([high_k] * pl.cdiv(hid, LANES), axis=1)[:, :hid]
        half = jnp.where(wide.astype(jnp.float32) < NO_CHUNK, half, OFF)
        twice = jnp.tanh(half) + 1.0
        act = half * twice
        grad = (twice + act * (2.0 - twice)).astype(jnp.bfloat16)
        terms = 0.0
        for i in range(together):
            terms += act[i * rows : (i + 1) * rows]
            slope[k * together + i] = grad[i * rows : (i + 1) * rows]
        total[...] += terms
        return carry

    lax.fori_loop(0, degree // together, step, 0, unroll=True)
    count = in_degree[:, span].astype(jnp.float32)
    message[...] = (total[...].T / count).astype(jnp.bfloat16)


def node_kernel(count, start, in_degree, *refs):
    blocks = refs[:count]
    w_both, w_both_t, pre, grad_hidden = refs[count : count + 4]
    hidden, grad_pre, scale, messages = refs[count + 4 :]
    assemble(messages, blocks, lax.axis_index("ch"))
    span = slice(start, start + hidden.shape[1])
    half = 0.5 * (pre[:, span] + dot(w_both[...], messages[...]))
    twice = jnp.tanh(half) + 1.0
    act = half * twice
    hidden[...] = act.astype(jnp.bfloat16)
    slope = 0.5 * (twice + act * (2.0 - twice))
    low_grad = (grad_hidden[:, span] * slope).astype(jnp.bfloat16)
    grad_pre[...] = low_grad
    grad_msg = dot(w_both_t[...], low_grad).astype(jnp.bfloat16).astype(jnp.float32)
    scale[...] = (grad_msg * (0.5 / in_degree[:, span].astype(jnp.float32))).T


def scatter(low, high, edges, chunks, total):
    one = jnp.bfloat16(1.0)
    zero = jnp.bfloat16(0.0)
    groups = CHUNK // PACK
    for step in edges:
        width = sum(rows for _, _, rows, _ in step)
        place = lax.broadcasted_iota(jnp.int32, (groups, PACK, width), 0) * PACK
        place = place + lax.broadcasted_iota(jnp.int32, (groups, PACK, width), 1)
        low_k = jnp.concatenate([low[m, :, s : s + r] for m, s, r, _ in step], axis=1)
        high_k = jnp.concatenate([high[m, :, s : s + r] for m, s, r, _ in step], axis=1)
        grads = jnp.concatenate([grad() for _, _, _, grad in step], axis=0)
        mark = jnp.where(low_k[None] == place.astype(jnp.bfloat16), one, zero)
        picker = jnp.concatenate(
            [jnp.where(high_k[None] == chunk, mark, zero) for chunk in chunks], axis=0
        ).reshape(len(chunks) * CHUNK, width)
        total[...] += dot(picker, grads)


def pairs(start, ref, nodes, grad_of):
    degree, rows, _ = ref.shape
    together = nodes // rows
    return [
        [
            (m, start, rows, functools.partial(grad_of, ref, m))
            for m in range(k * together, (k + 1) * together)
        ]
        for k in range(degree // together)
    ]


def fold(block, place, index, total):
    picks = picks_of(block, place)
    halves = []
    for half in range(len(picks)):
        terms = 0.0
        for t, pick in enumerate(picks):
            start = index * CHUNK + t * TILE
            hit = jnp.abs(pick - half) < 0.5
            terms += jnp.where(hit, total[start : start + TILE, :], 0.0)
        halves.append(terms)
    return jnp.concatenate(halves, axis=0).astype(jnp.bfloat16)


def early_kernel(low, high, slope, scale, grads, total):
    nodes = low.shape[2]

    def grad_of(ref, m):
        grads[m] = (ref[m].astype(jnp.float32) * scale[...]).astype(jnp.bfloat16)
        return grads[m]

    chunks = [chunk_of(place, nodes // CHUNK, (1, PACK, nodes)) for place in EARLY + LATE]
    total[...] = jnp.zeros_like(total)
    scatter(low, high, pairs(0, slope, nodes, grad_of), chunks, total)


def cross_kernel(start, low, high, slope, scale, before, cross, to_cross, grads, total):
    nodes = low.shape[2]

    def grad_of(ref, m):
        grads[m] = (ref[m].astype(jnp.float32) * scale[...]).astype(jnp.bfloat16)
        return grads[m]

    chunks = [chunk_of(EARLY[0], nodes // CHUNK, (1, PACK, nodes))]
    total[...] = before[:CHUNK, :]
    scatter(low, high, pairs(start, slope, nodes, grad_of), chunks, total)
    to_cross[...] = fold(cross, EARLY[0], 0, total)


def other_kernel(start, low, high, grads, before, west, east, to_other, total):
    nodes = low.shape[2]
    chunks = [chunk_of(place, nodes // CHUNK, (1, PACK, nodes)) for place in EARLY[1:]]
    total[...] = before[CHUNK : len(EARLY) * CHUNK, :]
    scatter(low, high, pairs(start, grads, nodes, lambda ref, m: ref[m]), chunks, total)
    to_other[0] = fold(west, EARLY[1], 0, total)
    to_other[1] = fold(east, EARLY[2], 1, total)


def all_pairs(parts, nodes):
    start, steps = 0, []
    for part in parts:
        steps += pairs(start, part, nodes, lambda ref, m: ref[m])
        start += part.shape[1]
    return steps


def late_kernel(
    start, low, high, grads, before, west, east, beside, to_west, to_east, to_beside, total
):
    nodes = low.shape[2]
    chunks = [chunk_of(place, nodes // CHUNK, (1, PACK, nodes)) for place in LATE]
    total[...] = before[len(EARLY) * CHUNK :, :]
    scatter(low, high, pairs(start, grads, nodes, lambda ref, m: ref[m]), chunks, total)
    to_west[...] = fold(west, 1, 0, total)
    to_east[...] = fold(east, 2, 1, total)
    to_beside[...] = fold(beside, 0, 2, total)


def own_kernel(low, high, *refs):
    *parts, total, recv = refs
    nodes = low.shape[2]
    chunks = [jnp.bfloat16(chunk) for chunk in range(nodes // CHUNK)]
    total[...] = jnp.zeros_like(total)
    scatter(low, high, all_pairs(parts, nodes), chunks, total)
    start = 0
    for part in parts:
        degree, rows, _ = part.shape
        terms = 0.0
        for m in range(degree):
            terms += part[m].astype(jnp.float32)
        recv[:, start : start + rows] = terms.T.astype(jnp.bfloat16)
        start += rows


def output_kernel(tiles, feats, cots, w_out, w_node_v_t, *refs):
    *parts, updated, direct = refs
    count = len(parts) // 2
    rows = parts[0].shape[1]
    for k in range(count):
        hidden, grad_pre = parts[k], parts[count + k]
        span = slice(k * rows, (k + 1) * rows)
        lane = lax.broadcasted_iota(jnp.int32, (1, rows), 1) + k * rows
        active = (lane < tiles[0] * TILE).astype(jnp.float32)
        node_out = dot(w_out[...], hidden[...])
        new = feats[:, span].astype(jnp.float32) + active * node_out
        updated[:, span] = new.astype(jnp.bfloat16)
        direct[:, span] = cots[:, span].astype(jnp.float32) + dot(w_node_v_t[...], grad_pre[...])


def pass_kernel(block, out):
    out[...] = block[...]


def add_kernel(left, right, more, west, east):
    to_west = left[...].astype(jnp.float32) + more[0].astype(jnp.float32)
    to_east = right[...].astype(jnp.float32) + more[1].astype(jnp.float32)
    west[...] = to_west.astype(jnp.bfloat16)
    east[...] = to_east.astype(jnp.bfloat16)


def back_kernel(start, inv_root, tiles, own, beside, across, feats, upper, *refs):
    *refs, total = refs
    sub = lax.axis_index("sub")
    offset = pl.multiple_of(tiles[0] // 2 * TILE, TILE)
    total[...] = own[...]
    near, far = beside[...].astype(jnp.float32), across[...].astype(jnp.float32)
    block = upper[...].astype(jnp.float32) + jnp.where(sub == 0, near, far)
    total[pl.ds(offset, block.shape[0]), :] += block
    if start:
        grad_send, weight = refs
    else:
        lower, before, grad_send, w_mine, w_beside, weight = refs
        block = lower[...].astype(jnp.float32) + jnp.where(sub == 0, far, near)
        total[: block.shape[0], :] += block
    rows = grad_send.shape[0]
    grad_send[...] = total[start : start + rows, :].astype(jnp.bfloat16)
    terms = dot(feats[:, start : start + rows], grad_send[...])
    if start:
        weight[...] = terms
        return
    weight[...] = (before[...] + terms) * inv_root
    lon = lax.axis_index("lon")
    lons, columns, _ = w_mine.shape
    for k in range(lons):
        band = (lon ^ k) * 2
        for out, core in ((w_mine, sub), (w_beside, 1 - sub)):
            spot = pl.multiple_of((band + core) * columns, columns)
            out[k] = weight[pl.ds(spot, columns), :].astype(out.dtype)


def terms_kernel(start, grad_send, recv, direct, w_send_t, w_recv_t, kept, sent, terms):
    span = slice(start, start + grad_send.shape[0])
    mine = lax.axis_index("ch")
    chans = kept.shape[0]
    grad_send_t = grad_send[...].astype(jnp.float32).T.astype(jnp.bfloat16)
    terms[...] = dot(w_send_t[...], grad_send_t) + dot(w_recv_t[...], recv[:, span])
    kept[...] = direct[:, span] + mine_of(terms, mine, chans)
    count = sent.shape[0] + 1
    for k in range(1, count):
        sent[k - 1] = mine_of(terms, lax.rem(mine + k, count), chans).astype(jnp.bfloat16)


def finish_kernel(count, *refs):
    kept, *others = refs[: count]
    *done, out = refs[count:]
    total = kept[...]
    for other in others:
        total += other[...].astype(jnp.float32)
    out[:, : kept.shape[1]] = total.astype(jnp.bfloat16)
    start = kept.shape[1]
    for part in done:
        out[:, start : start + part.shape[1]] = part[...]
        start += part.shape[1]


def sum_kernel(held, received, near, sent):
    half = near.shape[0]
    near[...] = held[:half] + received[:half].astype(jnp.float32)
    sent[...] = (held[half:] + received[half:].astype(jnp.float32)).astype(jnp.bfloat16)


def weight_kernel(held, received, out):
    out[...] = held[0] + received[0].astype(jnp.float32)


def shards(
    features,
    cotangent,
    senders,
    in_degree,
    tile_count,
    send_tiles,
    w_send,
    w_recv,
    bias_edge,
    w_msg,
    w_node_v,
    w_node_a,
    bias_node,
    w_out,
):
    chans, nodes = features.shape
    count = lax.axis_size("ch")
    lons = lax.axis_size("lon")
    hidden_all, chans_all = w_send.shape
    hid = hidden_all // count
    cycle = ("lon", "sub")
    shard_count = lax.axis_size(cycle)
    total_nodes = nodes * shard_count
    degree = senders.shape[0]
    slots = send_tiles.shape[1]
    slot_rows = send_tiles.shape[2] * TILE
    ext_len = nodes + slots * slot_rows
    bf16, f32 = jnp.bfloat16, jnp.float32
    shape = jax.ShapeDtypeStruct

    far_route = [(i, (i + (3 if i % 2 else -3)) % shard_count) for i in range(shard_count)]
    across_route = [(i, (i + (1 if i % 2 else -1)) % shard_count) for i in range(shard_count)]
    across = lambda block: lax.ppermute(block, cycle, across_route)
    degrees = in_degree[None, :]
    picks = jnp.transpose(send_tiles, (0, 2, 1))
    sub = lax.axis_index("sub")

    feat_blocks = gathered(features, "ch")

    whole_w = pltpu.VMEM((chans_all, hidden_all), bf16)
    (
        w_send_my,
        w_recv_my,
        w_out_my,
        features_held,
        w_send_t,
        w_recv_t,
        w_both_t,
        w_node_v_t,
        w_both,
        w_out_t,
    ) = call(
        weights_kernel,
        (
            shape((hid, chans_all), bf16),
            shape((hid, chans_all), bf16),
            shape((chans, hidden_all), bf16),
            shape((chans, nodes), bf16),
            shape((chans_all, hid), bf16),
            shape((chans_all, hid), bf16),
            shape((hid, hidden_all), bf16),
            shape((chans, hidden_all), bf16),
            shape((hidden_all, hidden_all), bf16),
            shape((hidden_all, chans_all), bf16),
        ),
        [w_msg, w_node_a, features, w_send, w_recv, w_node_v, w_out],
        away=7,
        scalars=0,
        scratch=[whole_w] * 5 + [pltpu.SemaphoreType.DMA((7,))],
        limit=WEIGHTS_LIMIT,
    )
    feat_blocks[0] = features_held

    block = shape((slot_rows + PACK, hid), bf16)
    feats, proj, upper, lower, beside, cross = call(
        functools.partial(project_kernel, count),
        (
            shape((chans_all, nodes), bf16),
            shape((nodes, hid), bf16),
            block,
            block,
            block,
            block,
        ),
        [tile_count, picks] + feat_blocks + [w_send_my],
    )
    west = shifted(upper, "lon", 1)
    east = shifted(lower, "lon", -1)
    cross = lax.ppermute(cross, cycle, far_route)
    base = call(
        receive_kernel,
        shape((nodes, hid), f32),
        [bias_edge[None, :], feats, w_recv_my],
        scalars=0,
    )
    base, senders, cotangent_late = lax.optimization_barrier((base, senders, cotangent))
    beside = shifted(beside, "sub", 1)
    cot_blocks = gathered(cotangent_late, "ch")
    low_cols, high_cols, low_rows, high_rows = call(
        edges_kernel,
        (
            shape((degree, nodes, LANES), bf16),
            shape((degree, nodes, LANES), bf16),
            shape((degree, PACK, nodes), bf16),
            shape((degree, PACK, nodes), bf16),
        ),
        [tile_count, senders, degrees],
        scalars=1,
    )
    cots, pre, grad_hidden = call(
        functools.partial(prepare_kernel, count),
        (
            shape((chans_all, nodes), bf16),
            shape((hidden_all, nodes), f32),
            shape((hidden_all, nodes), f32),
        ),
        [tile_count] + cot_blocks + [feats, w_node_v, bias_node[None, :], w_out_t],
        scalars=1,
    )

    part_shape = shape((degree, nodes, hid), bf16)
    part = call(
        near_kernel,
        part_shape,
        [low_cols, high_cols, proj, beside],
        scratch=[pltpu.VMEM((nodes + slot_rows, hid), bf16)],
        scalars=0,
    )
    west, east, part = lax.optimization_barrier((west, east, part))
    west_too = shifted(west, "sub", 1)
    east_too = shifted(east, "sub", 1)
    part, pre = lax.optimization_barrier((part, pre))
    part = call(
        line_kernel,
        part_shape,
        [low_cols, high_cols, part, west, east],
        scratch=[pltpu.VMEM((2 * slot_rows, hid), bf16)],
        scalars=0,
    )
    part, cross = lax.optimization_barrier((part, cross))
    cross_rows = call(
        cross_rows_kernel, shape((slot_rows, hid), bf16), [cross], scalars=0
    )
    halves = 2
    rows = nodes // halves
    slopes, messages, hiddens, grad_pres, grads = [], [], [], [], []
    for k in range(halves):
        message, slope = call(
            functools.partial(message_kernel, k * rows),
            (shape((hid, rows), bf16), shape((degree, rows, hid), bf16)),
            [low_cols, high_cols, base, degrees, part, cross_rows, west_too, east_too],
            scratch=[pltpu.VMEM((3 * slot_rows, hid), bf16), pltpu.VMEM((rows, hid), f32)],
            scalars=0,
        )
        slopes.append(slope)
        messages.append(gathered(message, "ch"))

    block = shape((slot_rows, hid), bf16)
    sums = shape((slots * slot_rows, hid), f32)
    grad_shape = shape((degree, rows, hid), bf16)
    for k in range(halves):
        hidden, grad_pre, scale = call(
            functools.partial(node_kernel, count, k * rows),
            (
                shape((hidden_all, rows), bf16),
                shape((hidden_all, rows), bf16),
                shape((rows, hid), f32),
            ),
            [degrees] + messages[k] + [w_both, w_both_t, pre, grad_hidden],
            scratch=[pltpu.VMEM((hidden_all, rows), bf16)],
            scalars=0,
        )
        hiddens.append(hidden)
        grad_pres.append(grad_pre)
        operands = [low_rows, high_rows, slopes[k], scale]
        if k == 0:
            grad, before = call(early_kernel, (grad_shape, sums), operands, scalars=0)
        else:
            to_cross, grad = call(
                functools.partial(cross_kernel, k * rows),
                (block, grad_shape),
                operands + [before, cross],
                scratch=[pltpu.VMEM((slot_rows, hid), f32)],
                scalars=0,
            )
            to_other = call(
                functools.partial(other_kernel, k * rows),
                shape((2, slot_rows, hid), bf16),
                [low_rows, high_rows, grad, before, west_too, east_too],
                scratch=[pltpu.VMEM((2 * slot_rows, hid), f32)],
                scalars=0,
            )
        grads.append(grad)

    before, to_other = lax.optimization_barrier((before, to_other))
    from_other = shifted(to_other, "sub", 1)
    from_cross = lax.ppermute(to_cross, cycle, far_route)
    to_west, to_east, to_beside = call(
        functools.partial(late_kernel, nodes - rows),
        (block, block, block),
        [low_rows, high_rows, grads[-1], before, west, east, beside],
        scratch=[pltpu.VMEM((len(LATE) * slot_rows, hid), f32)],
        scalars=0,
    )
    to_west, to_east = call(add_kernel, (block, block), [to_west, to_east, from_other], scalars=0)
    from_upper = shifted(to_west, "lon", -1)
    from_lower = shifted(to_east, "lon", 1)
    from_beside = shifted(to_beside, "sub", 1)
    to_west, grads[0] = lax.optimization_barrier((to_west, grads[0]))

    own, grad_recv = call(
        own_kernel,
        (shape((nodes, hid), f32), shape((hid, nodes), bf16)),
        [low_rows, high_rows] + grads,
        scalars=0,
    )
    own, hiddens[0] = lax.optimization_barrier((own, hiddens[0]))
    updated, direct = call(
        output_kernel,
        (shape((chans, nodes), bf16), shape((chans, nodes), f32)),
        [tile_count, features_held, cotangent, w_out_my, w_node_v_t] + hiddens + grad_pres,
        scalars=1,
    )
    direct, from_cross = lax.optimization_barrier((direct, from_cross))
    from_cross = call(pass_kernel, block, [from_cross], scalars=0, flops=10**9)
    columns = chans_all // shard_count
    inv_root = 1.0 / math.sqrt(total_nodes)
    inputs = [tile_count, own, from_beside, from_cross, feats, from_upper]
    weight_shape = shape((chans_all, hid), f32)
    grad_shape = shape((rows, hid), bf16)
    finals = []
    for k in reversed(range(halves)):
        kernel = functools.partial(back_kernel, k * rows, inv_root)
        if k:
            grad_send, weight = call(
                kernel,
                (grad_shape, weight_shape),
                inputs,
                scratch=[pltpu.VMEM((nodes, hid), f32)],
                scalars=1,
            )
        else:
            grad_send, w_mine, w_beside = call(
                kernel,
                (
                    grad_shape,
                    shape((lons, columns, hid), f32),
                    shape((lons, columns, hid), bf16),
                ),
                inputs + [from_lower, weight],
                scratch=[pltpu.VMEM(weight_shape.shape, f32), pltpu.VMEM((nodes, hid), f32)],
                scalars=1,
            )
            w_beside = shifted(w_beside, "sub", 1)
            w_beside, *finals = lax.optimization_barrier((w_beside, *finals))
        kept, sent = call(
            functools.partial(terms_kernel, k * rows),
            (shape((chans, rows), f32), shape((count - 1, chans, rows), bf16)),
            [grad_send, grad_recv, direct, w_send_t, w_recv_t],
            scratch=[pltpu.VMEM((chans_all, rows), f32)],
            scalars=0,
        )
        if k:
            weight, kept = lax.optimization_barrier((weight, kept))
        parts = [kept] + [shifted(sent[i - 1], "ch", i) for i in range(1, count)]
        grad_features = call(
            functools.partial(finish_kernel, count),
            shape((chans, nodes - k * rows), bf16),
            parts + finals,
            scalars=0,
        )
        finals = [grad_features]

    span = lons
    while span > 1:
        span //= 2
        w_mine, w_sent = call(
            sum_kernel,
            (shape((span, columns, hid), f32), shape((span, columns, hid), bf16)),
            [w_mine, w_beside],
            scalars=0,
        )
        w_beside = lax.ppermute(w_sent, "lon", [(i, i ^ span) for i in range(lons)])
    grad_w_send = call(
        weight_kernel, shape((columns, hid), f32), [w_mine, w_beside], scalars=0
    )
    return (updated, grad_features, grad_w_send.T)


def solution(mesh):
    nodes_last = P("ch", ("parts", "lon", "sub"))
    spread = ("parts", "lon", "sub")
    placed = (nodes_last, nodes_last, P(None, spread), P(spread), P(spread), P(spread, None, None))
    return jax.shard_map(
        shards,
        mesh=mesh,
        in_specs=placed + (P(),) * 8,
        out_specs=(nodes_last, nodes_last, P(("parts", "ch"), ("lon", "sub"))),
        check_vma=False,
    )
```

```python
import functools
import math

import jax
import jax.numpy as jnp
from jax import lax
from jax.experimental import pallas as pl
from jax.experimental.pallas import tpu as pltpu
from jax.sharding import PartitionSpec as P

TILE = 128
CHUNK = 256
LANES = 128
PACK = 16
MIB = 1 << 20
WEIGHTS_LIMIT = 52
NO_CHUNK = 64
SLOT_OF = ((3, 0), (1, 1), (4, 4), (2, 5), (0, 2), (5, 3))
EARLY, LATE = (3, 4, 5), (1, 2, 0)
OFF = -1e4


def shifted(block, axis, distance):
    size = lax.axis_size(axis)
    route = [((i - distance) % size, i) for i in range(size)]
    return lax.ppermute(block, axis, route)


def gathered(block, axis):
    return [block] + [shifted(block, axis, k) for k in range(1, lax.axis_size(axis))]


def dot(left, right):
    return jnp.dot(left, right, preferred_element_type=jnp.float32)


def dot_nt(left, right):
    return lax.dot_general(
        left, right, (((1,), (1,)), ((), ())), preferred_element_type=jnp.float32
    )


def sigmoid(value):
    return 0.5 * jnp.tanh(0.5 * value) + 0.5


def call(kernel, out_shape, operands, scratch=(), scalars=2, away=0, limit=24, flops=1024):
    vmem = pl.BlockSpec(memory_space=pltpu.VMEM)
    smem = pl.BlockSpec(memory_space=pltpu.SMEM)
    anywhere = pl.BlockSpec(memory_space=pltpu.HBM)
    return pl.pallas_call(
        kernel,
        out_shape=out_shape,
        in_specs=[smem] * scalars
        + [anywhere] * away
        + [vmem] * (len(operands) - scalars - away),
        out_specs=jax.tree.map(lambda _: vmem, out_shape),
        scratch_shapes=scratch,
        compiler_params=pltpu.CompilerParams(vmem_limit_bytes=limit * MIB),
        cost_estimate=pl.CostEstimate(flops=flops, bytes_accessed=1024, transcendentals=0),
    )(*operands)


def assemble(whole_ref, blocks, first):
    count = len(blocks)
    rows = blocks[0].shape[0]
    for k, block in enumerate(blocks):
        place = lax.rem(first - k + count, count) * rows
        whole_ref[pl.ds(pl.multiple_of(place, rows), rows), :] = block[...]


def mine_of(ref, index, rows):
    return ref[pl.ds(pl.multiple_of(index * rows, rows), rows), :]


def weights_kernel(*refs):
    sources, refs = refs[:7], refs[7:]
    w_send, w_recv, w_out, feats, w_send_t, w_recv_t, w_both_t, w_node_v_t, w_both, w_out_t = refs[:10]
    w_msg, w_node_v, w_node_a, w_out_all, turned, sems = refs[10:]
    mine = lax.axis_index("ch")
    hid = w_send.shape[0]
    targets = (w_msg, w_node_a, feats, w_send, w_recv, w_node_v, w_out_all)
    copies = []
    for k, (source, target) in enumerate(zip(sources, targets)):
        if k in (3, 4):
            source = source.at[pl.ds(pl.multiple_of(mine * hid, hid), hid), :]
        copies.append(pltpu.make_async_copy(source, target, sems.at[k]))
    for copy in copies:
        copy.start()
    for copy in copies[:2]:
        copy.wait()
    w_both[...] = dot(w_node_a[...], w_msg[...]).astype(jnp.bfloat16)
    turned[...] = w_both[...].T
    w_both_t[...] = mine_of(turned, mine, hid)
    for copy in copies[2:]:
        copy.wait()
    w_send_t[...] = w_send[...].T
    w_recv_t[...] = w_recv[...].T
    turned[...] = w_node_v[...].T
    w_node_v_t[...] = mine_of(turned, mine, w_node_v_t.shape[0])
    w_out_t[...] = w_out_all[...].T
    w_out[...] = mine_of(w_out_all, mine, w_out.shape[0])


def edges_kernel(tiles, senders, in_degree, low_cols, high_cols, low_rows, high_rows):
    degree, nodes = senders.shape
    lane = lax.broadcasted_iota(jnp.int32, (degree, nodes), 1)
    row = lax.broadcasted_iota(jnp.int32, (degree, nodes), 0)
    valid = (row < in_degree[...]) & (lane < tiles[0] * TILE)
    ids = senders[...]
    low = (ids & (CHUNK - 1)).astype(jnp.float32)
    high = jnp.where(valid, ids // CHUNK, NO_CHUNK).astype(jnp.float32)
    for m in range(degree):
        shape = (PACK, nodes)
        low_rows[m] = jnp.broadcast_to(low[m : m + 1], shape).astype(jnp.bfloat16)
        high_rows[m] = jnp.broadcast_to(high[m : m + 1], shape).astype(jnp.bfloat16)
    fill = jnp.zeros((PACK - degree, nodes), jnp.float32)
    depth = 2 * PACK
    both = jnp.concatenate([low, fill, high, fill], axis=0).T.astype(jnp.bfloat16)
    width = degree * LANES
    spot = lax.broadcasted_iota(jnp.int32, (depth, width), 0)
    group = lax.broadcasted_iota(jnp.int32, (depth, width), 1) // LANES
    for first, out in ((0, low_cols), (PACK, high_cols)):
        pick = (spot == group + first).astype(jnp.bfloat16)
        spread = dot(both, pick).astype(jnp.bfloat16)
        for m in range(degree):
            out[m] = spread[:, m * LANES : (m + 1) * LANES]


def project_kernel(count, tiles, picks, *refs):
    blocks = refs[:count]
    w_send, feats, proj, upper, lower, beside, cross = refs[count:]
    mine, sub = lax.axis_index("ch"), lax.axis_index("sub")
    first = tiles[0] // 2
    assemble(feats, blocks, mine)
    whole = feats[...]
    hid = proj.shape[1]
    proj[...] = (0.5 * dot(w_send[...], whole).T).astype(jnp.bfloat16)
    rows = upper.shape[0] - PACK
    upper[:rows, :] = proj[pl.ds(pl.multiple_of(first * TILE, TILE), rows), :]
    lower[:rows, :] = proj[:rows, :]
    spot = lax.broadcasted_iota(jnp.int32, (PACK, hid), 0)
    _, per_slot, slots = picks.shape
    half = slots // 2
    for start, out, lift in ((0, upper, first), (half, lower, 0)):
        marks = jnp.zeros((PACK, hid), jnp.float32)
        for k in range(half * per_slot):
            rel = picks[0, k % per_slot, start + k // per_slot] - lift
            marks = jnp.where(spot == k, rel.astype(jnp.float32), marks)
        out[rows:, :] = marks.astype(jnp.bfloat16)

    @pl.when(sub == 0)
    def _():
        beside[...] = upper[...]
        cross[...] = lower[...]

    @pl.when(sub != 0)
    def _():
        beside[...] = lower[...]
        cross[...] = upper[...]


def receive_kernel(bias, feats, w_recv, base):
    hid = base.shape[1]
    mine = lax.axis_index("ch")
    my_bias = jnp.zeros((1, hid), jnp.float32)
    for k in range(bias.shape[1] // hid):
        my_bias += jnp.where(mine == k, bias[:, k * hid : (k + 1) * hid], 0.0)
    recv = dot(w_recv[...], feats[...]).T
    base[...] = 0.5 * (recv.astype(jnp.bfloat16).astype(jnp.float32) + my_bias)


def prepare_kernel(count, tiles, *refs):
    blocks = refs[:count]
    feats, w_node_v, bias, w_out_t, cots, pre, grad_hidden = refs[count:]
    assemble(cots, blocks, lax.axis_index("ch"))
    column = jnp.broadcast_to(bias[...], (8, bias.shape[1])).T[:, :1]
    pre[...] = dot(w_node_v[...], feats[...]) + column
    lane = lax.broadcasted_iota(jnp.int32, (1, cots.shape[1]), 1)
    active = (lane < tiles[0] * TILE).astype(jnp.bfloat16)
    grad_hidden[...] = dot(w_out_t[...], cots[...] * active)


def chunk_of(place, first, shape):
    on_zero, on_one = (float(first + slot) for slot in SLOT_OF[place])
    chunk = jnp.where(lax.axis_index("sub") == 0, on_zero, on_one)
    return jnp.full(shape, chunk, jnp.float32).astype(jnp.bfloat16)


def picks_of(block, place):
    marks = block[CHUNK : CHUNK + PACK, :].astype(jnp.float32)
    per_slot = CHUNK // TILE
    half = len(SLOT_OF) // 2
    starts = [slot % half * per_slot for slot in SLOT_OF[place]]
    sub = lax.axis_index("sub")
    return [
        jnp.where(
            sub == 0,
            marks[starts[0] + t : starts[0] + t + 1],
            marks[starts[1] + t : starts[1] + t + 1],
        )
        for t in range(per_slot)
    ]


def fill(ext, start, block, place):
    for t, pick in enumerate(picks_of(block, place)):
        ext[start + t * TILE : start + (t + 1) * TILE, :] = jnp.where(
            pick > 0.5, block[TILE : 2 * TILE, :], block[:TILE, :]
        )


def pick_rows(low, high, chunks, ext):
    one = jnp.bfloat16(1.0)
    zero = jnp.bfloat16(0.0)
    lane = lax.broadcasted_iota(jnp.int32, low.shape, 1)
    marks = [
        jnp.where(low == (lane + half * LANES).astype(jnp.bfloat16), one, zero)
        for half in range(CHUNK // LANES)
    ]
    picker = jnp.concatenate(
        [jnp.where(high == chunk, mark, zero) for chunk in chunks for mark in marks], axis=1
    )
    return dot(picker, ext[...])


def near_kernel(low, high, proj, beside, part, ext):
    own = proj.shape[0]
    ext[:own, :] = proj[...]
    fill(ext, own, beside, 0)
    first = own // CHUNK
    chunks = [jnp.bfloat16(chunk) for chunk in range(first)]
    chunks.append(chunk_of(0, first, low.shape[1:]))

    def step(m, carry):
        part[m] = pick_rows(low[m], high[m], chunks, ext).astype(jnp.bfloat16)
        return carry

    lax.fori_loop(0, low.shape[0], step, 0, unroll=True)


def line_kernel(low, high, before, west, east, part, ext):
    first = low.shape[1] // CHUNK
    chunks = []
    for index, (place, block) in enumerate(((1, west), (2, east))):
        fill(ext, index * CHUNK, block, place)
        chunks.append(jnp.bfloat16(first + SLOT_OF[place][0]))

    def step(m, carry):
        more = pick_rows(low[m], high[m], chunks, ext)
        part[m] = (before[m].astype(jnp.float32) + more).astype(jnp.bfloat16)
        return carry

    lax.fori_loop(0, low.shape[0], step, 0, unroll=True)


def cross_rows_kernel(block, rows):
    fill(rows, 0, block, 3)


def message_kernel(
    start, low, high, base, in_degree, part, cross, west, east, message, slope, ext, total
):
    nodes = low.shape[1]
    degree, rows, hid = slope.shape
    first = nodes // CHUNK
    together = nodes // rows
    span = slice(start, start + rows)
    chunks = []
    ext[:CHUNK, :] = cross[...]
    for index, (place, block) in enumerate(((4, west), (5, east))):
        fill(ext, (index + 1) * CHUNK, block, place)
    for place in (3, 4, 5):
        chunks.append(chunk_of(place, first, (nodes, LANES)))
    total[...] = jnp.zeros_like(total)

    def rows_of(ref, k):
        return jnp.concatenate([ref[k * together + i, span, :] for i in range(together)], axis=0)

    def step(k, carry):
        low_k, high_k = rows_of(low, k), rows_of(high, k)
        half = pick_rows(low_k, high_k, chunks, ext) + rows_of(part, k).astype(jnp.float32)
        half += jnp.concatenate([base[span, :]] * together, axis=0)
        wide = jnp.concatenate([high_k] * pl.cdiv(hid, LANES), axis=1)[:, :hid]
        half = jnp.where(wide.astype(jnp.float32) < NO_CHUNK, half, OFF)
        twice = jnp.tanh(half) + 1.0
        act = half * twice
        grad = (twice + act * (2.0 - twice)).astype(jnp.bfloat16)
        terms = 0.0
        for i in range(together):
            terms += act[i * rows : (i + 1) * rows]
            slope[k * together + i] = grad[i * rows : (i + 1) * rows]
        total[...] += terms
        return carry

    lax.fori_loop(0, degree // together, step, 0, unroll=True)
    count = in_degree[:, span].astype(jnp.float32)
    message[...] = (total[...].T / count).astype(jnp.bfloat16)


def node_kernel(count, start, in_degree, *refs):
    blocks = refs[:count]
    w_both, w_both_t, pre, grad_hidden = refs[count : count + 4]
    hidden, grad_pre, scale, messages = refs[count + 4 :]
    assemble(messages, blocks, lax.axis_index("ch"))
    span = slice(start, start + hidden.shape[1])
    half = 0.5 * (pre[:, span] + dot(w_both[...], messages[...]))
    twice = jnp.tanh(half) + 1.0
    act = half * twice
    hidden[...] = act.astype(jnp.bfloat16)
    slope = 0.5 * (twice + act * (2.0 - twice))
    low_grad = (grad_hidden[:, span] * slope).astype(jnp.bfloat16)
    grad_pre[...] = low_grad
    grad_msg = dot(w_both_t[...], low_grad).astype(jnp.bfloat16).astype(jnp.float32)
    scale[...] = (grad_msg * (0.5 / in_degree[:, span].astype(jnp.float32))).T


def scatter(low, high, edges, chunks, total):
    one = jnp.bfloat16(1.0)
    zero = jnp.bfloat16(0.0)
    groups = CHUNK // PACK
    for step in edges:
        width = sum(rows for _, _, rows, _ in step)
        place = lax.broadcasted_iota(jnp.int32, (groups, PACK, width), 0) * PACK
        place = place + lax.broadcasted_iota(jnp.int32, (groups, PACK, width), 1)
        low_k = jnp.concatenate([low[m, :, s : s + r] for m, s, r, _ in step], axis=1)
        high_k = jnp.concatenate([high[m, :, s : s + r] for m, s, r, _ in step], axis=1)
        grads = jnp.concatenate([grad() for _, _, _, grad in step], axis=0)
        mark = jnp.where(low_k[None] == place.astype(jnp.bfloat16), one, zero)
        picker = jnp.concatenate(
            [jnp.where(high_k[None] == chunk, mark, zero) for chunk in chunks], axis=0
        ).reshape(len(chunks) * CHUNK, width)
        total[...] += dot(picker, grads)


def pairs(start, ref, nodes, grad_of):
    degree, rows, _ = ref.shape
    together = nodes // rows
    return [
        [
            (m, start, rows, functools.partial(grad_of, ref, m))
            for m in range(k * together, (k + 1) * together)
        ]
        for k in range(degree // together)
    ]


def fold(block, place, index, total):
    picks = picks_of(block, place)
    halves = []
    for half in range(len(picks)):
        terms = 0.0
        for t, pick in enumerate(picks):
            start = index * CHUNK + t * TILE
            hit = jnp.abs(pick - half) < 0.5
            terms += jnp.where(hit, total[start : start + TILE, :], 0.0)
        halves.append(terms)
    return jnp.concatenate(halves, axis=0).astype(jnp.bfloat16)


def early_kernel(low, high, slope, scale, grads, total):
    nodes = low.shape[2]

    def grad_of(ref, m):
        grads[m] = (ref[m].astype(jnp.float32) * scale[...]).astype(jnp.bfloat16)
        return grads[m]

    chunks = [chunk_of(place, nodes // CHUNK, (1, PACK, nodes)) for place in EARLY]
    total[...] = jnp.zeros_like(total)
    scatter(low, high, pairs(0, slope, nodes, grad_of), chunks, total)


def cross_kernel(start, low, high, slope, scale, before, cross, to_cross, grads, total):
    nodes = low.shape[2]

    def grad_of(ref, m):
        grads[m] = (ref[m].astype(jnp.float32) * scale[...]).astype(jnp.bfloat16)
        return grads[m]

    chunks = [chunk_of(EARLY[0], nodes // CHUNK, (1, PACK, nodes))]
    total[...] = before[:CHUNK, :]
    scatter(low, high, pairs(start, slope, nodes, grad_of), chunks, total)
    to_cross[...] = fold(cross, EARLY[0], 0, total)


def other_kernel(start, low, high, grads, before, west, east, to_other, total):
    nodes = low.shape[2]
    chunks = [chunk_of(place, nodes // CHUNK, (1, PACK, nodes)) for place in EARLY[1:]]
    total[...] = before[CHUNK:, :]
    scatter(low, high, pairs(start, grads, nodes, lambda ref, m: ref[m]), chunks, total)
    to_other[0] = fold(west, EARLY[1], 0, total)
    to_other[1] = fold(east, EARLY[2], 1, total)


def all_pairs(parts, nodes):
    start, steps = 0, []
    for part in parts:
        steps += pairs(start, part, nodes, lambda ref, m: ref[m])
        start += part.shape[1]
    return steps


def late_kernel(low, high, *refs):
    *parts, west, east, beside, to_west, to_east, to_beside, total = refs
    nodes = low.shape[2]
    first = nodes // CHUNK
    chunks = [chunk_of(place, first, (1, PACK, nodes)) for place in LATE]
    total[...] = jnp.zeros_like(total)
    scatter(low, high, all_pairs(parts, nodes), chunks, total)
    to_west[...] = fold(west, 1, 0, total)
    to_east[...] = fold(east, 2, 1, total)
    to_beside[...] = fold(beside, 0, 2, total)


def own_kernel(low, high, *refs):
    *parts, total, recv = refs
    nodes = low.shape[2]
    chunks = [jnp.bfloat16(chunk) for chunk in range(nodes // CHUNK)]
    total[...] = jnp.zeros_like(total)
    scatter(low, high, all_pairs(parts, nodes), chunks, total)
    start = 0
    for part in parts:
        degree, rows, _ = part.shape
        terms = 0.0
        for m in range(degree):
            terms += part[m].astype(jnp.float32)
        recv[:, start : start + rows] = terms.T.astype(jnp.bfloat16)
        start += rows


def output_kernel(tiles, feats, cots, w_out, w_node_v_t, *refs):
    *parts, updated, direct = refs
    count = len(parts) // 2
    rows = parts[0].shape[1]
    for k in range(count):
        hidden, grad_pre = parts[k], parts[count + k]
        span = slice(k * rows, (k + 1) * rows)
        lane = lax.broadcasted_iota(jnp.int32, (1, rows), 1) + k * rows
        active = (lane < tiles[0] * TILE).astype(jnp.float32)
        node_out = dot(w_out[...], hidden[...])
        new = feats[:, span].astype(jnp.float32) + active * node_out
        updated[:, span] = new.astype(jnp.bfloat16)
        direct[:, span] = cots[:, span].astype(jnp.float32) + dot(w_node_v_t[...], grad_pre[...])


def across_kernel(left, right, across, west, east):
    sub = lax.axis_index("sub")
    other = across[...].astype(jnp.float32)
    to_west = left[...].astype(jnp.float32) + jnp.where(sub == 0, 0.0, other)
    to_east = right[...].astype(jnp.float32) + jnp.where(sub == 0, other, 0.0)
    west[...] = to_west.astype(west.dtype)
    east[...] = to_east.astype(east.dtype)


def add_kernel(left, right, more, west, east):
    west[...] = (left[...] + more[0].astype(jnp.float32)).astype(jnp.bfloat16)
    east[...] = (right[...] + more[1].astype(jnp.float32)).astype(jnp.bfloat16)


def band_bits(place, lons):
    bits, weight = 0, 1
    while weight < lons:
        bits += weight if place * weight * 2 // lons % 2 else 0
        weight *= 2
    return bits


def back_kernel(start, inv_root, tiles, own, beside, feats, upper, *refs):
    *refs, total = refs
    sub = lax.axis_index("sub")
    offset = pl.multiple_of(tiles[0] // 2 * TILE, TILE)
    total[...] = own[...]
    near = beside[...].astype(jnp.float32)
    block = upper[...].astype(jnp.float32) + jnp.where(sub == 0, near, 0.0)
    total[pl.ds(offset, block.shape[0]), :] += block
    if start:
        grad_send, weight = refs
    else:
        lower, before, grad_send, w_mine, w_beside, weight = refs
        block = lower[...].astype(jnp.float32) + jnp.where(sub == 0, 0.0, near)
        total[: block.shape[0], :] += block
    rows = grad_send.shape[0]
    grad_send[...] = total[start : start + rows, :].astype(jnp.bfloat16)
    terms = dot(feats[:, start : start + rows], grad_send[...])
    if start:
        weight[...] = terms
        return
    weight[...] = (before[...] + terms) * inv_root
    lon = lax.axis_index("lon")
    lons, columns, _ = w_mine.shape
    for k in range(lons):
        band = (lon ^ band_bits(k, lons)) * 2
        for out, core in ((w_mine, sub), (w_beside, 1 - sub)):
            spot = pl.multiple_of((band + core) * columns, columns)
            out[k] = weight[pl.ds(spot, columns), :].astype(out.dtype)


def terms_kernel(start, grad_send, recv, direct, w_send_t, w_recv_t, kept, sent, terms):
    span = slice(start, start + grad_send.shape[0])
    mine = lax.axis_index("ch")
    chans = kept.shape[0]
    grad_send_t = grad_send[...].astype(jnp.float32).T.astype(jnp.bfloat16)
    terms[...] = dot(w_send_t[...], grad_send_t) + dot(w_recv_t[...], recv[:, span])
    kept[...] = direct[:, span] + mine_of(terms, mine, chans)
    count = sent.shape[0] + 1
    for k in range(1, count):
        sent[k - 1] = mine_of(terms, lax.rem(mine + k, count), chans).astype(jnp.bfloat16)


def finish_kernel(count, *refs):
    kept, *others = refs[: count]
    *done, out = refs[count:]
    total = kept[...]
    for other in others:
        total += other[...].astype(jnp.float32)
    out[:, : kept.shape[1]] = total.astype(jnp.bfloat16)
    start = kept.shape[1]
    for part in done:
        out[:, start : start + part.shape[1]] = part[...]
        start += part.shape[1]


def sum_kernel(held, received, near, sent):
    half = near.shape[0]
    near[...] = held[:half] + received[:half].astype(jnp.float32)
    sent[...] = (held[half:] + received[half:].astype(jnp.float32)).astype(jnp.bfloat16)


def weight_kernel(held, received, out):
    out[...] = held[0] + received[0].astype(jnp.float32)


def shards(
    features,
    cotangent,
    senders,
    in_degree,
    tile_count,
    send_tiles,
    w_send,
    w_recv,
    bias_edge,
    w_msg,
    w_node_v,
    w_node_a,
    bias_node,
    w_out,
):
    chans, nodes = features.shape
    count = lax.axis_size("ch")
    lons = lax.axis_size("lon")
    hidden_all, chans_all = w_send.shape
    hid = hidden_all // count
    cycle = ("lon", "sub")
    shard_count = lax.axis_size(cycle)
    total_nodes = nodes * shard_count
    degree = senders.shape[0]
    slots = send_tiles.shape[1]
    slot_rows = send_tiles.shape[2] * TILE
    ext_len = nodes + slots * slot_rows
    bf16, f32 = jnp.bfloat16, jnp.float32
    shape = jax.ShapeDtypeStruct

    far_route = [(i, (i + (3 if i % 2 else -3)) % shard_count) for i in range(shard_count)]
    across_route = [(i, (i + (1 if i % 2 else -1)) % shard_count) for i in range(shard_count)]
    across = lambda block: lax.ppermute(block, cycle, across_route)
    degrees = in_degree[None, :]
    picks = jnp.transpose(send_tiles, (0, 2, 1))
    sub = lax.axis_index("sub")

    feat_blocks = gathered(features, "ch")

    whole_w = pltpu.VMEM((chans_all, hidden_all), bf16)
    (
        w_send_my,
        w_recv_my,
        w_out_my,
        features_held,
        w_send_t,
        w_recv_t,
        w_both_t,
        w_node_v_t,
        w_both,
        w_out_t,
    ) = call(
        weights_kernel,
        (
            shape((hid, chans_all), bf16),
            shape((hid, chans_all), bf16),
            shape((chans, hidden_all), bf16),
            shape((chans, nodes), bf16),
            shape((chans_all, hid), bf16),
            shape((chans_all, hid), bf16),
            shape((hid, hidden_all), bf16),
            shape((chans, hidden_all), bf16),
            shape((hidden_all, hidden_all), bf16),
            shape((hidden_all, chans_all), bf16),
        ),
        [w_msg, w_node_a, features, w_send, w_recv, w_node_v, w_out],
        away=7,
        scalars=0,
        scratch=[whole_w] * 5 + [pltpu.SemaphoreType.DMA((7,))],
        limit=WEIGHTS_LIMIT,
    )
    feat_blocks[0] = features_held

    block = shape((slot_rows + PACK, hid), bf16)
    feats, proj, upper, lower, beside, cross = call(
        functools.partial(project_kernel, count),
        (
            shape((chans_all, nodes), bf16),
            shape((nodes, hid), bf16),
            block,
            block,
            block,
            block,
        ),
        [tile_count, picks] + feat_blocks + [w_send_my],
    )
    west = shifted(upper, "lon", 1)
    east = shifted(lower, "lon", -1)
    cross = lax.ppermute(cross, cycle, far_route)
    base = call(
        receive_kernel,
        shape((nodes, hid), f32),
        [bias_edge[None, :], feats, w_recv_my],
        scalars=0,
    )
    base, senders, cotangent_late = lax.optimization_barrier((base, senders, cotangent))
    beside = shifted(beside, "sub", 1)
    cot_blocks = gathered(cotangent_late, "ch")
    low_cols, high_cols, low_rows, high_rows = call(
        edges_kernel,
        (
            shape((degree, nodes, LANES), bf16),
            shape((degree, nodes, LANES), bf16),
            shape((degree, PACK, nodes), bf16),
            shape((degree, PACK, nodes), bf16),
        ),
        [tile_count, senders, degrees],
        scalars=1,
    )
    cots, pre, grad_hidden = call(
        functools.partial(prepare_kernel, count),
        (
            shape((chans_all, nodes), bf16),
            shape((hidden_all, nodes), f32),
            shape((hidden_all, nodes), f32),
        ),
        [tile_count] + cot_blocks + [feats, w_node_v, bias_node[None, :], w_out_t],
        scalars=1,
    )

    part_shape = shape((degree, nodes, hid), bf16)
    part = call(
        near_kernel,
        part_shape,
        [low_cols, high_cols, proj, beside],
        scratch=[pltpu.VMEM((nodes + slot_rows, hid), bf16)],
        scalars=0,
    )
    west, east, part = lax.optimization_barrier((west, east, part))
    west_too = shifted(west, "sub", 1)
    east_too = shifted(east, "sub", 1)
    part, pre = lax.optimization_barrier((part, pre))
    part = call(
        line_kernel,
        part_shape,
        [low_cols, high_cols, part, west, east],
        scratch=[pltpu.VMEM((2 * slot_rows, hid), bf16)],
        scalars=0,
    )
    part, cross = lax.optimization_barrier((part, cross))
    cross_rows = call(
        cross_rows_kernel, shape((slot_rows, hid), bf16), [cross], scalars=0
    )
    halves = 2
    rows = nodes // halves
    slopes, messages, hiddens, grad_pres, grads = [], [], [], [], []
    for k in range(halves):
        message, slope = call(
            functools.partial(message_kernel, k * rows),
            (shape((hid, rows), bf16), shape((degree, rows, hid), bf16)),
            [low_cols, high_cols, base, degrees, part, cross_rows, west_too, east_too],
            scratch=[pltpu.VMEM((3 * slot_rows, hid), bf16), pltpu.VMEM((rows, hid), f32)],
            scalars=0,
        )
        slopes.append(slope)
        messages.append(gathered(message, "ch"))

    block = shape((slot_rows, hid), bf16)
    sums = shape((len(EARLY) * slot_rows, hid), f32)
    grad_shape = shape((degree, rows, hid), bf16)
    for k in range(halves):
        hidden, grad_pre, scale = call(
            functools.partial(node_kernel, count, k * rows),
            (
                shape((hidden_all, rows), bf16),
                shape((hidden_all, rows), bf16),
                shape((rows, hid), f32),
            ),
            [degrees] + messages[k] + [w_both, w_both_t, pre, grad_hidden],
            scratch=[pltpu.VMEM((hidden_all, rows), bf16)],
            scalars=0,
        )
        hiddens.append(hidden)
        grad_pres.append(grad_pre)
        operands = [low_rows, high_rows, slopes[k], scale]
        if k == 0:
            grad, before = call(early_kernel, (grad_shape, sums), operands, scalars=0)
        else:
            to_cross, grad = call(
                functools.partial(cross_kernel, k * rows),
                (block, grad_shape),
                operands + [before, cross],
                scratch=[pltpu.VMEM((slot_rows, hid), f32)],
                scalars=0,
            )
            to_other = call(
                functools.partial(other_kernel, k * rows),
                shape((2, slot_rows, hid), bf16),
                [low_rows, high_rows, grad, before, west_too, east_too],
                scratch=[pltpu.VMEM((2 * slot_rows, hid), f32)],
                scalars=0,
            )
        grads.append(grad)

    grads[0], to_other = lax.optimization_barrier((grads[0], to_other))
    from_other = shifted(to_other, "sub", 1)
    from_cross = across(to_cross)
    to_west, to_east, to_beside = call(
        late_kernel,
        (block, block, block),
        [low_rows, high_rows] + grads + [west, east, beside],
        scratch=[pltpu.VMEM((len(LATE) * slot_rows, hid), f32)],
        scalars=0,
    )
    wide = shape((slot_rows, hid), f32)
    to_west, to_east = call(
        across_kernel, (wide, wide), [to_west, to_east, from_cross], scalars=0, flops=15 * 10**8
    )
    to_west, to_east = call(add_kernel, (block, block), [to_west, to_east, from_other], scalars=0)
    from_upper = shifted(to_west, "lon", -1)
    from_lower = shifted(to_east, "lon", 1)
    from_beside = shifted(to_beside, "sub", 1)
    to_west, grads[0] = lax.optimization_barrier((to_west, grads[0]))

    own, grad_recv = call(
        own_kernel,
        (shape((nodes, hid), f32), shape((hid, nodes), bf16)),
        [low_rows, high_rows] + grads,
        scalars=0,
    )
    own, hiddens[0] = lax.optimization_barrier((own, hiddens[0]))
    updated, direct = call(
        output_kernel,
        (shape((chans, nodes), bf16), shape((chans, nodes), f32)),
        [tile_count, features_held, cotangent, w_out_my, w_node_v_t] + hiddens + grad_pres,
        scalars=1,
    )
    columns = chans_all // shard_count
    inv_root = 1.0 / math.sqrt(total_nodes)
    inputs = [tile_count, own, from_beside, feats, from_upper]
    weight_shape = shape((chans_all, hid), f32)
    grad_shape = shape((rows, hid), bf16)
    finals = []
    for k in reversed(range(halves)):
        kernel = functools.partial(back_kernel, k * rows, inv_root)
        if k:
            grad_send, weight = call(
                kernel,
                (grad_shape, weight_shape),
                inputs,
                scratch=[pltpu.VMEM((nodes, hid), f32)],
                scalars=1,
            )
        else:
            grad_send, w_mine, w_beside = call(
                kernel,
                (
                    grad_shape,
                    shape((lons, columns, hid), f32),
                    shape((lons, columns, hid), bf16),
                ),
                inputs + [from_lower, weight],
                scratch=[pltpu.VMEM(weight_shape.shape, f32), pltpu.VMEM((nodes, hid), f32)],
                scalars=1,
            )
            w_beside = shifted(w_beside, "sub", 1)
            w_beside, *finals = lax.optimization_barrier((w_beside, *finals))
        kept, sent = call(
            functools.partial(terms_kernel, k * rows),
            (shape((chans, rows), f32), shape((count - 1, chans, rows), bf16)),
            [grad_send, grad_recv, direct, w_send_t, w_recv_t],
            scratch=[pltpu.VMEM((chans_all, rows), f32)],
            scalars=0,
        )
        if k:
            weight, kept = lax.optimization_barrier((weight, kept))
        parts = [kept] + [shifted(sent[i - 1], "ch", i) for i in range(1, count)]
        grad_features = call(
            functools.partial(finish_kernel, count),
            shape((chans, nodes - k * rows), bf16),
            parts + finals,
            scalars=0,
        )
        finals = [grad_features]

    span = lons
    while span > 1:
        span //= 2
        w_mine, w_sent = call(
            sum_kernel,
            (shape((span, columns, hid), f32), shape((span, columns, hid), bf16)),
            [w_mine, w_beside],
            scalars=0,
        )
        apart = lons // span // 2
        w_beside = lax.ppermute(w_sent, "lon", [(i, i ^ apart) for i in range(lons)])
    grad_w_send = call(
        weight_kernel, shape((columns, hid), f32), [w_mine, w_beside], scalars=0
    )
    return (updated, grad_features, grad_w_send.T)


def solution(mesh):
    nodes_last = P("ch", ("parts", "lon", "sub"))
    spread = ("parts", "lon", "sub")
    placed = (nodes_last, nodes_last, P(None, spread), P(spread), P(spread), P(spread, None, None))
    return jax.shard_map(
        shards,
        mesh=mesh,
        in_specs=placed + (P(),) * 8,
        out_specs=(nodes_last, nodes_last, P(("parts", "ch"), ("lon", "sub"))),
        check_vma=False,
    )
```
